32 devices in a mesh: dp: 8 (over z, x), tensor: 4 (over y, core).
Axes of the slice: x: 2, y: 2, z: 4, core: 2. Of those that a mesh axis runs over, the one named last changes fastest.
Arguments:
- inputs: bfloat16 [8, 256, 768], P('dp'), may hold values from -6 to 6
- encoded: bfloat16 [8, 512, 768], P('dp', 'tensor'), may hold values from -6 to 6
- dec_len: int32 [8], P('dp'), may hold values from 1 to 256
- enc_len: int32 [8], P('dp'), may hold values from 1 to 512
- language: int32 [8], P('dp'), may hold values from 0 to 7
- objective: int32 [8], P('dp'), may hold values from 0 to 1
- distance_bucket: int32 [256], replicated, may hold values from 0 to 31, as said below
- token_weights: float32 [16, 256], replicated, may hold values from 0.25 to 2
- cotangent: bfloat16 [8, 256, 768], P('dp'), may hold values from -6 to 6
- gain_self: float32 [768], replicated, may hold values from 0.5 to 1.5
- self_query: bfloat16 [768, 768], P(None, 'tensor'), may hold values from -0.21875 to 0.21875
- self_key: bfloat16 [768, 768], P(None, 'tensor'), may hold values from -0.21875 to 0.21875
- self_value: bfloat16 [768, 768], P(None, 'tensor'), may hold values from -0.21875 to 0.21875
- self_output: bfloat16 [768, 768], P('tensor'), may hold values from -1.25 to 1.25
- bias_table: float32 [32, 12], P(None, 'tensor'), may hold values from -4 to 4
- gain_cross: float32 [768], replicated, may hold values from 0.5 to 1.5
- cross_query: bfloat16 [768, 768], P(None, 'tensor'), may hold values from -0.21875 to 0.21875
- cross_key: bfloat16 [768, 768], P(None, 'tensor'), may hold values from -0.21875 to 0.21875
- cross_value: bfloat16 [768, 768], P(None, 'tensor'), may hold values from -0.21875 to 0.21875
- cross_output: bfloat16 [768, 768], P('tensor'), may hold values from -1.25 to 1.25
- gain_ffn: float32 [768], replicated, may hold values from 0.5 to 1.5
- ffn_up: bfloat16 [768, 3072], P(None, 'tensor'), may hold values from -0.21875 to 0.21875
- ffn_down: bfloat16 [3072, 768], P('tensor'), may hold values from -0.109375 to 0.109375
Outputs:
- layer_out: bfloat16 [8, 256, 768], P('dp')
- input_grad: bfloat16 [8, 256, 768], P('dp')
- encoded_grad: bfloat16 [8, 512, 768], P('dp', 'tensor')
- grad_gain_self: float32 [768], P('dp')
- grad_self_query: float32 [768, 768], P('dp', 'tensor')
- grad_self_key: float32 [768, 768], P('dp', 'tensor')
- grad_self_value: float32 [768, 768], P('dp', 'tensor')
- grad_self_output: float32 [768, 768], P('tensor', 'dp')
- grad_bias_table: float32 [32, 12], P(None, 'tensor')
- grad_gain_cross: float32 [768], P('dp')
- grad_cross_query: float32 [768, 768], P('dp', 'tensor')
- grad_cross_key: float32 [768, 768], P('dp', 'tensor')
- grad_cross_value: float32 [768, 768], P('dp', 'tensor')
- grad_cross_output: float32 [768, 768], P('tensor', 'dp')
- grad_gain_ffn: float32 [768], P('dp')
- grad_ffn_up: float32 [768, 3072], P('dp', 'tensor')
- grad_ffn_down: float32 [3072, 768], P('tensor', 'dp')
The draws below stay inside these ranges and needn't reach their ends.
Inputs may be any that keep to these rules, and one draw needn't show every extreme that they name: distance_bucket never falls as the distance grows, is 0 at distance 0 and 31 at distance 256 - 1.
All inputs are finite; a program needn't handle non-finite values.
Results may differ from the reference program's by a relative error of at most 0.033.
Values may be sent and summed in bfloat16 or wider, within the bound.
No kernel may reach another device: no remote copies, remote signals or barrier semaphores. Data moves between devices by JAX's collectives and lax.ppermute only.
A program may use at most 128 MiB of HBM per device.

```python
import jax
import jax.numpy as jnp
from jax import lax

D = 768
HEADS = 12
HEAD_DIM = 64
FF = 3072
BUCKETS = 32
LANGS = 8
LEN = 256
ENC_LEN = 512
SEQ_DEV = 1
SEQS = 8
N_TENSOR = 4


def draw_distance_bucket(key, part):
    key = jax.random.fold_in(key, 11)
    shuffled = jax.random.permutation(key, LEN - 1) + 1
    bounds = jnp.sort(shuffled[:BUCKETS - 1])
    distance = jnp.arange(LEN)
    return jnp.sum((distance[:, None] >= bounds[None, :]).astype(jnp.int32), 1).astype(jnp.int32)


def with_ends(values, rng, least, top_value):
    dims = values.shape
    place = [jax.random.randint(jax.random.fold_in(rng, axis), (), 0, dims[axis]) for axis in range(len(dims))]
    values = values.at[tuple(place)].set(least)
    longest = dims.index(max(dims))
    place[longest] = (place[longest] + 1) % dims[longest]
    return values.at[tuple(place)].set(top_value)


def strengthened(values, own_key, source, target, parts, factor):
    def block_of(dim):
        return (jnp.arange(values.shape[dim]) // (values.shape[dim] // parts)).reshape((-1,) + (1,) * (values.ndim - 1 - dim))

    one_side = jax.random.permutation(own_key, parts)[block_of(target)]
    far = (block_of(target) + parts // 2) % parts
    return jnp.where((block_of(source) == one_side) | (block_of(source) == far), factor * values, values)


def steps_of(key, extent, split, low, largest):
    def one(dim, parts):
        steps = jax.random.uniform(jax.random.fold_in(jax.random.fold_in(key, 6), dim), (parts,), jnp.float32, low / len(split), largest / len(split))
        return jnp.repeat(jnp.exp(steps), extent[dim] // parts).reshape((-1,) + (1,) * (len(extent) - dim - 1))

    level = one(*split[0])
    for cut in split[1:]:
        level = level * one(*cut)
    return level


def gaussian(own_key, shape, deviation, bound, cuts=(), held_as=jnp.bfloat16):
    loudness = steps_of(own_key, shape, cuts, -0.22, 0.18) if cuts else 1.0
    values = jax.random.normal(own_key, shape, jnp.float32) * deviation * loudness
    return jnp.minimum(jnp.maximum(values, -bound), bound).astype(held_as)


def gaussian_with(rng, shape, deviation, reach, cuts, heavy, kind=jnp.bfloat16):
    values = deviation * jax.random.normal(rng, shape, jnp.float32)
    if cuts:
        values = values * steps_of(rng, shape, cuts, -0.22, 0.18)
    return jnp.clip(strengthened(values, jax.random.fold_in(rng, 3), *heavy), -reach, reach).astype(kind)


def setup_inputs(seed: int = 0) -> dict:
    arg_keys = jax.random.split(jax.random.key(seed), 24)
    inputs = gaussian(arg_keys[0], (SEQS, LEN, D), 1.0, 6.0, ((0, 8),))
    encoded = gaussian(arg_keys[1], (SEQS, ENC_LEN, D), 1.0, 6.0, ((0, 8), (1, 4)))
    dec_len = with_ends(jax.random.randint(arg_keys[2], (SEQS,), 1, LEN + 1), jax.random.fold_in(arg_keys[2], 1), 1, LEN).astype(jnp.int32)
    enc_len = with_ends(jax.random.randint(arg_keys[3], (SEQS,), 1, ENC_LEN + 1), jax.random.fold_in(arg_keys[3], 1), 1, ENC_LEN).astype(jnp.int32)
    language = with_ends(jax.random.randint(arg_keys[4], (SEQS,), 0, LANGS), jax.random.fold_in(arg_keys[4], 1), 0, LANGS - 1).astype(jnp.int32)
    objective = with_ends(jax.random.randint(arg_keys[5], (SEQS,), 0, 2), jax.random.fold_in(arg_keys[5], 1), 0, 1).astype(jnp.int32)
    distance_bucket = draw_distance_bucket(jax.random.fold_in(arg_keys[23], 71), 0)
    token_weights = jnp.clip(jax.random.uniform(arg_keys[7], (2 * LANGS, LEN), jnp.float32, 0.25, 2.0), 0.25, 2.0)
    cotangent = gaussian_with(arg_keys[8], (SEQS, LEN, D), 1.0, 6.0, ((0, 8),), (0, 2, 8, 2.0))
    gain_self = jnp.clip(1.0 + 0.1 * jax.random.normal(arg_keys[9], (D,), jnp.float32), 0.5, 1.5)
    self_query = gaussian(arg_keys[10], (D, HEADS * HEAD_DIM), D ** -0.5, 0.21875, ((1, 4),))
    self_key = gaussian(arg_keys[11], (D, HEADS * HEAD_DIM), D ** -0.5, 0.21875, ((1, 4),))
    self_value = gaussian(arg_keys[12], (D, HEADS * HEAD_DIM), D ** -0.5, 0.21875, ((1, 4),))
    self_output = gaussian(arg_keys[13], (HEADS * HEAD_DIM, D), (HEADS * HEAD_DIM // 32) ** -0.5, 1.25, ((0, 4),))
    bias_table = gaussian(arg_keys[14], (BUCKETS, HEADS), 1.0, 4.0, ((1, 4),), jnp.float32)
    gain_cross = jnp.clip(1.0 + 0.1 * jax.random.normal(arg_keys[15], (D,), jnp.float32), 0.5, 1.5)
    cross_query = gaussian(arg_keys[16], (D, HEADS * HEAD_DIM), D ** -0.5, 0.21875, ((1, 4),))
    cross_key = gaussian(arg_keys[17], (D, HEADS * HEAD_DIM), D ** -0.5, 0.21875, ((1, 4),))
    cross_value = gaussian(arg_keys[18], (D, HEADS * HEAD_DIM), D ** -0.5, 0.21875, ((1, 4),))
    cross_output = gaussian(arg_keys[19], (HEADS * HEAD_DIM, D), (HEADS * HEAD_DIM // 32) ** -0.5, 1.25, ((0, 4),))
    gain_ffn = jnp.clip(1.0 + 0.1 * jax.random.normal(arg_keys[20], (D,), jnp.float32), 0.5, 1.5)
    ffn_up = gaussian(arg_keys[21], (D, FF), D ** -0.5, 0.21875, ((1, 4),))
    ffn_down = gaussian(arg_keys[22], (FF, D), FF ** -0.5, 0.109375, ((0, 4),))
    return dict(inputs=inputs, encoded=encoded, dec_len=dec_len, enc_len=enc_len, language=language, objective=objective, distance_bucket=distance_bucket, token_weights=token_weights, cotangent=cotangent, gain_self=gain_self, self_query=self_query, self_key=self_key, self_value=self_value, self_output=self_output, bias_table=bias_table, gain_cross=gain_cross, cross_query=cross_query, cross_key=cross_key, cross_value=cross_value, cross_output=cross_output, gain_ffn=gain_ffn, ffn_up=ffn_up, ffn_down=ffn_down)


EPSILON = 1e-06
SCALE = 0.125
NEGATIVE = -1e+30
PRECISE = lax.Precision.HIGHEST

@jax.custom_vjp
def low(v):
    return lax.optimization_barrier(v.astype(jnp.bfloat16)).astype(jnp.float32)

@jax.custom_vjp
def low_back(v):
    return v

def low_keep(v):
    return (low(v), None)

def low_pass(kept, grad):
    return (grad,)

def back_keep(v):
    return (v, None)

def back_low(kept, grad):
    return (low(grad),)
low.defvjp(low_keep, low_pass)
low_back.defvjp(back_keep, back_low)

def rms_norm(resid, gain):
    return resid * lax.rsqrt(lax.optimization_barrier(jnp.mean(resid * resid, -1, keepdims=True)) + EPSILON) * gain

def smooth_gate(value):
    return 0.5 * value * (1.0 + jnp.tanh(0.7978845608028654 * (value + 0.044715 * value * value * value)))

def project(rows, matrix):
    return jnp.einsum('gld,dk->glk', rows, matrix, precision=PRECISE)

def grouped_sum(activity, matrix):
    groups, length, inner = activity.shape
    width = matrix.shape[1]
    pieces = activity.reshape(groups, length, N_TENSOR, inner // N_TENSOR)
    blocks = matrix.reshape(N_TENSOR, inner // N_TENSOR, width)
    partial_value = low(jnp.einsum('gltk,tkd->tgld', pieces, blocks, precision=PRECISE))
    return low_back(lax.optimization_barrier(jnp.sum(partial_value, 0)))

def attend(rows, source, w_query, w_key, w_value, w_output, bias_full, allowed):
    groups, length, width = rows.shape
    span = source.shape[1]
    heads = w_query.shape[1] // HEAD_DIM
    queries = low(low_back(project(rows, w_query))).reshape(groups, length, heads, HEAD_DIM)
    keys_all = low(low_back(project(source, w_key))).reshape(groups, span, heads, HEAD_DIM)
    values_all = low(low_back(project(source, w_value))).reshape(groups, span, heads, HEAD_DIM)
    logits = SCALE * jnp.einsum('gihe,gjhe->ghij', queries, keys_all, precision=PRECISE) + bias_full
    logits = jnp.where(allowed, low_back(logits), NEGATIVE)
    highest = lax.optimization_barrier(jnp.max(logits, -1, keepdims=True))
    expo = jnp.exp(logits - highest)
    probs = low(expo / lax.optimization_barrier(jnp.sum(expo, -1, keepdims=True)))
    context = low(low_back(jnp.einsum('ghij,gjhe->gihe', probs, values_all, precision=PRECISE)))
    return grouped_sum(context.reshape(groups, length, heads * HEAD_DIM), w_output)

def layer(rows_in, encoded_in, params, dec_lens, enc_lens, distance_bucket):
    gain_self, self_query, self_key, self_value, self_output, bias_table, gain_cross, cross_query, cross_key, cross_value, cross_output, gain_ffn, ffn_up, ffn_down = params
    length = rows_in.shape[1]
    span = encoded_in.shape[1]
    position = jnp.arange(length)
    causal = position[None, :] <= position[:, None]
    allowed_self = causal[None, None] & (position[None, None, None, :] < dec_lens[:, None, None, None])
    allowed_cross = jnp.arange(span)[None, None, None, :] < enc_lens[:, None, None, None]
    distance_bias = bias_table[distance_bucket]
    offset = jnp.maximum(position[:, None] - position[None, :], 0)
    bias_full = jnp.transpose(distance_bias[offset], (2, 0, 1))
    normed_one = low(rms_norm(rows_in, gain_self))
    hidden_one = rows_in + attend(normed_one, normed_one, self_query, self_key, self_value, self_output, bias_full, allowed_self)
    normed_two = low(rms_norm(hidden_one, gain_cross))
    hidden_two = hidden_one + attend(normed_two, encoded_in, cross_query, cross_key, cross_value, cross_output, 0.0, allowed_cross)
    normed_three = low(rms_norm(hidden_two, gain_ffn))
    activity = low(smooth_gate(low_back(project(normed_three, ffn_up))))
    return hidden_two + grouped_sum(activity, ffn_down)

def reference(inputs, encoded, dec_len, enc_len, language, objective, distance_bucket, token_weights, cotangent, gain_self, self_query, self_key, self_value, self_output, bias_table, gain_cross, cross_query, cross_key, cross_value, cross_output, gain_ffn, ffn_up, ffn_down):
    weights = tuple((item.astype(jnp.float32) for item in (gain_self, self_query, self_key, self_value, self_output, bias_table, gain_cross, cross_query, cross_key, cross_value, cross_output, gain_ffn, ffn_up, ffn_down)))
    count = inputs.shape[0] // SEQ_DEV
    length = inputs.shape[1]
    row_pick = (objective * LANGS + language).astype(jnp.int32)
    weighting = token_weights[row_pick] * (jnp.arange(length)[None, :] < dec_len[:, None]).astype(jnp.float32)
    grad_out = cotangent.astype(jnp.float32) * weighting[:, :, None]

    def grouped(array):
        return array.reshape((count, SEQ_DEV) + array.shape[1:])

    def step(totals, item):
        rows_in, encoded_in, dec_lens, enc_lens, grad_rows = item

        def forward(rows_float, encoded_float, *params):
            return layer(rows_float, encoded_float, params, dec_lens, enc_lens, distance_bucket)
        result, pull = jax.vjp(forward, rows_in.astype(jnp.float32), encoded_in.astype(jnp.float32), *weights)
        grads = pull(grad_rows)
        totals = tuple((left + right for left, right in zip(totals, grads[2:])))
        return (totals, (result.astype(jnp.bfloat16), grads[0].astype(jnp.bfloat16), grads[1].astype(jnp.bfloat16)))
    start = tuple((jnp.zeros_like(item) for item in weights))
    totals, (outputs, input_grads, encoded_grads) = lax.scan(step, start, (grouped(inputs), grouped(encoded), grouped(dec_len), grouped(enc_len), grouped(grad_out)))
    layer_out = outputs.reshape(inputs.shape)
    input_grad = input_grads.reshape(inputs.shape)
    encoded_grad = encoded_grads.reshape(encoded.shape)
    return (layer_out, input_grad, encoded_grad) + tuple(totals)
```

```python
import jax
import jax.numpy as jnp
from jax import lax
from jax.experimental import pallas as pl
from jax.experimental.pallas import tpu as pltpu
from jax.sharding import PartitionSpec as P

HEAD_DIM = 64
LANGS = 8
EPSILON = 1e-06
SCALE = 0.125
NEGATIVE = -1e30
F32 = jnp.float32
BF16 = jnp.bfloat16
VMEM_LIMIT = 20 * 1024 * 1024
EXTRA = 16


def dot(left, right):
    return jnp.dot(left, right, preferred_element_type=F32)


def dot_nt(left, right):
    return lax.dot_general(left, right, (((1,), (1,)), ((), ())), preferred_element_type=F32)


def dot_tn(left, right):
    return lax.dot_general(left, right, (((0,), (0,)), ((), ())), preferred_element_type=F32)


def inverse_rms(resid):
    return lax.rsqrt(jnp.mean(resid * resid, -1, keepdims=True) + EPSILON)


def norm_back(resid, gain, incoming):
    scale = inverse_rms(resid)
    weighted = incoming * gain
    inner = jnp.mean(weighted * resid, -1, keepdims=True)
    grad = scale * weighted - resid * (scale * scale * scale * inner)
    gain_grad = jnp.sum(incoming * resid * scale, 0, keepdims=True)
    return grad, gain_grad


def groups_of(width):
    return [(start, min(2 * HEAD_DIM, width - start)) for start in range(0, width, 2 * HEAD_DIM)]


def head_mask(count, which, value):
    lane = lax.broadcasted_iota(jnp.int32, (1, count), 1)
    return jnp.where(lane // HEAD_DIM == which, value, 0.0).astype(BF16)


def merge_heads(parts):
    merged = []
    for pair in parts:
        if len(pair) == 1:
            merged.append(pair[0])
        else:
            lane = lax.broadcasted_iota(jnp.int32, (1, 2 * HEAD_DIM), 1)
            merged.append(jnp.where(lane < HEAD_DIM, pair[0], pair[1]))
    return jnp.concatenate(merged, -1) if len(merged) > 1 else merged[0]


def heads_forward(queries, keys, values, finish, probs_ref):
    parts = []
    head = 0
    for start, width in groups_of(queries.shape[1]):
        query, key, value = (item[:, start : start + width] for item in (queries, keys, values))
        pair = []
        for inside in range(width // HEAD_DIM):
            logits = finish(head, dot_nt(query * head_mask(width, inside, SCALE), key))
            expo = jnp.exp(logits - jnp.max(logits, -1, keepdims=True))
            probs = (expo * (1.0 / jnp.sum(expo, -1, keepdims=True))).astype(BF16)
            probs_ref[head] = probs
            pair.append(dot(probs, value))
            head += 1
        parts.append(pair)
    return merge_heads(parts).astype(BF16)


def heads_backward(grad_context, keys, values, probs_ref, grad_logits_ref):
    parts = []
    head = 0
    for start, width in groups_of(grad_context.shape[1]):
        grad, key, value = (item[:, start : start + width] for item in (grad_context, keys, values))
        pair = []
        for inside in range(width // HEAD_DIM):
            grad_probs = dot_nt(grad * head_mask(width, inside, 1.0), value)
            probs = probs_ref[head].astype(F32)
            weighted = jnp.sum(grad_probs * probs, -1, keepdims=True)
            grad_logits = (probs * (grad_probs - weighted)).astype(BF16)
            grad_logits_ref[head] = grad_logits
            pair.append(SCALE * dot(grad_logits, key))
            head += 1
        parts.append(pair)
    return merge_heads(parts).astype(BF16)


def heads_transposed(matrix_ref, rows, factor):
    parts = []
    head = 0
    for start, width in groups_of(rows.shape[1]):
        pair = []
        for _ in range(width // HEAD_DIM):
            pair.append(factor * dot_tn(matrix_ref[head], rows[:, start : start + width]))
            head += 1
        parts.append(pair)
    return merge_heads(parts).astype(BF16)


def own_rows(core, half):
    return pl.ds(pl.multiple_of(core * half, half), half)


def split_halves(whole_ref, keep_ref, send_ref):
    half = keep_ref.shape[0]
    core = lax.axis_index("tensor") % 2
    keep_ref[...] = whole_ref[own_rows(core, half), :]
    send_ref[...] = whole_ref[own_rows(1 - core, half), :]


def reversed_onehot(bucket_ref, buckets):
    length = bucket_ref.shape[1]
    row = lax.broadcasted_iota(jnp.int32, (length, length), 0)
    column = lax.broadcasted_iota(jnp.int32, (length, length), 1)
    turn = jnp.where((row + column == length) | (row + column == 0), 1.0, 0.0).astype(BF16)
    bucket = jnp.broadcast_to(bucket_ref[...], (8, length)).astype(F32).astype(BF16)
    turned = dot(bucket, turn)[:1]
    wanted = lax.broadcasted_iota(jnp.int32, (buckets, length), 0).astype(F32)
    return jnp.where(turned == wanted, 1.0, 0.0)


def add_kernel(left_ref, right_ref, out_ref):
    out_ref[...] = (left_ref[...].astype(F32) + right_ref[...].astype(F32)).astype(out_ref.dtype)


def self_forward_kernel(
    dec_len, x, gain, w_query, w_key, w_value, w_output, bucket, table,
    keep, send, normed_out, query_out, key_out, value_out, context_out, probs_out, whole,
):
    length = x.shape[0]
    resid = x[...].astype(F32)
    normed = (resid * inverse_rms(resid) * gain[...]).astype(BF16)
    normed_out[...] = normed
    queries = dot(normed, w_query[...]).astype(BF16)
    keys = dot(normed, w_key[...]).astype(BF16)
    values = dot(normed, w_value[...]).astype(BF16)
    query_out[...] = queries
    key_out[...] = keys
    value_out[...] = values
    onehot = reversed_onehot(bucket, table.shape[0])
    row = lax.broadcasted_iota(jnp.int32, (length, length), 0)
    column = lax.broadcasted_iota(jnp.int32, (length, length), 1)
    allowed = (column <= row) & (column < dec_len[0])

    def finish(head, scores):
        by_distance = jnp.sum(table[:, head : head + 1] * onehot, 0, keepdims=True)
        spread = jnp.broadcast_to(by_distance, (length, length))
        bias = pltpu.roll(spread, 0, 1, stride=1, stride_axis=0)
        return jnp.where(allowed, scores + bias, NEGATIVE)

    context = heads_forward(queries, keys, values, finish, probs_out)
    context_out[...] = context
    whole[...] = dot(context, w_output[...]).astype(BF16)
    split_halves(whole, keep, send)


def cross_source_kernel(e0, e1, e2, e3, wk_own, wv_own, wk_peer, wv_peer, k_own, v_own, k_peer, v_peer):
    rows = e0.shape[0]
    for index, part in enumerate((e0, e1, e2, e3)):
        for weight, out in ((wk_own, k_own), (wv_own, v_own), (wk_peer, k_peer), (wv_peer, v_peer)):
            out[index * rows : (index + 1) * rows, :] = dot(part[...], weight[...]).astype(BF16)


def out_grad_kernel(
    objective, language, dec_len, token_weights, cotangent, down_own, down_peer,
    grad_own, branch_own, branch_peer, act_grad_own, act_grad_peer,
):
    half = grad_own.shape[0]
    length = cotangent.shape[0]
    core = lax.axis_index("tensor") % 2
    weights = token_weights[pl.ds(objective[0] * LANGS + language[0], 1), :]
    position = lax.broadcasted_iota(jnp.int32, (1, length), 1)
    weights = jnp.where(position < dec_len[0], weights, 0.0)

    def rows_of(side):
        row = lax.broadcasted_iota(jnp.int32, (half, length), 0) + side * half
        column = lax.broadcasted_iota(jnp.int32, (half, length), 1)
        factor = jnp.sum(jnp.where(row == column, weights, 0.0), -1, keepdims=True)
        return cotangent[own_rows(side, half), :].astype(F32) * factor

    own = rows_of(core)
    grad_own[...] = own
    branch = own.astype(BF16)
    branch_own[...] = branch
    branch_peer[...] = rows_of(1 - core).astype(BF16)
    act_grad_own[...] = dot_nt(branch, down_own[...])
    act_grad_peer[...] = dot_nt(branch, down_peer[...])


def cross_forward_kernel(
    enc_len, chip_own, chip_other, x, gain, wq_own, wq_peer, wo_own, wo_peer, k_own, v_own, k_peer, v_peer,
    partial_out, hidden_out, normed_out, q_own, q_peer, context_own, probs_own, probs_peer, pack,
):
    half, width = chip_own.shape
    tensor = lax.axis_index("tensor")
    resid = x[own_rows(tensor % 2, half), :].astype(F32)
    resid = resid + (chip_own[...].astype(F32) + chip_other[...].astype(F32))
    hidden_out[...] = resid
    normed = (resid * inverse_rms(resid) * gain[...]).astype(BF16)
    normed_out[...] = normed
    pack[:, :width] = normed
    span = k_own.shape[0]
    column = lax.broadcasted_iota(jnp.int32, (1, span), 1)
    block = column // half
    flip = jnp.where(block % 2 == 1, 2, 0) + jnp.where(block >= 2, 1, 0)
    position = (tensor ^ flip) * half + column % half
    allowed = position < enc_len[0]

    def finish(head, scores):
        return jnp.where(allowed, scores, NEGATIVE)

    queries = dot(normed, wq_own[...]).astype(BF16)
    q_own[...] = queries
    first = heads_forward(queries, k_own[...], v_own[...], finish, probs_own)
    context_own[...] = first
    queries = dot(normed, wq_peer[...]).astype(BF16)
    q_peer[...] = queries
    second = heads_forward(queries, k_peer[...], v_peer[...], finish, probs_peer)
    pack[:, width:] = second
    partial_out[...] = (dot(first, wo_own[...]) + dot(second, wo_peer[...])).astype(BF16)


def ffn_kernel(
    chip_own, chip_other, hidden, gain, up_own, up_peer, act_grad_own, act_grad_peer,
    partial_out, hidden_out, normed_out, act_own, grad_pre_own, pack,
):
    width = hidden.shape[1]
    resid = hidden[...] + (chip_own[...].astype(F32) + chip_other[...].astype(F32))
    hidden_out[...] = resid
    normed = (resid * inverse_rms(resid) * gain[...]).astype(BF16)
    normed_out[...] = normed
    pack[:, :width] = normed

    def through(up, act_grad):
        pre = dot(normed, up[...])
        square = pre * pre
        tanh = jnp.tanh(0.7978845608028654 * (pre + 0.044715 * square * pre))
        half_sum = 0.5 * (1.0 + tanh)
        slope = half_sum + 0.5 * pre * (1.0 - tanh * tanh) * (
            0.7978845608028654 * (1.0 + 3.0 * 0.044715 * square)
        )
        return (pre * half_sum).astype(BF16), (act_grad[...] * slope).astype(BF16)

    act, grad_pre = through(up_own, act_grad_own)
    act_own[...] = act
    grad_pre_own[...] = grad_pre
    total = dot_nt(grad_pre, up_own[...])
    act, grad_pre = through(up_peer, act_grad_peer)
    units = act.shape[1]
    pack[:, width : width + units] = act
    pack[:, width + units :] = grad_pre
    total = total + dot_nt(grad_pre, up_peer[...])
    partial_out[...] = total.astype(BF16)


def ffn_out_kernel(act_own, pack, down_own, down_peer, out):
    units = act_own.shape[1]
    width = out.shape[1]
    out[...] = (
        dot(act_own[...], down_own[...]) + dot(pack[:, width : width + units], down_peer[...])
    ).astype(BF16)


def layer_out_kernel(hidden, chip_own, chip_other, out):
    out[...] = (hidden[...] + (chip_own[...].astype(F32) + chip_other[...].astype(F32))).astype(BF16)


def halves_kernel(own, peer, out):
    half = own.shape[0]
    core = lax.axis_index("tensor") % 2
    out[own_rows(core, half), :] = own[...]
    out[own_rows(1 - core, half), :] = peer[...]


def write_blocks(whole, first_bit, rest_bits, size, targets, extra=None):
    index = lax.axis_index("dp")
    count = 1 << len(rest_bits)
    for first, target in enumerate(targets):
        for entry in range(count):
            relative = first << first_bit
            for place, bit in enumerate(rest_bits):
                if entry >> (len(rest_bits) - 1 - place) & 1:
                    relative |= 1 << bit
            block = index ^ relative
            rows = whole[pl.ds(pl.multiple_of(block * size, size), size), :]
            target[entry, :size, :] = rows
            if extra is not None:
                target[entry, size:, :] = extra


def emit(whole, outs, order, size, extra=None):
    if order is None:
        outs[0][: whole.shape[0], :] = whole[...]
        if extra is not None:
            outs[0][whole.shape[0] :, :] = extra
    else:
        write_blocks(whole, order[0], order[1:], size, outs, extra)


def ffn_weights_kernel(orders, size, normed, pack, act_own, grad_pre_own, branch_own, branch_peer, *refs):
    *outs, whole, left, right = refs
    half, width = normed.shape
    units = act_own.shape[1]
    left[:half] = normed[...]
    left[half:] = pack[:, :width]
    right[:half] = grad_pre_own[...]
    right[half:] = pack[:, width + units :]
    whole[...] = dot_tn(left[...], right[...]).astype(BF16)
    count = 1 if orders[0] is None else 2
    emit(whole, outs[:count], orders[0], size)
    left[:half] = branch_own[...]
    left[half:] = branch_peer[...]
    right[:half] = act_own[...]
    right[half:] = pack[:, width : width + units]
    whole[...] = dot_tn(left[...], right[...]).astype(BF16)
    emit(whole, outs[count:], orders[1], size)


def cross_backward_kernel(
    chip_own, chip_other, hidden, gain, grad_out, wo_own, wo_peer, k_own, v_own, k_peer, v_peer,
    probs_own, probs_peer, wq_own, wq_peer,
    partial_out, grad_hidden, gain_grad, gl_own, gl_peer, gc_own, gc_peer, gq_own, branch, pack,
):
    width = hidden.shape[1]
    incoming = chip_own[...].astype(F32) + chip_other[...].astype(F32)
    added, gain_terms = norm_back(hidden[...], gain[...], incoming)
    gain_grad[...] = jnp.broadcast_to(gain_terms, gain_grad.shape)
    grad = grad_out[...] + added
    grad_hidden[...] = grad
    rounded = grad.astype(BF16)
    branch[...] = rounded
    pack[:, :width] = rounded
    context = dot_nt(rounded, wo_own[...]).astype(BF16)
    gc_own[...] = context
    queries = heads_backward(context, k_own[...], v_own[...], probs_own, gl_own)
    gq_own[...] = queries
    total = dot_nt(queries, wq_own[...])
    context = dot_nt(rounded, wo_peer[...]).astype(BF16)
    gc_peer[...] = context
    queries = heads_backward(context, k_peer[...], v_peer[...], probs_peer, gl_peer)
    pack[:, width:] = queries
    total = total + dot_nt(queries, wq_peer[...])
    partial_out[...] = total.astype(BF16)


def cross_source_grad_kernel(gl_peer, probs_peer, gc_peer, q_peer, out):
    span = out.shape[0] // 2
    middle = span // 2
    for start, grads in (
        (0, heads_transposed(gl_peer, q_peer[...], SCALE)),
        (span, heads_transposed(probs_peer, gc_peer[...], 1.0)),
    ):
        out[start : start + middle] = grads[middle:]
        out[start + middle : start + span] = grads[:middle]


def cross_weights_kernel(
    order, size, gl_own, probs_own, gc_own, q_own, other, e0, e1, e2, e3, normed, pack_forward,
    branch, pack_backward, context_own, gq_own, wk_own, wv_own, *refs,
):
    *outs, encoded_keep, encoded_send, whole, left, right = refs
    span = other.shape[0] // 2
    half, width = normed.shape
    columns = q_own.shape[1]
    grad_keys = heads_transposed(gl_own, q_own[...], SCALE).astype(F32) + other[:span].astype(F32)
    grad_values = heads_transposed(probs_own, gc_own[...], 1.0).astype(F32) + other[span:].astype(F32)
    grad_keys = grad_keys.astype(BF16)
    grad_values = grad_values.astype(BF16)
    terms = (dot_nt(grad_keys, wk_own[...]) + dot_nt(grad_values, wv_own[...])).astype(BF16)
    encoded_keep[...] = terms[: 2 * half]
    encoded_send[...] = terms[2 * half :]
    for index, part in enumerate((e0, e1, e2, e3)):
        left[index * half : (index + 1) * half] = part[...]
    right[:, :columns] = grad_keys
    right[:, columns:] = grad_values
    whole[:, : 2 * columns] = dot_tn(left[...], right[...]).astype(BF16)
    left[:half] = normed[...]
    left[half : 2 * half] = pack_forward[:, :width]
    left[2 * half : 3 * half] = branch[...]
    left[3 * half :] = pack_backward[:, :width]
    right[...] = jnp.zeros_like(right)
    right[:half, :columns] = gq_own[...]
    right[half : 2 * half, :columns] = pack_backward[:, width:]
    right[2 * half : 3 * half, columns:] = context_own[...]
    right[3 * half :, columns:] = pack_forward[:, width:]
    whole[:, 2 * columns :] = dot_tn(left[...], right[...]).astype(BF16)
    emit(whole, outs, order, size)


def encoded_sum_kernel(left, right, keep, send):
    half = keep.shape[0]
    total = (left[...].astype(F32) + right[...].astype(F32)).astype(BF16)
    keep[...] = total[:half]
    send[...] = total[half:]


def self_norm_kernel(chip_own, chip_other, hidden, gain, grad_hidden, gain_ffn, grad_out, pack):
    half = hidden.shape[0]
    incoming = chip_own[...].astype(F32) + chip_other[...].astype(F32)
    added, gain_terms = norm_back(hidden[...], gain[...], incoming)
    grad = grad_hidden[...] + added
    grad_out[...] = grad
    pack[:half] = grad.astype(BF16)
    row = lax.broadcasted_iota(jnp.int32, (EXTRA, hidden.shape[1]), 0)
    extra = jnp.where(row == 0, gain_terms, 0.0) + jnp.where(row == 1, gain_ffn[:1], 0.0)
    pack[half:] = extra.astype(BF16)


def self_backward_kernel(
    pack_own, pack_peer, w_output, w_query, w_key, w_value, queries, keys, values, probs,
    keep, send, branch_out, gq_out, gk_out, gv_out, gl_out, whole,
):
    half = keep.shape[0]
    core = lax.axis_index("tensor") % 2
    branch_out[own_rows(core, half), :] = pack_own[:half]
    branch_out[own_rows(1 - core, half), :] = pack_peer[:half]
    context = dot_nt(branch_out[...], w_output[...]).astype(BF16)
    grad_queries = heads_backward(context, keys[...], values[...], probs, gl_out)
    grad_keys = heads_transposed(gl_out, queries[...], SCALE)
    grad_values = heads_transposed(probs, context, 1.0)
    gq_out[...] = grad_queries
    gk_out[...] = grad_keys
    gv_out[...] = grad_values
    whole[...] = (
        dot_nt(grad_queries, w_query[...]) + dot_nt(grad_keys, w_key[...]) + dot_nt(grad_values, w_value[...])
    ).astype(BF16)
    split_halves(whole, keep, send)


def self_weights_kernel(
    order, size, normed, branch, gq, gk, gv, context, gl, bucket, pack_own, pack_peer, *refs
):
    *outs, whole, right, left = refs
    length, columns = gq.shape
    half = pack_own.shape[0] - EXTRA
    right[:length, :columns] = gq[...]
    right[:length, columns:] = gk[...]
    whole[:, : 2 * columns] = dot_tn(normed[...], right[:length]).astype(BF16)
    left[:length] = normed[...]
    left[length:] = branch[...]
    right[...] = jnp.zeros_like(right)
    right[:length, :columns] = gv[...]
    right[length:, columns:] = context[...]
    whole[:, 2 * columns :] = dot_tn(left[...], right[...]).astype(BF16)
    buckets = 32
    onehot = reversed_onehot(bucket, buckets)
    row = lax.broadcasted_iota(jnp.int32, (length, length), 0)
    column = lax.broadcasted_iota(jnp.int32, (length, length), 1)
    turn = jnp.where(row + column == length - 1, 1.0, 0.0).astype(BF16)
    place = lax.broadcasted_iota(jnp.int32, (8, length), 0)
    sums = jnp.zeros((8, length), F32)
    for head in range(gl.shape[0]):
        skewed = pltpu.roll(dot(turn, gl[head]), 1, 1, stride=1, stride_axis=0)
        sums = sums + jnp.where(place == head, jnp.sum(skewed, 0, keepdims=True), 0.0)
    table = lax.dot_general(
        sums, onehot, (((1,), (1,)), ((), ())), precision=lax.Precision.HIGHEST, preferred_element_type=F32
    )
    extra = pack_own[half:].astype(F32) + pack_peer[half:].astype(F32)
    wide = jnp.concatenate([table, jnp.zeros((8, extra.shape[1] - buckets), F32)], 1)
    extra = jnp.concatenate([extra[:8], wide], 0)
    emit(whole, outs, order, size, extra.astype(BF16))


def input_grad_kernel(chip_own, chip_other, x, gain, grad_hidden, out, gain_grad):
    half = out.shape[0]
    resid = x[own_rows(lax.axis_index("tensor") % 2, half), :].astype(F32)
    incoming = chip_own[...].astype(F32) + chip_other[...].astype(F32)
    added, gain_terms = norm_back(resid, gain[...], incoming)
    out[...] = (grad_hidden[...] + added).astype(BF16)
    gain_grad[...] = jnp.broadcast_to(gain_terms, gain_grad.shape)


def pass_on_kernel(keep, got, send_next, keep_next):
    count = keep_next.shape[0]
    for entry in range(count):
        keep_next[entry] = (keep[entry].astype(F32) + got[entry].astype(F32)).astype(BF16)
        send_next[entry] = (keep[count + entry].astype(F32) + got[count + entry].astype(F32)).astype(BF16)


def run(kernel, name, outs, ins, flops=0, scratch=(), scalars=0):
    shapes = [jax.ShapeDtypeStruct(shape, dtype) for shape, dtype in outs]
    moved = sum(item.size * item.dtype.itemsize for item in ins)
    moved += sum(item.size * item.dtype.itemsize for item in shapes)
    vmem = pl.BlockSpec(memory_space=pltpu.VMEM)
    smem = pl.BlockSpec(memory_space=pltpu.SMEM)
    result = pl.pallas_call(
        kernel,
        out_shape=shapes,
        in_specs=[smem] * scalars + [vmem] * (len(ins) - scalars),
        out_specs=[vmem] * len(shapes),
        scratch_shapes=[pltpu.VMEM(shape, dtype) for shape, dtype in scratch],
        compiler_params=pltpu.CompilerParams(vmem_limit_bytes=VMEM_LIMIT),
        cost_estimate=pl.CostEstimate(flops=int(flops), bytes_accessed=int(moved), transcendentals=0),
        name=name,
    )(*ins)
    return result[0] if len(shapes) == 1 else result


def to_core(value):
    return lax.ppermute(value, "tensor", [(i, i ^ 1) for i in range(lax.axis_size("tensor"))])


def to_chip(value):
    return lax.ppermute(value, "tensor", [(i, i ^ 2) for i in range(lax.axis_size("tensor"))])


def to_peer(value, bit):
    return lax.ppermute(value, "dp", [(i, i ^ (1 << bit)) for i in range(lax.axis_size("dp"))])


def add(left, right, name):
    return run(add_kernel, name, [(left.shape, left.dtype)], [left, right])


def scatter_sum(keep, send, order, name):
    for place, bit in enumerate(order):
        got = to_peer(send, bit)
        if place == len(order) - 1:
            return keep, got
        count, rows, columns = keep.shape
        shape = ((count // 2, rows, columns), BF16)
        send, keep = run(pass_on_kernel, f"{name}_{place}", [shape, shape], [keep, got])


def on_device(
    inputs, encoded, dec_len, enc_len, language, objective, distance_bucket, token_weights, cotangent,
    gain_self, self_query, self_key, self_value, self_output, bias_table,
    gain_cross, cross_query, cross_key, cross_value, cross_output, gain_ffn, ffn_up, ffn_down,
):
    seqs, length, width = inputs.shape
    half = length // 2
    columns = self_query.shape[1]
    heads = columns // HEAD_DIM
    units = ffn_up.shape[1]
    span_part = encoded.shape[1]
    span = span_part * lax.axis_size("tensor")
    dp = lax.axis_size("dp")
    size = width // dp
    bits = dp.bit_length() - 1
    halving = dp > 1 and dp == 1 << bits and size % 16 == 0
    if halving:
        along_x = tuple(range(bits))
        along_z = (1, 0) + tuple(range(2, bits)) if bits > 1 else along_x
    else:
        along_x = along_z = None

    def payload(order, extra=0):
        if order is None:
            return [((width + extra, width), BF16)]
        return [((dp // 2, size + extra, width), BF16)] * 2

    x = inputs.reshape(length, width)
    cot = cotangent.reshape(length, width)
    gain_one = gain_self.reshape(1, width)
    gain_two = gain_cross.reshape(1, width)
    gain_three = gain_ffn.reshape(1, width)
    bucket = distance_bucket.reshape(1, length)
    e0 = encoded.reshape(span_part, width)

    e1 = to_chip(e0)
    keep, send, normed_one, query_one, key_one, value_one, context_one, probs_one = run(
        self_forward_kernel, "self_forward",
        [((half, width), BF16)] * 2 + [((length, width), BF16)] + [((length, columns), BF16)] * 4
        + [((heads, length, length), BF16)],
        [dec_len, x, gain_one, self_query, self_key, self_value, self_output, bucket, bias_table],
        flops=2 * length * width * columns * 4 + 4 * length * length * columns,
        scratch=[((length, width), BF16)], scalars=1,
    )
    chip_one = add(keep, to_core(send), "self_sum")
    other_one = to_chip(chip_one)
    wk_peer = to_core(cross_key)
    wv_peer = to_core(cross_value)
    e2 = to_core(e0)
    e3 = to_core(e1)
    wq_peer = to_core(cross_query)
    wo_peer = to_core(cross_output)
    down_peer = to_core(ffn_down)
    up_peer = to_core(ffn_up)
    k_own, v_own, k_peer, v_peer = run(
        cross_source_kernel, "cross_source", [((span, columns), BF16)] * 4,
        [e0, e1, e2, e3, cross_key, cross_value, wk_peer, wv_peer], flops=8 * span * width * columns,
    )
    grad_full, branch_three, branch_three_peer, act_grad, act_grad_peer = run(
        out_grad_kernel, "out_grad",
        [((half, width), F32)] + [((half, width), BF16)] * 2 + [((half, units), F32)] * 2,
        [objective, language, dec_len, token_weights, cot, ffn_down, down_peer],
        flops=4 * half * width * units, scalars=3,
    )

    partial_two, hidden_one, normed_two, q_own, q_peer, context_two, probs_own, probs_peer, pack_forward = run(
        cross_forward_kernel, "cross_forward",
        [((half, width), BF16), ((half, width), F32), ((half, width), BF16)] + [((half, columns), BF16)] * 3
        + [((heads, half, span), BF16)] * 2 + [((half, width + columns), BF16)],
        [enc_len, chip_one, other_one, x, gain_two, cross_query, wq_peer, cross_output, wo_peer,
         k_own, v_own, k_peer, v_peer],
        flops=8 * half * width * columns + 8 * half * span * columns, scalars=1,
    )
    other_two = to_chip(partial_two)
    pack_forward_peer = to_core(pack_forward)

    partial_three, hidden_two, normed_three, act_own, grad_pre_own, pack_ffn = run(
        ffn_kernel, "ffn",
        [((half, width), BF16), ((half, width), F32), ((half, width), BF16)] + [((half, units), BF16)] * 2
        + [((half, width + 2 * units), BF16)],
        [partial_two, other_two, hidden_one, gain_three, ffn_up, up_peer, act_grad, act_grad_peer],
        flops=8 * half * width * units,
    )
    other_three = to_chip(partial_three)
    pack_ffn_peer = to_core(pack_ffn)
    branch_out = run(
        ffn_out_kernel, "ffn_out", [((half, width), BF16)], [act_own, pack_ffn, ffn_down, down_peer],
        flops=4 * half * width * units,
    )

    def ffn_weights(*refs):
        ffn_weights_kernel((along_x, along_z), size, *refs)

    ffn_payloads = run(
        ffn_weights, "ffn_weights", payload(along_x) + payload(along_z),
        [normed_three, pack_ffn_peer, act_own, grad_pre_own, branch_three, branch_three_peer],
        flops=8 * half * width * units,
        scratch=[((width, units), BF16), ((length, width), BF16), ((length, units), BF16)],
    )

    (partial_four, grad_two, gain_grad_three, gl_own, gl_peer, gc_own, gc_peer, gq_own, branch_two,
     pack_backward) = run(
        cross_backward_kernel, "cross_backward",
        [((half, width), BF16), ((half, width), F32), ((8, width), F32)] + [((heads, half, span), BF16)] * 2
        + [((half, columns), BF16)] * 3 + [((half, width), BF16), ((half, width + columns), BF16)],
        [partial_three, other_three, hidden_two, gain_three, grad_full, cross_output, wo_peer,
         k_own, v_own, k_peer, v_peer, probs_own, probs_peer, cross_query, wq_peer],
        flops=8 * half * width * columns + 8 * half * span * columns,
    )
    other_four = to_chip(partial_four)
    source_grad = run(
        cross_source_grad_kernel, "cross_source_grad", [((2 * span, columns), BF16)],
        [gl_peer, probs_peer, gc_peer, q_peer], flops=4 * half * span * columns,
    )
    source_grad_peer = to_core(source_grad)
    pack_backward_peer = to_core(pack_backward)
    other_out = to_chip(branch_out)
    out_own = run(layer_out_kernel, "layer_out", [((half, width), BF16)], [hidden_two, branch_out, other_out])
    layer_out = run(halves_kernel, "layer_out_halves", [((length, width), BF16)], [out_own, to_core(out_own)])

    def cross_weights(*refs):
        cross_weights_kernel(along_x, size, *refs)

    *cross_payload, encoded_keep, encoded_send = run(
        cross_weights, "cross_weights", payload(along_x) + [((span // 2, width), BF16)] * 2,
        [gl_own, probs_own, gc_own, q_own, source_grad_peer, e0, e1, e2, e3, normed_two, pack_forward_peer,
         branch_two, pack_backward_peer, context_two, gq_own, cross_key, cross_value],
        flops=4 * half * span * columns + 4 * span * width * columns + 4 * span * width * columns,
        scratch=[((width, 4 * columns), BF16), ((span, width), BF16), ((span, 2 * columns), BF16)],
    )

    grad_one, pack_self = run(
        self_norm_kernel, "self_norm", [((half, width), F32), ((half + EXTRA, width), BF16)],
        [partial_four, other_four, hidden_one, gain_two, grad_two, gain_grad_three],
    )
    pack_self_peer = to_core(pack_self)
    keep, send, branch_one, gq_one, gk_one, gv_one, gl_one = run(
        self_backward_kernel, "self_backward",
        [((half, width), BF16)] * 2 + [((length, width), BF16)] + [((length, columns), BF16)] * 3
        + [((heads, length, length), BF16)],
        [pack_self, pack_self_peer, self_output, self_query, self_key, self_value, query_one, key_one, value_one,
         probs_one],
        flops=8 * length * width * columns + 8 * length * length * columns,
        scratch=[((length, width), BF16)],
    )
    chip_five = add(keep, to_core(send), "input_sum")
    other_five = to_chip(chip_five)

    def self_weights(*refs):
        self_weights_kernel(along_x, size, *refs)

    self_payload = run(
        self_weights, "self_weights", payload(along_x, EXTRA),
        [normed_one, branch_one, gq_one, gk_one, gv_one, context_one, gl_one, bucket, pack_self, pack_self_peer],
        flops=8 * length * width * columns + 2 * heads * length**3,
        scratch=[((width, 4 * columns), BF16), ((2 * length, 2 * columns), BF16), ((2 * length, width), BF16)],
    )
    if not isinstance(self_payload, (list, tuple)):
        self_payload = [self_payload]

    encoded_part, encoded_pass = run(
        encoded_sum_kernel, "encoded_sum", [((span_part, width), BF16)] * 2, [encoded_keep, to_core(encoded_send)]
    )
    encoded_grad = add(encoded_part, to_chip(encoded_pass), "encoded_grad")

    input_own, gain_terms = run(
        input_grad_kernel, "input_grad", [((half, width), BF16), ((8, width), F32)],
        [chip_five, other_five, x, gain_one, grad_one],
    )
    input_grad = run(halves_kernel, "input_grad_halves", [((length, width), BF16)], [input_own, to_core(input_own)])
    gain_terms = add(gain_terms, to_core(gain_terms), "gain_core")

    if halving:
        for bit in along_x:
            gain_terms = add(gain_terms, to_peer(gain_terms, bit), f"gain_{bit}")
        last = [
            scatter_sum(*ffn_payloads[:2], along_x, "up"),
            scatter_sum(*ffn_payloads[2:], along_z, "down"),
            scatter_sum(*cross_payload, along_x, "cross"),
            scatter_sum(*self_payload, along_x, "self"),
        ]
        up, down, cross, own = ((left[0].astype(F32) + right[0].astype(F32)) for left, right in last)
    else:
        gain_terms = lax.psum(gain_terms, "dp")
        up, down, cross = (
            lax.psum_scatter(item.astype(F32), "dp", scatter_dimension=0, tiled=True)
            for item in (ffn_payloads[0], ffn_payloads[1], cross_payload[0])
        )
        item = self_payload[0].astype(F32)
        own = lax.psum_scatter(item[:width], "dp", scatter_dimension=0, tiled=True)
        own = jnp.concatenate([own, lax.psum(item[width:], "dp")], 0)

    index = lax.axis_index("dp")

    def gain_part(row):
        return lax.dynamic_slice(row, (index * size,), (size,))

    return (
        layer_out.reshape(seqs, length, width),
        input_grad.reshape(seqs, length, width),
        encoded_grad.reshape(seqs, span_part, width),
        gain_part(gain_terms[0]),
        own[:size, :columns],
        own[:size, columns : 2 * columns],
        own[:size, 2 * columns : 3 * columns],
        own[:size, 3 * columns :].T,
        own[size + 8 : size + 8 + heads, : bias_table.shape[0]].T,
        gain_part(own[size]),
        cross[:, 2 * columns : 3 * columns],
        cross[:, :columns],
        cross[:, columns : 2 * columns],
        cross[:, 3 * columns :].T,
        gain_part(own[size + 1]),
        up,
        down.T,
    )


def solution(mesh):
    return jax.shard_map(
        on_device,
        mesh=mesh,
        in_specs=(
            P("dp", None, None),
            P("dp", "tensor", None),
            P("dp"),
            P("dp"),
            P("dp"),
            P("dp"),
            P(),
            P(),
            P("dp", None, None),
            P(),
            P(None, "tensor"),
            P(None, "tensor"),
            P(None, "tensor"),
            P("tensor", None),
            P(None, "tensor"),
            P(),
            P(None, "tensor"),
            P(None, "tensor"),
            P(None, "tensor"),
            P("tensor", None),
            P(),
            P(None, "tensor"),
            P("tensor", None),
        ),
        out_specs=(
            P("dp", None, None),
            P("dp", None, None),
            P("dp", "tensor", None),
            P("dp"),
            P("dp", "tensor"),
            P("dp", "tensor"),
            P("dp", "tensor"),
            P("tensor", "dp"),
            P(None, "tensor"),
            P("dp"),
            P("dp", "tensor"),
            P("dp", "tensor"),
            P("dp", "tensor"),
            P("tensor", "dp"),
            P("dp"),
            P("dp", "tensor"),
            P("tensor", "dp"),
        ),
        check_vma=False,
    )
```

```python
import jax
import jax.numpy as jnp
from jax import lax
from jax.experimental import pallas as pl
from jax.experimental.pallas import tpu as pltpu
from jax.sharding import PartitionSpec as P

HEAD_DIM = 64
LANGS = 8
EPSILON = 1e-06
SCALE = 0.125
NEGATIVE = -1e30
F32 = jnp.float32
BF16 = jnp.bfloat16
VMEM_LIMIT = 20 * 1024 * 1024
EXTRA = 16
FILL = 5.0
LONG = 20.0


def dot(left, right):
    return jnp.dot(left, right, preferred_element_type=F32)


def dot_nt(left, right):
    return lax.dot_general(left, right, (((1,), (1,)), ((), ())), preferred_element_type=F32)


def dot_tn(left, right):
    return lax.dot_general(left, right, (((0,), (0,)), ((), ())), preferred_element_type=F32)


def row_of(vector_ref):
    return vector_ref[...].reshape(1, vector_ref.shape[0])


def inverse_rms(resid):
    return lax.rsqrt(jnp.mean(resid * resid, -1, keepdims=True) + EPSILON)


def norm_back(resid, gain, incoming):
    scale = inverse_rms(resid)
    weighted = incoming * gain
    inner = jnp.mean(weighted * resid, -1, keepdims=True)
    grad = scale * weighted - resid * (scale * scale * scale * inner)
    gain_grad = jnp.sum(incoming * resid * scale, 0, keepdims=True)
    return grad, gain_grad


def groups_of(width):
    return [(start, min(2 * HEAD_DIM, width - start)) for start in range(0, width, 2 * HEAD_DIM)]


def head_mask(count, which, value):
    lane = lax.broadcasted_iota(jnp.int32, (1, count), 1)
    return jnp.where(lane // HEAD_DIM == which, value, 0.0).astype(BF16)


def merge_heads(parts):
    merged = []
    for pair in parts:
        if len(pair) == 1:
            merged.append(pair[0])
        else:
            lane = lax.broadcasted_iota(jnp.int32, (1, 2 * HEAD_DIM), 1)
            merged.append(jnp.where(lane < HEAD_DIM, pair[0], pair[1]))
    return jnp.concatenate(merged, -1) if len(merged) > 1 else merged[0]


def heads_forward(queries, keys, values, finish, probs_ref):
    parts = []
    head = 0
    for start, width in groups_of(queries.shape[1]):
        query, key, value = (item[:, start : start + width] for item in (queries, keys, values))
        pair = []
        for inside in range(width // HEAD_DIM):
            logits = finish(head, dot_nt(query * head_mask(width, inside, SCALE), key))
            expo = jnp.exp(logits - jnp.max(logits, -1, keepdims=True))
            probs = (expo * (1.0 / jnp.sum(expo, -1, keepdims=True))).astype(BF16)
            probs_ref[head] = probs
            pair.append(dot(probs, value))
            head += 1
        parts.append(pair)
    return merge_heads(parts).astype(BF16)


def heads_backward(grad_context, keys, values, probs_ref, grad_logits_ref):
    parts = []
    head = 0
    for start, width in groups_of(grad_context.shape[1]):
        grad, key, value = (item[:, start : start + width] for item in (grad_context, keys, values))
        pair = []
        for inside in range(width // HEAD_DIM):
            grad_probs = dot_nt(grad * head_mask(width, inside, 1.0), value)
            probs = probs_ref[head].astype(F32)
            weighted = jnp.sum(grad_probs * probs, -1, keepdims=True)
            grad_logits = (probs * (grad_probs - weighted)).astype(BF16)
            grad_logits_ref[head] = grad_logits
            pair.append(SCALE * dot(grad_logits, key))
            head += 1
        parts.append(pair)
    return merge_heads(parts).astype(BF16)


def heads_transposed(matrix_ref, rows, factor):
    parts = []
    head = 0
    for start, width in groups_of(rows.shape[1]):
        pair = []
        for _ in range(width // HEAD_DIM):
            pair.append(factor * dot_tn(matrix_ref[head], rows[:, start : start + width]))
            head += 1
        parts.append(pair)
    return merge_heads(parts).astype(BF16)


def own_rows(core, half):
    return pl.ds(pl.multiple_of(core * half, half), half)


def split_halves(whole_ref, keep_ref, send_ref):
    half = keep_ref.shape[0]
    core = lax.axis_index("tensor") % 2
    keep_ref[...] = whole_ref[own_rows(core, half), :]
    send_ref[...] = whole_ref[own_rows(1 - core, half), :]


def reversed_onehot(bucket_ref, buckets):
    length = bucket_ref.shape[1]
    row = lax.broadcasted_iota(jnp.int32, (length, length), 0)
    column = lax.broadcasted_iota(jnp.int32, (length, length), 1)
    turn = jnp.where((row + column == length) | (row + column == 0), 1.0, 0.0).astype(BF16)
    bucket = jnp.broadcast_to(bucket_ref[...], (8, length)).astype(F32).astype(BF16)
    turned = dot(bucket, turn)[:1]
    wanted = lax.broadcasted_iota(jnp.int32, (buckets, length), 0).astype(F32)
    return jnp.where(turned == wanted, 1.0, 0.0)


def add_kernel(left_ref, right_ref, out_ref):
    out_ref[...] = (left_ref[...].astype(F32) + right_ref[...].astype(F32)).astype(out_ref.dtype)


def self_forward_kernel(
    dec_len, x, gain, w_query, w_key, w_value, w_output, bucket, table,
    keep, send, normed_out, query_out, key_out, value_out, context_out, probs_out,
    whole, x_here, gain_here, query_here, key_here, value_here, output_here, bucket_here, table_here, sems,
):
    sources = (x, gain, w_query, w_key, w_value, bucket, table, w_output)
    places = (x_here, gain_here, query_here, key_here, value_here, bucket_here, table_here, output_here)
    copies = [
        pltpu.make_async_copy(source, place, sems.at[index])
        for index, (source, place) in enumerate(zip(sources, places))
    ]
    for copy in copies:
        copy.start()
    length = x.shape[0]
    copies[0].wait()
    copies[1].wait()
    resid = x_here[...].astype(F32)
    normed = (resid * inverse_rms(resid) * row_of(gain_here)).astype(BF16)
    normed_out[...] = normed
    copies[2].wait()
    queries = dot_nt(normed, query_here[...]).astype(BF16)
    copies[3].wait()
    keys = dot_nt(normed, key_here[...]).astype(BF16)
    copies[4].wait()
    values = dot_nt(normed, value_here[...]).astype(BF16)
    query_out[...] = queries
    key_out[...] = keys
    value_out[...] = values
    copies[5].wait()
    copies[6].wait()
    by_distance = lax.dot_general(
        table_here[...],
        reversed_onehot(bucket_here, table.shape[1]),
        (((1,), (0,)), ((), ())),
        precision=lax.Precision.HIGHEST,
        preferred_element_type=F32,
    )
    row = lax.broadcasted_iota(jnp.int32, (length, length), 0)
    column = lax.broadcasted_iota(jnp.int32, (length, length), 1)
    allowed = (column <= row) & (column < dec_len[0])

    def finish(head, scores):
        spread = jnp.broadcast_to(by_distance[head : head + 1], (length, length))
        bias = pltpu.roll(spread, 0, 1, stride=1, stride_axis=0)
        return jnp.where(allowed, scores + bias, NEGATIVE)

    context = heads_forward(queries, keys, values, finish, probs_out)
    context_out[...] = context
    copies[7].wait()
    whole[...] = dot(context, output_here[...]).astype(BF16)
    split_halves(whole, keep, send)


def cross_source_kernel(first, second, wk_own, wv_own, wk_peer, wv_peer, k_own, v_own, k_peer, v_peer):
    rows = first.shape[0]
    for index, part in enumerate((first, second)):
        for weight, out in ((wk_own, k_own), (wv_own, v_own), (wk_peer, k_peer), (wv_peer, v_peer)):
            out[index * rows : (index + 1) * rows, :] = dot_nt(part[...], weight[...]).astype(BF16)


def out_grad_kernel(
    objective, language, dec_len, token_weights, cotangent, down_own, down_peer,
    grad_own, branch_own, branch_peer, act_grad_own, act_grad_peer,
):
    half = grad_own.shape[0]
    length = cotangent.shape[0]
    core = lax.axis_index("tensor") % 2
    weights = token_weights[pl.ds(objective[0] * LANGS + language[0], 1), :]
    position = lax.broadcasted_iota(jnp.int32, (1, length), 1)
    weights = jnp.where(position < dec_len[0], weights, 0.0)

    def rows_of(side):
        row = lax.broadcasted_iota(jnp.int32, (half, length), 0) + side * half
        column = lax.broadcasted_iota(jnp.int32, (half, length), 1)
        factor = jnp.sum(jnp.where(row == column, weights, 0.0), -1, keepdims=True)
        return cotangent[own_rows(side, half), :].astype(F32) * factor

    own = rows_of(core)
    grad_own[...] = own
    branch = own.astype(BF16)
    branch_own[...] = branch
    branch_peer[...] = rows_of(1 - core).astype(BF16)
    act_grad_own[...] = dot_nt(branch, down_own[...])
    act_grad_peer[...] = dot_nt(branch, down_peer[...])


def cross_forward_kernel(
    enc_len, chip_own, chip_other, x, gain, wq_own, wq_peer, wo_own, wo_peer, k_own, v_own, k_peer, v_peer,
    more_k_own, more_v_own, more_k_peer, more_v_peer,
    partial_out, hidden_out, normed_out, q_own, q_peer, context_own, probs_own, probs_peer, pack,
    keys_own, values_own, keys_peer, values_peer,
):
    half, width = chip_own.shape
    tensor = lax.axis_index("tensor")
    resid = x[own_rows(tensor % 2, half), :].astype(F32)
    resid = resid + (chip_own[...].astype(F32) + chip_other[...].astype(F32))
    hidden_out[...] = resid
    normed = (resid * inverse_rms(resid) * row_of(gain)).astype(BF16)
    normed_out[...] = normed
    pack[:, :width] = normed
    part = k_own.shape[0]
    for whole, first, second in (
        (keys_own, k_own, more_k_own),
        (values_own, v_own, more_v_own),
        (keys_peer, k_peer, more_k_peer),
        (values_peer, v_peer, more_v_peer),
    ):
        whole[:part] = first[...]
        whole[part:] = second[...]
    span = 2 * part
    column = lax.broadcasted_iota(jnp.int32, (1, span), 1)
    block = column // half
    flip = jnp.where(block % 2 == 1, 2, 0) + jnp.where(block >= 2, 1, 0)
    position = (tensor ^ flip) * half + column % half
    allowed = position < enc_len[0]

    def finish(head, scores):
        return jnp.where(allowed, scores, NEGATIVE)

    queries = dot_nt(normed, wq_own[...]).astype(BF16)
    q_own[...] = queries
    first = heads_forward(queries, keys_own[...], values_own[...], finish, probs_own)
    context_own[...] = first
    queries = dot_nt(normed, wq_peer[...]).astype(BF16)
    q_peer[...] = queries
    second = heads_forward(queries, keys_peer[...], values_peer[...], finish, probs_peer)
    pack[:, width:] = second
    partial_out[...] = (dot(first, wo_own[...]) + dot(second, wo_peer[...])).astype(BF16)


def ffn_kernel(
    chip_own, chip_other, hidden, gain, up_own, up_peer, act_grad_own, act_grad_peer,
    partial_out, hidden_out, normed_out, act_own, grad_pre_own, pack,
):
    width = hidden.shape[1]
    resid = hidden[...] + (chip_own[...].astype(F32) + chip_other[...].astype(F32))
    hidden_out[...] = resid
    normed = (resid * inverse_rms(resid) * row_of(gain)).astype(BF16)
    normed_out[...] = normed
    pack[:, :width] = normed

    def through(up, act_grad):
        pre = dot(normed, up[...])
        square = pre * pre
        tanh = jnp.tanh(0.7978845608028654 * (pre + 0.044715 * square * pre))
        half_sum = 0.5 * (1.0 + tanh)
        slope = half_sum + 0.5 * pre * (1.0 - tanh * tanh) * (
            0.7978845608028654 * (1.0 + 3.0 * 0.044715 * square)
        )
        return (pre * half_sum).astype(BF16), (act_grad[...] * slope).astype(BF16)

    act, grad_pre = through(up_own, act_grad_own)
    act_own[...] = act
    grad_pre_own[...] = grad_pre
    total = dot_nt(grad_pre, up_own[...])
    act, grad_pre = through(up_peer, act_grad_peer)
    units = act.shape[1]
    pack[:, width : width + units] = act
    pack[:, width + units :] = grad_pre
    total = total + dot_nt(grad_pre, up_peer[...])
    partial_out[...] = total.astype(BF16)


def ffn_out_kernel(act_own, pack, down_own, down_peer, encoded_own, encoded_other, out, encoded_keep, send):
    units = act_own.shape[1]
    half, width = out.shape
    total = dot(act_own[...], down_own[...]) + dot(pack[:, width : width + units], down_peer[...])
    total = total.astype(BF16)
    out[...] = total
    send[:half] = total
    rows = encoded_keep.shape[0]
    encoded_keep[...] = both(encoded_own[:rows], encoded_other[:rows]).astype(BF16)
    send[half:] = both(encoded_own[rows:], encoded_other[rows:]).astype(BF16)


def write_blocks(whole, first_bit, rest_bits, size, targets, extra=None):
    index = lax.axis_index("dp")
    count = 1 << len(rest_bits)
    for first, target in enumerate(targets):
        for entry in range(count):
            relative = first << first_bit
            for place, bit in enumerate(rest_bits):
                if entry >> (len(rest_bits) - 1 - place) & 1:
                    relative |= 1 << bit
            block = index ^ relative
            rows = whole[pl.ds(pl.multiple_of(block * size, size), size), :]
            target[entry, :size, :] = rows
            if extra is not None:
                target[entry, size:, :] = extra


def emit(whole, outs, order, size, extra=None):
    if order is None:
        outs[0][: whole.shape[0], :] = whole[...]
        if extra is not None:
            outs[0][whole.shape[0] :, :] = extra
    else:
        write_blocks(whole, order[0], order[1:], size, outs, extra)


def ffn_weights_kernel(orders, size, normed, pack, act_own, grad_pre_own, branch_own, branch_peer, *refs):
    *outs, whole, left, right = refs
    half, width = normed.shape
    units = act_own.shape[1]
    left[:half] = normed[...]
    left[half:] = pack[:, :width]
    right[:half] = grad_pre_own[...]
    right[half:] = pack[:, width + units :]
    whole[...] = dot_tn(left[...], right[...]).astype(BF16)
    count = 1 if orders[0] is None else 2
    emit(whole, outs[:count], orders[0], size)
    left[:half] = branch_own[...]
    left[half:] = branch_peer[...]
    right[:half] = act_own[...]
    right[half:] = pack[:, width : width + units]
    whole[...] = dot_tn(left[...], right[...]).astype(BF16)
    emit(whole, outs[count:], orders[1], size)


def cross_backward_kernel(
    chip_own, chip_other, hidden, gain, grad_out, wo_own, wo_peer, k_own, v_own, k_peer, v_peer,
    probs_own, probs_peer, wq_own, wq_peer,
    partial_out, grad_hidden, gain_grad, gl_own, gl_peer, gc_own, gc_peer, gq_own, branch, pack,
):
    incoming = chip_own[...].astype(F32) + chip_other[...].astype(F32)
    added, gain_terms = norm_back(hidden[...], row_of(gain), incoming)
    gain_grad[...] = jnp.broadcast_to(gain_terms, gain_grad.shape)
    grad = grad_out[...] + added
    grad_hidden[...] = grad
    rounded = grad.astype(BF16)
    branch[...] = rounded
    width = rounded.shape[1]
    pack[:, :width] = rounded
    context = dot_nt(rounded, wo_own[...]).astype(BF16)
    gc_own[...] = context
    queries = heads_backward(context, k_own[...], v_own[...], probs_own, gl_own)
    gq_own[...] = queries
    total = dot(queries, wq_own[...])
    context = dot_nt(rounded, wo_peer[...]).astype(BF16)
    gc_peer[...] = context
    queries = heads_backward(context, k_peer[...], v_peer[...], probs_peer, gl_peer)
    pack[:, width:] = queries
    total = total + dot(queries, wq_peer[...])
    partial_out[...] = total.astype(BF16)


def source_grad_kernel(gl_peer, probs_peer, gc_peer, q_peer, out):
    span = out.shape[0] // 2
    middle = span // 2
    for start, grads in (
        (0, heads_transposed(gl_peer, q_peer[...], SCALE)),
        (span, heads_transposed(probs_peer, gc_peer[...], 1.0)),
    ):
        out[start : start + middle] = grads[middle:]
        out[start + middle : start + span] = grads[:middle]


def cross_weights_kernel(
    orders, size, gl_own, probs_own, gc_own, q_own, other, e0, e1, e2, e3, normed, pack_forward,
    branch, pack_backward, context_own, gq_own, *refs,
):
    *outs, source, whole, left, right = refs
    count = len(outs) // 2
    span = other.shape[0] // 2
    half, width = normed.shape
    columns = q_own.shape[1]
    source[:, :columns] = low_sum(heads_transposed(gl_own, q_own[...], SCALE), other[:span])
    source[:, columns:] = low_sum(heads_transposed(probs_own, gc_own[...], 1.0), other[span:])
    for index, part in enumerate((e0, e1, e2, e3)):
        left[index * half : (index + 1) * half] = part[...]
    whole[...] = dot_tn(left[...], source[...]).astype(BF16)
    emit(whole, outs[:count], orders[0], size)
    left[:half] = normed[...]
    left[half : 2 * half] = pack_forward[:, :width]
    left[2 * half : 3 * half] = branch[...]
    left[3 * half :] = pack_backward[:, :width]
    right[...] = jnp.zeros_like(right)
    right[:half, :columns] = gq_own[...]
    right[half : 2 * half, :columns] = pack_backward[:, width:]
    right[2 * half : 3 * half, columns:] = context_own[...]
    right[3 * half :, columns:] = pack_forward[:, width:]
    whole[...] = dot_tn(left[...], right[...]).astype(BF16)
    emit(whole, outs[count:], orders[1], size)


def encoded_kernel(source, wk_own, wv_own, keep, send):
    columns = wk_own.shape[0]
    terms = dot(source[:, :columns], wk_own[...]) + dot(source[:, columns:], wv_own[...])
    terms = terms.astype(BF16)
    rows = keep.shape[0]
    keep[...] = terms[:rows]
    send[...] = terms[rows:]


def self_norm_kernel(chip_own, chip_other, hidden, gain, grad_hidden, gain_ffn, grad_out, pack):
    half = hidden.shape[0]
    incoming = chip_own[...].astype(F32) + chip_other[...].astype(F32)
    added, gain_terms = norm_back(hidden[...], row_of(gain), incoming)
    grad = grad_hidden[...] + added
    grad_out[...] = grad
    pack[:half] = grad.astype(BF16)
    row = lax.broadcasted_iota(jnp.int32, (EXTRA, hidden.shape[1]), 0)
    extra = jnp.where(row == 0, gain_terms, 0.0) + jnp.where(row == 1, gain_ffn[:1], 0.0)
    pack[half:] = extra.astype(BF16)


def high_low(vector):
    high = vector.astype(BF16).astype(F32)
    row = lax.broadcasted_iota(jnp.int32, (EXTRA, vector.shape[1]), 0)
    return (jnp.where(row == 0, high, 0.0) + jnp.where(row == 1, vector - high, 0.0)).astype(BF16)


def of_high_low(rows):
    rows = rows.astype(F32)
    return rows[:1] + rows[1:2]


def self_backward_kernel(
    pack_own, pack_peer, w_output, w_query, w_key, w_value, queries, keys, values, probs, x,
    keep, send, branch_out, gq_out, gk_out, gv_out, gl_out, whole,
):
    half = keep.shape[0] - EXTRA
    core = lax.axis_index("tensor") % 2
    branch_out[own_rows(core, half), :] = pack_own[:half]
    branch_out[own_rows(1 - core, half), :] = pack_peer[:half]
    context = dot_nt(branch_out[...], w_output[...]).astype(BF16)
    grad_queries = heads_backward(context, keys[...], values[...], probs, gl_out)
    grad_keys = heads_transposed(gl_out, queries[...], SCALE)
    grad_values = heads_transposed(probs, context, 1.0)
    gq_out[...] = grad_queries
    gk_out[...] = grad_keys
    gv_out[...] = grad_values
    total = dot(grad_queries, w_query[...]) + dot(grad_keys, w_key[...]) + dot(grad_values, w_value[...])
    whole[...] = total.astype(BF16)
    keep[:half] = whole[own_rows(core, half), :]
    send[:half] = whole[own_rows(1 - core, half), :]
    resid = x[...].astype(F32)
    gain_terms = high_low(jnp.sum(total * resid * inverse_rms(resid), 0, keepdims=True))
    keep[half:] = gain_terms
    send[half:] = gain_terms


def input_sum_kernel(own, peer, out):
    half = out.shape[0] - EXTRA
    out[:half] = both(own[:half], peer[:half]).astype(BF16)
    out[half:] = high_low(of_high_low(own[half:]) + of_high_low(peer[half:]))


def self_first_kernel(order, size, normed, gq, gk, *refs):
    *outs, whole, right = refs
    columns = gq.shape[1]
    right[:, :columns] = gq[...]
    right[:, columns:] = gk[...]
    whole[...] = dot_tn(normed[...], right[...]).astype(BF16)
    emit(whole, outs, order, size)


def self_second_kernel(order, size, buckets, normed, branch, gv, context, gl, bucket, pack_own, pack_peer, *refs):
    *outs, whole, right, left = refs
    length, columns = gv.shape
    half = pack_own.shape[0] - EXTRA
    left[:length] = normed[...]
    left[length:] = branch[...]
    right[...] = jnp.zeros_like(right)
    right[:length, :columns] = gv[...]
    right[length:, columns:] = context[...]
    whole[...] = dot_tn(left[...], right[...]).astype(BF16)
    onehot = reversed_onehot(bucket, buckets)
    row = lax.broadcasted_iota(jnp.int32, (length, length), 0)
    column = lax.broadcasted_iota(jnp.int32, (length, length), 1)
    turn = jnp.where(row + column == length - 1, 1.0, 0.0).astype(BF16)
    place = lax.broadcasted_iota(jnp.int32, (8, length), 0)
    sums = jnp.zeros((8, length), F32)
    for head in range(gl.shape[0]):
        skewed = pltpu.roll(dot(turn, gl[head]), 1, 1, stride=1, stride_axis=0)
        sums = sums + jnp.where(place == head, jnp.sum(skewed, 0, keepdims=True), 0.0)
    table = lax.dot_general(
        sums, onehot, (((1,), (1,)), ((), ())), precision=lax.Precision.HIGHEST, preferred_element_type=F32
    )
    gains = both(pack_own[half:], pack_peer[half:])
    wide = whole.shape[1]
    extra = two_rows(gains[:1], wide, 8, 0) + two_rows(gains[1:2], wide, 8, 2)
    table = jnp.concatenate([table, jnp.zeros((8, wide - buckets), F32)], 1)
    emit(whole, outs, order, size, jnp.concatenate([extra, table], 0).astype(BF16))


def two_rows(vector, wide, count, first):
    row = lax.broadcasted_iota(jnp.int32, (count, wide), 0)
    return jnp.where(row == first, vector[:, :wide], 0.0) + jnp.where(row == first + 1, vector[:, wide:], 0.0)


def input_grad_kernel(chip_own, chip_other, x, gain, grad_hidden, hidden_two, out_own, out_other, pack):
    half = hidden_two.shape[0]
    resid = x[own_rows(lax.axis_index("tensor") % 2, half), :].astype(F32)
    added, _ = norm_back(resid, row_of(gain), both(chip_own[:half], chip_other[:half]))
    pack[:half] = (grad_hidden[...] + added).astype(BF16)
    pack[half:] = (hidden_two[...] + both(out_own[...], out_other[:half])).astype(BF16)


def rows_kernel(own, peer, encoded_own, encoded_other, input_grad, layer_out, encoded_grad):
    half = own.shape[0] // 2
    core = lax.axis_index("tensor") % 2
    for place, out in ((0, input_grad), (half, layer_out)):
        out[own_rows(core, half), :] = own[place : place + half]
        out[own_rows(1 - core, half), :] = peer[place : place + half]
    encoded_grad[...] = both(encoded_own[...], encoded_other[half:]).astype(BF16)


def both(left, right):
    return left.astype(F32) + right.astype(F32)


def low_sum(left, right):
    return both(left, right).astype(BF16)


def round_two_kernel(
    up_keep, up_got, down_keep, down_got, ca_send, cb_send, zo_send, up_next, x_send, down_next
):
    wide = ca_send.shape[2]
    for keep, got, new, send, other in (
        (up_keep, up_got, up_next, zo_send, cb_send),
        (down_keep, down_got, down_next, x_send, ca_send),
    ):
        for entry in range(2):
            new[entry] = low_sum(keep[entry], got[entry])
            send[entry] = low_sum(keep[2 + entry], got[2 + entry])
            send[2 + entry, :, :wide] = other[2 * entry]
            send[2 + entry, :, wide:] = other[2 * entry + 1]


def round_three_kernel(
    up_keep, down_keep, zo_got, x_got, ca_keep, cb_keep, sa_send, sb_send, chip_own, chip_other,
    ffn_send, ffn_keep, x_send, zo_send, ca_next, cb_next, gains,
):
    size, wide = ca_keep.shape[1:]
    more = sb_send.shape[1]
    for entry, target in enumerate((ffn_keep, ffn_send)):
        target[:size] = low_sum(up_keep[entry], zo_got[entry])
        target[size:] = low_sum(down_keep[entry], x_got[entry])

    def first_sum(keep, got, entry):
        side = (entry % 2) * wide
        return low_sum(keep[entry], got[2 + entry // 2, :, side : side + wide])

    half = chip_own.shape[0] - EXTRA
    gain = of_high_low(chip_own[half:]) + of_high_low(chip_other[half:])
    gain = two_rows(gain, wide, EXTRA, 4).astype(BF16)
    gains[...] = gain
    for entry in range(2):
        ca_next[entry] = first_sum(ca_keep, x_got, entry)
        cb_next[entry] = first_sum(cb_keep, zo_got, entry)
        x_send[entry] = first_sum(cb_keep, zo_got, 2 + entry)
        zo_send[entry * size : (entry + 1) * size] = first_sum(ca_keep, x_got, 2 + entry)
    for entry in range(4):
        x_send[2 + entry] = sa_send[entry]
        start = 2 * size + entry * more
        zo_send[start : start + size] = sb_send[entry, :size]
        zo_send[start + size : start + more] = low_sum(sb_send[entry, size:], gain)


def round_four_kernel(
    x_got, zo_got, ca_keep, cb_keep, sa_keep, sb_keep, gains,
    cross_send, cross_keep, sa_send, sa_next, sb_send, sb_next,
):
    size = ca_keep.shape[1]
    more = sb_keep.shape[1]
    for entry, target in enumerate((cross_keep, cross_send)):
        target[:size] = low_sum(ca_keep[entry], zo_got[entry * size : (entry + 1) * size])
        target[size:] = low_sum(cb_keep[entry], x_got[entry])
    for first, sa_out, sb_out in ((0, sa_next, sb_next), (2, sa_send, sb_send)):
        for entry in range(2):
            sa_out[entry] = low_sum(sa_keep[first + entry], x_got[2 + first + entry])
            start = 2 * size + (first + entry) * more
            sb_out[entry, :size] = low_sum(sb_keep[first + entry, :size], zo_got[start : start + size])
            extra = low_sum(sb_keep[first + entry, size:], gains[...])
            sb_out[entry, size:] = low_sum(extra, zo_got[start + size : start + more])


def round_five_kernel(sa_keep, sa_got, sb_keep, sb_got, send, keep):
    size = sa_keep.shape[1]
    for entry, target in enumerate((keep, send)):
        target[:size] = low_sum(sa_keep[entry], sa_got[entry])
        target[size:] = low_sum(sb_keep[entry], sb_got[entry])


def ffn_final_kernel(keep, got, up, down):
    size = up.shape[0]
    up[...] = both(keep[:size], got[:size])
    down[...] = both(keep[size:], got[size:])


def pair_final(keep, got, rows, first, second, turn):
    count = first.shape[1]
    total = both(keep[rows], got[rows])
    first[...] = total[:, :count]
    second[...] = total[:, count:].T if turn else total[:, count:]


def cross_final_kernel(keep, got, key, value, query, output):
    size = key.shape[0]
    pair_final(keep, got, slice(0, size), key, value, False)
    pair_final(keep, got, slice(size, 2 * size), query, output, True)


def self_final_kernel(keep, got, query, key, value, output, table, gain_two, gain_three, gain_one):
    size = key.shape[0]
    pair_final(keep, got, slice(0, size), query, key, False)
    pair_final(keep, got, slice(size, 2 * size), value, output, True)
    extra = both(keep[2 * size :], got[2 * size :])
    table[...] = extra[8 : 8 + table.shape[0], : table.shape[1]]
    wide = 2 * extra.shape[1]
    back = wide - lax.axis_index("dp") * size
    for row, out in ((0, gain_two), (2, gain_three), (4, gain_one)):
        whole = jnp.concatenate([extra[row : row + 1], extra[row + 1 : row + 2]], 1)
        out[...] = pltpu.roll(jnp.broadcast_to(whole, (8, wide)), back, 1)[:1, :size]


def run(kernel, name, outs, ins, us=0.0, scratch=(), scalars=0, far=0, sems=0, after=(), limit=VMEM_LIMIT):
    shapes = [jax.ShapeDtypeStruct(shape, dtype) for shape, dtype in outs]
    idle = len(after)
    body = kernel
    if idle:

        def body(*refs):
            kernel(*refs[: len(ins)], *refs[len(ins) + idle :])

    vmem = pl.BlockSpec(memory_space=pltpu.VMEM)
    smem = pl.BlockSpec(memory_space=pltpu.SMEM)
    hbm = pl.BlockSpec(memory_space=pltpu.HBM)
    free = pl.BlockSpec(memory_space=pl.ANY)
    place = [smem] * scalars + [hbm] * far + [vmem] * (len(ins) - scalars - far) + [free] * idle
    ins = [
        pltpu.with_memory_space_constraint(item, pltpu.HBM) if spec is hbm else item for item, spec in zip(ins, place)
    ]
    result = pl.pallas_call(
        body,
        out_shape=shapes,
        in_specs=place,
        out_specs=[vmem] * len(shapes),
        scratch_shapes=[pltpu.VMEM(shape, dtype) for shape, dtype in scratch]
        + ([pltpu.SemaphoreType.DMA((sems,))] if sems else []),
        compiler_params=pltpu.CompilerParams(vmem_limit_bytes=limit),
        cost_estimate=pl.CostEstimate(flops=int(us * 1.15e9), bytes_accessed=0, transcendentals=0),
        name=name,
    )(*ins, *after)
    return result[0] if len(shapes) == 1 else result


def listed(result):
    return list(result) if isinstance(result, (list, tuple)) else [result]


def to_core(value):
    return lax.ppermute(value, "tensor", [(i, i ^ 1) for i in range(lax.axis_size("tensor"))])


def to_chip(value):
    return lax.ppermute(value, "tensor", [(i, i ^ 2) for i in range(lax.axis_size("tensor"))])


def to_peer(value, bit):
    return lax.ppermute(value, "dp", [(i, i ^ (1 << bit)) for i in range(lax.axis_size("dp"))])


def on_device(
    inputs, encoded, dec_len, enc_len, language, objective, distance_bucket, token_weights, cotangent,
    gain_self, self_query, self_key, self_value, self_output, bias_table,
    gain_cross, cross_query, cross_key, cross_value, cross_output, gain_ffn, ffn_up, ffn_down,
):
    seqs, length, width = inputs.shape
    half = length // 2
    columns = self_query.shape[1]
    heads = columns // HEAD_DIM
    units = ffn_up.shape[1]
    span_part = encoded.shape[1]
    span = span_part * lax.axis_size("tensor")
    dp = lax.axis_size("dp")
    size = width // dp
    bits = dp.bit_length() - 1
    halving = bits == 3 and dp == 8 and size % 16 == 0
    along_x, along_z = ((0, 1, 2), (1, 0, 2)) if halving else (None, None)
    latest = []

    def go(kernel, name, outs, ins, last=False, **how):
        after = [item for item in latest if not any(item is one for one in ins)]
        result = run(kernel, name, outs, ins, after=after, **how)
        if not last:
            results = result if isinstance(result, (list, tuple)) else [result]
            latest[:] = [min(results, key=lambda item: item.size * item.dtype.itemsize)]
        return result

    def plus(left, right, name):
        return go(add_kernel, name, [(left.shape, left.dtype)], [left, right])

    def payload(order, wide, extra=0):
        if order is None:
            return [((width + extra, wide), BF16)]
        return [((dp // 2, size + extra, wide), BF16)] * 2

    x = inputs.reshape(length, width)
    cot = cotangent.reshape(length, width)
    gain_one, gain_two, gain_three = gain_self, gain_cross, gain_ffn
    self_query, self_key, self_value = self_query.T, self_key.T, self_value.T
    cross_query, cross_key, cross_value = cross_query.T, cross_key.T, cross_value.T
    table = bias_table.T
    bucket = distance_bucket.reshape(1, length)
    e0 = encoded.reshape(span_part, width)

    e1 = to_chip(e0)
    e2 = to_core(e0)
    e3 = to_core(e1)
    wk_peer = to_core(cross_key)
    wv_peer = to_core(cross_value)
    keep, send, normed_one, query_one, key_one, value_one, context_one, probs_one = go(
        self_forward_kernel, "self_forward",
        [((half, width), BF16)] * 2 + [((length, width), BF16)] + [((length, columns), BF16)] * 4
        + [((heads, length, length), BF16)],
        [dec_len, x, gain_one, self_query, self_key, self_value, self_output, bucket, table],
        scratch=[((length, width), BF16), (x.shape, BF16), (gain_one.shape, F32)] + [(self_query.shape, BF16)] * 3
        + [(self_output.shape, BF16), (bucket.shape, jnp.int32), (table.shape, F32)],
        scalars=1, far=8, sems=8, us=3.5,
    )
    latest.append(e2)
    got = to_core(send)
    source_outs = [((span // 2, columns), BF16)] * 4
    early = go(
        cross_source_kernel, "source_first", source_outs, [e0, e1, cross_key, cross_value, wk_peer, wv_peer], us=LONG
    )
    chip_one = plus(keep, got, "self_sum")
    other_one = to_chip(chip_one)
    wq_source, wo_source, _ = lax.optimization_barrier((cross_query, cross_output, chip_one))
    wq_peer = to_core(wq_source)
    wo_peer = to_core(wo_source)
    late = go(
        cross_source_kernel, "source_second", source_outs, [e2, e3, cross_key, cross_value, wk_peer, wv_peer],
        us=LONG,
    )

    (partial_two, hidden_one, normed_two, q_own, q_peer, context_own, probs_own, probs_peer, pack_forward,
     k_own, v_own, k_peer, v_peer) = go(
        cross_forward_kernel, "cross_forward",
        [((half, width), BF16), ((half, width), F32), ((half, width), BF16)] + [((half, columns), BF16)] * 3
        + [((heads, half, span), BF16)] * 2 + [((half, width + columns), BF16)] + [((span, columns), BF16)] * 4,
        [enc_len, chip_one, other_one, x, gain_two, cross_query, wq_peer, cross_output, wo_peer, *early, *late],
        scalars=1,
    )
    other_two = to_chip(partial_two)
    up_source, down_source, _ = lax.optimization_barrier((ffn_up, ffn_down, partial_two))
    down_peer = to_core(down_source)
    up_peer = to_core(up_source)
    pack_forward_peer = to_core(pack_forward)
    grad_full, branch_three, branch_three_peer, act_grad, act_grad_peer = go(
        out_grad_kernel, "out_grad",
        [((half, width), F32)] + [((half, width), BF16)] * 2 + [((half, units), F32)] * 2,
        [objective, language, dec_len, token_weights, cot, ffn_down, down_peer],
        scalars=3, us=FILL,
    )

    latest.append(pack_forward_peer)
    partial_three, hidden_two, normed_three, act_own, grad_pre_own, pack_ffn = go(
        ffn_kernel, "ffn",
        [((half, width), BF16), ((half, width), F32), ((half, width), BF16)] + [((half, units), BF16)] * 2
        + [((half, width + 2 * units), BF16)],
        [partial_two, other_two, hidden_one, gain_three, ffn_up, up_peer, act_grad, act_grad_peer],
    )
    other_three = to_chip(partial_three)
    pack_ffn_peer = to_core(pack_ffn)

    def ffn_weights(*refs):
        ffn_weights_kernel((along_x, along_z), size, *refs)

    ffn_payloads = go(
        ffn_weights, "ffn_weights", payload(along_x, width) + payload(along_z, width),
        [normed_three, pack_ffn_peer, act_own, grad_pre_own, branch_three, branch_three_peer],
        scratch=[((width, units), BF16), ((length, width), BF16), ((length, units), BF16)], us=FILL,
    )

    (partial_four, grad_two, gain_grad_three, gl_own, gl_peer, gc_own, gc_peer, gq_own, branch_two,
     pack_backward) = go(
        cross_backward_kernel, "cross_backward",
        [((half, width), BF16), ((half, width), F32), ((8, width), F32)] + [((heads, half, span), BF16)] * 2
        + [((half, columns), BF16)] * 3 + [((half, width), BF16), ((half, width + columns), BF16)],
        [partial_three, other_three, hidden_two, gain_three, grad_full, cross_output, wo_peer,
         k_own, v_own, k_peer, v_peer, probs_own, probs_peer, cross_query, wq_peer],
    )
    other_four = to_chip(partial_four)
    pack_backward_peer = to_core(pack_backward)
    source_grad = go(
        source_grad_kernel, "source_grad", [((2 * span, columns), BF16)], [gl_peer, probs_peer, gc_peer, q_peer]
    )
    source_grad_peer = to_core(source_grad)
    wide = 2 * columns

    def cross_weights(*refs):
        cross_weights_kernel((along_x, along_z), size, *refs)

    *cross_payload, source_total = go(
        cross_weights, "cross_weights", payload(along_x, wide) + payload(along_z, wide) + [((span, wide), BF16)],
        [gl_own, probs_own, gc_own, q_own, source_grad_peer, e0, e1, e2, e3, normed_two, pack_forward_peer,
         branch_two, pack_backward_peer, context_own, gq_own],
        scratch=[((width, wide), BF16), ((span, width), BF16), ((4 * half, wide), BF16)],
    )
    ca_payload, cb_payload = cross_payload[: len(cross_payload) // 2], cross_payload[len(cross_payload) // 2 :]

    if halving:
        up_keep, up_send, down_keep, down_send = ffn_payloads
        ca_keep, ca_send = ca_payload
        cb_keep, cb_send = cb_payload
        zo_send, up_keep, x_send, down_keep = go(
            round_two_kernel, "round_two",
            [((4, size, width), BF16), ((2, size, width), BF16)] * 2,
            [up_keep, to_peer(up_send, 0), down_keep, to_peer(down_send, 1), ca_send, cb_send],
        )
        x_got = to_peer(x_send, 0)
        zo_got = to_peer(zo_send, 1)

    grad_one, pack_self = go(
        self_norm_kernel, "self_norm", [((half, width), F32), ((half + EXTRA, width), BF16)],
        [partial_four, other_four, hidden_one, gain_two, grad_two, gain_grad_three],
    )
    pack_self_peer = to_core(pack_self)
    encoded_keep, encoded_send = go(
        encoded_kernel, "encoded", [((span // 2, width), BF16)] * 2, [source_total, cross_key, cross_value], us=FILL
    )
    encoded_got = to_core(encoded_send)
    keep, send, branch_one, gq_one, gk_one, gv_one, gl_one = go(
        self_backward_kernel, "self_backward",
        [((half + EXTRA, width), BF16)] * 2 + [((length, width), BF16)] + [((length, columns), BF16)] * 3
        + [((heads, length, length), BF16)],
        [pack_self, pack_self_peer, self_output, self_query, self_key, self_value, query_one, key_one, value_one,
         probs_one, x],
        scratch=[((length, width), BF16)],
    )
    got = to_core(send)

    def self_first(*refs):
        self_first_kernel(along_x, size, *refs)

    def self_second(*refs):
        self_second_kernel(along_z, size, table.shape[1], *refs)

    sb_payload = listed(go(
        self_second, "self_second", payload(along_z, wide, EXTRA),
        [normed_one, branch_one, gv_one, context_one, gl_one, bucket, pack_self, pack_self_peer],
        scratch=[((width, wide), BF16), ((2 * length, wide), BF16), ((2 * length, width), BF16)], us=FILL,
    ))
    chip_five = go(input_sum_kernel, "input_sum", [(keep.shape, BF16)], [keep, got])
    other_five = to_chip(chip_five)
    sa_payload = listed(go(
        self_first, "self_first", payload(along_x, wide), [normed_one, gq_one, gk_one],
        scratch=[((width, wide), BF16), ((length, wide), BF16)], us=FILL,
    ))

    if halving:
        sa_keep, sa_send = sa_payload
        sb_keep, sb_send = sb_payload
        more = size + EXTRA
        ffn_send, ffn_keep, x_send, zo_send, ca_keep, cb_keep, gains = go(
            round_three_kernel, "round_three",
            [((2 * size, width), BF16)] * 2 + [((6, size, wide), BF16), ((2 * size + 4 * more, wide), BF16)]
            + [((2, size, wide), BF16)] * 2 + [((EXTRA, wide), BF16)],
            [up_keep, down_keep, zo_got, x_got, ca_keep, cb_keep, sa_send, sb_send, chip_five, other_five],
        )
        x_got = to_peer(x_send, 0)
        zo_got = to_peer(zo_send, 1)
        ffn_got = to_peer(ffn_send, 2)

    branch_out, encoded_part, out_send = go(
        ffn_out_kernel, "ffn_out", [((half, width), BF16), ((span_part, width), BF16), ((half + span_part, width), BF16)],
        [act_own, pack_ffn, ffn_down, down_peer, encoded_keep, encoded_got],
    )
    out_other = to_chip(out_send)

    if halving:
        cross_send, cross_keep, sa_send, sa_keep, sb_send, sb_keep = go(
            round_four_kernel, "round_four",
            [((2 * size, wide), BF16)] * 2 + [((2, size, wide), BF16)] * 2 + [((2, more, wide), BF16)] * 2,
            [x_got, zo_got, ca_keep, cb_keep, sa_keep, sb_keep, gains],
        )
        sa_got = to_peer(sa_send, 1)
        sb_got = to_peer(sb_send, 0)
        cross_got = to_peer(cross_send, 2)
        up, down = go(ffn_final_kernel, "ffn_final", [((size, width), F32)] * 2, [ffn_keep, ffn_got], us=LONG, last=True)

    pack_rows = go(
        input_grad_kernel, "input_grad", [((2 * half, width), BF16)],
        [chip_five, other_five, x, gain_one, grad_one, hidden_two, branch_out, out_other],
    )
    pack_rows_peer = to_core(pack_rows)

    if halving:
        self_send, self_keep = go(
            round_five_kernel, "round_five", [((size + more, wide), BF16)] * 2, [sa_keep, sa_got, sb_keep, sb_got]
        )
        self_got = to_peer(self_send, 2)

    input_grad, layer_out, encoded_grad = go(
        rows_kernel, "rows", [((length, width), BF16)] * 2 + [((span_part, width), BF16)],
        [pack_rows, pack_rows_peer, encoded_part, out_other], last=True,
    )

    if halving:
        square = ((size, columns), F32)
        turned = ((columns, size), F32)
        grad_cross_key, grad_cross_value, grad_cross_query, grad_cross_output = go(
            cross_final_kernel, "cross_final", [square] * 3 + [turned], [cross_keep, cross_got], us=LONG, last=True
        )
        (grad_self_query, grad_self_key, grad_self_value, grad_self_output, grad_table, grad_gain_two,
         grad_gain_three, grad_gain_one) = go(
            self_final_kernel, "self_final",
            [square] * 3 + [turned, (table.shape, F32)] + [((1, size), F32)] * 3, [self_keep, self_got], last=True,
        )
        grad_gain_one, grad_gain_two, grad_gain_three = (
            item.reshape(size) for item in (grad_gain_one, grad_gain_two, grad_gain_three)
        )
    else:
        index = lax.axis_index("dp")

        def gain_part(*rows):
            row = lax.psum(jnp.concatenate(rows, 0).astype(F32), "dp")
            return lax.dynamic_slice(row, (index * size,), (size,))

        def scattered(item):
            return lax.psum_scatter(item.astype(F32), "dp", scatter_dimension=0, tiled=True)

        def pair_of(item):
            item = scattered(item)
            return item[:, :columns], item[:, columns:]

        up, down = (scattered(item) for item in ffn_payloads)
        grad_cross_key, grad_cross_value = pair_of(ca_payload[0])
        grad_cross_query, grad_cross_output = pair_of(cb_payload[0])
        grad_self_query, grad_self_key = pair_of(sa_payload[0])
        grad_self_value, grad_self_output = pair_of(sb_payload[0][:width])
        grad_cross_output, grad_self_output = grad_cross_output.T, grad_self_output.T
        extra = sb_payload[0][width:]
        grad_table = lax.psum(extra[8 : 8 + heads, : table.shape[1]].astype(F32), "dp")
        gain_rows = [item[half : half + 2] for item in (chip_five, other_five)]
        grad_gain_one = gain_part(jnp.sum(jnp.concatenate(gain_rows, 0).astype(F32), 0))
        grad_gain_two = gain_part(extra[0], extra[1])
        grad_gain_three = gain_part(extra[2], extra[3])

    return (
        layer_out.reshape(seqs, length, width),
        input_grad.reshape(seqs, length, width),
        encoded_grad.reshape(seqs, span_part, width),
        grad_gain_one,
        grad_self_query,
        grad_self_key,
        grad_self_value,
        grad_self_output,
        grad_table.T,
        grad_gain_two,
        grad_cross_query,
        grad_cross_key,
        grad_cross_value,
        grad_cross_output,
        grad_gain_three,
        up,
        down.T,
    )


def solution(mesh):
    return jax.shard_map(
        on_device,
        mesh=mesh,
        in_specs=(
            P("dp", None, None),
            P("dp", "tensor", None),
            P("dp"),
            P("dp"),
            P("dp"),
            P("dp"),
            P(),
            P(),
            P("dp", None, None),
            P(),
            P(None, "tensor"),
            P(None, "tensor"),
            P(None, "tensor"),
            P("tensor", None),
            P(None, "tensor"),
            P(),
            P(None, "tensor"),
            P(None, "tensor"),
            P(None, "tensor"),
            P("tensor", None),
            P(),
            P(None, "tensor"),
            P("tensor", None),
        ),
        out_specs=(
            P("dp", None, None),
            P("dp", None, None),
            P("dp", "tensor", None),
            P("dp"),
            P("dp", "tensor"),
            P("dp", "tensor"),
            P("dp", "tensor"),
            P("tensor", "dp"),
            P(None, "tensor"),
            P("dp"),
            P("dp", "tensor"),
            P("dp", "tensor"),
            P("dp", "tensor"),
            P("tensor", "dp"),
            P("dp"),
            P("dp", "tensor"),
            P("tensor", "dp"),
        ),
        check_vma=False,
    )
```

```python
import jax
import jax.numpy as jnp
from jax import lax
from jax.experimental import pallas as pl
from jax.experimental.pallas import tpu as pltpu
from jax.sharding import PartitionSpec as P

HEAD_DIM = 64
LANGS = 8
EPSILON = 1e-06
SCALE = 0.125
NEGATIVE = -1e30
F32 = jnp.float32
BF16 = jnp.bfloat16
VMEM_LIMIT = 20 * 1024 * 1024
EXTRA = 16
PIECE = 128
CROSS_X = 384
SELF_X = 512
FILL = 5.0
LONG = 20.0


def dot(left, right):
    return jnp.dot(left, right, preferred_element_type=F32)


def dot_nt(left, right):
    return lax.dot_general(left, right, (((1,), (1,)), ((), ())), preferred_element_type=F32)


def dot_tn(left, right):
    return lax.dot_general(left, right, (((0,), (0,)), ((), ())), preferred_element_type=F32)


def row_of(vector_ref):
    return vector_ref[...].reshape(1, vector_ref.shape[0])


def inverse_rms(resid):
    return lax.rsqrt(jnp.mean(resid * resid, -1, keepdims=True) + EPSILON)


def norm_back(resid, gain, incoming):
    scale = inverse_rms(resid)
    weighted = incoming * gain
    inner = jnp.mean(weighted * resid, -1, keepdims=True)
    grad = scale * weighted - resid * (scale * scale * scale * inner)
    gain_grad = jnp.sum(incoming * resid * scale, 0, keepdims=True)
    return grad, gain_grad


def groups_of(width):
    return [(start, min(2 * HEAD_DIM, width - start)) for start in range(0, width, 2 * HEAD_DIM)]


def head_mask(count, which, value):
    lane = lax.broadcasted_iota(jnp.int32, (1, count), 1)
    return jnp.where(lane // HEAD_DIM == which, value, 0.0).astype(BF16)


def stacked_heads(rows, value):
    width = rows.shape[1]
    if width == HEAD_DIM:
        return rows * jnp.asarray(value, BF16)
    return jnp.concatenate([rows * head_mask(width, inside, value) for inside in range(width // HEAD_DIM)], 0)


def own_blocks(product, count):
    rows = product.shape[1] // count
    return [
        product[inside * HEAD_DIM : (inside + 1) * HEAD_DIM, inside * rows : (inside + 1) * rows]
        for inside in range(count)
    ]


def heads_forward(queries, keys, values_turned, finish, probs_ref):
    rows = queries.shape[0]
    parts = []
    for start, width in groups_of(queries.shape[1]):
        head, count = start // HEAD_DIM, width // HEAD_DIM
        stacked = stacked_heads(queries[:, start : start + width], SCALE)
        logits = finish(head, count, dot_nt(keys[:, start : start + width], stacked))
        expo = jnp.exp(logits - jnp.max(logits, 0, keepdims=True))
        probs = (expo * (1.0 / jnp.sum(expo, 0, keepdims=True))).astype(BF16)
        probs_ref[:, head * rows : (head + count) * rows] = probs
        parts += own_blocks(dot(values_turned[start : start + width], probs), count)
    return jnp.concatenate(parts, 0).astype(BF16)


def heads_backward(grad_context, keys_turned, values, probs_ref, grad_logits_ref):
    rows = grad_context.shape[0]
    parts = []
    for start, width in groups_of(grad_context.shape[1]):
        head, count = start // HEAD_DIM, width // HEAD_DIM
        place = slice(head * rows, (head + count) * rows)
        stacked = stacked_heads(grad_context[:, start : start + width], 1.0)
        grad_probs = dot_nt(values[:, start : start + width], stacked)
        probs = probs_ref[:, place].astype(F32)
        weighted = jnp.sum(grad_probs * probs, 0, keepdims=True)
        grad_logits = (probs * (grad_probs - weighted)).astype(BF16)
        grad_logits_ref[:, place] = grad_logits
        parts += own_blocks(SCALE * dot(keys_turned[start : start + width], grad_logits), count)
    return jnp.concatenate(parts, 0).astype(BF16)


def heads_spread(matrix_ref, rows, factor):
    length = rows.shape[0]
    parts = []
    for start, width in groups_of(rows.shape[1]):
        head, count = start // HEAD_DIM, width // HEAD_DIM
        stacked = stacked_heads(rows[:, start : start + width], 1.0)
        parts.append(factor * dot(matrix_ref[:, head * length : (head + count) * length], stacked))
    return jnp.concatenate(parts, 1).astype(BF16)


def own_rows(core, half):
    return pl.ds(pl.multiple_of(core * half, half), half)


def bucket_onehot(bucket_ref, buckets):
    wanted = lax.broadcasted_iota(jnp.int32, (buckets, bucket_ref.shape[1]), 0)
    return jnp.where(bucket_ref[...] == wanted, 1.0, 0.0)


def add_kernel(left_ref, right_ref, out_ref):
    out_ref[...] = (left_ref[...].astype(F32) + right_ref[...].astype(F32)).astype(out_ref.dtype)


def first_kernel(out):
    out[...] = jnp.zeros_like(out)


def step_kernel(enc_len, objective, language, info, mask):
    info[...] = jnp.full(info.shape, objective[0] * LANGS + language[0], jnp.int32)
    rows = mask.shape[0] // 4
    row = lax.broadcasted_iota(jnp.int32, mask.shape, 0)
    block = row // rows
    flip = jnp.where(block % 2 == 1, 1, 0) + jnp.where(block >= 2, 2, 0)
    position = (lax.axis_index("tensor") ^ flip) * rows + row % rows
    mask[...] = jnp.where(position < enc_len[0], 0.0, NEGATIVE)


def self_sum_kernel(own, first, second, out):
    rows = first.shape[0]
    out[:rows] = both(own[:rows], first[...]).astype(BF16)
    out[rows : 2 * rows] = both(own[rows:], second[...]).astype(BF16)
    out[2 * rows :] = jnp.zeros((out.shape[0] - 2 * rows, out.shape[1]), BF16)


def self_forward_kernel(
    dec_len, bucket, table, x, gain, w_query, w_key, w_value, w_output,
    keep, send, more, normed_out, query_out, context_out, probs_out, dec_out, whole,
):
    dec_out[...] = jnp.full(dec_out.shape, dec_len[0], jnp.int32)
    length = x.shape[0]
    resid = x[...].astype(F32)
    normed = (resid * inverse_rms(resid) * row_of(gain)).astype(BF16)
    normed_out[...] = normed
    queries = dot_nt(normed, w_query[...]).astype(BF16)
    keys = dot_nt(normed, w_key[...]).astype(BF16)
    values = dot_nt(w_value[...], normed).astype(BF16)
    query_out[...] = queries
    by_distance = lax.dot_general(
        table[...],
        bucket_onehot(bucket, table.shape[1]),
        (((1,), (0,)), ((), ())),
        precision=lax.Precision.HIGHEST,
        preferred_element_type=F32,
    )
    row = lax.broadcasted_iota(jnp.int32, (length, length), 0)
    column = lax.broadcasted_iota(jnp.int32, (length, length), 1)
    allowed = (row <= column) & (row < dec_len[0])

    def finish(head, count, scores):
        parts = []
        for inside in range(count):
            spread = jnp.broadcast_to(by_distance[head + inside : head + inside + 1], (length, length))
            bias = pltpu.roll(spread, 0, 1, stride=1, stride_axis=0)
            part = scores[:, inside * length : (inside + 1) * length]
            parts.append(jnp.where(allowed, part + bias, NEGATIVE))
        return jnp.concatenate(parts, 1) if count > 1 else parts[0]

    context = heads_forward(queries, keys, values, finish, probs_out)
    context_out[...] = context.T
    whole[...] = dot_tn(context, w_output[...]).astype(BF16)
    half = keep.shape[0]
    core = lax.axis_index("tensor") % 2
    keep[...] = whole[own_rows(core, half), :]
    rows = send.shape[0]
    send[...] = whole[own_rows(2 - 2 * core, rows), :]
    more[...] = whole[own_rows(3 - 2 * core, rows), :]


def source_first_kernel(first, second, wk_own, wv_own, wk_peer, wv_peer, k_own, v_own, k_peer, v_peer):
    rows = first.shape[0]
    for index, part in enumerate((first, second)):
        place = slice(index * rows, (index + 1) * rows)
        for weight, out in ((wk_own, k_own), (wk_peer, k_peer)):
            out[place, :] = dot_nt(part[...], weight[...]).astype(BF16)
        for weight, out in ((wv_own, v_own), (wv_peer, v_peer)):
            out[:, place] = dot_nt(weight[...], part[...]).astype(BF16)


def source_second_kernel(
    first, second, wk_own, wv_own, wk_peer, wv_peer, early_k_own, early_v_own, early_k_peer, early_v_peer,
    k_own, v_own, k_peer, v_peer,
):
    rows = first.shape[0]
    for early, out in ((early_k_own, k_own), (early_k_peer, k_peer)):
        out[: 2 * rows] = early[...]
    for early, out in ((early_v_own, v_own), (early_v_peer, v_peer)):
        out[:, : 2 * rows] = early[...]
    for index, part in enumerate((first, second)):
        place = slice((2 + index) * rows, (3 + index) * rows)
        for weight, out in ((wk_own, k_own), (wk_peer, k_peer)):
            out[place, :] = dot_nt(part[...], weight[...]).astype(BF16)
        for weight, out in ((wv_own, v_own), (wv_peer, v_peer)):
            out[:, place] = dot_nt(weight[...], part[...]).astype(BF16)


def source_back_kernel(
    normed, w_key, w_value, e0, e1, e2, e3, wk_own, wv_own, wk_peer, wv_peer,
    keys_turned, values, k_own, v_own, k_peer, v_peer,
):
    keys_turned[...] = dot_nt(w_key[...], normed[...]).astype(BF16)
    values[...] = dot_nt(normed[...], w_value[...]).astype(BF16)
    rows = e0.shape[0]
    for index, part in enumerate((e0, e2, e1, e3)):
        place = slice(index * rows, (index + 1) * rows)
        for weight, out in ((wk_own, k_own), (wk_peer, k_peer)):
            out[:, place] = dot_nt(weight[...], part[...]).astype(BF16)
        for weight, out in ((wv_own, v_own), (wv_peer, v_peer)):
            out[place, :] = dot_nt(part[...], weight[...]).astype(BF16)


def out_grad_kernel(info, dec_len, token_weights, cotangent, grad_own, branch_own, branch_peer):
    half = grad_own.shape[0]
    length = cotangent.shape[0]
    core = lax.axis_index("tensor") % 2
    row = lax.broadcasted_iota(jnp.int32, token_weights.shape, 0)
    weights = jnp.sum(jnp.where(row == info[:1, :1], token_weights[...], 0.0), 0, keepdims=True)
    position = lax.broadcasted_iota(jnp.int32, (1, length), 1)
    weights = jnp.where(position < dec_len[:1, :1], weights, 0.0)

    def rows_of(side):
        row = lax.broadcasted_iota(jnp.int32, (half, length), 0) + side * half
        column = lax.broadcasted_iota(jnp.int32, (half, length), 1)
        factor = jnp.sum(jnp.where(row == column, weights, 0.0), -1, keepdims=True)
        return cotangent[own_rows(side, half), :].astype(F32) * factor

    own = rows_of(core)
    grad_own[...] = own
    branch_own[...] = own.astype(BF16)
    branch_peer[...] = rows_of(1 - core).astype(BF16)


def act_grad_kernel(branch, down_own, down_peer, own, peer):
    own[...] = dot_nt(branch[...], down_own[...])
    peer[...] = dot_nt(branch[...], down_peer[...])


def cross_forward_kernel(
    mask, chip_own, chip_other, x, gain, wq_own, wq_peer, wo_own, wo_peer, k_own, v_own, k_peer, v_peer,
    partial_out, hidden_out, normed_out, q_own, q_peer, context_own, probs_own, probs_peer, pack,
):
    half, width = hidden_out.shape
    core = lax.axis_index("tensor") % 2
    resid = x[own_rows(core, half), :].astype(F32)
    resid = resid + both(chip_own[:half], chip_other[:half])
    hidden_out[...] = resid
    normed = (resid * inverse_rms(resid) * row_of(gain)).astype(BF16)
    normed_out[...] = normed
    pack[:, :width] = normed

    def finish(head, count, scores):
        return scores + jnp.concatenate([mask[...]] * count, 1)

    queries = dot_nt(normed, wq_own[...]).astype(BF16)
    q_own[...] = queries
    first = heads_forward(queries, k_own[...], v_own[...], finish, probs_own)
    context_own[...] = first.T
    queries = dot_nt(normed, wq_peer[...]).astype(BF16)
    q_peer[...] = queries
    second = heads_forward(queries, k_peer[...], v_peer[...], finish, probs_peer)
    pack[:, width:] = second.T
    partial_out[...] = (dot_tn(first, wo_own[...]) + dot_tn(second, wo_peer[...])).astype(BF16)


def ffn_kernel(
    chip_own, chip_other, hidden, gain, up_own, up_peer, act_grad_own, act_grad_peer,
    partial_out, hidden_out, normed_out, act_own, grad_pre_own, pack,
):
    width = hidden.shape[1]
    resid = hidden[...] + (chip_own[...].astype(F32) + chip_other[...].astype(F32))
    hidden_out[...] = resid
    normed = (resid * inverse_rms(resid) * row_of(gain)).astype(BF16)
    normed_out[...] = normed
    pack[:, :width] = normed

    def through(up, act_grad):
        pre = dot(normed, up[...])
        square = pre * pre
        tanh = jnp.tanh(0.7978845608028654 * (pre + 0.044715 * square * pre))
        half_sum = 0.5 * (1.0 + tanh)
        slope = half_sum + 0.5 * pre * (1.0 - tanh * tanh) * (
            0.7978845608028654 * (1.0 + 3.0 * 0.044715 * square)
        )
        return (pre * half_sum).astype(BF16), (act_grad[...] * slope).astype(BF16)

    act, grad_pre = through(up_own, act_grad_own)
    act_own[...] = act
    grad_pre_own[...] = grad_pre
    total = dot_nt(grad_pre, up_own[...])
    act, grad_pre = through(up_peer, act_grad_peer)
    units = act.shape[1]
    pack[:, width : width + units] = act
    pack[:, width + units :] = grad_pre
    total = total + dot_nt(grad_pre, up_peer[...])
    partial_out[...] = total.astype(BF16)


def ffn_out_kernel(act_own, pack, down_own, down_peer, out):
    units = act_own.shape[1]
    width = out.shape[1]
    total = dot(act_own[...], down_own[...]) + dot(pack[:, width : width + units], down_peer[...])
    out[...] = total.astype(BF16)


def write_blocks(whole, columns, first_bit, rest_bits, size, targets, extra=None):
    index = lax.axis_index("dp")
    count = 1 << len(rest_bits)
    for first, target in enumerate(targets):
        for entry in range(count):
            relative = first << first_bit
            for place, bit in enumerate(rest_bits):
                if entry >> (len(rest_bits) - 1 - place) & 1:
                    relative |= 1 << bit
            block = index ^ relative
            rows = whole[pl.ds(pl.multiple_of(block * size, size), size), columns]
            target[entry, :size, :] = rows
            if extra is not None:
                target[entry, size:, :] = extra


def emit(whole, outs, order, size, extra=None, columns=slice(None)):
    if order is None:
        outs[0][: whole.shape[0], :] = whole[:, columns]
        if extra is not None:
            outs[0][whole.shape[0] :, :] = extra
    else:
        write_blocks(whole, columns, order[0], order[1:], size, outs, extra)


def ffn_weights_kernel(orders, size, normed, pack, act_own, grad_pre_own, branch_own, branch_peer, *refs):
    *outs, whole, left, right = refs
    half, width = normed.shape
    units = act_own.shape[1]
    left[:half] = normed[...]
    left[half:] = pack[:, :width]
    right[:half] = grad_pre_own[...]
    right[half:] = pack[:, width + units :]
    whole[...] = dot_tn(left[...], right[...]).astype(BF16)
    count = 1 if orders[0] is None else 2
    emit(whole, outs[:count], orders[0], size)
    left[:half] = branch_own[...]
    left[half:] = branch_peer[...]
    right[:half] = act_own[...]
    right[half:] = pack[:, width : width + units]
    whole[...] = dot_tn(left[...], right[...]).astype(BF16)
    emit(whole, outs[count:], orders[1], size)


def cross_backward_kernel(
    chip_own, chip_other, hidden, gain, grad_out, wo_own, wo_peer, k_own, v_own, k_peer, v_peer,
    probs_own, probs_peer, wq_own, wq_peer,
    partial_out, grad_hidden, gain_grad, gl_own, gl_peer, gc_own, gc_peer, gq_own, branch, pack,
):
    incoming = chip_own[...].astype(F32) + chip_other[...].astype(F32)
    added, gain_terms = norm_back(hidden[...], row_of(gain), incoming)
    gain_grad[...] = jnp.broadcast_to(gain_terms, gain_grad.shape)
    grad = grad_out[...] + added
    grad_hidden[...] = grad
    rounded = grad.astype(BF16)
    branch[...] = rounded
    width = rounded.shape[1]
    pack[:, :width] = rounded
    context = dot_nt(rounded, wo_own[...]).astype(BF16)
    gc_own[...] = context
    queries = heads_backward(context, k_own[...], v_own[...], probs_own, gl_own)
    gq_own[...] = queries.T
    total = dot_tn(queries, wq_own[...])
    context = dot_nt(rounded, wo_peer[...]).astype(BF16)
    gc_peer[...] = context
    queries = heads_backward(context, k_peer[...], v_peer[...], probs_peer, gl_peer)
    pack[:, width:] = queries.T
    total = total + dot_tn(queries, wq_peer[...])
    partial_out[...] = total.astype(BF16)


def source_grad_kernel(gl_peer, probs_peer, gc_peer, q_peer, out):
    span = out.shape[0] // 2
    rows = span // 4
    for start, grads in (
        (0, heads_spread(gl_peer, q_peer[...], SCALE)),
        (span, heads_spread(probs_peer, gc_peer[...], 1.0)),
    ):
        for block in range(4):
            there = start + (block ^ 1) * rows
            out[there : there + rows] = grads[block * rows : (block + 1) * rows]


def cross_weights_kernel(
    orders, size, gl_own, probs_own, gc_own, q_own, other, e0, e1, e2, e3, normed, pack_forward,
    branch, pack_backward, context_own, gq_own, *refs,
):
    *outs, source, whole, left, right = refs
    count = len(outs) // 2
    span = other.shape[0] // 2
    half, width = normed.shape
    columns = q_own.shape[1]
    source[:, :columns] = low_sum(heads_spread(gl_own, q_own[...], SCALE), other[:span])
    source[:, columns:] = low_sum(heads_spread(probs_own, gc_own[...], 1.0), other[span:])
    for index, part in enumerate((e0, e2, e1, e3)):
        left[index * half : (index + 1) * half] = part[...]
    whole[:, : 2 * columns] = dot_tn(left[...], source[...]).astype(BF16)
    left[:half] = normed[...]
    left[half : 2 * half] = pack_forward[:, :width]
    left[2 * half : 3 * half] = branch[...]
    left[3 * half :] = pack_backward[:, :width]
    right[...] = jnp.zeros_like(right)
    right[:half, :columns] = gq_own[...]
    right[half : 2 * half, :columns] = pack_backward[:, width:]
    right[2 * half : 3 * half, columns:] = context_own[...]
    right[3 * half :, columns:] = pack_forward[:, width:]
    whole[:, 2 * columns :] = dot_tn(left[...], right[...]).astype(BF16)
    wide = outs[0].shape[-1]
    emit(whole, outs[:count], orders[0], size, columns=slice(0, wide))
    emit(whole, outs[count:], orders[1], size, columns=slice(wide, None))


def encoded_kernel(source, wk_own, wv_own, keep, send):
    columns = wk_own.shape[0]
    terms = dot(source[:, :columns], wk_own[...]) + dot(source[:, columns:], wv_own[...])
    terms = terms.astype(BF16)
    rows = keep.shape[0] // 2
    for block in range(4):
        target = send if block % 2 else keep
        target[block // 2 * rows : (block // 2 + 1) * rows] = terms[block * rows : (block + 1) * rows]


def self_norm_kernel(chip_own, chip_other, hidden, gain, grad_hidden, gain_ffn, grad_out, pack):
    half = hidden.shape[0]
    incoming = chip_own[...].astype(F32) + chip_other[...].astype(F32)
    added, gain_terms = norm_back(hidden[...], row_of(gain), incoming)
    grad = grad_hidden[...] + added
    grad_out[...] = grad
    pack[:half] = grad.astype(BF16)
    row = lax.broadcasted_iota(jnp.int32, (EXTRA, hidden.shape[1]), 0)
    extra = jnp.where(row == 0, gain_terms, 0.0) + jnp.where(row == 1, gain_ffn[:1], 0.0)
    pack[half:] = extra.astype(BF16)


def high_low(vector):
    high = vector.astype(BF16).astype(F32)
    row = lax.broadcasted_iota(jnp.int32, (EXTRA, vector.shape[1]), 0)
    return (jnp.where(row == 0, high, 0.0) + jnp.where(row == 1, vector - high, 0.0)).astype(BF16)


def of_high_low(rows):
    rows = rows.astype(F32)
    return rows[:1] + rows[1:2]


def self_backward_kernel(
    pack_own, pack_peer, w_output, w_query, w_key, w_value, queries, keys, values, probs, x,
    keep, send, branch_out, gq_out, gk_out, gv_out, gl_out, whole,
):
    half = keep.shape[0] - EXTRA
    core = lax.axis_index("tensor") % 2
    branch_out[own_rows(core, half), :] = pack_own[:half]
    branch_out[own_rows(1 - core, half), :] = pack_peer[:half]
    context = dot_nt(branch_out[...], w_output[...]).astype(BF16)
    grad_queries = heads_backward(context, keys[...], values[...], probs, gl_out)
    grad_keys = heads_spread(gl_out, queries[...], SCALE)
    grad_values = heads_spread(probs, context, 1.0)
    gq_out[...] = grad_queries.T
    gk_out[...] = grad_keys
    gv_out[...] = grad_values
    total = dot_tn(grad_queries, w_query[...]) + dot(grad_keys, w_key[...]) + dot(grad_values, w_value[...])
    whole[...] = total.astype(BF16)
    keep[:half] = whole[own_rows(core, half), :]
    send[:half] = whole[own_rows(1 - core, half), :]
    resid = x[...].astype(F32)
    gain_terms = high_low(jnp.sum(total * resid * inverse_rms(resid), 0, keepdims=True))
    keep[half:] = gain_terms
    send[half:] = gain_terms


def input_sum_kernel(own, peer, out):
    half = out.shape[0] - EXTRA
    out[:half] = both(own[:half], peer[:half]).astype(BF16)
    out[half:] = high_low(of_high_low(own[half:]) + of_high_low(peer[half:]))


def self_weights_kernel(
    orders, size, buckets, normed, branch, gq, gk, gv, context, gl, bucket, pack_own, pack_peer, *refs
):
    *outs, whole, right, left = refs
    count = len(outs) // 2
    length, columns = gq.shape
    half = pack_own.shape[0] - EXTRA
    right[:length, :columns] = gq[...]
    right[:length, columns:] = gk[...]
    whole[:, : 2 * columns] = dot_tn(normed[...], right[:length]).astype(BF16)
    left[:length] = normed[...]
    left[length:] = branch[...]
    right[...] = jnp.zeros_like(right)
    right[:length, :columns] = gv[...]
    right[length:, columns:] = context[...]
    whole[:, 2 * columns :] = dot_tn(left[...], right[...]).astype(BF16)
    wide = outs[0].shape[-1]
    emit(whole, outs[:count], orders[0], size, columns=slice(0, wide))
    onehot = bucket_onehot(bucket, buckets)
    row = lax.broadcasted_iota(jnp.int32, (length, length), 0)
    column = lax.broadcasted_iota(jnp.int32, (length, length), 1)
    turn = jnp.where(row + column == length - 1, 1.0, 0.0).astype(BF16)
    place = lax.broadcasted_iota(jnp.int32, (8, length), 0)
    sums = jnp.zeros((8, length), F32)
    heads = gl.shape[1] // length
    for head in range(heads):
        skewed = pltpu.roll(dot(turn, gl[:, head * length : (head + 1) * length]), 1, 1, stride=1, stride_axis=0)
        sums = sums + jnp.where(place == head, jnp.sum(skewed, 0, keepdims=True), 0.0)
    table = lax.dot_general(
        sums, onehot, (((1,), (1,)), ((), ())), precision=lax.Precision.HIGHEST, preferred_element_type=F32
    )
    gains = both(pack_own[half:], pack_peer[half:])
    narrow = outs[-1].shape[-1]
    first, count_rows = extra_rows(gains.shape[1], narrow, heads)
    extra = vector_rows(gains[:1], narrow, count_rows, 0) + vector_rows(gains[1:2], narrow, count_rows, 1)
    table = jnp.concatenate([table, jnp.zeros((8, narrow - buckets), F32)], 1)
    row = lax.broadcasted_iota(jnp.int32, (count_rows, narrow), 0)
    for head in range(heads):
        extra = extra + jnp.where(row == first + head, table[head : head + 1], 0.0)
    extra = extra.astype(BF16)
    emit(whole, outs[count:], orders[1], size, extra, columns=slice(wide, None))


def extra_rows(width, wide, heads):
    first = -(-3 * (width // wide) // 4) * 4
    return first, -(-(first + heads) // 16) * 16


def vector_rows(vector, wide, count, which):
    rows = vector.shape[1] // wide
    row = lax.broadcasted_iota(jnp.int32, (count, wide), 0)
    placed = jnp.zeros((count, wide), F32)
    for index in range(rows):
        piece = vector[:, index * wide : (index + 1) * wide]
        placed = placed + jnp.where(row == which * rows + index, piece, 0.0)
    return placed


def encoded_sum_kernel(own, other, keep, send):
    rows = keep.shape[0]
    keep[...] = low_sum(own[:rows], other[:rows])
    send[...] = low_sum(own[rows:], other[rows:])


def input_grad_kernel(chip_own, chip_other, x, gain, grad_hidden, hidden_two, out_own, out_other, pack):
    half = hidden_two.shape[0]
    resid = x[own_rows(lax.axis_index("tensor") % 2, half), :].astype(F32)
    added, _ = norm_back(resid, row_of(gain), both(chip_own[:half], chip_other[:half]))
    pack[:half] = (grad_hidden[...] + added).astype(BF16)
    pack[half:] = (hidden_two[...] + both(out_own[...], out_other[...])).astype(BF16)


def rows_kernel(own, peer, input_grad, layer_out, token):
    half = own.shape[0] // 2
    core = lax.axis_index("tensor") % 2
    for place, out in ((0, input_grad), (half, layer_out)):
        out[own_rows(core, half), :] = own[place : place + half]
        out[own_rows(1 - core, half), :] = peer[place : place + half]
    token[...] = own[: token.shape[0], : token.shape[1]]


def both(left, right):
    return left.astype(F32) + right.astype(F32)


def low_sum(left, right):
    return both(left, right).astype(BF16)


def ffn_second_kernel(up_keep, up_got, down_keep, down_got, up_send, up_next, down_send, down_next):
    for keep, got, send, new in (
        (up_keep, up_got, up_send, up_next),
        (down_keep, down_got, down_send, down_next),
    ):
        for entry in range(2):
            new[entry] = low_sum(keep[entry], got[entry])
            send[entry] = low_sum(keep[2 + entry], got[2 + entry])


def ffn_third_kernel(up_keep, up_got, down_keep, down_got, send, keep):
    size = up_keep.shape[1]
    for entry, target in enumerate((keep, send)):
        target[:size] = low_sum(up_keep[entry], up_got[entry])
        target[size:] = low_sum(down_keep[entry], down_got[entry])


def round_three_kernel(ca_keep, ca_got, cb_keep, cb_got, sa_send, sb_send, x_send, zo_send, ca_next, cb_next):
    for entry in range(2):
        ca_next[entry] = low_sum(ca_keep[entry], ca_got[entry])
        cb_next[entry] = low_sum(cb_keep[entry], cb_got[entry])
    base = spread_out(x_send, [low_sum(cb_keep[2 + entry], cb_got[2 + entry]) for entry in range(2)])
    spread_out(x_send, [sa_send[entry] for entry in range(4)], base)
    base = spread_out(zo_send, [low_sum(ca_keep[2 + entry], ca_got[2 + entry]) for entry in range(2)])
    spread_out(zo_send, [sb_send[entry] for entry in range(4)], base)


def gain_kernel(chip_own, chip_other, out):
    half = chip_own.shape[0] - EXTRA
    gain = of_high_low(chip_own[half:]) + of_high_low(chip_other[half:])
    out[...] = vector_rows(gain, out.shape[1], out.shape[0], 2).astype(BF16)


def spread_out(target, parts, start=0):
    for part in parts:
        rows = part.shape[0]
        for side in range(part.shape[1] // PIECE):
            target[start : start + rows] = part[:, side * PIECE : (side + 1) * PIECE]
            start += rows
    return start


def gathered(source, rows, wide, start):
    pieces = [source[start + side * rows : start + (side + 1) * rows] for side in range(wide // PIECE)]
    return jnp.concatenate(pieces, 1) if len(pieces) > 1 else pieces[0]


def round_four_kernel(
    x_got, zo_got, ca_keep, cb_keep, sa_keep, sb_keep, gains, gains_got,
    cross_send, cross_keep, sa_send, sa_next, sb_send, sb_next,
):
    size, ca_wide = ca_keep.shape[1:]
    cb_wide = cb_keep.shape[2]
    large, small = sa_keep.shape[2], sb_keep.shape[2]
    more = sb_keep.shape[1]
    zo_base = 2 * size * ca_wide // PIECE
    x_base = 2 * size * cb_wide // PIECE
    for entry, target in enumerate((cross_keep, cross_send)):
        part = low_sum(ca_keep[entry], gathered(zo_got, size, ca_wide, entry * (zo_base // 2)))
        base = spread_out(target, [part])
        part = low_sum(cb_keep[entry], gathered(x_got, size, cb_wide, entry * (x_base // 2)))
        spread_out(target, [part], base)
    gain = low_sum(gains[...], gains_got[...])
    for first, sa_out, sb_out in ((0, sa_next, sb_next), (2, sa_send, sb_send)):
        for entry in range(2):
            start = x_base + (first + entry) * size * (large // PIECE)
            part = slice(entry * size, (entry + 1) * size)
            sa_out[part] = low_sum(sa_keep[first + entry], gathered(x_got, size, large, start))
            start = zo_base + (first + entry) * more * (small // PIECE)
            other = gathered(zo_got, more, small, start)
            sb_out[entry] = low_sum(sb_keep[first + entry], other)
        sa_out[2 * size :, :small] = gain


def round_five_kernel(sa_keep, sa_got, sb_keep, sb_got, send, keep):
    large, small = sa_keep.shape[1], sb_keep.shape[2]
    size = sa_keep.shape[0] - sb_keep.shape[1]
    gain = low_sum(sa_keep[2 * size :, :small], sa_got[2 * size :, :small])
    for entry, target in enumerate((keep, send)):
        part = slice(entry * size, (entry + 1) * size)
        spread_out(target, [low_sum(sa_keep[part], sa_got[part])])
        part = low_sum(sb_keep[entry], sb_got[entry])
        part = jnp.concatenate([part[:size], low_sum(part[size:], gain)], 0)
        spread_out(target, [part], size * (large // PIECE))


def ffn_final_kernel(keep, got, up, down):
    size = up.shape[0]
    up[...] = both(keep[:size], got[:size])
    down[...] = both(keep[size:], got[size:])


def cross_final_kernel(keep, got, key, value, query, output):
    size, count = key.shape
    total = both(gathered(keep, size, 4 * count, 0), gathered(got, size, 4 * count, 0))
    for place, out in enumerate((key, value, query)):
        out[...] = total[:, place * count : (place + 1) * count]
    output[...] = total[:, 3 * count :].T


def self_final_kernel(
    large, keep, got, encoded_own, encoded_other,
    encoded_grad, query, key, value, output, table, gain_two, gain_three, gain_one,
):
    encoded_grad[...] = low_sum(encoded_own[...], encoded_other[...])
    size, count = key.shape
    small = 4 * count - large
    start = size * (large // PIECE)
    first = both(gathered(keep, size, large, 0), gathered(got, size, large, 0))
    table_row, more = extra_rows(4 * count, small, table.shape[0])
    more += size
    second = both(gathered(keep, more, small, start), gathered(got, more, small, start))
    total = jnp.concatenate([first, second[:size]], 1)
    for place, out in enumerate((query, key, value)):
        out[...] = total[:, place * count : (place + 1) * count]
    output[...] = total[:, 3 * count :].T
    extra = second[size:]
    table[...] = extra[table_row : table_row + table.shape[0], : table.shape[1]]
    wide = 4 * count
    back = wide - lax.axis_index("dp") * size
    rows = wide // small
    for which, out in enumerate((gain_two, gain_three, gain_one)):
        pieces = [extra[which * rows + index : which * rows + index + 1] for index in range(rows)]
        whole = jnp.concatenate(pieces, 1)
        out[...] = pltpu.roll(jnp.broadcast_to(whole, (8, wide)), back, 1)[:1, :size]


def run(kernel, name, outs, ins, us=0.0, scratch=(), scalars=0, far=0, sems=0, after=(), limit=VMEM_LIMIT):
    shapes = [jax.ShapeDtypeStruct(shape, dtype) for shape, dtype in outs]
    idle = len(after)
    body = kernel
    if idle:

        def body(*refs):
            kernel(*refs[: len(ins)], *refs[len(ins) + idle :])

    vmem = pl.BlockSpec(memory_space=pltpu.VMEM)
    hbm = pl.BlockSpec(memory_space=pltpu.HBM)
    free = pl.BlockSpec(memory_space=pl.ANY)
    smem = pl.BlockSpec(memory_space=pltpu.SMEM)
    place = [smem] * scalars + [hbm] * far + [vmem] * (len(ins) - scalars - far) + [free] * idle
    ins = [
        pltpu.with_memory_space_constraint(item, pltpu.HBM) if spec is hbm else item for item, spec in zip(ins, place)
    ]
    result = pl.pallas_call(
        body,
        out_shape=shapes,
        in_specs=place,
        out_specs=[vmem] * len(shapes),
        scratch_shapes=[pltpu.VMEM(shape, dtype) for shape, dtype in scratch]
        + ([pltpu.SemaphoreType.DMA((sems,))] if sems else []),
        compiler_params=pltpu.CompilerParams(vmem_limit_bytes=limit),
        cost_estimate=pl.CostEstimate(flops=int(us * 1.15e9), bytes_accessed=0, transcendentals=0),
        name=name,
    )(*ins, *after)
    return result[0] if len(shapes) == 1 else result


def listed(result):
    return list(result) if isinstance(result, (list, tuple)) else [result]


def to_core(value):
    return lax.ppermute(value, "tensor", [(i, i ^ 1) for i in range(lax.axis_size("tensor"))])


def to_chip(value):
    return lax.ppermute(value, "tensor", [(i, i ^ 2) for i in range(lax.axis_size("tensor"))])


def to_peer(value, bit):
    return lax.ppermute(value, "dp", [(i, i ^ (1 << bit)) for i in range(lax.axis_size("dp"))])


def on_device(
    inputs, encoded, dec_len, enc_len, language, objective, distance_bucket, token_weights, cotangent,
    gain_self, self_query, self_key, self_value, self_output, bias_table,
    gain_cross, cross_query, cross_key, cross_value, cross_output, gain_ffn, ffn_up, ffn_down,
):
    seqs, length, width = inputs.shape
    half = length // 2
    columns = self_query.shape[1]
    heads = columns // HEAD_DIM
    units = ffn_up.shape[1]
    span_part = encoded.shape[1]
    span = span_part * lax.axis_size("tensor")
    dp = lax.axis_size("dp")
    size = width // dp
    bits = dp.bit_length() - 1
    halving = bits == 3 and dp == 8 and size % 16 == 0
    along_x, along_z = ((0, 1, 2), (1, 0, 2)) if halving else (None, None)
    latest = []

    def go(kernel, name, outs, ins, last=False, **how):
        after = [item for item in latest if not any(item is one for one in ins)]
        result = run(kernel, name, outs, ins, after=after, **how)
        if not last:
            results = result if isinstance(result, (list, tuple)) else [result]
            latest[:] = [min(results, key=lambda item: item.size * item.dtype.itemsize)]
        return result

    def plus(left, right, name):
        return go(add_kernel, name, [(left.shape, left.dtype)], [left, right])

    def payload(order, wide, extra=0):
        if order is None:
            return [((width + extra, wide), BF16)]
        return [((dp // 2, size + extra, wide), BF16)] * 2

    x = inputs.reshape(length, width)
    cot = cotangent.reshape(length, width)
    gain_one, gain_two, gain_three = gain_self, gain_cross, gain_ffn
    self_query, self_key, self_value = self_query.T, self_key.T, self_value.T
    cross_query, cross_key, cross_value = cross_query.T, cross_key.T, cross_value.T
    table = bias_table.T
    bucket = distance_bucket.reshape(1, length)
    e0 = encoded.reshape(span_part, width)

    first = go(first_kernel, "first", [((8, 128), F32)], [], us=LONG)
    key_source, value_source, _ = lax.optimization_barrier((cross_key, cross_value, first))
    e1 = to_chip(e0)
    e2 = to_core(e0)
    wk_peer = to_core(key_source)
    wv_peer = to_core(value_source)
    keep, send, more, normed_one, query_one, context_one, probs_one, dec_rows = go(
        self_forward_kernel, "self_forward",
        [((half, width), BF16)] + [((half // 2, width), BF16)] * 2 + [((length, width), BF16)]
        + [((length, columns), BF16)] * 2 + [((length, heads * length), BF16), ((8, 128), jnp.int32)],
        [dec_len, bucket, table, x, gain_one, self_query, self_key, self_value, self_output],
        scratch=[((length, width), BF16)], scalars=1, us=3.5,
    )
    first_half, second_half = to_core(send), to_core(more)
    early = go(
        source_first_kernel, "source_first", [((span // 2, columns), BF16), ((columns, span // 2), BF16)] * 2,
        [e0, e2, cross_key, cross_value, wk_peer, wv_peer],
    )
    chip_one = go(self_sum_kernel, "self_sum", [((half + EXTRA, width), BF16)], [keep, first_half, second_half])
    other_one = to_chip(chip_one)
    wq_source, wo_source, _ = lax.optimization_barrier((cross_query, cross_output, chip_one))
    wq_peer = to_core(wq_source)
    wo_peer = to_core(wo_source)
    e3 = to_core(e1)
    late = go(
        source_second_kernel, "source_second", [((span, columns), BF16), ((columns, span), BF16)] * 2,
        [e1, e3, cross_key, cross_value, wk_peer, wv_peer, *early],
    )
    enc_len, objective, language, _ = lax.optimization_barrier((enc_len, objective, language, late[0]))
    info, mask = go(
        step_kernel, "step", [((8, 128), jnp.int32), ((span, half), F32)], [enc_len, objective, language], scalars=3
    )
    up_source, down_source, _ = lax.optimization_barrier((ffn_up, ffn_down, late[0]))
    down_peer = to_core(down_source)
    up_peer = to_core(up_source)

    partial_two, hidden_one, normed_two, q_own, q_peer, context_own, probs_own, probs_peer, pack_forward = go(
        cross_forward_kernel, "cross_forward",
        [((half, width), BF16), ((half, width), F32), ((half, width), BF16)] + [((half, columns), BF16)] * 3
        + [((span, heads * half), BF16)] * 2 + [((half, width + columns), BF16)],
        [mask, chip_one, other_one, x, gain_two, cross_query, wq_peer, cross_output, wo_peer, *late],
    )
    other_two = to_chip(partial_two)
    pack_forward_peer = to_core(pack_forward)
    grad_full, branch_three, branch_three_peer = go(
        out_grad_kernel, "out_grad", [((half, width), F32)] + [((half, width), BF16)] * 2,
        [info, dec_rows, token_weights, cot], us=LONG,
    )
    act_grad, act_grad_peer = go(
        act_grad_kernel, "act_grad", [((half, units), F32)] * 2, [branch_three, ffn_down, down_peer]
    )
    key_one, value_one, k_own, v_own, k_peer, v_peer = go(
        source_back_kernel, "source_back",
        [((columns, length), BF16), ((length, columns), BF16)] + [((columns, span), BF16), ((span, columns), BF16)] * 2,
        [normed_one, self_key, self_value, e0, e1, e2, e3, cross_key, cross_value, wk_peer, wv_peer],
    )

    latest.append(pack_forward_peer)
    partial_three, hidden_two, normed_three, act_own, grad_pre_own, pack_ffn = go(
        ffn_kernel, "ffn",
        [((half, width), BF16), ((half, width), F32), ((half, width), BF16)] + [((half, units), BF16)] * 2
        + [((half, width + 2 * units), BF16)],
        [partial_two, other_two, hidden_one, gain_three, ffn_up, up_peer, act_grad, act_grad_peer],
    )
    other_three = to_chip(partial_three)
    pack_ffn_peer = to_core(pack_ffn)

    def ffn_weights(*refs):
        ffn_weights_kernel((along_x, along_z), size, *refs)

    ffn_payloads = go(
        ffn_weights, "ffn_weights", payload(along_x, width) + payload(along_z, width),
        [normed_three, pack_ffn_peer, act_own, grad_pre_own, branch_three, branch_three_peer],
        scratch=[((width, units), BF16), ((length, width), BF16), ((length, units), BF16)], us=FILL,
    )

    (partial_four, grad_two, gain_grad_three, gl_own, gl_peer, gc_own, gc_peer, gq_own, branch_two,
     pack_backward) = go(
        cross_backward_kernel, "cross_backward",
        [((half, width), BF16), ((half, width), F32), ((8, width), F32)] + [((span, heads * half), BF16)] * 2
        + [((half, columns), BF16)] * 3 + [((half, width), BF16), ((half, width + columns), BF16)],
        [partial_three, other_three, hidden_two, gain_three, grad_full, cross_output, wo_peer,
         k_own, v_own, k_peer, v_peer, probs_own, probs_peer, cross_query, wq_peer],
    )
    other_four = to_chip(partial_four)
    pack_backward_peer = to_core(pack_backward)
    source_grad = go(
        source_grad_kernel, "source_grad", [((2 * span, columns), BF16)], [gl_peer, probs_peer, gc_peer, q_peer]
    )
    source_grad_peer = to_core(source_grad)
    wide = 2 * columns
    ca_wide, cb_wide = (CROSS_X, 2 * wide - CROSS_X) if halving else (wide, wide)

    def cross_weights(*refs):
        cross_weights_kernel((along_x, along_z), size, *refs)

    *cross_payload, source_total = go(
        cross_weights, "cross_weights",
        payload(along_x, ca_wide) + payload(along_z, cb_wide) + [((span, wide), BF16)],
        [gl_own, probs_own, gc_own, q_own, source_grad_peer, e0, e1, e2, e3, normed_two, pack_forward_peer,
         branch_two, pack_backward_peer, context_own, gq_own],
        scratch=[((width, 2 * wide), BF16), ((span, width), BF16), ((4 * half, wide), BF16)],
    )
    ca_payload, cb_payload = cross_payload[: len(cross_payload) // 2], cross_payload[len(cross_payload) // 2 :]
    branch_out = go(ffn_out_kernel, "ffn_out", [((half, width), BF16)], [act_own, pack_ffn, ffn_down, down_peer])

    grad_one, pack_self = go(
        self_norm_kernel, "self_norm", [((half, width), F32), ((half + EXTRA, width), BF16)],
        [partial_four, other_four, hidden_one, gain_two, grad_two, gain_grad_three],
    )
    pack_self_peer = to_core(pack_self)

    if halving:
        up_keep, up_send, down_keep, down_send = ffn_payloads
        half_sent = ((2, size, width), BF16)
        up_send, up_keep, down_send, down_keep = go(
            ffn_second_kernel, "ffn_second", [half_sent] * 4,
            [up_keep, to_peer(up_send, 0), down_keep, to_peer(down_send, 1)], us=1.0,
        )
        up_got = to_peer(up_send, 1)
        down_got = to_peer(down_send, 0)

    keep, send, branch_one, gq_one, gk_one, gv_one, gl_one = go(
        self_backward_kernel, "self_backward",
        [((half + EXTRA, width), BF16)] * 2 + [((length, width), BF16)] + [((length, columns), BF16)] * 3
        + [((length, heads * length), BF16)],
        [pack_self, pack_self_peer, self_output, self_query, self_key, self_value, query_one, key_one, value_one,
         probs_one, x],
        scratch=[((length, width), BF16)],
    )
    got = to_core(send)
    large, small = (SELF_X, 2 * wide - SELF_X) if halving else (wide, wide)
    table_row, extra_count = extra_rows(width, small, heads)

    def self_weights(*refs):
        self_weights_kernel((along_x, along_z), size, table.shape[1], *refs)

    self_payload = listed(go(
        self_weights, "self_weights", payload(along_x, large) + payload(along_z, small, extra_count),
        [normed_one, branch_one, gq_one, gk_one, gv_one, context_one, gl_one, bucket, pack_self, pack_self_peer],
        scratch=[((width, 2 * wide), BF16), ((2 * length, wide), BF16), ((2 * length, width), BF16)],
    ))
    sa_payload, sb_payload = self_payload[: len(self_payload) // 2], self_payload[len(self_payload) // 2 :]

    if halving:
        ca_keep, ca_send = ca_payload
        cb_keep, cb_send = cb_payload
        sa_keep, sa_send = sa_payload
        sb_keep, sb_send = sb_payload
        more = size + extra_count
        x_rows = (2 * size * cb_wide + 4 * size * large) // PIECE
        zo_rows = (2 * size * ca_wide + 4 * more * small) // PIECE
        x_send, zo_send, ca_keep, cb_keep = go(
            round_three_kernel, "round_three",
            [((x_rows, PIECE), BF16), ((zo_rows, PIECE), BF16), ((2, size, ca_wide), BF16), ((2, size, cb_wide), BF16)],
            [ca_keep, to_peer(ca_send, 0), cb_keep, to_peer(cb_send, 1), sa_send, sb_send], us=1.6,
        )
        x_got = to_peer(x_send, 0)
        zo_got = to_peer(zo_send, 1)

    chip_five = go(input_sum_kernel, "input_sum", [(keep.shape, BF16)], [keep, got])
    other_five = to_chip(chip_five)

    if halving:
        ffn_send, ffn_keep = go(
            ffn_third_kernel, "ffn_third", [((2 * size, width), BF16)] * 2, [up_keep, up_got, down_keep, down_got]
        )
        ffn_got = to_peer(ffn_send, 2)
        gains = go(gain_kernel, "gain", [((extra_count, small), BF16)], [chip_five, other_five], us=LONG)
        gains_got = to_peer(gains, 0)
        branch_source, _ = lax.optimization_barrier((branch_out, gains))
    else:
        branch_source = branch_out
    out_other = to_chip(branch_source)
    pack_rows = go(
        input_grad_kernel, "input_grad", [((2 * half, width), BF16)],
        [chip_five, other_five, x, gain_one, grad_one, hidden_two, branch_out, out_other],
    )
    pack_rows_peer = to_core(pack_rows)

    if halving:
        rows = 2 * size + extra_count
        cross_send, cross_keep, sa_send, sa_keep, sb_send, sb_keep = go(
            round_four_kernel, "round_four",
            [((size * 2 * wide // PIECE, PIECE), BF16)] * 2 + [((rows, large), BF16)] * 2 + [((2, more, small), BF16)] * 2,
            [x_got, zo_got, ca_keep, cb_keep, sa_keep, sb_keep, gains, gains_got],
        )
        sa_got = to_peer(sa_send, 1)
        sb_got = to_peer(sb_send, 0)
        up, down = go(ffn_final_kernel, "ffn_final", [((size, width), F32)] * 2, [ffn_keep, ffn_got], us=LONG, last=True)

    encoded_keep, encoded_send = go(
        encoded_kernel, "encoded", [((span // 2, width), BF16)] * 2, [source_total, cross_key, cross_value]
    )
    encoded_got = to_core(encoded_send)
    if halving:
        cross_send, _ = lax.optimization_barrier((cross_send, encoded_send))
        cross_got = to_peer(cross_send, 2)
    encoded_part, encoded_pass = go(
        encoded_sum_kernel, "encoded_sum", [((span_part, width), BF16)] * 2, [encoded_keep, encoded_got]
    )
    encoded_other = to_chip(encoded_pass)

    if halving:
        rows = (size * large + more * small) // PIECE
        self_send, self_keep = go(
            round_five_kernel, "round_five", [((rows, PIECE), BF16)] * 2, [sa_keep, sa_got, sb_keep, sb_got]
        )
        self_got = to_peer(self_send, 2)
        square = ((size, columns), F32)
        turned = ((columns, size), F32)
        grad_cross_key, grad_cross_value, grad_cross_query, grad_cross_output = go(
            cross_final_kernel, "cross_final", [square] * 3 + [turned], [cross_keep, cross_got], us=LONG, last=True
        )

    input_grad, layer_out, _ = go(
        rows_kernel, "rows", [((length, width), BF16)] * 2 + [((16, 128), BF16)], [pack_rows, pack_rows_peer]
    )

    if halving:

        def self_final(*refs):
            self_final_kernel(large, *refs)

        (encoded_grad, grad_self_query, grad_self_key, grad_self_value, grad_self_output, grad_table, grad_gain_two,
         grad_gain_three, grad_gain_one) = go(
            self_final, "self_final",
            [((span_part, width), BF16)] + [square] * 3 + [turned, (table.shape, F32)] + [((1, size), F32)] * 3,
            [self_keep, self_got, encoded_part, encoded_other], last=True,
        )
        grad_gain_one, grad_gain_two, grad_gain_three = (
            item.reshape(size) for item in (grad_gain_one, grad_gain_two, grad_gain_three)
        )
    else:
        index = lax.axis_index("dp")

        def gain_part(*rows):
            row = lax.psum(jnp.concatenate(rows, 0).astype(F32), "dp")
            return lax.dynamic_slice(row, (index * size,), (size,))

        def scattered(item):
            return lax.psum_scatter(item.astype(F32), "dp", scatter_dimension=0, tiled=True)

        def pair_of(item):
            item = scattered(item)
            return item[:, :columns], item[:, columns:]

        up, down = (scattered(item) for item in ffn_payloads)
        grad_cross_key, grad_cross_value = pair_of(ca_payload[0])
        grad_cross_query, grad_cross_output = pair_of(cb_payload[0])
        grad_self_query, grad_self_key = pair_of(sa_payload[0])
        grad_self_value, grad_self_output = pair_of(sb_payload[0][:width])
        grad_cross_output, grad_self_output = grad_cross_output.T, grad_self_output.T
        extra = sb_payload[0][width:]
        grad_table = lax.psum(extra[table_row : table_row + heads, : table.shape[1]].astype(F32), "dp")
        encoded_grad = plus(encoded_part, encoded_other, "encoded_grad")
        gain_rows = [item[half : half + 2] for item in (chip_five, other_five)]
        grad_gain_one = gain_part(jnp.sum(jnp.concatenate(gain_rows, 0).astype(F32), 0))
        grad_gain_two = gain_part(extra[0], extra[1])
        grad_gain_three = gain_part(extra[2], extra[3])

    return (
        layer_out.reshape(seqs, length, width),
        input_grad.reshape(seqs, length, width),
        encoded_grad.reshape(seqs, span_part, width),
        grad_gain_one,
        grad_self_query,
        grad_self_key,
        grad_self_value,
        grad_self_output,
        grad_table.T,
        grad_gain_two,
        grad_cross_query,
        grad_cross_key,
        grad_cross_value,
        grad_cross_output,
        grad_gain_three,
        up,
        down.T,
    )


def solution(mesh):
    return jax.shard_map(
        on_device,
        mesh=mesh,
        in_specs=(
            P("dp", None, None),
            P("dp", "tensor", None),
            P("dp"),
            P("dp"),
            P("dp"),
            P("dp"),
            P(),
            P(),
            P("dp", None, None),
            P(),
            P(None, "tensor"),
            P(None, "tensor"),
            P(None, "tensor"),
            P("tensor", None),
            P(None, "tensor"),
            P(),
            P(None, "tensor"),
            P(None, "tensor"),
            P(None, "tensor"),
            P("tensor", None),
            P(),
            P(None, "tensor"),
            P("tensor", None),
        ),
        out_specs=(
            P("dp", None, None),
            P("dp", None, None),
            P("dp", "tensor", None),
            P("dp"),
            P("dp", "tensor"),
            P("dp", "tensor"),
            P("dp", "tensor"),
            P("tensor", "dp"),
            P(None, "tensor"),
            P("dp"),
            P("dp", "tensor"),
            P("dp", "tensor"),
            P("dp", "tensor"),
            P("tensor", "dp"),
            P("dp"),
            P("dp", "tensor"),
            P("tensor", "dp"),
        ),
        check_vma=False,
    )
```

```python
import jax
import jax.numpy as jnp
from jax import lax
from jax.experimental import pallas as pl
from jax.experimental.pallas import tpu as pltpu
from jax.sharding import PartitionSpec as P

HEAD_DIM = 64
LANGS = 8
EPSILON = 1e-06
SCALE = 0.125
NEGATIVE = -1e30
F32 = jnp.float32
BF16 = jnp.bfloat16
VMEM_LIMIT = 20 * 1024 * 1024
EXTRA = 16
PIECE = 128
CROSS_X = 384
SELF_X = 512
FILL = 5.0
LONG = 20.0


def dot(left, right):
    return jnp.dot(left, right, preferred_element_type=F32)


def dot_nt(left, right):
    return lax.dot_general(left, right, (((1,), (1,)), ((), ())), preferred_element_type=F32)


def dot_tn(left, right):
    return lax.dot_general(left, right, (((0,), (0,)), ((), ())), preferred_element_type=F32)


def row_of(vector_ref):
    return vector_ref[...].reshape(1, vector_ref.shape[0])


def inverse_rms(resid):
    return lax.rsqrt(jnp.mean(resid * resid, -1, keepdims=True) + EPSILON)


def norm_back(resid, gain, incoming):
    scale = inverse_rms(resid)
    weighted = incoming * gain
    inner = jnp.mean(weighted * resid, -1, keepdims=True)
    grad = scale * weighted - resid * (scale * scale * scale * inner)
    gain_grad = jnp.sum(incoming * resid * scale, 0, keepdims=True)
    return grad, gain_grad


def groups_of(width):
    return [(start, min(2 * HEAD_DIM, width - start)) for start in range(0, width, 2 * HEAD_DIM)]


def head_mask(count, which, value):
    lane = lax.broadcasted_iota(jnp.int32, (1, count), 1)
    return jnp.where(lane // HEAD_DIM == which, value, 0.0).astype(BF16)


def stacked_heads(rows, value):
    width = rows.shape[1]
    if width == HEAD_DIM:
        return rows * jnp.asarray(value, BF16)
    return jnp.concatenate([rows * head_mask(width, inside, value) for inside in range(width // HEAD_DIM)], 0)


def own_blocks(product, count):
    rows = product.shape[1] // count
    return [
        product[inside * HEAD_DIM : (inside + 1) * HEAD_DIM, inside * rows : (inside + 1) * rows]
        for inside in range(count)
    ]


def heads_forward(queries, keys, values_turned, finish, probs_ref):
    rows = queries.shape[0]
    parts = []
    for start, width in groups_of(queries.shape[1]):
        head, count = start // HEAD_DIM, width // HEAD_DIM
        stacked = stacked_heads(queries[:, start : start + width], SCALE)
        logits = finish(head, count, dot_nt(keys[:, start : start + width], stacked))
        expo = jnp.exp(logits - jnp.max(logits, 0, keepdims=True))
        probs = (expo * (1.0 / jnp.sum(expo, 0, keepdims=True))).astype(BF16)
        probs_ref[:, head * rows : (head + count) * rows] = probs
        parts += own_blocks(dot(values_turned[start : start + width], probs), count)
    return jnp.concatenate(parts, 0).astype(BF16)


def heads_backward(grad_context, keys_turned, values, probs_ref, grad_logits_ref):
    rows = grad_context.shape[0]
    parts = []
    for start, width in groups_of(grad_context.shape[1]):
        head, count = start // HEAD_DIM, width // HEAD_DIM
        place = slice(head * rows, (head + count) * rows)
        stacked = stacked_heads(grad_context[:, start : start + width], 1.0)
        grad_probs = dot_nt(values[:, start : start + width], stacked)
        probs = probs_ref[:, place].astype(F32)
        weighted = jnp.sum(grad_probs * probs, 0, keepdims=True)
        grad_logits = (probs * (grad_probs - weighted)).astype(BF16)
        grad_logits_ref[:, place] = grad_logits
        parts += own_blocks(SCALE * dot(keys_turned[start : start + width], grad_logits), count)
    return jnp.concatenate(parts, 0).astype(BF16)


def heads_spread(matrix_ref, rows, factor):
    length = rows.shape[0]
    parts = []
    for start, width in groups_of(rows.shape[1]):
        head, count = start // HEAD_DIM, width // HEAD_DIM
        stacked = stacked_heads(rows[:, start : start + width], 1.0)
        parts.append(factor * dot(matrix_ref[:, head * length : (head + count) * length], stacked))
    return jnp.concatenate(parts, 1).astype(BF16)


def own_rows(core, half):
    return pl.ds(pl.multiple_of(core * half, half), half)


def bucket_onehot(bucket_ref, buckets):
    wanted = lax.broadcasted_iota(jnp.int32, (buckets, bucket_ref.shape[1]), 0)
    return jnp.where(bucket_ref[...] == wanted, 1.0, 0.0)


def add_kernel(left_ref, right_ref, out_ref):
    out_ref[...] = (left_ref[...].astype(F32) + right_ref[...].astype(F32)).astype(out_ref.dtype)


def first_kernel(out):
    out[...] = jnp.zeros_like(out)


def step_kernel(enc_len, objective, language, info, mask):
    info[...] = jnp.full(info.shape, objective[0] * LANGS + language[0], jnp.int32)
    rows = mask.shape[0] // 4
    row = lax.broadcasted_iota(jnp.int32, mask.shape, 0)
    block = row // rows
    flip = jnp.where(block % 2 == 1, 1, 0) + jnp.where(block >= 2, 2, 0)
    position = (lax.axis_index("tensor") ^ flip) * rows + row % rows
    mask[...] = jnp.where(position < enc_len[0], 0.0, NEGATIVE)


def self_sum_kernel(own, first, second, out):
    rows = first.shape[0]
    out[:rows] = both(own[:rows], first[...]).astype(BF16)
    out[rows : 2 * rows] = both(own[rows:], second[...]).astype(BF16)
    out[2 * rows :] = jnp.zeros((out.shape[0] - 2 * rows, out.shape[1]), BF16)


def self_forward_kernel(
    dec_len, bucket, table, x, gain, w_query, w_key, w_value, w_output,
    keep, send, more, normed_out, query_out, context_out, probs_out, dec_out, whole,
):
    dec_out[...] = jnp.full(dec_out.shape, dec_len[0], jnp.int32)
    length = x.shape[0]
    resid = x[...].astype(F32)
    normed = (resid * inverse_rms(resid) * row_of(gain)).astype(BF16)
    normed_out[...] = normed
    queries = dot_nt(normed, w_query[...]).astype(BF16)
    keys = dot_nt(normed, w_key[...]).astype(BF16)
    values = dot_nt(w_value[...], normed).astype(BF16)
    query_out[...] = queries
    by_distance = lax.dot_general(
        table[...],
        bucket_onehot(bucket, table.shape[1]),
        (((1,), (0,)), ((), ())),
        precision=lax.Precision.HIGHEST,
        preferred_element_type=F32,
    )
    row = lax.broadcasted_iota(jnp.int32, (length, length), 0)
    column = lax.broadcasted_iota(jnp.int32, (length, length), 1)
    allowed = (row <= column) & (row < dec_len[0])

    def finish(head, count, scores):
        parts = []
        for inside in range(count):
            spread = jnp.broadcast_to(by_distance[head + inside : head + inside + 1], (length, length))
            bias = pltpu.roll(spread, 0, 1, stride=1, stride_axis=0)
            part = scores[:, inside * length : (inside + 1) * length]
            parts.append(jnp.where(allowed, part + bias, NEGATIVE))
        return jnp.concatenate(parts, 1) if count > 1 else parts[0]

    context = heads_forward(queries, keys, values, finish, probs_out)
    context_out[...] = context.T
    whole[...] = dot_tn(context, w_output[...]).astype(BF16)
    half = keep.shape[0]
    core = lax.axis_index("tensor") % 2
    keep[...] = whole[own_rows(core, half), :]
    rows = send.shape[0]
    send[...] = whole[own_rows(2 - 2 * core, rows), :]
    more[...] = whole[own_rows(3 - 2 * core, rows), :]


def source_first_kernel(first, second, wk_own, wv_own, wk_peer, wv_peer, k_own, v_own, k_peer, v_peer):
    rows = first.shape[0]
    for index, part in enumerate((first, second)):
        place = slice(index * rows, (index + 1) * rows)
        for weight, out in ((wk_own, k_own), (wk_peer, k_peer)):
            out[place, :] = dot_nt(part[...], weight[...]).astype(BF16)
        for weight, out in ((wv_own, v_own), (wv_peer, v_peer)):
            out[:, place] = dot_nt(weight[...], part[...]).astype(BF16)


def source_second_kernel(
    first, second, wk_own, wv_own, wk_peer, wv_peer, early_k_own, early_v_own, early_k_peer, early_v_peer,
    k_own, v_own, k_peer, v_peer,
):
    rows = first.shape[0]
    for early, out in ((early_k_own, k_own), (early_k_peer, k_peer)):
        out[: 2 * rows] = early[...]
    for early, out in ((early_v_own, v_own), (early_v_peer, v_peer)):
        out[:, : 2 * rows] = early[...]
    for index, part in enumerate((first, second)):
        place = slice((2 + index) * rows, (3 + index) * rows)
        for weight, out in ((wk_own, k_own), (wk_peer, k_peer)):
            out[place, :] = dot_nt(part[...], weight[...]).astype(BF16)
        for weight, out in ((wv_own, v_own), (wv_peer, v_peer)):
            out[:, place] = dot_nt(weight[...], part[...]).astype(BF16)


def source_back_kernel(
    normed, w_key, w_value, e0, e1, e2, e3, wk_own, wv_own, wk_peer, wv_peer,
    keys_turned, values, k_own, v_own, k_peer, v_peer,
):
    keys_turned[...] = dot_nt(w_key[...], normed[...]).astype(BF16)
    values[...] = dot_nt(normed[...], w_value[...]).astype(BF16)
    rows = e0.shape[0]
    for index, part in enumerate((e0, e2, e1, e3)):
        place = slice(index * rows, (index + 1) * rows)
        for weight, out in ((wk_own, k_own), (wk_peer, k_peer)):
            out[:, place] = dot_nt(weight[...], part[...]).astype(BF16)
        for weight, out in ((wv_own, v_own), (wv_peer, v_peer)):
            out[place, :] = dot_nt(part[...], weight[...]).astype(BF16)


def out_grad_kernel(info, dec_len, token_weights, cotangent, grad_own, branch_own, branch_peer):
    half = grad_own.shape[0]
    length = cotangent.shape[0]
    core = lax.axis_index("tensor") % 2
    row = lax.broadcasted_iota(jnp.int32, token_weights.shape, 0)
    weights = jnp.sum(jnp.where(row == info[:1, :1], token_weights[...], 0.0), 0, keepdims=True)
    position = lax.broadcasted_iota(jnp.int32, (1, length), 1)
    weights = jnp.where(position < dec_len[:1, :1], weights, 0.0)

    def rows_of(side):
        row = lax.broadcasted_iota(jnp.int32, (half, length), 0) + side * half
        column = lax.broadcasted_iota(jnp.int32, (half, length), 1)
        factor = jnp.sum(jnp.where(row == column, weights, 0.0), -1, keepdims=True)
        return cotangent[own_rows(side, half), :].astype(F32) * factor

    own = rows_of(core)
    grad_own[...] = own
    branch_own[...] = own.astype(BF16)
    branch_peer[...] = rows_of(1 - core).astype(BF16)


def act_grad_kernel(branch, down_own, down_peer, own, peer):
    own[...] = dot_nt(branch[...], down_own[...])
    peer[...] = dot_nt(branch[...], down_peer[...])


def cross_forward_kernel(
    mask, chip_own, chip_other, x, gain, wq_own, wq_peer, wo_own, wo_peer, k_own, v_own, k_peer, v_peer,
    partial_out, hidden_out, normed_out, q_own, q_peer, context_own, probs_own, probs_peer, pack,
):
    half, width = hidden_out.shape
    core = lax.axis_index("tensor") % 2
    resid = x[own_rows(core, half), :].astype(F32)
    resid = resid + both(chip_own[:half], chip_other[:half])
    hidden_out[...] = resid
    normed = (resid * inverse_rms(resid) * row_of(gain)).astype(BF16)
    normed_out[...] = normed
    pack[:, :width] = normed

    def finish(head, count, scores):
        return scores + jnp.concatenate([mask[...]] * count, 1)

    queries = dot_nt(normed, wq_own[...]).astype(BF16)
    q_own[...] = queries
    first = heads_forward(queries, k_own[...], v_own[...], finish, probs_own)
    context_own[...] = first.T
    queries = dot_nt(normed, wq_peer[...]).astype(BF16)
    q_peer[...] = queries
    second = heads_forward(queries, k_peer[...], v_peer[...], finish, probs_peer)
    pack[:, width:] = second.T
    partial_out[...] = (dot_tn(first, wo_own[...]) + dot_tn(second, wo_peer[...])).astype(BF16)


def ffn_kernel(
    chip_own, chip_other, hidden, gain, up_own, up_peer, act_grad_own, act_grad_peer,
    partial_out, hidden_out, normed_out, act_own, grad_pre_own, pack,
):
    width = hidden.shape[1]
    resid = hidden[...] + (chip_own[...].astype(F32) + chip_other[...].astype(F32))
    hidden_out[...] = resid
    normed = (resid * inverse_rms(resid) * row_of(gain)).astype(BF16)
    normed_out[...] = normed
    pack[:, :width] = normed

    def through(up, act_grad):
        pre = dot(normed, up[...])
        square = pre * pre
        tanh = jnp.tanh(0.7978845608028654 * (pre + 0.044715 * square * pre))
        half_sum = 0.5 * (1.0 + tanh)
        slope = half_sum + 0.5 * pre * (1.0 - tanh * tanh) * (
            0.7978845608028654 * (1.0 + 3.0 * 0.044715 * square)
        )
        return (pre * half_sum).astype(BF16), (act_grad[...] * slope).astype(BF16)

    act, grad_pre = through(up_own, act_grad_own)
    act_own[...] = act
    grad_pre_own[...] = grad_pre
    total = dot_nt(grad_pre, up_own[...])
    act, grad_pre = through(up_peer, act_grad_peer)
    units = act.shape[1]
    pack[:, width : width + units] = act
    pack[:, width + units :] = grad_pre
    total = total + dot_nt(grad_pre, up_peer[...])
    partial_out[...] = total.astype(BF16)


def ffn_out_kernel(act_own, pack, down_own, down_peer, out):
    units = act_own.shape[1]
    width = out.shape[1]
    total = dot(act_own[...], down_own[...]) + dot(pack[:, width : width + units], down_peer[...])
    out[...] = total.astype(BF16)


def write_blocks(whole, columns, first_bit, rest_bits, size, targets):
    index = lax.axis_index("dp")
    count = 1 << len(rest_bits)
    for first, target in enumerate(targets):
        for entry in range(count):
            relative = first << first_bit
            for place, bit in enumerate(rest_bits):
                if entry >> (len(rest_bits) - 1 - place) & 1:
                    relative |= 1 << bit
            block = index ^ relative
            target[entry] = whole[pl.ds(pl.multiple_of(block * size, size), size), columns]


def emit(whole, outs, order, size, columns=slice(None)):
    if order is None:
        outs[0][...] = whole[:, columns]
    else:
        write_blocks(whole, columns, order[0], order[1:], size, outs)


def ffn_weights_kernel(orders, size, normed, pack, act_own, grad_pre_own, branch_own, branch_peer, *refs):
    *outs, whole, left, right = refs
    half, width = normed.shape
    units = act_own.shape[1]
    left[:half] = normed[...]
    left[half:] = pack[:, :width]
    right[:half] = grad_pre_own[...]
    right[half:] = pack[:, width + units :]
    whole[...] = dot_tn(left[...], right[...]).astype(BF16)
    count = 1 if orders[0] is None else 2
    emit(whole, outs[:count], orders[0], size)
    left[:half] = branch_own[...]
    left[half:] = branch_peer[...]
    right[:half] = act_own[...]
    right[half:] = pack[:, width : width + units]
    whole[...] = dot_tn(left[...], right[...]).astype(BF16)
    emit(whole, outs[count:], orders[1], size)


def cross_backward_kernel(
    chip_own, chip_other, hidden, gain, grad_out, wo_own, wo_peer, k_own, v_own, k_peer, v_peer,
    probs_own, probs_peer, wq_own, wq_peer,
    partial_out, grad_hidden, gain_grad, gl_own, gl_peer, gc_own, gc_peer, gq_own, branch, pack,
):
    incoming = chip_own[...].astype(F32) + chip_other[...].astype(F32)
    added, gain_terms = norm_back(hidden[...], row_of(gain), incoming)
    gain_grad[...] = jnp.broadcast_to(gain_terms, gain_grad.shape)
    grad = grad_out[...] + added
    grad_hidden[...] = grad
    rounded = grad.astype(BF16)
    branch[...] = rounded
    width = rounded.shape[1]
    pack[:, :width] = rounded
    context = dot_nt(rounded, wo_own[...]).astype(BF16)
    gc_own[...] = context
    queries = heads_backward(context, k_own[...], v_own[...], probs_own, gl_own)
    gq_own[...] = queries.T
    total = dot_tn(queries, wq_own[...])
    context = dot_nt(rounded, wo_peer[...]).astype(BF16)
    gc_peer[...] = context
    queries = heads_backward(context, k_peer[...], v_peer[...], probs_peer, gl_peer)
    pack[:, width:] = queries.T
    total = total + dot_tn(queries, wq_peer[...])
    partial_out[...] = total.astype(BF16)


def source_grad_kernel(gl_peer, probs_peer, gc_peer, q_peer, out):
    span = out.shape[0] // 2
    rows = span // 4
    for start, grads in (
        (0, heads_spread(gl_peer, q_peer[...], SCALE)),
        (span, heads_spread(probs_peer, gc_peer[...], 1.0)),
    ):
        for block in range(4):
            there = start + (block ^ 1) * rows
            out[there : there + rows] = grads[block * rows : (block + 1) * rows]


def cross_weights_kernel(
    orders, size, gl_own, probs_own, gc_own, q_own, other, e0, e1, e2, e3, normed, pack_forward,
    branch, pack_backward, context_own, gq_own, *refs,
):
    *outs, source, whole, left, right = refs
    count = len(outs) // 2
    span = other.shape[0] // 2
    half, width = normed.shape
    columns = q_own.shape[1]
    source[:, :columns] = low_sum(heads_spread(gl_own, q_own[...], SCALE), other[:span])
    source[:, columns:] = low_sum(heads_spread(probs_own, gc_own[...], 1.0), other[span:])
    for index, part in enumerate((e0, e2, e1, e3)):
        left[index * half : (index + 1) * half] = part[...]
    whole[:, : 2 * columns] = dot_tn(left[...], source[...]).astype(BF16)
    left[:half] = normed[...]
    left[half : 2 * half] = pack_forward[:, :width]
    left[2 * half : 3 * half] = branch[...]
    left[3 * half :] = pack_backward[:, :width]
    right[...] = jnp.zeros_like(right)
    right[:half, :columns] = gq_own[...]
    right[half : 2 * half, :columns] = pack_backward[:, width:]
    right[2 * half : 3 * half, columns:] = context_own[...]
    right[3 * half :, columns:] = pack_forward[:, width:]
    whole[:, 2 * columns :] = dot_tn(left[...], right[...]).astype(BF16)
    wide = outs[0].shape[-1]
    emit(whole, outs[:count], orders[0], size, columns=slice(0, wide))
    emit(whole, outs[count:], orders[1], size, columns=slice(wide, None))


def encoded_kernel(source, wk_own, wv_own, keep, send):
    columns = wk_own.shape[0]
    terms = dot(source[:, :columns], wk_own[...]) + dot(source[:, columns:], wv_own[...])
    terms = terms.astype(BF16)
    rows = keep.shape[0] // 2
    for block in range(4):
        target = send if block % 2 else keep
        target[block // 2 * rows : (block // 2 + 1) * rows] = terms[block * rows : (block + 1) * rows]


def self_norm_kernel(chip_own, chip_other, hidden, gain, grad_hidden, gain_ffn, grad_out, pack):
    half = hidden.shape[0]
    incoming = chip_own[...].astype(F32) + chip_other[...].astype(F32)
    added, gain_terms = norm_back(hidden[...], row_of(gain), incoming)
    grad = grad_hidden[...] + added
    grad_out[...] = grad
    pack[:half] = grad.astype(BF16)
    row = lax.broadcasted_iota(jnp.int32, (EXTRA, hidden.shape[1]), 0)
    extra = jnp.where(row == 0, gain_terms, 0.0) + jnp.where(row == 1, gain_ffn[:1], 0.0)
    pack[half:] = extra.astype(BF16)


def high_low(vector):
    high = vector.astype(BF16).astype(F32)
    row = lax.broadcasted_iota(jnp.int32, (EXTRA, vector.shape[1]), 0)
    return (jnp.where(row == 0, high, 0.0) + jnp.where(row == 1, vector - high, 0.0)).astype(BF16)


def of_high_low(rows):
    rows = rows.astype(F32)
    return rows[:1] + rows[1:2]


def self_backward_kernel(
    pack_own, pack_peer, w_output, w_query, w_key, w_value, queries, keys, values, probs, x,
    keep, send, branch_out, gq_out, gk_out, gv_out, gl_out, whole,
):
    half = keep.shape[0] - EXTRA
    core = lax.axis_index("tensor") % 2
    branch_out[own_rows(core, half), :] = pack_own[:half]
    branch_out[own_rows(1 - core, half), :] = pack_peer[:half]
    context = dot_nt(branch_out[...], w_output[...]).astype(BF16)
    grad_queries = heads_backward(context, keys[...], values[...], probs, gl_out)
    grad_keys = heads_spread(gl_out, queries[...], SCALE)
    grad_values = heads_spread(probs, context, 1.0)
    gq_out[...] = grad_queries.T
    gk_out[...] = grad_keys
    gv_out[...] = grad_values
    total = dot_tn(grad_queries, w_query[...]) + dot(grad_keys, w_key[...]) + dot(grad_values, w_value[...])
    whole[...] = total.astype(BF16)
    keep[:half] = whole[own_rows(core, half), :]
    send[:half] = whole[own_rows(1 - core, half), :]
    resid = x[...].astype(F32)
    gain_terms = high_low(jnp.sum(total * resid * inverse_rms(resid), 0, keepdims=True))
    keep[half:] = gain_terms
    send[half:] = gain_terms


def input_sum_kernel(own, peer, out):
    half = out.shape[0] - EXTRA
    out[:half] = both(own[:half], peer[:half]).astype(BF16)
    out[half:] = high_low(of_high_low(own[half:]) + of_high_low(peer[half:]))


def self_weights_kernel(
    orders, size, buckets, normed, branch, gq, gk, gv, context, gl, bucket, pack_own, pack_peer, *refs
):
    *outs, extra_out, whole, right, left = refs
    count = len(outs) // 2
    length, columns = gq.shape
    half = pack_own.shape[0] - EXTRA
    right[:length, :columns] = gq[...]
    right[:length, columns:] = gk[...]
    whole[:, : 2 * columns] = dot_tn(normed[...], right[:length]).astype(BF16)
    left[:length] = normed[...]
    left[length:] = branch[...]
    right[...] = jnp.zeros_like(right)
    right[:length, :columns] = gv[...]
    right[length:, columns:] = context[...]
    whole[:, 2 * columns :] = dot_tn(left[...], right[...]).astype(BF16)
    wide = outs[0].shape[-1]
    emit(whole, outs[:count], orders[0], size, columns=slice(0, wide))
    onehot = bucket_onehot(bucket, buckets)
    row = lax.broadcasted_iota(jnp.int32, (length, length), 0)
    column = lax.broadcasted_iota(jnp.int32, (length, length), 1)
    turn = jnp.where(row + column == length - 1, 1.0, 0.0).astype(BF16)
    place = lax.broadcasted_iota(jnp.int32, (8, length), 0)
    sums = jnp.zeros((8, length), F32)
    heads = gl.shape[1] // length
    for head in range(heads):
        skewed = pltpu.roll(dot(turn, gl[:, head * length : (head + 1) * length]), 1, 1, stride=1, stride_axis=0)
        sums = sums + jnp.where(place == head, jnp.sum(skewed, 0, keepdims=True), 0.0)
    table = lax.dot_general(
        sums, onehot, (((1,), (1,)), ((), ())), precision=lax.Precision.HIGHEST, preferred_element_type=F32
    )
    gains = both(pack_own[half:], pack_peer[half:])
    narrow = outs[-1].shape[-1]
    first, count_rows = extra_rows(gains.shape[1], narrow, heads)
    extra = vector_rows(gains[:1], narrow, count_rows, 0) + vector_rows(gains[1:2], narrow, count_rows, 1)
    table = jnp.concatenate([table, jnp.zeros((8, narrow - buckets), F32)], 1)
    row = lax.broadcasted_iota(jnp.int32, (count_rows, narrow), 0)
    for head in range(heads):
        extra = extra + jnp.where(row == first + head, table[head : head + 1], 0.0)
    extra_out[...] = extra.astype(BF16)
    emit(whole, outs[count:], orders[1], size, columns=slice(wide, None))


def extra_rows(width, wide, heads):
    first = -(-3 * (width // wide) // 4) * 4
    return first, -(-(first + heads) // 16) * 16


def vector_rows(vector, wide, count, which):
    rows = vector.shape[1] // wide
    row = lax.broadcasted_iota(jnp.int32, (count, wide), 0)
    placed = jnp.zeros((count, wide), F32)
    for index in range(rows):
        piece = vector[:, index * wide : (index + 1) * wide]
        placed = placed + jnp.where(row == which * rows + index, piece, 0.0)
    return placed


def encoded_sum_kernel(own, other, keep, send):
    rows = keep.shape[0]
    keep[...] = low_sum(own[:rows], other[:rows])
    send[...] = low_sum(own[rows:], other[rows:])


def input_grad_kernel(chip_own, chip_other, x, gain, grad_hidden, hidden_two, out_own, out_other, pack):
    half = hidden_two.shape[0]
    resid = x[own_rows(lax.axis_index("tensor") % 2, half), :].astype(F32)
    added, _ = norm_back(resid, row_of(gain), both(chip_own[:half], chip_other[:half]))
    pack[:half] = (grad_hidden[...] + added).astype(BF16)
    pack[half:] = (hidden_two[...] + both(out_own[...], out_other[...])).astype(BF16)


def rows_kernel(own, peer, input_grad, layer_out, token):
    half = own.shape[0] // 2
    core = lax.axis_index("tensor") % 2
    for place, out in ((0, input_grad), (half, layer_out)):
        out[own_rows(core, half), :] = own[place : place + half]
        out[own_rows(1 - core, half), :] = peer[place : place + half]
    token[...] = own[: token.shape[0], : token.shape[1]]


def both(left, right):
    return left.astype(F32) + right.astype(F32)


def low_sum(left, right):
    return both(left, right).astype(BF16)


def ffn_second_kernel(up_keep, up_got, down_keep, down_got, up_send, up_next, down_send, down_next):
    for keep, got, send, new in (
        (up_keep, up_got, up_send, up_next),
        (down_keep, down_got, down_send, down_next),
    ):
        for entry in range(2):
            new[entry] = low_sum(keep[entry], got[entry])
            send[entry] = low_sum(keep[2 + entry], got[2 + entry])


def ffn_third_kernel(up_keep, up_got, down_keep, down_got, send, keep):
    size = up_keep.shape[1]
    for entry, target in enumerate((keep, send)):
        target[:size] = low_sum(up_keep[entry], up_got[entry])
        target[size:] = low_sum(down_keep[entry], down_got[entry])


def round_three_kernel(
    ca_keep, ca_got, cb_keep, cb_got, sa_send, sb_send, extra, x_send, zo_send, ca_next, cb_next
):
    for entry in range(2):
        ca_next[entry] = low_sum(ca_keep[entry], ca_got[entry])
        cb_next[entry] = low_sum(cb_keep[entry], cb_got[entry])
    base = spread_out(x_send, [low_sum(cb_keep[2 + entry], cb_got[2 + entry]) for entry in range(2)])
    spread_out(x_send, [sa_send[entry] for entry in range(4)], base)
    base = spread_out(zo_send, [low_sum(ca_keep[2 + entry], ca_got[2 + entry]) for entry in range(2)])
    base = spread_out(zo_send, [sb_send[entry] for entry in range(4)], base)
    spread_out(zo_send, [extra[...]], base)


def gain_kernel(chip_own, chip_other, out):
    half = chip_own.shape[0] - EXTRA
    gain = of_high_low(chip_own[half:]) + of_high_low(chip_other[half:])
    out[...] = vector_rows(gain, out.shape[1], out.shape[0], 2).astype(BF16)


def spread_out(target, parts, start=0):
    for part in parts:
        rows = part.shape[0]
        for side in range(part.shape[1] // PIECE):
            target[start : start + rows] = part[:, side * PIECE : (side + 1) * PIECE]
            start += rows
    return start


def gathered(source, rows, wide, start):
    pieces = [source[start + side * rows : start + (side + 1) * rows] for side in range(wide // PIECE)]
    return jnp.concatenate(pieces, 1) if len(pieces) > 1 else pieces[0]


def round_four_kernel(
    x_got, zo_got, ca_keep, cb_keep, sa_keep, sb_keep, extra, gains, gains_got,
    cross_send, cross_keep, sa_send, sa_next, sb_send, sb_next,
):
    size, ca_wide = ca_keep.shape[1:]
    cb_wide = cb_keep.shape[2]
    large, small = sa_keep.shape[2], sb_keep.shape[2]
    zo_base = 2 * size * ca_wide // PIECE
    x_base = 2 * size * cb_wide // PIECE
    for entry, target in enumerate((cross_keep, cross_send)):
        part = low_sum(ca_keep[entry], gathered(zo_got, size, ca_wide, entry * (zo_base // 2)))
        base = spread_out(target, [part])
        part = low_sum(cb_keep[entry], gathered(x_got, size, cb_wide, entry * (x_base // 2)))
        spread_out(target, [part], base)
    gain = low_sum(gains[...], gains_got[...])
    step = size * (small // PIECE)
    extra = low_sum(extra[...], gathered(zo_got, extra.shape[0], small, zo_base + 4 * step))
    for first, sa_out, sb_out in ((0, sa_next, sb_next), (2, sa_send, sb_send)):
        for entry in range(2):
            part = slice(entry * size, (entry + 1) * size)
            start = x_base + (first + entry) * size * (large // PIECE)
            sa_out[part] = low_sum(sa_keep[first + entry], gathered(x_got, size, large, start))
            start = zo_base + (first + entry) * step
            sb_out[part] = low_sum(sb_keep[first + entry], gathered(zo_got, size, small, start))
        sa_out[2 * size :, :small] = gain
        sb_out[2 * size :] = extra


def round_five_kernel(size, sa_keep, sa_got, sb_keep, sb_got, send, keep):
    large, small = sa_keep.shape[1], sb_keep.shape[1]
    extra = low_sum(
        low_sum(sa_keep[2 * size :, :small], sa_got[2 * size :, :small]), low_sum(sb_keep[2 * size :], sb_got[2 * size :])
    )
    for entry, target in enumerate((keep, send)):
        part = slice(entry * size, (entry + 1) * size)
        base = spread_out(target, [low_sum(sa_keep[part], sa_got[part])])
        part = jnp.concatenate([low_sum(sb_keep[part], sb_got[part]), extra], 0)
        spread_out(target, [part], base)


def ffn_final_kernel(keep, got, up, down):
    size = up.shape[0]
    up[...] = both(keep[:size], got[:size])
    down[...] = both(keep[size:], got[size:])


def cross_final_kernel(keep, got, key, value, query, output):
    size, count = key.shape
    total = both(gathered(keep, size, 4 * count, 0), gathered(got, size, 4 * count, 0))
    for place, out in enumerate((key, value, query)):
        out[...] = total[:, place * count : (place + 1) * count]
    output[...] = total[:, 3 * count :].T


def self_final_kernel(
    large, keep, got, encoded_own, encoded_other,
    encoded_grad, query, key, value, output, table, gain_two, gain_three, gain_one,
):
    encoded_grad[...] = low_sum(encoded_own[...], encoded_other[...])
    size, count = key.shape
    small = 4 * count - large
    start = size * (large // PIECE)
    first = both(gathered(keep, size, large, 0), gathered(got, size, large, 0))
    table_row, more = extra_rows(4 * count, small, table.shape[0])
    more += size
    second = both(gathered(keep, more, small, start), gathered(got, more, small, start))
    total = jnp.concatenate([first, second[:size]], 1)
    for place, out in enumerate((query, key, value)):
        out[...] = total[:, place * count : (place + 1) * count]
    output[...] = total[:, 3 * count :].T
    extra = second[size:]
    table[...] = extra[table_row : table_row + table.shape[0], : table.shape[1]]
    wide = 4 * count
    back = wide - lax.axis_index("dp") * size
    rows = wide // small
    for which, out in enumerate((gain_two, gain_three, gain_one)):
        pieces = [extra[which * rows + index : which * rows + index + 1] for index in range(rows)]
        whole = jnp.concatenate(pieces, 1)
        out[...] = pltpu.roll(jnp.broadcast_to(whole, (8, wide)), back, 1)[:1, :size]


def run(kernel, name, outs, ins, us=0.0, scratch=(), scalars=0, far=0, sems=0, after=(), limit=VMEM_LIMIT):
    shapes = [jax.ShapeDtypeStruct(shape, dtype) for shape, dtype in outs]
    idle = len(after)
    body = kernel
    if idle:

        def body(*refs):
            kernel(*refs[: len(ins)], *refs[len(ins) + idle :])

    vmem = pl.BlockSpec(memory_space=pltpu.VMEM)
    hbm = pl.BlockSpec(memory_space=pltpu.HBM)
    free = pl.BlockSpec(memory_space=pl.ANY)
    smem = pl.BlockSpec(memory_space=pltpu.SMEM)
    place = [smem] * scalars + [hbm] * far + [vmem] * (len(ins) - scalars - far) + [free] * idle
    ins = [
        pltpu.with_memory_space_constraint(item, pltpu.HBM) if spec is hbm else item for item, spec in zip(ins, place)
    ]
    result = pl.pallas_call(
        body,
        out_shape=shapes,
        in_specs=place,
        out_specs=[vmem] * len(shapes),
        scratch_shapes=[pltpu.VMEM(shape, dtype) for shape, dtype in scratch]
        + ([pltpu.SemaphoreType.DMA((sems,))] if sems else []),
        compiler_params=pltpu.CompilerParams(vmem_limit_bytes=limit),
        cost_estimate=pl.CostEstimate(flops=int(us * 1.15e9), bytes_accessed=0, transcendentals=0),
        name=name,
    )(*ins, *after)
    return result[0] if len(shapes) == 1 else result


def listed(result):
    return list(result) if isinstance(result, (list, tuple)) else [result]


def to_core(value):
    return lax.ppermute(value, "tensor", [(i, i ^ 1) for i in range(lax.axis_size("tensor"))])


def to_chip(value):
    return lax.ppermute(value, "tensor", [(i, i ^ 2) for i in range(lax.axis_size("tensor"))])


def to_peer(value, bit):
    return lax.ppermute(value, "dp", [(i, i ^ (1 << bit)) for i in range(lax.axis_size("dp"))])


def on_device(
    inputs, encoded, dec_len, enc_len, language, objective, distance_bucket, token_weights, cotangent,
    gain_self, self_query, self_key, self_value, self_output, bias_table,
    gain_cross, cross_query, cross_key, cross_value, cross_output, gain_ffn, ffn_up, ffn_down,
):
    seqs, length, width = inputs.shape
    half = length // 2
    columns = self_query.shape[1]
    heads = columns // HEAD_DIM
    units = ffn_up.shape[1]
    span_part = encoded.shape[1]
    span = span_part * lax.axis_size("tensor")
    dp = lax.axis_size("dp")
    size = width // dp
    bits = dp.bit_length() - 1
    halving = bits == 3 and dp == 8 and size % 16 == 0
    along_x, along_z = ((0, 1, 2), (1, 0, 2)) if halving else (None, None)
    latest = []

    def go(kernel, name, outs, ins, last=False, **how):
        after = [item for item in latest if not any(item is one for one in ins)]
        result = run(kernel, name, outs, ins, after=after, **how)
        if not last:
            results = result if isinstance(result, (list, tuple)) else [result]
            latest[:] = [min(results, key=lambda item: item.size * item.dtype.itemsize)]
        return result

    def plus(left, right, name):
        return go(add_kernel, name, [(left.shape, left.dtype)], [left, right])

    def payload(order, wide):
        if order is None:
            return [((width, wide), BF16)]
        return [((dp // 2, size, wide), BF16)] * 2

    x = inputs.reshape(length, width)
    cot = cotangent.reshape(length, width)
    gain_one, gain_two, gain_three = gain_self, gain_cross, gain_ffn
    self_query, self_key, self_value = self_query.T, self_key.T, self_value.T
    cross_query, cross_key, cross_value = cross_query.T, cross_key.T, cross_value.T
    table = bias_table.T
    bucket = distance_bucket.reshape(1, length)
    e0 = encoded.reshape(span_part, width)

    first = go(first_kernel, "first", [((8, 128), F32)], [], us=LONG)
    key_source, value_source, _ = lax.optimization_barrier((cross_key, cross_value, first))
    e1 = to_chip(e0)
    e2 = to_core(e0)
    wk_peer = to_core(key_source)
    wv_peer = to_core(value_source)
    keep, send, more, normed_one, query_one, context_one, probs_one, dec_rows = go(
        self_forward_kernel, "self_forward",
        [((half, width), BF16)] + [((half // 2, width), BF16)] * 2 + [((length, width), BF16)]
        + [((length, columns), BF16)] * 2 + [((length, heads * length), BF16), ((8, 128), jnp.int32)],
        [dec_len, bucket, table, x, gain_one, self_query, self_key, self_value, self_output],
        scratch=[((length, width), BF16)], scalars=1, us=3.5,
    )
    first_half, second_half = to_core(send), to_core(more)
    early = go(
        source_first_kernel, "source_first", [((span // 2, columns), BF16), ((columns, span // 2), BF16)] * 2,
        [e0, e2, cross_key, cross_value, wk_peer, wv_peer],
    )
    chip_one = go(self_sum_kernel, "self_sum", [((half + EXTRA, width), BF16)], [keep, first_half, second_half])
    other_one = to_chip(chip_one)
    wq_peer = to_core(cross_query)
    wo_peer = to_core(cross_output)
    e3 = to_core(e1)
    late = go(
        source_second_kernel, "source_second", [((span, columns), BF16), ((columns, span), BF16)] * 2,
        [e1, e3, cross_key, cross_value, wk_peer, wv_peer, *early],
    )
    enc_len, objective, language, _ = lax.optimization_barrier((enc_len, objective, language, late[0]))
    info, mask = go(
        step_kernel, "step", [((8, 128), jnp.int32), ((span, half), F32)], [enc_len, objective, language], scalars=3
    )
    up_source, down_source, _ = lax.optimization_barrier((ffn_up, ffn_down, late[0]))
    down_peer = to_core(down_source)
    up_peer = to_core(up_source)

    partial_two, hidden_one, normed_two, q_own, q_peer, context_own, probs_own, probs_peer, pack_forward = go(
        cross_forward_kernel, "cross_forward",
        [((half, width), BF16), ((half, width), F32), ((half, width), BF16)] + [((half, columns), BF16)] * 3
        + [((span, heads * half), BF16)] * 2 + [((half, width + columns), BF16)],
        [mask, chip_one, other_one, x, gain_two, cross_query, wq_peer, cross_output, wo_peer, *late],
    )
    other_two = to_chip(partial_two)
    pack_forward_peer = to_core(pack_forward)
    grad_full, branch_three, branch_three_peer = go(
        out_grad_kernel, "out_grad", [((half, width), F32)] + [((half, width), BF16)] * 2,
        [info, dec_rows, token_weights, cot], us=LONG,
    )
    act_grad, act_grad_peer = go(
        act_grad_kernel, "act_grad", [((half, units), F32)] * 2, [branch_three, ffn_down, down_peer]
    )
    key_one, value_one, k_own, v_own, k_peer, v_peer = go(
        source_back_kernel, "source_back",
        [((columns, length), BF16), ((length, columns), BF16)] + [((columns, span), BF16), ((span, columns), BF16)] * 2,
        [normed_one, self_key, self_value, e0, e1, e2, e3, cross_key, cross_value, wk_peer, wv_peer],
    )

    latest.append(pack_forward_peer)
    partial_three, hidden_two, normed_three, act_own, grad_pre_own, pack_ffn = go(
        ffn_kernel, "ffn",
        [((half, width), BF16), ((half, width), F32), ((half, width), BF16)] + [((half, units), BF16)] * 2
        + [((half, width + 2 * units), BF16)],
        [partial_two, other_two, hidden_one, gain_three, ffn_up, up_peer, act_grad, act_grad_peer],
    )
    other_three = to_chip(partial_three)
    pack_ffn_peer = to_core(pack_ffn)

    def ffn_weights(*refs):
        ffn_weights_kernel((along_x, along_z), size, *refs)

    ffn_payloads = go(
        ffn_weights, "ffn_weights", payload(along_x, width) + payload(along_z, width),
        [normed_three, pack_ffn_peer, act_own, grad_pre_own, branch_three, branch_three_peer],
        scratch=[((width, units), BF16), ((length, width), BF16), ((length, units), BF16)], us=FILL,
    )

    (partial_four, grad_two, gain_grad_three, gl_own, gl_peer, gc_own, gc_peer, gq_own, branch_two,
     pack_backward) = go(
        cross_backward_kernel, "cross_backward",
        [((half, width), BF16), ((half, width), F32), ((8, width), F32)] + [((span, heads * half), BF16)] * 2
        + [((half, columns), BF16)] * 3 + [((half, width), BF16), ((half, width + columns), BF16)],
        [partial_three, other_three, hidden_two, gain_three, grad_full, cross_output, wo_peer,
         k_own, v_own, k_peer, v_peer, probs_own, probs_peer, cross_query, wq_peer],
    )
    other_four = to_chip(partial_four)
    pack_backward_peer = to_core(pack_backward)
    source_grad = go(
        source_grad_kernel, "source_grad", [((2 * span, columns), BF16)], [gl_peer, probs_peer, gc_peer, q_peer]
    )
    source_grad_peer = to_core(source_grad)
    wide = 2 * columns
    ca_wide, cb_wide = (CROSS_X, 2 * wide - CROSS_X) if halving else (wide, wide)

    def cross_weights(*refs):
        cross_weights_kernel((along_x, along_z), size, *refs)

    *cross_payload, source_total = go(
        cross_weights, "cross_weights",
        payload(along_x, ca_wide) + payload(along_z, cb_wide) + [((span, wide), BF16)],
        [gl_own, probs_own, gc_own, q_own, source_grad_peer, e0, e1, e2, e3, normed_two, pack_forward_peer,
         branch_two, pack_backward_peer, context_own, gq_own],
        scratch=[((width, 2 * wide), BF16), ((span, width), BF16), ((4 * half, wide), BF16)],
    )
    ca_payload, cb_payload = cross_payload[: len(cross_payload) // 2], cross_payload[len(cross_payload) // 2 :]
    branch_out = go(ffn_out_kernel, "ffn_out", [((half, width), BF16)], [act_own, pack_ffn, ffn_down, down_peer])

    grad_one, pack_self = go(
        self_norm_kernel, "self_norm", [((half, width), F32), ((half + EXTRA, width), BF16)],
        [partial_four, other_four, hidden_one, gain_two, grad_two, gain_grad_three],
    )
    pack_self_peer = to_core(pack_self)

    if halving:
        up_keep, up_send, down_keep, down_send = ffn_payloads
        half_sent = ((2, size, width), BF16)
        up_send, up_keep, down_send, down_keep = go(
            ffn_second_kernel, "ffn_second", [half_sent] * 4,
            [up_keep, to_peer(up_send, 0), down_keep, to_peer(down_send, 1)], us=1.0,
        )
        up_got = to_peer(up_send, 1)
        down_got = to_peer(down_send, 0)

    keep, send, branch_one, gq_one, gk_one, gv_one, gl_one = go(
        self_backward_kernel, "self_backward",
        [((half + EXTRA, width), BF16)] * 2 + [((length, width), BF16)] + [((length, columns), BF16)] * 3
        + [((length, heads * length), BF16)],
        [pack_self, pack_self_peer, self_output, self_query, self_key, self_value, query_one, key_one, value_one,
         probs_one, x],
        scratch=[((length, width), BF16)],
    )
    got = to_core(send)
    large, small = (SELF_X, 2 * wide - SELF_X) if halving else (wide, wide)
    table_row, extra_count = extra_rows(width, small, heads)

    def self_weights(*refs):
        self_weights_kernel((along_x, along_z), size, table.shape[1], *refs)

    *self_payload, extra = listed(go(
        self_weights, "self_weights",
        payload(along_x, large) + payload(along_z, small) + [((extra_count, small), BF16)],
        [normed_one, branch_one, gq_one, gk_one, gv_one, context_one, gl_one, bucket, pack_self, pack_self_peer],
        scratch=[((width, 2 * wide), BF16), ((2 * length, wide), BF16), ((2 * length, width), BF16)],
    ))
    sa_payload, sb_payload = self_payload[: len(self_payload) // 2], self_payload[len(self_payload) // 2 :]

    if halving:
        ca_keep, ca_send = ca_payload
        cb_keep, cb_send = cb_payload
        sa_keep, sa_send = sa_payload
        sb_keep, sb_send = sb_payload
        more = size + extra_count
        x_rows = (2 * size * cb_wide + 4 * size * large) // PIECE
        zo_rows = (2 * size * ca_wide + (4 * size + extra_count) * small) // PIECE
        x_send, zo_send, ca_keep, cb_keep = go(
            round_three_kernel, "round_three",
            [((x_rows, PIECE), BF16), ((zo_rows, PIECE), BF16), ((2, size, ca_wide), BF16), ((2, size, cb_wide), BF16)],
            [ca_keep, to_peer(ca_send, 0), cb_keep, to_peer(cb_send, 1), sa_send, sb_send, extra], us=1.6,
        )
        x_got = to_peer(x_send, 0)
        zo_got = to_peer(zo_send, 1)

    chip_five = go(input_sum_kernel, "input_sum", [(keep.shape, BF16)], [keep, got])
    other_five = to_chip(chip_five)

    if halving:
        ffn_send, ffn_keep = go(
            ffn_third_kernel, "ffn_third", [((2 * size, width), BF16)] * 2, [up_keep, up_got, down_keep, down_got]
        )
        ffn_got = to_peer(ffn_send, 2)
        gains = go(gain_kernel, "gain", [((extra_count, small), BF16)], [chip_five, other_five], us=LONG)
        gains_got = to_peer(gains, 0)
        branch_source, _ = lax.optimization_barrier((branch_out, gains))
    else:
        branch_source = branch_out
    out_other = to_chip(branch_source)

    if halving:
        rows = 2 * size + extra_count
        cross_send, cross_keep, sa_send, sa_keep, sb_send, sb_keep = go(
            round_four_kernel, "round_four",
            [((size * 2 * wide // PIECE, PIECE), BF16)] * 2 + [((rows, large), BF16)] * 2 + [((rows, small), BF16)] * 2,
            [x_got, zo_got, ca_keep, cb_keep, sa_keep, sb_keep, extra, gains, gains_got],
        )
        sa_got = to_peer(sa_send, 1)
        sb_got = to_peer(sb_send, 0)

    encoded_keep, encoded_send = go(
        encoded_kernel, "encoded", [((span // 2, width), BF16)] * 2, [source_total, cross_key, cross_value]
    )
    encoded_got = to_core(encoded_send)
    pack_rows = go(
        input_grad_kernel, "input_grad", [((2 * half, width), BF16)],
        [chip_five, other_five, x, gain_one, grad_one, hidden_two, branch_out, out_other],
    )
    pack_rows_peer = to_core(pack_rows)
    if halving:
        up, down = go(ffn_final_kernel, "ffn_final", [((size, width), F32)] * 2, [ffn_keep, ffn_got], us=LONG, last=True)
        cross_send, _ = lax.optimization_barrier((cross_send, encoded_send))
        cross_got = to_peer(cross_send, 2)
    encoded_part, encoded_pass = go(
        encoded_sum_kernel, "encoded_sum", [((span_part, width), BF16)] * 2, [encoded_keep, encoded_got]
    )
    encoded_other = to_chip(encoded_pass)

    if halving:
        rows = (size * large + more * small) // PIECE

        def round_five(*refs):
            round_five_kernel(size, *refs)

        self_send, self_keep = go(
            round_five, "round_five", [((rows, PIECE), BF16)] * 2, [sa_keep, sa_got, sb_keep, sb_got]
        )
        self_got = to_peer(self_send, 2)
        square = ((size, columns), F32)
        turned = ((columns, size), F32)
        grad_cross_key, grad_cross_value, grad_cross_query, grad_cross_output = go(
            cross_final_kernel, "cross_final", [square] * 3 + [turned], [cross_keep, cross_got], us=LONG, last=True
        )

    input_grad, layer_out, _ = go(
        rows_kernel, "rows", [((length, width), BF16)] * 2 + [((16, 128), BF16)], [pack_rows, pack_rows_peer]
    )

    if halving:

        def self_final(*refs):
            self_final_kernel(large, *refs)

        (encoded_grad, grad_self_query, grad_self_key, grad_self_value, grad_self_output, grad_table, grad_gain_two,
         grad_gain_three, grad_gain_one) = go(
            self_final, "self_final",
            [((span_part, width), BF16)] + [square] * 3 + [turned, (table.shape, F32)] + [((1, size), F32)] * 3,
            [self_keep, self_got, encoded_part, encoded_other], last=True,
        )
        grad_gain_one, grad_gain_two, grad_gain_three = (
            item.reshape(size) for item in (grad_gain_one, grad_gain_two, grad_gain_three)
        )
    else:
        index = lax.axis_index("dp")

        def gain_part(*rows):
            row = lax.psum(jnp.concatenate(rows, 0).astype(F32), "dp")
            return lax.dynamic_slice(row, (index * size,), (size,))

        def scattered(item):
            return lax.psum_scatter(item.astype(F32), "dp", scatter_dimension=0, tiled=True)

        def pair_of(item):
            item = scattered(item)
            return item[:, :columns], item[:, columns:]

        up, down = (scattered(item) for item in ffn_payloads)
        grad_cross_key, grad_cross_value = pair_of(ca_payload[0])
        grad_cross_query, grad_cross_output = pair_of(cb_payload[0])
        grad_self_query, grad_self_key = pair_of(sa_payload[0])
        grad_self_value, grad_self_output = pair_of(sb_payload[0])
        grad_cross_output, grad_self_output = grad_cross_output.T, grad_self_output.T
        grad_table = lax.psum(extra[table_row : table_row + heads, : table.shape[1]].astype(F32), "dp")
        encoded_grad = plus(encoded_part, encoded_other, "encoded_grad")
        gain_rows = [item[half : half + 2] for item in (chip_five, other_five)]
        grad_gain_one = gain_part(jnp.sum(jnp.concatenate(gain_rows, 0).astype(F32), 0))
        grad_gain_two = gain_part(extra[0], extra[1])
        grad_gain_three = gain_part(extra[2], extra[3])

    return (
        layer_out.reshape(seqs, length, width),
        input_grad.reshape(seqs, length, width),
        encoded_grad.reshape(seqs, span_part, width),
        grad_gain_one,
        grad_self_query,
        grad_self_key,
        grad_self_value,
        grad_self_output,
        grad_table.T,
        grad_gain_two,
        grad_cross_query,
        grad_cross_key,
        grad_cross_value,
        grad_cross_output,
        grad_gain_three,
        up,
        down.T,
    )


def solution(mesh):
    return jax.shard_map(
        on_device,
        mesh=mesh,
        in_specs=(
            P("dp", None, None),
            P("dp", "tensor", None),
            P("dp"),
            P("dp"),
            P("dp"),
            P("dp"),
            P(),
            P(),
            P("dp", None, None),
            P(),
            P(None, "tensor"),
            P(None, "tensor"),
            P(None, "tensor"),
            P("tensor", None),
            P(None, "tensor"),
            P(),
            P(None, "tensor"),
            P(None, "tensor"),
            P(None, "tensor"),
            P("tensor", None),
            P(),
            P(None, "tensor"),
            P("tensor", None),
        ),
        out_specs=(
            P("dp", None, None),
            P("dp", None, None),
            P("dp", "tensor", None),
            P("dp"),
            P("dp", "tensor"),
            P("dp", "tensor"),
            P("dp", "tensor"),
            P("tensor", "dp"),
            P(None, "tensor"),
            P("dp"),
            P("dp", "tensor"),
            P("dp", "tensor"),
            P("dp", "tensor"),
            P("tensor", "dp"),
            P("dp"),
            P("dp", "tensor"),
            P("tensor", "dp"),
        ),
        check_vma=False,
    )
```

```python
import jax
import jax.numpy as jnp
from jax import lax
from jax.experimental import pallas as pl
from jax.experimental.pallas import tpu as pltpu
from jax.sharding import PartitionSpec as P

HEAD_DIM = 64
LANGS = 8
EPSILON = 1e-06
SCALE = 0.125
NEGATIVE = -1e30
F32 = jnp.float32
BF16 = jnp.bfloat16
VMEM_LIMIT = 20 * 1024 * 1024
EXTRA = 16
PIECE = 128
CROSS_X = 384
SELF_X = 512
FILL = 5.0
LONG = 20.0


def dot(left, right):
    return jnp.dot(left, right, preferred_element_type=F32)


def dot_nt(left, right):
    return lax.dot_general(left, right, (((1,), (1,)), ((), ())), preferred_element_type=F32)


def dot_tn(left, right):
    return lax.dot_general(left, right, (((0,), (0,)), ((), ())), preferred_element_type=F32)


def row_of(vector_ref):
    return vector_ref[...].reshape(1, vector_ref.shape[0])


def inverse_rms(resid):
    return lax.rsqrt(jnp.mean(resid * resid, -1, keepdims=True) + EPSILON)


def norm_back(resid, gain, incoming):
    scale = inverse_rms(resid)
    weighted = incoming * gain
    inner = jnp.mean(weighted * resid, -1, keepdims=True)
    grad = scale * weighted - resid * (scale * scale * scale * inner)
    gain_grad = jnp.sum(incoming * resid * scale, 0, keepdims=True)
    return grad, gain_grad


def groups_of(width):
    return [(start, min(2 * HEAD_DIM, width - start)) for start in range(0, width, 2 * HEAD_DIM)]


def head_mask(count, which, value):
    lane = lax.broadcasted_iota(jnp.int32, (1, count), 1)
    return jnp.where(lane // HEAD_DIM == which, value, 0.0).astype(BF16)


def stacked_heads(rows, value):
    width = rows.shape[1]
    if width == HEAD_DIM:
        return rows * jnp.asarray(value, BF16)
    return jnp.concatenate([rows * head_mask(width, inside, value) for inside in range(width // HEAD_DIM)], 0)


def own_blocks(product, count):
    rows = product.shape[1] // count
    return [
        product[inside * HEAD_DIM : (inside + 1) * HEAD_DIM, inside * rows : (inside + 1) * rows]
        for inside in range(count)
    ]


def heads_forward(queries, keys, values_turned, finish, probs_ref):
    rows = queries.shape[0]
    parts = []
    for start, width in groups_of(queries.shape[1]):
        head, count = start // HEAD_DIM, width // HEAD_DIM
        stacked = stacked_heads(queries[:, start : start + width], SCALE)
        logits = finish(head, count, dot_nt(keys[:, start : start + width], stacked))
        expo = jnp.exp(logits - jnp.max(logits, 0, keepdims=True))
        probs = (expo * (1.0 / jnp.sum(expo, 0, keepdims=True))).astype(BF16)
        probs_ref[:, head * rows : (head + count) * rows] = probs
        parts += own_blocks(dot(values_turned[start : start + width], probs), count)
    return jnp.concatenate(parts, 0).astype(BF16)


def heads_backward(grad_context, keys_turned, values, probs_ref, grad_logits_ref):
    rows = grad_context.shape[0]
    parts = []
    for start, width in groups_of(grad_context.shape[1]):
        head, count = start // HEAD_DIM, width // HEAD_DIM
        place = slice(head * rows, (head + count) * rows)
        stacked = stacked_heads(grad_context[:, start : start + width], 1.0)
        grad_probs = dot_nt(values[:, start : start + width], stacked)
        probs = probs_ref[:, place].astype(F32)
        weighted = jnp.sum(grad_probs * probs, 0, keepdims=True)
        grad_logits = (probs * (grad_probs - weighted)).astype(BF16)
        grad_logits_ref[:, place] = grad_logits
        parts += own_blocks(SCALE * dot(keys_turned[start : start + width], grad_logits), count)
    return jnp.concatenate(parts, 0).astype(BF16)


def heads_spread(matrix_ref, rows, factor):
    length = rows.shape[0]
    parts = []
    for start, width in groups_of(rows.shape[1]):
        head, count = start // HEAD_DIM, width // HEAD_DIM
        stacked = stacked_heads(rows[:, start : start + width], 1.0)
        parts.append(factor * dot(matrix_ref[:, head * length : (head + count) * length], stacked))
    return jnp.concatenate(parts, 1).astype(BF16)


def own_rows(core, half):
    return pl.ds(pl.multiple_of(core * half, half), half)


def bucket_onehot(bucket_ref, buckets):
    wanted = lax.broadcasted_iota(jnp.int32, (buckets, bucket_ref.shape[1]), 0)
    return jnp.where(bucket_ref[...] == wanted, 1.0, 0.0)


def add_kernel(left_ref, right_ref, out_ref):
    out_ref[...] = (left_ref[...].astype(F32) + right_ref[...].astype(F32)).astype(out_ref.dtype)


def first_kernel(out):
    out[...] = jnp.zeros_like(out)


def step_kernel(enc_len, objective, language, info, mask):
    info[...] = jnp.full(info.shape, objective[0] * LANGS + language[0], jnp.int32)
    rows = mask.shape[0] // 4
    row = lax.broadcasted_iota(jnp.int32, mask.shape, 0)
    block = row // rows
    flip = jnp.where(block % 2 == 1, 1, 0) + jnp.where(block >= 2, 2, 0)
    position = (lax.axis_index("tensor") ^ flip) * rows + row % rows
    mask[...] = jnp.where(position < enc_len[0], 0.0, NEGATIVE)


def self_sum_kernel(own, first, second, out):
    rows = first.shape[0]
    out[:rows] = both(own[:rows], first[...]).astype(BF16)
    out[rows : 2 * rows] = both(own[rows:], second[...]).astype(BF16)
    out[2 * rows :] = jnp.zeros((out.shape[0] - 2 * rows, out.shape[1]), BF16)


def self_forward_kernel(
    dec_len, bucket, table, x, gain, w_query, w_key, w_value, w_output,
    keep, send, more, normed_out, query_out, context_out, probs_out, dec_out, whole,
):
    dec_out[...] = jnp.full(dec_out.shape, dec_len[0], jnp.int32)
    length = x.shape[0]
    resid = x[...].astype(F32)
    normed = (resid * inverse_rms(resid) * row_of(gain)).astype(BF16)
    normed_out[...] = normed
    queries = dot_nt(normed, w_query[...]).astype(BF16)
    keys = dot_nt(normed, w_key[...]).astype(BF16)
    values = dot_nt(w_value[...], normed).astype(BF16)
    query_out[...] = queries
    by_distance = lax.dot_general(
        table[...],
        bucket_onehot(bucket, table.shape[1]),
        (((1,), (0,)), ((), ())),
        precision=lax.Precision.HIGHEST,
        preferred_element_type=F32,
    )
    row = lax.broadcasted_iota(jnp.int32, (length, length), 0)
    column = lax.broadcasted_iota(jnp.int32, (length, length), 1)
    allowed = (row <= column) & (row < dec_len[0])

    def finish(head, count, scores):
        parts = []
        for inside in range(count):
            spread = jnp.broadcast_to(by_distance[head + inside : head + inside + 1], (length, length))
            bias = pltpu.roll(spread, 0, 1, stride=1, stride_axis=0)
            part = scores[:, inside * length : (inside + 1) * length]
            parts.append(jnp.where(allowed, part + bias, NEGATIVE))
        return jnp.concatenate(parts, 1) if count > 1 else parts[0]

    context = heads_forward(queries, keys, values, finish, probs_out)
    context_out[...] = context.T
    whole[...] = dot_tn(context, w_output[...]).astype(BF16)
    half = keep.shape[0]
    core = lax.axis_index("tensor") % 2
    keep[...] = whole[own_rows(core, half), :]
    rows = send.shape[0]
    send[...] = whole[own_rows(2 - 2 * core, rows), :]
    more[...] = whole[own_rows(3 - 2 * core, rows), :]


def source_rows(parts, start, wk_own, wv_own, wk_peer, wv_peer, k_own, v_own, k_peer, v_peer):
    rows = parts[0].shape[0]
    for index, part in enumerate(parts):
        place = slice(start + index * rows, start + (index + 1) * rows)
        for weight, out in ((wk_own, k_own), (wk_peer, k_peer)):
            out[place, :] = dot_nt(part[...], weight[...]).astype(BF16)
        for weight, out in ((wv_own, v_own), (wv_peer, v_peer)):
            out[:, place] = dot_nt(weight[...], part[...]).astype(BF16)


def source_first_kernel(first, *refs):
    source_rows([first], 0, *refs)


def source_second_kernel(
    first, second, third, wk_own, wv_own, wk_peer, wv_peer, early_k_own, early_v_own, early_k_peer, early_v_peer,
    k_own, v_own, k_peer, v_peer,
):
    rows = first.shape[0]
    for early, out in ((early_k_own, k_own), (early_k_peer, k_peer)):
        out[:rows] = early[...]
    for early, out in ((early_v_own, v_own), (early_v_peer, v_peer)):
        out[:, :rows] = early[...]
    source_rows([first, second, third], rows, wk_own, wv_own, wk_peer, wv_peer, k_own, v_own, k_peer, v_peer)


def source_back_kernel(
    normed, w_key, w_value, e0, e1, e2, e3, wk_own, wv_own, wk_peer, wv_peer,
    keys_turned, values, k_own, v_own, k_peer, v_peer,
):
    keys_turned[...] = dot_nt(w_key[...], normed[...]).astype(BF16)
    values[...] = dot_nt(normed[...], w_value[...]).astype(BF16)
    rows = e0.shape[0]
    for index, part in enumerate((e0, e2, e1, e3)):
        place = slice(index * rows, (index + 1) * rows)
        for weight, out in ((wk_own, k_own), (wk_peer, k_peer)):
            out[:, place] = dot_nt(weight[...], part[...]).astype(BF16)
        for weight, out in ((wv_own, v_own), (wv_peer, v_peer)):
            out[place, :] = dot_nt(part[...], weight[...]).astype(BF16)


def out_grad_kernel(info, dec_len, token_weights, cotangent, grad_own, branch_own, branch_peer):
    half = grad_own.shape[0]
    length = cotangent.shape[0]
    core = lax.axis_index("tensor") % 2
    row = lax.broadcasted_iota(jnp.int32, token_weights.shape, 0)
    weights = jnp.sum(jnp.where(row == info[:1, :1], token_weights[...], 0.0), 0, keepdims=True)
    position = lax.broadcasted_iota(jnp.int32, (1, length), 1)
    weights = jnp.where(position < dec_len[:1, :1], weights, 0.0)

    def rows_of(side):
        row = lax.broadcasted_iota(jnp.int32, (half, length), 0) + side * half
        column = lax.broadcasted_iota(jnp.int32, (half, length), 1)
        factor = jnp.sum(jnp.where(row == column, weights, 0.0), -1, keepdims=True)
        return cotangent[own_rows(side, half), :].astype(F32) * factor

    own = rows_of(core)
    grad_own[...] = own
    branch_own[...] = own.astype(BF16)
    branch_peer[...] = rows_of(1 - core).astype(BF16)


def act_grad_kernel(branch, down_own, down_peer, own, peer):
    own[...] = dot_nt(branch[...], down_own[...])
    peer[...] = dot_nt(branch[...], down_peer[...])


def cross_forward_kernel(
    mask, chip_own, chip_other, x, gain, wq_own, wq_peer, wo_own, wo_peer, k_own, v_own, k_peer, v_peer,
    partial_out, hidden_out, normed_out, q_own, q_peer, context_own, probs_own, probs_peer, pack,
):
    half, width = hidden_out.shape
    core = lax.axis_index("tensor") % 2
    resid = x[own_rows(core, half), :].astype(F32)
    resid = resid + both(chip_own[:half], chip_other[:half])
    hidden_out[...] = resid
    normed = (resid * inverse_rms(resid) * row_of(gain)).astype(BF16)
    normed_out[...] = normed
    pack[:, :width] = normed

    def finish(head, count, scores):
        return scores + jnp.concatenate([mask[...]] * count, 1)

    queries = dot_nt(normed, wq_own[...]).astype(BF16)
    q_own[...] = queries
    first = heads_forward(queries, k_own[...], v_own[...], finish, probs_own)
    context_own[...] = first.T
    queries = dot_nt(normed, wq_peer[...]).astype(BF16)
    q_peer[...] = queries
    second = heads_forward(queries, k_peer[...], v_peer[...], finish, probs_peer)
    pack[:, width:] = second.T
    partial_out[...] = (dot_tn(first, wo_own[...]) + dot_tn(second, wo_peer[...])).astype(BF16)


def through_units(normed, up, act_grad):
    pre = dot(normed, up[...])
    square = pre * pre
    tanh = jnp.tanh(0.7978845608028654 * (pre + 0.044715 * square * pre))
    half_sum = 0.5 * (1.0 + tanh)
    slope = half_sum + 0.5 * pre * (1.0 - tanh * tanh) * (
        0.7978845608028654 * (1.0 + 3.0 * 0.044715 * square)
    )
    return (pre * half_sum).astype(BF16), (act_grad[...] * slope).astype(BF16)


def ffn_peer_kernel(chip_own, chip_other, hidden, gain, up_peer, act_grad_peer, hidden_out, normed_out, part_out, pack):
    width = hidden.shape[1]
    resid = hidden[...] + both(chip_own[...], chip_other[...])
    hidden_out[...] = resid
    normed = (resid * inverse_rms(resid) * row_of(gain)).astype(BF16)
    normed_out[...] = normed
    pack[:, :width] = normed
    act, grad_pre = through_units(normed, up_peer, act_grad_peer)
    units = act.shape[1]
    pack[:, width : width + units] = act
    pack[:, width + units :] = grad_pre
    part_out[...] = dot_nt(grad_pre, up_peer[...])


def ffn_own_kernel(normed, up_own, act_grad_own, part, partial_out, act_own, grad_pre_own):
    act, grad_pre = through_units(normed[...], up_own, act_grad_own)
    act_own[...] = act
    grad_pre_own[...] = grad_pre
    partial_out[...] = (part[...] + dot_nt(grad_pre, up_own[...])).astype(BF16)


def ffn_out_kernel(act_own, pack, down_own, down_peer, out):
    units = act_own.shape[1]
    width = out.shape[1]
    total = dot(act_own[...], down_own[...]) + dot(pack[:, width : width + units], down_peer[...])
    out[...] = total.astype(BF16)


def write_blocks(whole, columns, first_bit, rest_bits, size, targets):
    index = lax.axis_index("dp")
    count = 1 << len(rest_bits)
    for first, target in enumerate(targets):
        for entry in range(count):
            relative = first << first_bit
            for place, bit in enumerate(rest_bits):
                if entry >> (len(rest_bits) - 1 - place) & 1:
                    relative |= 1 << bit
            block = index ^ relative
            target[entry] = whole[pl.ds(pl.multiple_of(block * size, size), size), columns]


def emit(whole, outs, order, size, columns=slice(None)):
    if order is None:
        outs[0][...] = whole[:, columns]
    else:
        write_blocks(whole, columns, order[0], order[1:], size, outs)


def ffn_weights_kernel(orders, size, normed, pack, act_own, grad_pre_own, branch_own, branch_peer, *refs):
    *outs, whole, left, right = refs
    half, width = normed.shape
    units = act_own.shape[1]
    left[:half] = normed[...]
    left[half:] = pack[:, :width]
    right[:half] = grad_pre_own[...]
    right[half:] = pack[:, width + units :]
    whole[...] = dot_tn(left[...], right[...]).astype(BF16)
    count = 1 if orders[0] is None else 2
    emit(whole, outs[:count], orders[0], size)
    left[:half] = branch_own[...]
    left[half:] = branch_peer[...]
    right[:half] = act_own[...]
    right[half:] = pack[:, width : width + units]
    whole[...] = dot_tn(left[...], right[...]).astype(BF16)
    emit(whole, outs[count:], orders[1], size)


def cross_backward_kernel(
    chip_own, chip_other, hidden, gain, grad_out, wo_own, wo_peer, k_own, v_own, k_peer, v_peer,
    probs_own, probs_peer, wq_own, wq_peer,
    partial_out, grad_hidden, gain_grad, gl_own, gl_peer, gc_own, gc_peer, gq_own, branch, pack,
):
    incoming = chip_own[...].astype(F32) + chip_other[...].astype(F32)
    added, gain_terms = norm_back(hidden[...], row_of(gain), incoming)
    gain_grad[...] = jnp.broadcast_to(gain_terms, gain_grad.shape)
    grad = grad_out[...] + added
    grad_hidden[...] = grad
    rounded = grad.astype(BF16)
    branch[...] = rounded
    width = rounded.shape[1]
    pack[:, :width] = rounded
    context = dot_nt(rounded, wo_own[...]).astype(BF16)
    gc_own[...] = context
    queries = heads_backward(context, k_own[...], v_own[...], probs_own, gl_own)
    gq_own[...] = queries.T
    total = dot_tn(queries, wq_own[...])
    context = dot_nt(rounded, wo_peer[...]).astype(BF16)
    gc_peer[...] = context
    queries = heads_backward(context, k_peer[...], v_peer[...], probs_peer, gl_peer)
    pack[:, width:] = queries.T
    total = total + dot_tn(queries, wq_peer[...])
    partial_out[...] = total.astype(BF16)


def source_grad_kernel(gl_peer, probs_peer, gc_peer, q_peer, out):
    span = out.shape[0] // 2
    rows = span // 4
    for start, grads in (
        (0, heads_spread(gl_peer, q_peer[...], SCALE)),
        (span, heads_spread(probs_peer, gc_peer[...], 1.0)),
    ):
        for block in range(4):
            there = start + (block ^ 1) * rows
            out[there : there + rows] = grads[block * rows : (block + 1) * rows]


def cross_weights_kernel(
    orders, size, gl_own, probs_own, gc_own, q_own, other, e0, e1, e2, e3, normed, pack_forward,
    branch, pack_backward, context_own, gq_own, *refs,
):
    *outs, source, whole, left, right = refs
    count = len(outs) // 2
    span = other.shape[0] // 2
    half, width = normed.shape
    columns = q_own.shape[1]
    source[:, :columns] = low_sum(heads_spread(gl_own, q_own[...], SCALE), other[:span])
    source[:, columns:] = low_sum(heads_spread(probs_own, gc_own[...], 1.0), other[span:])
    for index, part in enumerate((e0, e2, e1, e3)):
        left[index * half : (index + 1) * half] = part[...]
    whole[:, : 2 * columns] = dot_tn(left[...], source[...]).astype(BF16)
    left[:half] = normed[...]
    left[half : 2 * half] = pack_forward[:, :width]
    left[2 * half : 3 * half] = branch[...]
    left[3 * half :] = pack_backward[:, :width]
    right[...] = jnp.zeros_like(right)
    right[:half, :columns] = gq_own[...]
    right[half : 2 * half, :columns] = pack_backward[:, width:]
    right[2 * half : 3 * half, columns:] = context_own[...]
    right[3 * half :, columns:] = pack_forward[:, width:]
    whole[:, 2 * columns :] = dot_tn(left[...], right[...]).astype(BF16)
    wide = outs[0].shape[-1]
    emit(whole, outs[:count], orders[0], size, columns=slice(0, wide))
    emit(whole, outs[count:], orders[1], size, columns=slice(wide, None))


def encoded_kernel(source, wk_own, wv_own, keep, send):
    columns = wk_own.shape[0]
    terms = dot(source[:, :columns], wk_own[...]) + dot(source[:, columns:], wv_own[...])
    terms = terms.astype(BF16)
    rows = keep.shape[0] // 2
    for block in range(4):
        target = send if block % 2 else keep
        target[block // 2 * rows : (block // 2 + 1) * rows] = terms[block * rows : (block + 1) * rows]


def self_norm_kernel(chip_own, chip_other, hidden, gain, grad_hidden, gain_ffn, grad_out, pack):
    half = hidden.shape[0]
    incoming = chip_own[...].astype(F32) + chip_other[...].astype(F32)
    added, gain_terms = norm_back(hidden[...], row_of(gain), incoming)
    grad = grad_hidden[...] + added
    grad_out[...] = grad
    pack[:half] = grad.astype(BF16)
    row = lax.broadcasted_iota(jnp.int32, (EXTRA, hidden.shape[1]), 0)
    extra = jnp.where(row == 0, gain_terms, 0.0) + jnp.where(row == 1, gain_ffn[:1], 0.0)
    pack[half:] = extra.astype(BF16)


def high_low(vector):
    high = vector.astype(BF16).astype(F32)
    row = lax.broadcasted_iota(jnp.int32, (EXTRA, vector.shape[1]), 0)
    return (jnp.where(row == 0, high, 0.0) + jnp.where(row == 1, vector - high, 0.0)).astype(BF16)


def of_high_low(rows):
    rows = rows.astype(F32)
    return rows[:1] + rows[1:2]


def self_backward_kernel(
    pack_own, pack_peer, w_output, w_query, w_key, w_value, queries, keys, values, probs, x,
    keep, send, branch_out, gq_out, gk_out, gv_out, gl_out, whole,
):
    half = keep.shape[0] - EXTRA
    core = lax.axis_index("tensor") % 2
    branch_out[own_rows(core, half), :] = pack_own[:half]
    branch_out[own_rows(1 - core, half), :] = pack_peer[:half]
    context = dot_nt(branch_out[...], w_output[...]).astype(BF16)
    grad_queries = heads_backward(context, keys[...], values[...], probs, gl_out)
    grad_keys = heads_spread(gl_out, queries[...], SCALE)
    grad_values = heads_spread(probs, context, 1.0)
    gq_out[...] = grad_queries.T
    gk_out[...] = grad_keys
    gv_out[...] = grad_values
    total = dot_tn(grad_queries, w_query[...]) + dot(grad_keys, w_key[...]) + dot(grad_values, w_value[...])
    whole[...] = total.astype(BF16)
    keep[:half] = whole[own_rows(core, half), :]
    send[:half] = whole[own_rows(1 - core, half), :]
    resid = x[...].astype(F32)
    gain_terms = high_low(jnp.sum(total * resid * inverse_rms(resid), 0, keepdims=True))
    keep[half:] = gain_terms
    send[half:] = gain_terms


def input_sum_kernel(own, peer, out):
    half = out.shape[0] - EXTRA
    out[:half] = both(own[:half], peer[:half]).astype(BF16)
    out[half:] = high_low(of_high_low(own[half:]) + of_high_low(peer[half:]))


def self_weights_kernel(
    orders, size, buckets, normed, branch, gq, gk, gv, context, gl, bucket, pack_own, pack_peer, *refs
):
    *outs, extra_out, whole, right, left = refs
    count = len(outs) // 2
    length, columns = gq.shape
    half = pack_own.shape[0] - EXTRA
    right[:length, :columns] = gq[...]
    right[:length, columns:] = gk[...]
    whole[:, : 2 * columns] = dot_tn(normed[...], right[:length]).astype(BF16)
    left[:length] = normed[...]
    left[length:] = branch[...]
    right[...] = jnp.zeros_like(right)
    right[:length, :columns] = gv[...]
    right[length:, columns:] = context[...]
    whole[:, 2 * columns :] = dot_tn(left[...], right[...]).astype(BF16)
    wide = outs[0].shape[-1]
    emit(whole, outs[:count], orders[0], size, columns=slice(0, wide))
    onehot = bucket_onehot(bucket, buckets)
    row = lax.broadcasted_iota(jnp.int32, (length, length), 0)
    column = lax.broadcasted_iota(jnp.int32, (length, length), 1)
    turn = jnp.where(row + column == length - 1, 1.0, 0.0).astype(BF16)
    place = lax.broadcasted_iota(jnp.int32, (8, length), 0)
    sums = jnp.zeros((8, length), F32)
    heads = gl.shape[1] // length
    for head in range(heads):
        skewed = pltpu.roll(dot(turn, gl[:, head * length : (head + 1) * length]), 1, 1, stride=1, stride_axis=0)
        sums = sums + jnp.where(place == head, jnp.sum(skewed, 0, keepdims=True), 0.0)
    table = lax.dot_general(
        sums, onehot, (((1,), (1,)), ((), ())), precision=lax.Precision.HIGHEST, preferred_element_type=F32
    )
    gains = both(pack_own[half:], pack_peer[half:])
    narrow = outs[-1].shape[-1]
    first, count_rows = extra_rows(gains.shape[1], narrow, heads)
    extra = vector_rows(gains[:1], narrow, count_rows, 0) + vector_rows(gains[1:2], narrow, count_rows, 1)
    table = jnp.concatenate([table, jnp.zeros((8, narrow - buckets), F32)], 1)
    row = lax.broadcasted_iota(jnp.int32, (count_rows, narrow), 0)
    for head in range(heads):
        extra = extra + jnp.where(row == first + head, table[head : head + 1], 0.0)
    extra_out[...] = extra.astype(BF16)
    emit(whole, outs[count:], orders[1], size, columns=slice(wide, None))


def extra_rows(width, wide, heads):
    first = -(-3 * (width // wide) // 4) * 4
    return first, -(-(first + heads) // 16) * 16


def vector_rows(vector, wide, count, which):
    rows = vector.shape[1] // wide
    row = lax.broadcasted_iota(jnp.int32, (count, wide), 0)
    placed = jnp.zeros((count, wide), F32)
    for index in range(rows):
        piece = vector[:, index * wide : (index + 1) * wide]
        placed = placed + jnp.where(row == which * rows + index, piece, 0.0)
    return placed


def encoded_sum_kernel(own, other, keep, send):
    rows = keep.shape[0]
    keep[...] = low_sum(own[:rows], other[:rows])
    send[...] = low_sum(own[rows:], other[rows:])


def input_grad_kernel(chip_own, chip_other, x, gain, grad_hidden, hidden_two, out_own, out_other, pack):
    half = hidden_two.shape[0]
    resid = x[own_rows(lax.axis_index("tensor") % 2, half), :].astype(F32)
    added, _ = norm_back(resid, row_of(gain), both(chip_own[:half], chip_other[:half]))
    pack[:half] = (grad_hidden[...] + added).astype(BF16)
    pack[half:] = (hidden_two[...] + both(out_own[...], out_other[...])).astype(BF16)


def rows_kernel(own, peer, input_grad, layer_out, token):
    half = own.shape[0] // 2
    core = lax.axis_index("tensor") % 2
    for place, out in ((0, input_grad), (half, layer_out)):
        out[own_rows(core, half), :] = own[place : place + half]
        out[own_rows(1 - core, half), :] = peer[place : place + half]
    token[...] = own[: token.shape[0], : token.shape[1]]


def both(left, right):
    return left.astype(F32) + right.astype(F32)


def low_sum(left, right):
    return both(left, right).astype(BF16)


def ffn_second_kernel(up_keep, up_got, down_keep, down_got, up_send, up_next, down_send, down_next):
    for keep, got, send, new in (
        (up_keep, up_got, up_send, up_next),
        (down_keep, down_got, down_send, down_next),
    ):
        for entry in range(2):
            new[entry] = low_sum(keep[entry], got[entry])
            send[entry] = low_sum(keep[2 + entry], got[2 + entry])


def ffn_third_kernel(up_keep, up_got, down_keep, down_got, send, keep):
    size = up_keep.shape[1]
    for entry, target in enumerate((keep, send)):
        target[:size] = low_sum(up_keep[entry], up_got[entry])
        target[size:] = low_sum(down_keep[entry], down_got[entry])


def round_three_kernel(
    ca_keep, ca_got, cb_keep, cb_got, sa_send, sb_send, extra, x_send, zo_send, ca_next, cb_next
):
    for entry in range(2):
        ca_next[entry] = low_sum(ca_keep[entry], ca_got[entry])
        cb_next[entry] = low_sum(cb_keep[entry], cb_got[entry])
    base = spread_out(x_send, [low_sum(cb_keep[2 + entry], cb_got[2 + entry]) for entry in range(2)])
    spread_out(x_send, [sa_send[entry] for entry in range(4)], base)
    base = spread_out(zo_send, [low_sum(ca_keep[2 + entry], ca_got[2 + entry]) for entry in range(2)])
    base = spread_out(zo_send, [sb_send[entry] for entry in range(4)], base)
    spread_out(zo_send, [extra[...]], base)


def gain_kernel(chip_own, chip_other, out):
    half = chip_own.shape[0] - EXTRA
    gain = of_high_low(chip_own[half:]) + of_high_low(chip_other[half:])
    out[...] = vector_rows(gain, out.shape[1], out.shape[0], 2).astype(BF16)


def spread_out(target, parts, start=0):
    for part in parts:
        rows = part.shape[0]
        for side in range(part.shape[1] // PIECE):
            target[start : start + rows] = part[:, side * PIECE : (side + 1) * PIECE]
            start += rows
    return start


def gathered(source, rows, wide, start):
    pieces = [source[start + side * rows : start + (side + 1) * rows] for side in range(wide // PIECE)]
    return jnp.concatenate(pieces, 1) if len(pieces) > 1 else pieces[0]


def round_four_kernel(
    x_got, zo_got, ca_keep, cb_keep, sa_keep, sb_keep, extra, gains, gains_got,
    cross_send, cross_keep, sa_send, sa_next, sb_send, sb_next,
):
    size, ca_wide = ca_keep.shape[1:]
    cb_wide = cb_keep.shape[2]
    large, small = sa_keep.shape[2], sb_keep.shape[2]
    zo_base = 2 * size * ca_wide // PIECE
    x_base = 2 * size * cb_wide // PIECE
    for entry, target in enumerate((cross_keep, cross_send)):
        part = low_sum(ca_keep[entry], gathered(zo_got, size, ca_wide, entry * (zo_base // 2)))
        base = spread_out(target, [part])
        part = low_sum(cb_keep[entry], gathered(x_got, size, cb_wide, entry * (x_base // 2)))
        spread_out(target, [part], base)
    gain = low_sum(gains[...], gains_got[...])
    step = size * (small // PIECE)
    extra = low_sum(extra[...], gathered(zo_got, extra.shape[0], small, zo_base + 4 * step))
    for first, sa_out, sb_out in ((0, sa_next, sb_next), (2, sa_send, sb_send)):
        for entry in range(2):
            part = slice(entry * size, (entry + 1) * size)
            start = x_base + (first + entry) * size * (large // PIECE)
            sa_out[part] = low_sum(sa_keep[first + entry], gathered(x_got, size, large, start))
            start = zo_base + (first + entry) * step
            sb_out[part] = low_sum(sb_keep[first + entry], gathered(zo_got, size, small, start))
        sa_out[2 * size :, :small] = gain
        sb_out[2 * size :] = extra


def round_five_kernel(size, sa_keep, sa_got, sb_keep, sb_got, send, keep):
    large, small = sa_keep.shape[1], sb_keep.shape[1]
    extra = low_sum(
        low_sum(sa_keep[2 * size :, :small], sa_got[2 * size :, :small]), low_sum(sb_keep[2 * size :], sb_got[2 * size :])
    )
    for entry, target in enumerate((keep, send)):
        part = slice(entry * size, (entry + 1) * size)
        base = spread_out(target, [low_sum(sa_keep[part], sa_got[part])])
        part = jnp.concatenate([low_sum(sb_keep[part], sb_got[part]), extra], 0)
        spread_out(target, [part], base)


def ffn_final_kernel(keep, got, up, down):
    size = up.shape[0]
    up[...] = both(keep[:size], got[:size])
    down[...] = both(keep[size:], got[size:])


def cross_final_kernel(keep, got, key, value, query, output):
    size, count = key.shape
    total = both(gathered(keep, size, 4 * count, 0), gathered(got, size, 4 * count, 0))
    for place, out in enumerate((key, value, query)):
        out[...] = total[:, place * count : (place + 1) * count]
    output[...] = total[:, 3 * count :].T


def self_final_kernel(
    large, keep, got, encoded_own, encoded_other,
    encoded_grad, query, key, value, output, table, gain_two, gain_three, gain_one,
):
    encoded_grad[...] = low_sum(encoded_own[...], encoded_other[...])
    size, count = key.shape
    small = 4 * count - large
    start = size * (large // PIECE)
    first = both(gathered(keep, size, large, 0), gathered(got, size, large, 0))
    table_row, more = extra_rows(4 * count, small, table.shape[0])
    more += size
    second = both(gathered(keep, more, small, start), gathered(got, more, small, start))
    total = jnp.concatenate([first, second[:size]], 1)
    for place, out in enumerate((query, key, value)):
        out[...] = total[:, place * count : (place + 1) * count]
    output[...] = total[:, 3 * count :].T
    extra = second[size:]
    table[...] = extra[table_row : table_row + table.shape[0], : table.shape[1]]
    wide = 4 * count
    back = wide - lax.axis_index("dp") * size
    rows = wide // small
    for which, out in enumerate((gain_two, gain_three, gain_one)):
        pieces = [extra[which * rows + index : which * rows + index + 1] for index in range(rows)]
        whole = jnp.concatenate(pieces, 1)
        out[...] = pltpu.roll(jnp.broadcast_to(whole, (8, wide)), back, 1)[:1, :size]


def run(kernel, name, outs, ins, us=0.0, scratch=(), scalars=0, far=0, sems=0, after=(), limit=VMEM_LIMIT):
    shapes = [jax.ShapeDtypeStruct(shape, dtype) for shape, dtype in outs]
    idle = len(after)
    body = kernel
    if idle:

        def body(*refs):
            kernel(*refs[: len(ins)], *refs[len(ins) + idle :])

    vmem = pl.BlockSpec(memory_space=pltpu.VMEM)
    hbm = pl.BlockSpec(memory_space=pltpu.HBM)
    free = pl.BlockSpec(memory_space=pl.ANY)
    smem = pl.BlockSpec(memory_space=pltpu.SMEM)
    place = [smem] * scalars + [hbm] * far + [vmem] * (len(ins) - scalars - far) + [free] * idle
    ins = [
        pltpu.with_memory_space_constraint(item, pltpu.HBM) if spec is hbm else item for item, spec in zip(ins, place)
    ]
    result = pl.pallas_call(
        body,
        out_shape=shapes,
        in_specs=place,
        out_specs=[vmem] * len(shapes),
        scratch_shapes=[pltpu.VMEM(shape, dtype) for shape, dtype in scratch]
        + ([pltpu.SemaphoreType.DMA((sems,))] if sems else []),
        compiler_params=pltpu.CompilerParams(vmem_limit_bytes=limit),
        cost_estimate=pl.CostEstimate(flops=int(us * 1.15e9), bytes_accessed=0, transcendentals=0),
        name=name,
    )(*ins, *after)
    return result[0] if len(shapes) == 1 else result


def listed(result):
    return list(result) if isinstance(result, (list, tuple)) else [result]


def to_core(value):
    return lax.ppermute(value, "tensor", [(i, i ^ 1) for i in range(lax.axis_size("tensor"))])


def to_chip(value):
    return lax.ppermute(value, "tensor", [(i, i ^ 2) for i in range(lax.axis_size("tensor"))])


def to_peer(value, bit):
    return lax.ppermute(value, "dp", [(i, i ^ (1 << bit)) for i in range(lax.axis_size("dp"))])


def on_device(
    inputs, encoded, dec_len, enc_len, language, objective, distance_bucket, token_weights, cotangent,
    gain_self, self_query, self_key, self_value, self_output, bias_table,
    gain_cross, cross_query, cross_key, cross_value, cross_output, gain_ffn, ffn_up, ffn_down,
):
    seqs, length, width = inputs.shape
    half = length // 2
    columns = self_query.shape[1]
    heads = columns // HEAD_DIM
    units = ffn_up.shape[1]
    span_part = encoded.shape[1]
    span = span_part * lax.axis_size("tensor")
    dp = lax.axis_size("dp")
    size = width // dp
    bits = dp.bit_length() - 1
    halving = bits == 3 and dp == 8 and size % 16 == 0
    along_x, along_z = ((0, 1, 2), (1, 0, 2)) if halving else (None, None)
    latest = []

    def go(kernel, name, outs, ins, last=False, **how):
        after = [item for item in latest if not any(item is one for one in ins)]
        result = run(kernel, name, outs, ins, after=after, **how)
        if not last:
            results = result if isinstance(result, (list, tuple)) else [result]
            latest[:] = [min(results, key=lambda item: item.size * item.dtype.itemsize)]
        return result

    def plus(left, right, name):
        return go(add_kernel, name, [(left.shape, left.dtype)], [left, right])

    def payload(order, wide):
        if order is None:
            return [((width, wide), BF16)]
        return [((dp // 2, size, wide), BF16)] * 2

    x = inputs.reshape(length, width)
    cot = cotangent.reshape(length, width)
    gain_one, gain_two, gain_three = gain_self, gain_cross, gain_ffn
    self_query, self_key, self_value = self_query.T, self_key.T, self_value.T
    cross_query, cross_key, cross_value = cross_query.T, cross_key.T, cross_value.T
    table = bias_table.T
    bucket = distance_bucket.reshape(1, length)
    e0 = encoded.reshape(span_part, width)

    first = go(first_kernel, "first", [((8, 128), F32)], [], us=LONG)
    key_source, value_source, _ = lax.optimization_barrier((cross_key, cross_value, first))
    e1 = to_chip(e0)
    e2 = to_core(e0)
    wk_peer = to_core(key_source)
    wv_peer = to_core(value_source)
    keep, send, more, normed_one, query_one, context_one, probs_one, dec_rows = go(
        self_forward_kernel, "self_forward",
        [((half, width), BF16)] + [((half // 2, width), BF16)] * 2 + [((length, width), BF16)]
        + [((length, columns), BF16)] * 2 + [((length, heads * length), BF16), ((8, 128), jnp.int32)],
        [dec_len, bucket, table, x, gain_one, self_query, self_key, self_value, self_output],
        scratch=[((length, width), BF16)], scalars=1, us=3.5,
    )
    first_half, second_half = to_core(send), to_core(more)
    early = go(
        source_first_kernel, "source_first", [((span_part, columns), BF16), ((columns, span_part), BF16)] * 2,
        [e0, cross_key, cross_value, wk_peer, wv_peer],
    )
    chip_one = go(self_sum_kernel, "self_sum", [((half + EXTRA, width), BF16)], [keep, first_half, second_half])
    other_one = to_chip(chip_one)
    wq_peer = to_core(cross_query)
    wo_peer = to_core(cross_output)
    e3 = to_core(e1)
    late = go(
        source_second_kernel, "source_second", [((span, columns), BF16), ((columns, span), BF16)] * 2,
        [e2, e1, e3, cross_key, cross_value, wk_peer, wv_peer, *early],
    )
    enc_len, objective, language, _ = lax.optimization_barrier((enc_len, objective, language, late[0]))
    info, mask = go(
        step_kernel, "step", [((8, 128), jnp.int32), ((span, half), F32)], [enc_len, objective, language], scalars=3
    )
    up_source, down_source, _ = lax.optimization_barrier((ffn_up, ffn_down, late[0]))
    down_peer = to_core(down_source)
    up_peer = to_core(up_source)

    partial_two, hidden_one, normed_two, q_own, q_peer, context_own, probs_own, probs_peer, pack_forward = go(
        cross_forward_kernel, "cross_forward",
        [((half, width), BF16), ((half, width), F32), ((half, width), BF16)] + [((half, columns), BF16)] * 3
        + [((span, heads * half), BF16)] * 2 + [((half, width + columns), BF16)],
        [mask, chip_one, other_one, x, gain_two, cross_query, wq_peer, cross_output, wo_peer, *late],
    )
    other_two = to_chip(partial_two)
    pack_forward_peer = to_core(pack_forward)
    grad_full, branch_three, branch_three_peer = go(
        out_grad_kernel, "out_grad", [((half, width), F32)] + [((half, width), BF16)] * 2,
        [info, dec_rows, token_weights, cot], us=LONG,
    )
    act_grad, act_grad_peer = go(
        act_grad_kernel, "act_grad", [((half, units), F32)] * 2, [branch_three, ffn_down, down_peer]
    )
    key_one, value_one, k_own, v_own, k_peer, v_peer = go(
        source_back_kernel, "source_back",
        [((columns, length), BF16), ((length, columns), BF16)] + [((columns, span), BF16), ((span, columns), BF16)] * 2,
        [normed_one, self_key, self_value, e0, e1, e2, e3, cross_key, cross_value, wk_peer, wv_peer],
    )

    latest.append(pack_forward_peer)
    hidden_two, normed_three, part_three, pack_ffn = go(
        ffn_peer_kernel, "ffn_peer",
        [((half, width), F32), ((half, width), BF16), ((half, width), F32), ((half, width + 2 * units), BF16)],
        [partial_two, other_two, hidden_one, gain_three, up_peer, act_grad_peer],
    )
    pack_ffn_peer = to_core(pack_ffn)
    partial_three, act_own, grad_pre_own = go(
        ffn_own_kernel, "ffn_own", [((half, width), BF16)] + [((half, units), BF16)] * 2,
        [normed_three, ffn_up, act_grad, part_three],
    )
    other_three = to_chip(partial_three)

    def ffn_weights(*refs):
        ffn_weights_kernel((along_x, along_z), size, *refs)

    ffn_payloads = go(
        ffn_weights, "ffn_weights", payload(along_x, width) + payload(along_z, width),
        [normed_three, pack_ffn_peer, act_own, grad_pre_own, branch_three, branch_three_peer],
        scratch=[((width, units), BF16), ((length, width), BF16), ((length, units), BF16)], us=FILL,
    )

    (partial_four, grad_two, gain_grad_three, gl_own, gl_peer, gc_own, gc_peer, gq_own, branch_two,
     pack_backward) = go(
        cross_backward_kernel, "cross_backward",
        [((half, width), BF16), ((half, width), F32), ((8, width), F32)] + [((span, heads * half), BF16)] * 2
        + [((half, columns), BF16)] * 3 + [((half, width), BF16), ((half, width + columns), BF16)],
        [partial_three, other_three, hidden_two, gain_three, grad_full, cross_output, wo_peer,
         k_own, v_own, k_peer, v_peer, probs_own, probs_peer, cross_query, wq_peer],
    )
    other_four = to_chip(partial_four)
    pack_backward_peer = to_core(pack_backward)
    source_grad = go(
        source_grad_kernel, "source_grad", [((2 * span, columns), BF16)], [gl_peer, probs_peer, gc_peer, q_peer]
    )
    source_grad_peer = to_core(source_grad)
    wide = 2 * columns
    ca_wide, cb_wide = (CROSS_X, 2 * wide - CROSS_X) if halving else (wide, wide)

    def cross_weights(*refs):
        cross_weights_kernel((along_x, along_z), size, *refs)

    *cross_payload, source_total = go(
        cross_weights, "cross_weights",
        payload(along_x, ca_wide) + payload(along_z, cb_wide) + [((span, wide), BF16)],
        [gl_own, probs_own, gc_own, q_own, source_grad_peer, e0, e1, e2, e3, normed_two, pack_forward_peer,
         branch_two, pack_backward_peer, context_own, gq_own],
        scratch=[((width, 2 * wide), BF16), ((span, width), BF16), ((4 * half, wide), BF16)],
    )
    ca_payload, cb_payload = cross_payload[: len(cross_payload) // 2], cross_payload[len(cross_payload) // 2 :]
    branch_out = go(ffn_out_kernel, "ffn_out", [((half, width), BF16)], [act_own, pack_ffn, ffn_down, down_peer])

    grad_one, pack_self = go(
        self_norm_kernel, "self_norm", [((half, width), F32), ((half + EXTRA, width), BF16)],
        [partial_four, other_four, hidden_one, gain_two, grad_two, gain_grad_three],
    )
    pack_self_peer = to_core(pack_self)

    if halving:
        up_keep, up_send, down_keep, down_send = ffn_payloads
        half_sent = ((2, size, width), BF16)
        up_send, up_keep, down_send, down_keep = go(
            ffn_second_kernel, "ffn_second", [half_sent] * 4,
            [up_keep, to_peer(up_send, 0), down_keep, to_peer(down_send, 1)], us=1.0,
        )
        up_got = to_peer(up_send, 1)
        down_got = to_peer(down_send, 0)

    keep, send, branch_one, gq_one, gk_one, gv_one, gl_one = go(
        self_backward_kernel, "self_backward",
        [((half + EXTRA, width), BF16)] * 2 + [((length, width), BF16)] + [((length, columns), BF16)] * 3
        + [((length, heads * length), BF16)],
        [pack_self, pack_self_peer, self_output, self_query, self_key, self_value, query_one, key_one, value_one,
         probs_one, x],
        scratch=[((length, width), BF16)],
    )
    got = to_core(send)
    large, small = (SELF_X, 2 * wide - SELF_X) if halving else (wide, wide)
    table_row, extra_count = extra_rows(width, small, heads)

    def self_weights(*refs):
        self_weights_kernel((along_x, along_z), size, table.shape[1], *refs)

    *self_payload, extra = listed(go(
        self_weights, "self_weights",
        payload(along_x, large) + payload(along_z, small) + [((extra_count, small), BF16)],
        [normed_one, branch_one, gq_one, gk_one, gv_one, context_one, gl_one, bucket, pack_self, pack_self_peer],
        scratch=[((width, 2 * wide), BF16), ((2 * length, wide), BF16), ((2 * length, width), BF16)],
    ))
    sa_payload, sb_payload = self_payload[: len(self_payload) // 2], self_payload[len(self_payload) // 2 :]

    if halving:
        ca_keep, ca_send = ca_payload
        cb_keep, cb_send = cb_payload
        sa_keep, sa_send = sa_payload
        sb_keep, sb_send = sb_payload
        more = size + extra_count
        x_rows = (2 * size * cb_wide + 4 * size * large) // PIECE
        zo_rows = (2 * size * ca_wide + (4 * size + extra_count) * small) // PIECE
        x_send, zo_send, ca_keep, cb_keep = go(
            round_three_kernel, "round_three",
            [((x_rows, PIECE), BF16), ((zo_rows, PIECE), BF16), ((2, size, ca_wide), BF16), ((2, size, cb_wide), BF16)],
            [ca_keep, to_peer(ca_send, 0), cb_keep, to_peer(cb_send, 1), sa_send, sb_send, extra], us=1.6,
        )
        x_got = to_peer(x_send, 0)
        zo_got = to_peer(zo_send, 1)

    chip_five = go(input_sum_kernel, "input_sum", [(keep.shape, BF16)], [keep, got])
    other_five = to_chip(chip_five)

    if halving:
        ffn_send, ffn_keep = go(
            ffn_third_kernel, "ffn_third", [((2 * size, width), BF16)] * 2, [up_keep, up_got, down_keep, down_got]
        )
        ffn_got = to_peer(ffn_send, 2)
        gains = go(gain_kernel, "gain", [((extra_count, small), BF16)], [chip_five, other_five], us=LONG)
        gains_got = to_peer(gains, 0)
        branch_source, _ = lax.optimization_barrier((branch_out, gains))
    else:
        branch_source = branch_out
    out_other = to_chip(branch_source)

    if halving:
        rows = 2 * size + extra_count
        cross_send, cross_keep, sa_send, sa_keep, sb_send, sb_keep = go(
            round_four_kernel, "round_four",
            [((size * 2 * wide // PIECE, PIECE), BF16)] * 2 + [((rows, large), BF16)] * 2 + [((rows, small), BF16)] * 2,
            [x_got, zo_got, ca_keep, cb_keep, sa_keep, sb_keep, extra, gains, gains_got],
        )
        sa_got = to_peer(sa_send, 1)
        sb_got = to_peer(sb_send, 0)

    encoded_keep, encoded_send = go(
        encoded_kernel, "encoded", [((span // 2, width), BF16)] * 2, [source_total, cross_key, cross_value]
    )
    encoded_got = to_core(encoded_send)
    pack_rows = go(
        input_grad_kernel, "input_grad", [((2 * half, width), BF16)],
        [chip_five, other_five, x, gain_one, grad_one, hidden_two, branch_out, out_other],
    )
    pack_rows_peer = to_core(pack_rows)
    if halving:
        up, down = go(ffn_final_kernel, "ffn_final", [((size, width), F32)] * 2, [ffn_keep, ffn_got], us=LONG, last=True)
        cross_send, _ = lax.optimization_barrier((cross_send, encoded_send))
        cross_got = to_peer(cross_send, 2)
    encoded_part, encoded_pass = go(
        encoded_sum_kernel, "encoded_sum", [((span_part, width), BF16)] * 2, [encoded_keep, encoded_got]
    )
    encoded_other = to_chip(encoded_pass)

    if halving:
        rows = (size * large + more * small) // PIECE

        def round_five(*refs):
            round_five_kernel(size, *refs)

        self_send, self_keep = go(
            round_five, "round_five", [((rows, PIECE), BF16)] * 2, [sa_keep, sa_got, sb_keep, sb_got]
        )
        self_got = to_peer(self_send, 2)
        square = ((size, columns), F32)
        turned = ((columns, size), F32)
        grad_cross_key, grad_cross_value, grad_cross_query, grad_cross_output = go(
            cross_final_kernel, "cross_final", [square] * 3 + [turned], [cross_keep, cross_got], us=LONG, last=True
        )

    input_grad, layer_out, _ = go(
        rows_kernel, "rows", [((length, width), BF16)] * 2 + [((16, 128), BF16)], [pack_rows, pack_rows_peer]
    )

    if halving:

        def self_final(*refs):
            self_final_kernel(large, *refs)

        (encoded_grad, grad_self_query, grad_self_key, grad_self_value, grad_self_output, grad_table, grad_gain_two,
         grad_gain_three, grad_gain_one) = go(
            self_final, "self_final",
            [((span_part, width), BF16)] + [square] * 3 + [turned, (table.shape, F32)] + [((1, size), F32)] * 3,
            [self_keep, self_got, encoded_part, encoded_other], last=True,
        )
        grad_gain_one, grad_gain_two, grad_gain_three = (
            item.reshape(size) for item in (grad_gain_one, grad_gain_two, grad_gain_three)
        )
    else:
        index = lax.axis_index("dp")

        def gain_part(*rows):
            row = lax.psum(jnp.concatenate(rows, 0).astype(F32), "dp")
            return lax.dynamic_slice(row, (index * size,), (size,))

        def scattered(item):
            return lax.psum_scatter(item.astype(F32), "dp", scatter_dimension=0, tiled=True)

        def pair_of(item):
            item = scattered(item)
            return item[:, :columns], item[:, columns:]

        up, down = (scattered(item) for item in ffn_payloads)
        grad_cross_key, grad_cross_value = pair_of(ca_payload[0])
        grad_cross_query, grad_cross_output = pair_of(cb_payload[0])
        grad_self_query, grad_self_key = pair_of(sa_payload[0])
        grad_self_value, grad_self_output = pair_of(sb_payload[0])
        grad_cross_output, grad_self_output = grad_cross_output.T, grad_self_output.T
        grad_table = lax.psum(extra[table_row : table_row + heads, : table.shape[1]].astype(F32), "dp")
        encoded_grad = plus(encoded_part, encoded_other, "encoded_grad")
        gain_rows = [item[half : half + 2] for item in (chip_five, other_five)]
        grad_gain_one = gain_part(jnp.sum(jnp.concatenate(gain_rows, 0).astype(F32), 0))
        grad_gain_two = gain_part(extra[0], extra[1])
        grad_gain_three = gain_part(extra[2], extra[3])

    return (
        layer_out.reshape(seqs, length, width),
        input_grad.reshape(seqs, length, width),
        encoded_grad.reshape(seqs, span_part, width),
        grad_gain_one,
        grad_self_query,
        grad_self_key,
        grad_self_value,
        grad_self_output,
        grad_table.T,
        grad_gain_two,
        grad_cross_query,
        grad_cross_key,
        grad_cross_value,
        grad_cross_output,
        grad_gain_three,
        up,
        down.T,
    )


def solution(mesh):
    return jax.shard_map(
        on_device,
        mesh=mesh,
        in_specs=(
            P("dp", None, None),
            P("dp", "tensor", None),
            P("dp"),
            P("dp"),
            P("dp"),
            P("dp"),
            P(),
            P(),
            P("dp", None, None),
            P(),
            P(None, "tensor"),
            P(None, "tensor"),
            P(None, "tensor"),
            P("tensor", None),
            P(None, "tensor"),
            P(),
            P(None, "tensor"),
            P(None, "tensor"),
            P(None, "tensor"),
            P("tensor", None),
            P(),
            P(None, "tensor"),
            P("tensor", None),
        ),
        out_specs=(
            P("dp", None, None),
            P("dp", None, None),
            P("dp", "tensor", None),
            P("dp"),
            P("dp", "tensor"),
            P("dp", "tensor"),
            P("dp", "tensor"),
            P("tensor", "dp"),
            P(None, "tensor"),
            P("dp"),
            P("dp", "tensor"),
            P("dp", "tensor"),
            P("dp", "tensor"),
            P("tensor", "dp"),
            P("dp"),
            P("dp", "tensor"),
            P("tensor", "dp"),
        ),
        check_vma=False,
    )
```

```python
import jax
import jax.numpy as jnp
from jax import lax
from jax.experimental import pallas as pl
from jax.experimental.pallas import tpu as pltpu
from jax.sharding import PartitionSpec as P

HEAD_DIM = 64
LANGS = 8
EPSILON = 1e-06
SCALE = 0.125
NEGATIVE = -1e30
F32 = jnp.float32
BF16 = jnp.bfloat16
VMEM_LIMIT = 20 * 1024 * 1024
EXTRA = 16
PIECE = 128
CROSS_X = 384
SELF_X = 512
FILL = 5.0
LONG = 20.0


def dot(left, right):
    return jnp.dot(left, right, preferred_element_type=F32)


def dot_nt(left, right):
    return lax.dot_general(left, right, (((1,), (1,)), ((), ())), preferred_element_type=F32)


def dot_tn(left, right):
    return lax.dot_general(left, right, (((0,), (0,)), ((), ())), preferred_element_type=F32)


def row_of(vector_ref):
    return vector_ref[...].reshape(1, vector_ref.shape[0])


def inverse_rms(resid):
    return lax.rsqrt(jnp.mean(resid * resid, -1, keepdims=True) + EPSILON)


def norm_back(resid, gain, incoming):
    scale = inverse_rms(resid)
    weighted = incoming * gain
    inner = jnp.mean(weighted * resid, -1, keepdims=True)
    grad = scale * weighted - resid * (scale * scale * scale * inner)
    gain_grad = jnp.sum(incoming * resid * scale, 0, keepdims=True)
    return grad, gain_grad


def groups_of(width):
    return [(start, min(2 * HEAD_DIM, width - start)) for start in range(0, width, 2 * HEAD_DIM)]


def head_mask(count, which, value):
    lane = lax.broadcasted_iota(jnp.int32, (1, count), 1)
    return jnp.where(lane // HEAD_DIM == which, value, 0.0).astype(BF16)


def stacked_heads(rows, value):
    width = rows.shape[1]
    if width == HEAD_DIM:
        return rows * jnp.asarray(value, BF16)
    return jnp.concatenate([rows * head_mask(width, inside, value) for inside in range(width // HEAD_DIM)], 0)


def own_blocks(product, count):
    rows = product.shape[1] // count
    return [
        product[inside * HEAD_DIM : (inside + 1) * HEAD_DIM, inside * rows : (inside + 1) * rows]
        for inside in range(count)
    ]


def heads_forward(queries, keys, values_turned, finish, probs_ref):
    rows = queries.shape[0]
    parts = []
    for start, width in groups_of(queries.shape[1]):
        head, count = start // HEAD_DIM, width // HEAD_DIM
        stacked = stacked_heads(queries[:, start : start + width], SCALE)
        logits = finish(head, count, dot_nt(keys[:, start : start + width], stacked))
        expo = jnp.exp(logits - jnp.max(logits, 0, keepdims=True))
        probs = (expo * (1.0 / jnp.sum(expo, 0, keepdims=True))).astype(BF16)
        probs_ref[:, head * rows : (head + count) * rows] = probs
        parts += own_blocks(dot(values_turned[start : start + width], probs), count)
    return jnp.concatenate(parts, 0).astype(BF16)


def heads_backward(grad_context, keys_turned, values, probs_ref, grad_logits_ref):
    rows = grad_context.shape[0]
    parts = []
    for start, width in groups_of(grad_context.shape[1]):
        head, count = start // HEAD_DIM, width // HEAD_DIM
        place = slice(head * rows, (head + count) * rows)
        stacked = stacked_heads(grad_context[:, start : start + width], 1.0)
        grad_probs = dot_nt(values[:, start : start + width], stacked)
        probs = probs_ref[:, place].astype(F32)
        weighted = jnp.sum(grad_probs * probs, 0, keepdims=True)
        grad_logits = (probs * (grad_probs - weighted)).astype(BF16)
        grad_logits_ref[:, place] = grad_logits
        parts += own_blocks(SCALE * dot(keys_turned[start : start + width], grad_logits), count)
    return jnp.concatenate(parts, 0).astype(BF16)


def heads_spread(matrix_ref, rows, factor):
    length = rows.shape[0]
    parts = []
    for start, width in groups_of(rows.shape[1]):
        head, count = start // HEAD_DIM, width // HEAD_DIM
        stacked = stacked_heads(rows[:, start : start + width], 1.0)
        parts.append(factor * dot(matrix_ref[:, head * length : (head + count) * length], stacked))
    return jnp.concatenate(parts, 1).astype(BF16)


def own_rows(core, half):
    return pl.ds(pl.multiple_of(core * half, half), half)


def bucket_onehot(bucket_ref, buckets):
    wanted = lax.broadcasted_iota(jnp.int32, (buckets, bucket_ref.shape[1]), 0)
    return jnp.where(bucket_ref[...] == wanted, 1.0, 0.0)


def add_kernel(left_ref, right_ref, out_ref):
    out_ref[...] = (left_ref[...].astype(F32) + right_ref[...].astype(F32)).astype(out_ref.dtype)


def first_kernel(out):
    out[...] = jnp.zeros_like(out)


def step_kernel(enc_len, objective, language, info, mask):
    info[...] = jnp.full(info.shape, objective[0] * LANGS + language[0], jnp.int32)
    rows = mask.shape[0] // 4
    row = lax.broadcasted_iota(jnp.int32, mask.shape, 0)
    block = row // rows
    flip = jnp.where(block % 2 == 1, 1, 0) + jnp.where(block >= 2, 2, 0)
    position = (lax.axis_index("tensor") ^ flip) * rows + row % rows
    mask[...] = jnp.where(position < enc_len[0], 0.0, NEGATIVE)


def self_sum_kernel(own, first, second, out):
    rows = first.shape[0]
    out[:rows] = both(own[:rows], first[...]).astype(BF16)
    out[rows : 2 * rows] = both(own[rows:], second[...]).astype(BF16)
    out[2 * rows :] = jnp.zeros((out.shape[0] - 2 * rows, out.shape[1]), BF16)


def self_forward_kernel(
    dec_len, bucket, table, x, gain, w_query, w_key, w_value, w_output,
    keep, send, more, normed_out, query_out, context_out, probs_out, dec_out, whole,
):
    dec_out[...] = jnp.full(dec_out.shape, dec_len[0], jnp.int32)
    length = x.shape[0]
    resid = x[...].astype(F32)
    normed = (resid * inverse_rms(resid) * row_of(gain)).astype(BF16)
    normed_out[...] = normed
    queries = dot_nt(normed, w_query[...]).astype(BF16)
    keys = dot_nt(normed, w_key[...]).astype(BF16)
    values = dot_nt(w_value[...], normed).astype(BF16)
    query_out[...] = queries
    by_distance = lax.dot_general(
        table[...],
        bucket_onehot(bucket, table.shape[1]),
        (((1,), (0,)), ((), ())),
        precision=lax.Precision.HIGHEST,
        preferred_element_type=F32,
    )
    row = lax.broadcasted_iota(jnp.int32, (length, length), 0)
    column = lax.broadcasted_iota(jnp.int32, (length, length), 1)
    allowed = (row <= column) & (row < dec_len[0])

    def finish(head, count, scores):
        parts = []
        for inside in range(count):
            spread = jnp.broadcast_to(by_distance[head + inside : head + inside + 1], (length, length))
            bias = pltpu.roll(spread, 0, 1, stride=1, stride_axis=0)
            part = scores[:, inside * length : (inside + 1) * length]
            parts.append(jnp.where(allowed, part + bias, NEGATIVE))
        return jnp.concatenate(parts, 1) if count > 1 else parts[0]

    context = heads_forward(queries, keys, values, finish, probs_out)
    context_out[...] = context.T
    whole[...] = dot_tn(context, w_output[...]).astype(BF16)
    half = keep.shape[0]
    core = lax.axis_index("tensor") % 2
    keep[...] = whole[own_rows(core, half), :]
    rows = send.shape[0]
    send[...] = whole[own_rows(2 - 2 * core, rows), :]
    more[...] = whole[own_rows(3 - 2 * core, rows), :]


def source_rows(parts, start, wk_own, wv_own, wk_peer, wv_peer, k_own, v_own, k_peer, v_peer):
    rows = parts[0].shape[0]
    for index, part in enumerate(parts):
        place = slice(start + index * rows, start + (index + 1) * rows)
        for weight, out in ((wk_own, k_own), (wk_peer, k_peer)):
            out[place, :] = dot_nt(part[...], weight[...]).astype(BF16)
        for weight, out in ((wv_own, v_own), (wv_peer, v_peer)):
            out[:, place] = dot_nt(weight[...], part[...]).astype(BF16)


def source_first_kernel(first, *refs):
    source_rows([first], 0, *refs)


def source_second_kernel(
    first, second, third, wk_own, wv_own, wk_peer, wv_peer, early_k_own, early_v_own, early_k_peer, early_v_peer,
    k_own, v_own, k_peer, v_peer,
):
    rows = first.shape[0]
    for early, out in ((early_k_own, k_own), (early_k_peer, k_peer)):
        out[:rows] = early[...]
    for early, out in ((early_v_own, v_own), (early_v_peer, v_peer)):
        out[:, :rows] = early[...]
    source_rows([first, second, third], rows, wk_own, wv_own, wk_peer, wv_peer, k_own, v_own, k_peer, v_peer)


def source_back_kernel(
    normed, w_key, w_value, e0, e1, e2, e3, wk_own, wv_own, wk_peer, wv_peer,
    keys_turned, values, k_own, v_own, k_peer, v_peer,
):
    keys_turned[...] = dot_nt(w_key[...], normed[...]).astype(BF16)
    values[...] = dot_nt(normed[...], w_value[...]).astype(BF16)
    rows = e0.shape[0]
    for index, part in enumerate((e0, e2, e1, e3)):
        place = slice(index * rows, (index + 1) * rows)
        for weight, out in ((wk_own, k_own), (wk_peer, k_peer)):
            out[:, place] = dot_nt(weight[...], part[...]).astype(BF16)
        for weight, out in ((wv_own, v_own), (wv_peer, v_peer)):
            out[place, :] = dot_nt(part[...], weight[...]).astype(BF16)


def out_grad_kernel(info, dec_len, token_weights, cotangent, grad_own, branch_own, branch_peer):
    half = grad_own.shape[0]
    length = cotangent.shape[0]
    core = lax.axis_index("tensor") % 2
    row = lax.broadcasted_iota(jnp.int32, token_weights.shape, 0)
    weights = jnp.sum(jnp.where(row == info[:1, :1], token_weights[...], 0.0), 0, keepdims=True)
    position = lax.broadcasted_iota(jnp.int32, (1, length), 1)
    weights = jnp.where(position < dec_len[:1, :1], weights, 0.0)

    def rows_of(side):
        row = lax.broadcasted_iota(jnp.int32, (half, length), 0) + side * half
        column = lax.broadcasted_iota(jnp.int32, (half, length), 1)
        factor = jnp.sum(jnp.where(row == column, weights, 0.0), -1, keepdims=True)
        return cotangent[own_rows(side, half), :].astype(F32) * factor

    own = rows_of(core)
    grad_own[...] = own
    branch_own[...] = own.astype(BF16)
    branch_peer[...] = rows_of(1 - core).astype(BF16)


def act_grad_kernel(branch, down_own, down_peer, own, peer):
    own[...] = dot_nt(branch[...], down_own[...])
    peer[...] = dot_nt(branch[...], down_peer[...])


def cross_forward_kernel(
    mask, chip_own, chip_other, x, gain, wq_own, wq_peer, wo_own, wo_peer, k_own, v_own, k_peer, v_peer,
    partial_out, hidden_out, normed_out, q_own, q_peer, context_own, probs_own, probs_peer, pack,
):
    half, width = hidden_out.shape
    core = lax.axis_index("tensor") % 2
    resid = x[own_rows(core, half), :].astype(F32)
    resid = resid + both(chip_own[:half], chip_other[:half])
    hidden_out[...] = resid
    normed = (resid * inverse_rms(resid) * row_of(gain)).astype(BF16)
    normed_out[...] = normed
    pack[:, :width] = normed

    def finish(head, count, scores):
        return scores + jnp.concatenate([mask[...]] * count, 1)

    queries = dot_nt(normed, wq_own[...]).astype(BF16)
    q_own[...] = queries
    first = heads_forward(queries, k_own[...], v_own[...], finish, probs_own)
    context_own[...] = first.T
    queries = dot_nt(normed, wq_peer[...]).astype(BF16)
    q_peer[...] = queries
    second = heads_forward(queries, k_peer[...], v_peer[...], finish, probs_peer)
    pack[:, width:] = second.T
    partial_out[...] = (dot_tn(first, wo_own[...]) + dot_tn(second, wo_peer[...])).astype(BF16)


def through_units(normed, up, act_grad):
    pre = dot(normed, up[...])
    square = pre * pre
    tanh = jnp.tanh(0.7978845608028654 * (pre + 0.044715 * square * pre))
    half_sum = 0.5 * (1.0 + tanh)
    slope = half_sum + 0.5 * pre * (1.0 - tanh * tanh) * (
        0.7978845608028654 * (1.0 + 3.0 * 0.044715 * square)
    )
    return (pre * half_sum).astype(BF16), (act_grad[...] * slope).astype(BF16)


def ffn_peer_kernel(chip_own, chip_other, hidden, gain, up_peer, act_grad_peer, hidden_out, normed_out, part_out, pack):
    width = hidden.shape[1]
    resid = hidden[...] + both(chip_own[...], chip_other[...])
    hidden_out[...] = resid
    normed = (resid * inverse_rms(resid) * row_of(gain)).astype(BF16)
    normed_out[...] = normed
    pack[:, :width] = normed
    act, grad_pre = through_units(normed, up_peer, act_grad_peer)
    units = act.shape[1]
    pack[:, width : width + units] = act
    pack[:, width + units :] = grad_pre
    part_out[...] = dot_nt(grad_pre, up_peer[...])


def ffn_own_kernel(normed, up_own, act_grad_own, part, partial_out, act_own, grad_pre_own):
    act, grad_pre = through_units(normed[...], up_own, act_grad_own)
    act_own[...] = act
    grad_pre_own[...] = grad_pre
    partial_out[...] = (part[...] + dot_nt(grad_pre, up_own[...])).astype(BF16)


def ffn_out_kernel(act_own, pack, down_own, down_peer, out):
    units = act_own.shape[1]
    width = out.shape[1]
    total = dot(act_own[...], down_own[...]) + dot(pack[:, width : width + units], down_peer[...])
    out[...] = total.astype(BF16)


def write_blocks(whole, columns, first_bit, rest_bits, size, targets):
    index = lax.axis_index("dp")
    count = 1 << len(rest_bits)
    for first, target in enumerate(targets):
        for entry in range(count):
            relative = first << first_bit
            for place, bit in enumerate(rest_bits):
                if entry >> (len(rest_bits) - 1 - place) & 1:
                    relative |= 1 << bit
            block = index ^ relative
            target[entry] = whole[pl.ds(pl.multiple_of(block * size, size), size), columns]


def emit(whole, outs, order, size, columns=slice(None)):
    if order is None:
        outs[0][...] = whole[:, columns]
    else:
        write_blocks(whole, columns, order[0], order[1:], size, outs)


def ffn_weights_kernel(orders, size, normed, pack, act_own, grad_pre_own, branch_own, branch_peer, *refs):
    *outs, whole, left, right = refs
    half, width = normed.shape
    units = act_own.shape[1]
    left[:half] = normed[...]
    left[half:] = pack[:, :width]
    right[:half] = grad_pre_own[...]
    right[half:] = pack[:, width + units :]
    whole[...] = dot_tn(left[...], right[...]).astype(BF16)
    count = 1 if orders[0] is None else 2
    emit(whole, outs[:count], orders[0], size)
    left[:half] = branch_own[...]
    left[half:] = branch_peer[...]
    right[:half] = act_own[...]
    right[half:] = pack[:, width : width + units]
    whole[...] = dot_tn(left[...], right[...]).astype(BF16)
    emit(whole, outs[count:], orders[1], size)


def cross_backward_kernel(
    chip_own, chip_other, hidden, gain, grad_out, wo_own, wo_peer, k_own, v_own, k_peer, v_peer,
    probs_own, probs_peer, wq_own, wq_peer,
    partial_out, grad_hidden, gain_grad, gl_own, gl_peer, gc_own, gc_peer, gq_own, branch, pack,
):
    incoming = chip_own[...].astype(F32) + chip_other[...].astype(F32)
    added, gain_terms = norm_back(hidden[...], row_of(gain), incoming)
    gain_grad[...] = jnp.broadcast_to(gain_terms, gain_grad.shape)
    grad = grad_out[...] + added
    grad_hidden[...] = grad
    rounded = grad.astype(BF16)
    branch[...] = rounded
    width = rounded.shape[1]
    pack[:, :width] = rounded
    context = dot_nt(rounded, wo_own[...]).astype(BF16)
    gc_own[...] = context
    queries = heads_backward(context, k_own[...], v_own[...], probs_own, gl_own)
    gq_own[...] = queries.T
    total = dot_tn(queries, wq_own[...])
    context = dot_nt(rounded, wo_peer[...]).astype(BF16)
    gc_peer[...] = context
    queries = heads_backward(context, k_peer[...], v_peer[...], probs_peer, gl_peer)
    pack[:, width:] = queries.T
    total = total + dot_tn(queries, wq_peer[...])
    partial_out[...] = total.astype(BF16)


def source_grad_kernel(gl_peer, probs_peer, gc_peer, q_peer, out):
    span = out.shape[0] // 2
    rows = span // 4
    for start, grads in (
        (0, heads_spread(gl_peer, q_peer[...], SCALE)),
        (span, heads_spread(probs_peer, gc_peer[...], 1.0)),
    ):
        for block in range(4):
            there = start + (block ^ 1) * rows
            out[there : there + rows] = grads[block * rows : (block + 1) * rows]


def cross_weights_kernel(
    orders, size, gl_own, probs_own, gc_own, q_own, other, e0, e1, e2, e3, normed, pack_forward,
    branch, pack_backward, context_own, gq_own, *refs,
):
    *outs, source, whole, left, right = refs
    count = len(outs) // 2
    span = other.shape[0] // 2
    half, width = normed.shape
    columns = q_own.shape[1]
    source[:, :columns] = low_sum(heads_spread(gl_own, q_own[...], SCALE), other[:span])
    source[:, columns:] = low_sum(heads_spread(probs_own, gc_own[...], 1.0), other[span:])
    for index, part in enumerate((e0, e2, e1, e3)):
        left[index * half : (index + 1) * half] = part[...]
    whole[:, : 2 * columns] = dot_tn(left[...], source[...]).astype(BF16)
    left[:half] = normed[...]
    left[half : 2 * half] = pack_forward[:, :width]
    left[2 * half : 3 * half] = branch[...]
    left[3 * half :] = pack_backward[:, :width]
    right[...] = jnp.zeros_like(right)
    right[:half, :columns] = gq_own[...]
    right[half : 2 * half, :columns] = pack_backward[:, width:]
    right[2 * half : 3 * half, columns:] = context_own[...]
    right[3 * half :, columns:] = pack_forward[:, width:]
    whole[:, 2 * columns :] = dot_tn(left[...], right[...]).astype(BF16)
    wide = outs[0].shape[-1]
    emit(whole, outs[:count], orders[0], size, columns=slice(0, wide))
    emit(whole, outs[count:], orders[1], size, columns=slice(wide, None))


def encoded_kernel(source, wk_own, wv_own, keep, send):
    columns = wk_own.shape[0]
    terms = dot(source[:, :columns], wk_own[...]) + dot(source[:, columns:], wv_own[...])
    terms = terms.astype(BF16)
    rows = keep.shape[0] // 2
    for block in range(4):
        target = send if block % 2 else keep
        target[block // 2 * rows : (block // 2 + 1) * rows] = terms[block * rows : (block + 1) * rows]


def self_norm_kernel(chip_own, chip_other, hidden, gain, grad_hidden, gain_ffn, grad_out, pack):
    half = hidden.shape[0]
    incoming = chip_own[...].astype(F32) + chip_other[...].astype(F32)
    added, gain_terms = norm_back(hidden[...], row_of(gain), incoming)
    grad = grad_hidden[...] + added
    grad_out[...] = grad
    pack[:half] = grad.astype(BF16)
    row = lax.broadcasted_iota(jnp.int32, (EXTRA, hidden.shape[1]), 0)
    extra = jnp.where(row == 0, gain_terms, 0.0) + jnp.where(row == 1, gain_ffn[:1], 0.0)
    pack[half:] = extra.astype(BF16)


def high_low(vector):
    high = vector.astype(BF16).astype(F32)
    row = lax.broadcasted_iota(jnp.int32, (EXTRA, vector.shape[1]), 0)
    return (jnp.where(row == 0, high, 0.0) + jnp.where(row == 1, vector - high, 0.0)).astype(BF16)


def of_high_low(rows):
    rows = rows.astype(F32)
    return rows[:1] + rows[1:2]


def self_backward_kernel(
    pack_own, pack_peer, w_output, w_query, w_key, w_value, queries, keys, values, probs, x,
    keep, send, branch_out, gq_out, gk_out, gv_out, gl_out, whole,
):
    half = keep.shape[0] - EXTRA
    core = lax.axis_index("tensor") % 2
    branch_out[own_rows(core, half), :] = pack_own[:half]
    branch_out[own_rows(1 - core, half), :] = pack_peer[:half]
    context = dot_nt(branch_out[...], w_output[...]).astype(BF16)
    grad_queries = heads_backward(context, keys[...], values[...], probs, gl_out)
    grad_keys = heads_spread(gl_out, queries[...], SCALE)
    grad_values = heads_spread(probs, context, 1.0)
    gq_out[...] = grad_queries.T
    gk_out[...] = grad_keys
    gv_out[...] = grad_values
    total = dot_tn(grad_queries, w_query[...]) + dot(grad_keys, w_key[...]) + dot(grad_values, w_value[...])
    whole[...] = total.astype(BF16)
    keep[:half] = whole[own_rows(core, half), :]
    send[:half] = whole[own_rows(1 - core, half), :]
    resid = x[...].astype(F32)
    gain_terms = high_low(jnp.sum(total * resid * inverse_rms(resid), 0, keepdims=True))
    keep[half:] = gain_terms
    send[half:] = gain_terms


def input_sum_kernel(own, peer, out):
    half = out.shape[0] - EXTRA
    out[:half] = both(own[:half], peer[:half]).astype(BF16)
    out[half:] = high_low(of_high_low(own[half:]) + of_high_low(peer[half:]))


def self_weights_kernel(
    orders, size, buckets, normed, branch, gq, gk, gv, context, gl, bucket, pack_own, pack_peer, *refs
):
    *outs, extra_out, whole, right, left = refs
    count = len(outs) // 2
    length, columns = gq.shape
    half = pack_own.shape[0] - EXTRA
    right[:length, :columns] = gq[...]
    right[:length, columns:] = gk[...]
    whole[:, : 2 * columns] = dot_tn(normed[...], right[:length]).astype(BF16)
    left[:length] = normed[...]
    left[length:] = branch[...]
    right[...] = jnp.zeros_like(right)
    right[:length, :columns] = gv[...]
    right[length:, columns:] = context[...]
    whole[:, 2 * columns :] = dot_tn(left[...], right[...]).astype(BF16)
    wide = outs[0].shape[-1]
    emit(whole, outs[:count], orders[0], size, columns=slice(0, wide))
    onehot = bucket_onehot(bucket, buckets)
    row = lax.broadcasted_iota(jnp.int32, (length, length), 0)
    column = lax.broadcasted_iota(jnp.int32, (length, length), 1)
    turn = jnp.where(row + column == length - 1, 1.0, 0.0).astype(BF16)
    place = lax.broadcasted_iota(jnp.int32, (8, length), 0)
    sums = jnp.zeros((8, length), F32)
    heads = gl.shape[1] // length
    for head in range(heads):
        skewed = pltpu.roll(dot(turn, gl[:, head * length : (head + 1) * length]), 1, 1, stride=1, stride_axis=0)
        sums = sums + jnp.where(place == head, jnp.sum(skewed, 0, keepdims=True), 0.0)
    table = lax.dot_general(
        sums, onehot, (((1,), (1,)), ((), ())), precision=lax.Precision.HIGHEST, preferred_element_type=F32
    )
    gains = both(pack_own[half:], pack_peer[half:])
    narrow = outs[-1].shape[-1]
    first, count_rows = extra_rows(gains.shape[1], narrow, heads)
    extra = vector_rows(gains[:1], narrow, count_rows, 0) + vector_rows(gains[1:2], narrow, count_rows, 1)
    table = jnp.concatenate([table, jnp.zeros((8, narrow - buckets), F32)], 1)
    row = lax.broadcasted_iota(jnp.int32, (count_rows, narrow), 0)
    for head in range(heads):
        extra = extra + jnp.where(row == first + head, table[head : head + 1], 0.0)
    extra_out[...] = extra.astype(BF16)
    emit(whole, outs[count:], orders[1], size, columns=slice(wide, None))


def extra_rows(width, wide, heads):
    first = -(-3 * (width // wide) // 4) * 4
    return first, -(-(first + heads) // 16) * 16


def vector_rows(vector, wide, count, which):
    rows = vector.shape[1] // wide
    row = lax.broadcasted_iota(jnp.int32, (count, wide), 0)
    placed = jnp.zeros((count, wide), F32)
    for index in range(rows):
        piece = vector[:, index * wide : (index + 1) * wide]
        placed = placed + jnp.where(row == which * rows + index, piece, 0.0)
    return placed


def encoded_sum_kernel(own, other, keep, send):
    rows = keep.shape[0]
    keep[...] = low_sum(own[:rows], other[:rows])
    send[...] = low_sum(own[rows:], other[rows:])


def input_grad_kernel(chip_own, chip_other, x, gain, grad_hidden, hidden_two, out_own, out_other, pack):
    half = hidden_two.shape[0]
    resid = x[own_rows(lax.axis_index("tensor") % 2, half), :].astype(F32)
    added, _ = norm_back(resid, row_of(gain), both(chip_own[:half], chip_other[:half]))
    pack[:half] = (grad_hidden[...] + added).astype(BF16)
    pack[half:] = (hidden_two[...] + both(out_own[...], out_other[...])).astype(BF16)


def rows_kernel(own, peer, input_grad, layer_out, token):
    half = own.shape[0] // 2
    core = lax.axis_index("tensor") % 2
    for place, out in ((0, input_grad), (half, layer_out)):
        out[own_rows(core, half), :] = own[place : place + half]
        out[own_rows(1 - core, half), :] = peer[place : place + half]
    token[...] = own[: token.shape[0], : token.shape[1]]


def both(left, right):
    return left.astype(F32) + right.astype(F32)


def low_sum(left, right):
    return both(left, right).astype(BF16)


def ffn_second_kernel(up_keep, up_got, down_keep, down_got, up_send, up_next, down_send, down_next):
    for keep, got, send, new in (
        (up_keep, up_got, up_send, up_next),
        (down_keep, down_got, down_send, down_next),
    ):
        for entry in range(2):
            new[entry] = low_sum(keep[entry], got[entry])
            send[entry] = low_sum(keep[2 + entry], got[2 + entry])


def ffn_third_kernel(up_keep, up_got, down_keep, down_got, send, keep):
    size = up_keep.shape[1]
    for entry, target in enumerate((keep, send)):
        target[:size] = low_sum(up_keep[entry], up_got[entry])
        target[size:] = low_sum(down_keep[entry], down_got[entry])


def round_three_kernel(
    ca_keep, ca_got, cb_keep, cb_got, sa_send, sb_send, extra, x_send, zo_send, ca_next, cb_next
):
    for entry in range(2):
        ca_next[entry] = low_sum(ca_keep[entry], ca_got[entry])
        cb_next[entry] = low_sum(cb_keep[entry], cb_got[entry])
    base = spread_out(x_send, [low_sum(cb_keep[2 + entry], cb_got[2 + entry]) for entry in range(2)])
    spread_out(x_send, [sa_send[entry] for entry in range(4)], base)
    base = spread_out(zo_send, [low_sum(ca_keep[2 + entry], ca_got[2 + entry]) for entry in range(2)])
    base = spread_out(zo_send, [sb_send[entry] for entry in range(4)], base)
    spread_out(zo_send, [extra[...]], base)


def gain_kernel(chip_own, chip_other, out):
    half = chip_own.shape[0] - EXTRA
    gain = of_high_low(chip_own[half:]) + of_high_low(chip_other[half:])
    out[...] = vector_rows(gain, out.shape[1], out.shape[0], 2).astype(BF16)


def spread_out(target, parts, start=0):
    for part in parts:
        rows = part.shape[0]
        for side in range(part.shape[1] // PIECE):
            target[start : start + rows] = part[:, side * PIECE : (side + 1) * PIECE]
            start += rows
    return start


def gathered(source, rows, wide, start):
    pieces = [source[start + side * rows : start + (side + 1) * rows] for side in range(wide // PIECE)]
    return jnp.concatenate(pieces, 1) if len(pieces) > 1 else pieces[0]


def round_four_kernel(
    x_got, zo_got, ca_keep, cb_keep, sa_keep, sb_keep, extra, gains, gains_got,
    cross_send, cross_keep, sa_send, sa_next, sb_send, sb_next,
):
    size, ca_wide = ca_keep.shape[1:]
    cb_wide = cb_keep.shape[2]
    large, small = sa_keep.shape[2], sb_keep.shape[2]
    zo_base = 2 * size * ca_wide // PIECE
    x_base = 2 * size * cb_wide // PIECE
    for entry, target in enumerate((cross_keep, cross_send)):
        part = low_sum(ca_keep[entry], gathered(zo_got, size, ca_wide, entry * (zo_base // 2)))
        base = spread_out(target, [part])
        part = low_sum(cb_keep[entry], gathered(x_got, size, cb_wide, entry * (x_base // 2)))
        spread_out(target, [part], base)
    gain = low_sum(gains[...], gains_got[...])
    step = size * (small // PIECE)
    extra = low_sum(extra[...], gathered(zo_got, extra.shape[0], small, zo_base + 4 * step))
    for first, sa_out, sb_out in ((0, sa_next, sb_next), (2, sa_send, sb_send)):
        for entry in range(2):
            part = slice(entry * size, (entry + 1) * size)
            start = x_base + (first + entry) * size * (large // PIECE)
            sa_out[part] = low_sum(sa_keep[first + entry], gathered(x_got, size, large, start))
            start = zo_base + (first + entry) * step
            sb_out[part] = low_sum(sb_keep[first + entry], gathered(zo_got, size, small, start))
        sa_out[2 * size :, :small] = gain
        sb_out[2 * size :] = extra


def round_five_kernel(size, sa_keep, sa_got, sb_keep, sb_got, send, keep):
    large, small = sa_keep.shape[1], sb_keep.shape[1]
    extra = low_sum(
        low_sum(sa_keep[2 * size :, :small], sa_got[2 * size :, :small]), low_sum(sb_keep[2 * size :], sb_got[2 * size :])
    )
    for entry, target in enumerate((keep, send)):
        part = slice(entry * size, (entry + 1) * size)
        base = spread_out(target, [low_sum(sa_keep[part], sa_got[part])])
        part = jnp.concatenate([low_sum(sb_keep[part], sb_got[part]), extra], 0)
        spread_out(target, [part], base)


def ffn_final_kernel(keep, got, up, down):
    size = up.shape[0]
    up[...] = both(keep[:size], got[:size])
    down[...] = both(keep[size:], got[size:])


def cross_final_kernel(keep, got, key, value, query, output):
    size, count = key.shape
    total = both(gathered(keep, size, 4 * count, 0), gathered(got, size, 4 * count, 0))
    for place, out in enumerate((key, value, query)):
        out[...] = total[:, place * count : (place + 1) * count]
    output[...] = total[:, 3 * count :].T


def self_final_kernel(
    large, keep, got, encoded_own, encoded_other,
    encoded_grad, query, key, value, output, table, gain_two, gain_three, gain_one,
):
    encoded_grad[...] = low_sum(encoded_own[...], encoded_other[...])
    size, count = key.shape
    small = 4 * count - large
    start = size * (large // PIECE)
    first = both(gathered(keep, size, large, 0), gathered(got, size, large, 0))
    table_row, more = extra_rows(4 * count, small, table.shape[0])
    more += size
    second = both(gathered(keep, more, small, start), gathered(got, more, small, start))
    total = jnp.concatenate([first, second[:size]], 1)
    for place, out in enumerate((query, key, value)):
        out[...] = total[:, place * count : (place + 1) * count]
    output[...] = total[:, 3 * count :].T
    extra = second[size:]
    table[...] = extra[table_row : table_row + table.shape[0], : table.shape[1]]
    wide = 4 * count
    back = wide - lax.axis_index("dp") * size
    rows = wide // small
    for which, out in enumerate((gain_two, gain_three, gain_one)):
        pieces = [extra[which * rows + index : which * rows + index + 1] for index in range(rows)]
        whole = jnp.concatenate(pieces, 1)
        out[...] = pltpu.roll(jnp.broadcast_to(whole, (8, wide)), back, 1)[:1, :size]


def run(kernel, name, outs, ins, us=0.0, scratch=(), scalars=0, far=0, sems=0, after=(), limit=VMEM_LIMIT):
    shapes = [jax.ShapeDtypeStruct(shape, dtype) for shape, dtype in outs]
    idle = len(after)
    body = kernel
    if idle:

        def body(*refs):
            kernel(*refs[: len(ins)], *refs[len(ins) + idle :])

    vmem = pl.BlockSpec(memory_space=pltpu.VMEM)
    hbm = pl.BlockSpec(memory_space=pltpu.HBM)
    free = pl.BlockSpec(memory_space=pl.ANY)
    smem = pl.BlockSpec(memory_space=pltpu.SMEM)
    place = [smem] * scalars + [hbm] * far + [vmem] * (len(ins) - scalars - far) + [free] * idle
    ins = [
        pltpu.with_memory_space_constraint(item, pltpu.HBM) if spec is hbm else item for item, spec in zip(ins, place)
    ]
    result = pl.pallas_call(
        body,
        out_shape=shapes,
        in_specs=place,
        out_specs=[vmem] * len(shapes),
        scratch_shapes=[pltpu.VMEM(shape, dtype) for shape, dtype in scratch]
        + ([pltpu.SemaphoreType.DMA((sems,))] if sems else []),
        compiler_params=pltpu.CompilerParams(vmem_limit_bytes=limit),
        cost_estimate=pl.CostEstimate(flops=int(us * 1.15e9), bytes_accessed=0, transcendentals=0),
        name=name,
    )(*ins, *after)
    return result[0] if len(shapes) == 1 else result


def listed(result):
    return list(result) if isinstance(result, (list, tuple)) else [result]


def to_core(value):
    return lax.ppermute(value, "tensor", [(i, i ^ 1) for i in range(lax.axis_size("tensor"))])


def to_chip(value):
    return lax.ppermute(value, "tensor", [(i, i ^ 2) for i in range(lax.axis_size("tensor"))])


def to_peer(value, bit):
    return lax.ppermute(value, "dp", [(i, i ^ (1 << bit)) for i in range(lax.axis_size("dp"))])


def on_device(
    inputs, encoded, dec_len, enc_len, language, objective, distance_bucket, token_weights, cotangent,
    gain_self, self_query, self_key, self_value, self_output, bias_table,
    gain_cross, cross_query, cross_key, cross_value, cross_output, gain_ffn, ffn_up, ffn_down,
):
    seqs, length, width = inputs.shape
    half = length // 2
    columns = self_query.shape[1]
    heads = columns // HEAD_DIM
    units = ffn_up.shape[1]
    span_part = encoded.shape[1]
    span = span_part * lax.axis_size("tensor")
    dp = lax.axis_size("dp")
    size = width // dp
    bits = dp.bit_length() - 1
    halving = bits == 3 and dp == 8 and size % 16 == 0
    along_x, along_z = ((0, 1, 2), (1, 0, 2)) if halving else (None, None)
    latest = []

    def go(kernel, name, outs, ins, last=False, **how):
        after = [item for item in latest if not any(item is one for one in ins)]
        result = run(kernel, name, outs, ins, after=after, **how)
        if not last:
            results = result if isinstance(result, (list, tuple)) else [result]
            latest[:] = [min(results, key=lambda item: item.size * item.dtype.itemsize)]
        return result

    def plus(left, right, name):
        return go(add_kernel, name, [(left.shape, left.dtype)], [left, right])

    def payload(order, wide):
        if order is None:
            return [((width, wide), BF16)]
        return [((dp // 2, size, wide), BF16)] * 2

    x = inputs.reshape(length, width)
    cot = cotangent.reshape(length, width)
    gain_one, gain_two, gain_three = gain_self, gain_cross, gain_ffn
    self_query, self_key, self_value = self_query.T, self_key.T, self_value.T
    cross_query, cross_key, cross_value = cross_query.T, cross_key.T, cross_value.T
    table = bias_table.T
    bucket = distance_bucket.reshape(1, length)
    e0 = encoded.reshape(span_part, width)

    first = go(first_kernel, "first", [((8, 128), F32)], [], us=LONG)
    key_source, value_source, _ = lax.optimization_barrier((cross_key, cross_value, first))
    e1 = to_chip(e0)
    e2 = to_core(e0)
    wk_peer = to_core(key_source)
    wv_peer = to_core(value_source)
    keep, send, more, normed_one, query_one, context_one, probs_one, dec_rows = go(
        self_forward_kernel, "self_forward",
        [((half, width), BF16)] + [((half // 2, width), BF16)] * 2 + [((length, width), BF16)]
        + [((length, columns), BF16)] * 2 + [((length, heads * length), BF16), ((8, 128), jnp.int32)],
        [dec_len, bucket, table, x, gain_one, self_query, self_key, self_value, self_output],
        scratch=[((length, width), BF16)], scalars=1, us=3.5,
    )
    first_half, second_half = to_core(send), to_core(more)
    early = go(
        source_first_kernel, "source_first", [((span_part, columns), BF16), ((columns, span_part), BF16)] * 2,
        [e0, cross_key, cross_value, wk_peer, wv_peer],
    )
    chip_one = go(self_sum_kernel, "self_sum", [((half + EXTRA, width), BF16)], [keep, first_half, second_half])
    other_one = to_chip(chip_one)
    wq_peer = to_core(cross_query)
    wo_peer = to_core(cross_output)
    e3 = to_core(e1)
    late = go(
        source_second_kernel, "source_second", [((span, columns), BF16), ((columns, span), BF16)] * 2,
        [e2, e1, e3, cross_key, cross_value, wk_peer, wv_peer, *early],
    )
    enc_len, objective, language, _ = lax.optimization_barrier((enc_len, objective, language, late[0]))
    info, mask = go(
        step_kernel, "step", [((8, 128), jnp.int32), ((span, half), F32)], [enc_len, objective, language], scalars=3
    )
    up_source, down_source, _ = lax.optimization_barrier((ffn_up, ffn_down, late[0]))
    down_peer = to_core(down_source)
    up_peer = to_core(up_source)

    partial_two, hidden_one, normed_two, q_own, q_peer, context_own, probs_own, probs_peer, pack_forward = go(
        cross_forward_kernel, "cross_forward",
        [((half, width), BF16), ((half, width), F32), ((half, width), BF16)] + [((half, columns), BF16)] * 3
        + [((span, heads * half), BF16)] * 2 + [((half, width + columns), BF16)],
        [mask, chip_one, other_one, x, gain_two, cross_query, wq_peer, cross_output, wo_peer, *late],
    )
    other_two = to_chip(partial_two)
    pack_forward_peer = to_core(pack_forward)
    grad_full, branch_three, branch_three_peer = go(
        out_grad_kernel, "out_grad", [((half, width), F32)] + [((half, width), BF16)] * 2,
        [info, dec_rows, token_weights, cot], us=LONG,
    )
    act_grad, act_grad_peer = go(
        act_grad_kernel, "act_grad", [((half, units), F32)] * 2, [branch_three, ffn_down, down_peer]
    )
    key_one, value_one, k_own, v_own, k_peer, v_peer = go(
        source_back_kernel, "source_back",
        [((columns, length), BF16), ((length, columns), BF16)] + [((columns, span), BF16), ((span, columns), BF16)] * 2,
        [normed_one, self_key, self_value, e0, e1, e2, e3, cross_key, cross_value, wk_peer, wv_peer],
    )

    latest.append(pack_forward_peer)
    hidden_two, normed_three, part_three, pack_ffn = go(
        ffn_peer_kernel, "ffn_peer",
        [((half, width), F32), ((half, width), BF16), ((half, width), F32), ((half, width + 2 * units), BF16)],
        [partial_two, other_two, hidden_one, gain_three, up_peer, act_grad_peer],
    )
    pack_ffn_peer = to_core(pack_ffn)
    partial_three, act_own, grad_pre_own = go(
        ffn_own_kernel, "ffn_own", [((half, width), BF16)] + [((half, units), BF16)] * 2,
        [normed_three, ffn_up, act_grad, part_three],
    )
    other_three = to_chip(partial_three)

    def ffn_weights(*refs):
        ffn_weights_kernel((along_x, along_z), size, *refs)

    ffn_payloads = go(
        ffn_weights, "ffn_weights", payload(along_x, width) + payload(along_z, width),
        [normed_three, pack_ffn_peer, act_own, grad_pre_own, branch_three, branch_three_peer],
        scratch=[((width, units), BF16), ((length, width), BF16), ((length, units), BF16)], us=FILL,
    )

    (partial_four, grad_two, gain_grad_three, gl_own, gl_peer, gc_own, gc_peer, gq_own, branch_two,
     pack_backward) = go(
        cross_backward_kernel, "cross_backward",
        [((half, width), BF16), ((half, width), F32), ((8, width), F32)] + [((span, heads * half), BF16)] * 2
        + [((half, columns), BF16)] * 3 + [((half, width), BF16), ((half, width + columns), BF16)],
        [partial_three, other_three, hidden_two, gain_three, grad_full, cross_output, wo_peer,
         k_own, v_own, k_peer, v_peer, probs_own, probs_peer, cross_query, wq_peer],
    )
    other_four = to_chip(partial_four)
    pack_backward_peer = to_core(pack_backward)
    source_grad = go(
        source_grad_kernel, "source_grad", [((2 * span, columns), BF16)], [gl_peer, probs_peer, gc_peer, q_peer]
    )
    source_grad_peer = to_core(source_grad)
    wide = 2 * columns
    ca_wide, cb_wide = (CROSS_X, 2 * wide - CROSS_X) if halving else (wide, wide)

    def cross_weights(*refs):
        cross_weights_kernel((along_x, along_z), size, *refs)

    *cross_payload, source_total = go(
        cross_weights, "cross_weights",
        payload(along_x, ca_wide) + payload(along_z, cb_wide) + [((span, wide), BF16)],
        [gl_own, probs_own, gc_own, q_own, source_grad_peer, e0, e1, e2, e3, normed_two, pack_forward_peer,
         branch_two, pack_backward_peer, context_own, gq_own],
        scratch=[((width, 2 * wide), BF16), ((span, width), BF16), ((4 * half, wide), BF16)],
    )
    ca_payload, cb_payload = cross_payload[: len(cross_payload) // 2], cross_payload[len(cross_payload) // 2 :]
    branch_out = go(ffn_out_kernel, "ffn_out", [((half, width), BF16)], [act_own, pack_ffn, ffn_down, down_peer])

    grad_one, pack_self = go(
        self_norm_kernel, "self_norm", [((half, width), F32), ((half + EXTRA, width), BF16)],
        [partial_four, other_four, hidden_one, gain_two, grad_two, gain_grad_three],
    )
    pack_self_peer = to_core(pack_self)

    if halving:
        up_keep, up_send, down_keep, down_send = ffn_payloads
        half_sent = ((2, size, width), BF16)
        up_send, up_keep, down_send, down_keep = go(
            ffn_second_kernel, "ffn_second", [half_sent] * 4,
            [up_keep, to_peer(up_send, 0), down_keep, to_peer(down_send, 1)], us=1.0,
        )
        up_got = to_peer(up_send, 1)
        down_got = to_peer(down_send, 0)

    keep, send, branch_one, gq_one, gk_one, gv_one, gl_one = go(
        self_backward_kernel, "self_backward",
        [((half + EXTRA, width), BF16)] * 2 + [((length, width), BF16)] + [((length, columns), BF16)] * 3
        + [((length, heads * length), BF16)],
        [pack_self, pack_self_peer, self_output, self_query, self_key, self_value, query_one, key_one, value_one,
         probs_one, x],
        scratch=[((length, width), BF16)],
    )
    got = to_core(send)
    large, small = (SELF_X, 2 * wide - SELF_X) if halving else (wide, wide)
    table_row, extra_count = extra_rows(width, small, heads)

    def self_weights(*refs):
        self_weights_kernel((along_x, along_z), size, table.shape[1], *refs)

    *self_payload, extra = listed(go(
        self_weights, "self_weights",
        payload(along_x, large) + payload(along_z, small) + [((extra_count, small), BF16)],
        [normed_one, branch_one, gq_one, gk_one, gv_one, context_one, gl_one, bucket, pack_self, pack_self_peer],
        scratch=[((width, 2 * wide), BF16), ((2 * length, wide), BF16), ((2 * length, width), BF16)],
    ))
    sa_payload, sb_payload = self_payload[: len(self_payload) // 2], self_payload[len(self_payload) // 2 :]

    if halving:
        ca_keep, ca_send = ca_payload
        cb_keep, cb_send = cb_payload
        sa_keep, sa_send = sa_payload
        sb_keep, sb_send = sb_payload
        more = size + extra_count
        x_rows = (2 * size * cb_wide + 4 * size * large) // PIECE
        zo_rows = (2 * size * ca_wide + (4 * size + extra_count) * small) // PIECE
        x_send, zo_send, ca_keep, cb_keep = go(
            round_three_kernel, "round_three",
            [((x_rows, PIECE), BF16), ((zo_rows, PIECE), BF16), ((2, size, ca_wide), BF16), ((2, size, cb_wide), BF16)],
            [ca_keep, to_peer(ca_send, 0), cb_keep, to_peer(cb_send, 1), sa_send, sb_send, extra], us=1.6,
        )
        x_got = to_peer(x_send, 0)
        zo_got = to_peer(zo_send, 1)

    chip_five = go(input_sum_kernel, "input_sum", [(keep.shape, BF16)], [keep, got])
    other_five = to_chip(chip_five)

    if halving:
        ffn_send, ffn_keep = go(
            ffn_third_kernel, "ffn_third", [((2 * size, width), BF16)] * 2, [up_keep, up_got, down_keep, down_got]
        )
        ffn_got = to_peer(ffn_send, 2)
        gains = go(gain_kernel, "gain", [((extra_count, small), BF16)], [chip_five, other_five], us=LONG)
        gains_got = to_peer(gains, 0)
        branch_source, _ = lax.optimization_barrier((branch_out, gains))
    else:
        branch_source = branch_out
    out_other = to_chip(branch_source)

    if halving:
        rows = 2 * size + extra_count
        cross_send, cross_keep, sa_send, sa_keep, sb_send, sb_keep = go(
            round_four_kernel, "round_four",
            [((size * 2 * wide // PIECE, PIECE), BF16)] * 2 + [((rows, large), BF16)] * 2 + [((rows, small), BF16)] * 2,
            [x_got, zo_got, ca_keep, cb_keep, sa_keep, sb_keep, extra, gains, gains_got],
        )
        sa_got = to_peer(sa_send, 1)
        sb_got = to_peer(sb_send, 0)

    pack_rows = go(
        input_grad_kernel, "input_grad", [((2 * half, width), BF16)],
        [chip_five, other_five, x, gain_one, grad_one, hidden_two, branch_out, out_other],
    )
    pack_rows_peer = to_core(pack_rows)
    if halving:
        cross_send, _ = lax.optimization_barrier((cross_send, pack_rows))
        cross_got = to_peer(cross_send, 2)

    encoded_keep, encoded_send = go(
        encoded_kernel, "encoded", [((span // 2, width), BF16)] * 2, [source_total, cross_key, cross_value]
    )
    encoded_got = to_core(encoded_send)

    if halving:
        up, down = go(ffn_final_kernel, "ffn_final", [((size, width), F32)] * 2, [ffn_keep, ffn_got], us=LONG, last=True)

    encoded_part, encoded_pass = go(
        encoded_sum_kernel, "encoded_sum", [((span_part, width), BF16)] * 2, [encoded_keep, encoded_got]
    )
    encoded_other = to_chip(encoded_pass)

    if halving:
        rows = (size * large + more * small) // PIECE

        def round_five(*refs):
            round_five_kernel(size, *refs)

        self_send, self_keep = go(
            round_five, "round_five", [((rows, PIECE), BF16)] * 2, [sa_keep, sa_got, sb_keep, sb_got]
        )
        self_got = to_peer(self_send, 2)
        square = ((size, columns), F32)
        turned = ((columns, size), F32)
        grad_cross_key, grad_cross_value, grad_cross_query, grad_cross_output = go(
            cross_final_kernel, "cross_final", [square] * 3 + [turned], [cross_keep, cross_got], us=LONG, last=True
        )

    input_grad, layer_out, _ = go(
        rows_kernel, "rows", [((length, width), BF16)] * 2 + [((16, 128), BF16)], [pack_rows, pack_rows_peer]
    )

    if halving:

        def self_final(*refs):
            self_final_kernel(large, *refs)

        (encoded_grad, grad_self_query, grad_self_key, grad_self_value, grad_self_output, grad_table, grad_gain_two,
         grad_gain_three, grad_gain_one) = go(
            self_final, "self_final",
            [((span_part, width), BF16)] + [square] * 3 + [turned, (table.shape, F32)] + [((1, size), F32)] * 3,
            [self_keep, self_got, encoded_part, encoded_other], last=True,
        )
        grad_gain_one, grad_gain_two, grad_gain_three = (
            item.reshape(size) for item in (grad_gain_one, grad_gain_two, grad_gain_three)
        )
    else:
        index = lax.axis_index("dp")

        def gain_part(*rows):
            row = lax.psum(jnp.concatenate(rows, 0).astype(F32), "dp")
            return lax.dynamic_slice(row, (index * size,), (size,))

        def scattered(item):
            return lax.psum_scatter(item.astype(F32), "dp", scatter_dimension=0, tiled=True)

        def pair_of(item):
            item = scattered(item)
            return item[:, :columns], item[:, columns:]

        up, down = (scattered(item) for item in ffn_payloads)
        grad_cross_key, grad_cross_value = pair_of(ca_payload[0])
        grad_cross_query, grad_cross_output = pair_of(cb_payload[0])
        grad_self_query, grad_self_key = pair_of(sa_payload[0])
        grad_self_value, grad_self_output = pair_of(sb_payload[0])
        grad_cross_output, grad_self_output = grad_cross_output.T, grad_self_output.T
        grad_table = lax.psum(extra[table_row : table_row + heads, : table.shape[1]].astype(F32), "dp")
        encoded_grad = plus(encoded_part, encoded_other, "encoded_grad")
        gain_rows = [item[half : half + 2] for item in (chip_five, other_five)]
        grad_gain_one = gain_part(jnp.sum(jnp.concatenate(gain_rows, 0).astype(F32), 0))
        grad_gain_two = gain_part(extra[0], extra[1])
        grad_gain_three = gain_part(extra[2], extra[3])

    return (
        layer_out.reshape(seqs, length, width),
        input_grad.reshape(seqs, length, width),
        encoded_grad.reshape(seqs, span_part, width),
        grad_gain_one,
        grad_self_query,
        grad_self_key,
        grad_self_value,
        grad_self_output,
        grad_table.T,
        grad_gain_two,
        grad_cross_query,
        grad_cross_key,
        grad_cross_value,
        grad_cross_output,
        grad_gain_three,
        up,
        down.T,
    )


def solution(mesh):
    return jax.shard_map(
        on_device,
        mesh=mesh,
        in_specs=(
            P("dp", None, None),
            P("dp", "tensor", None),
            P("dp"),
            P("dp"),
            P("dp"),
            P("dp"),
            P(),
            P(),
            P("dp", None, None),
            P(),
            P(None, "tensor"),
            P(None, "tensor"),
            P(None, "tensor"),
            P("tensor", None),
            P(None, "tensor"),
            P(),
            P(None, "tensor"),
            P(None, "tensor"),
            P(None, "tensor"),
            P("tensor", None),
            P(),
            P(None, "tensor"),
            P("tensor", None),
        ),
        out_specs=(
            P("dp", None, None),
            P("dp", None, None),
            P("dp", "tensor", None),
            P("dp"),
            P("dp", "tensor"),
            P("dp", "tensor"),
            P("dp", "tensor"),
            P("tensor", "dp"),
            P(None, "tensor"),
            P("dp"),
            P("dp", "tensor"),
            P("dp", "tensor"),
            P("dp", "tensor"),
            P("tensor", "dp"),
            P("dp"),
            P("dp", "tensor"),
            P("tensor", "dp"),
        ),
        check_vma=False,
    )
```

```python
import jax
import jax.numpy as jnp
from jax import lax
from jax.experimental import pallas as pl
from jax.experimental.pallas import tpu as pltpu
from jax.sharding import PartitionSpec as P

HEAD_DIM = 64
LANGS = 8
EPSILON = 1e-06
SCALE = 0.125
NEGATIVE = -1e30
F32 = jnp.float32
BF16 = jnp.bfloat16
VMEM_LIMIT = 20 * 1024 * 1024
EXTRA = 16
PIECE = 128
CROSS_X = 384
SELF_X = 512
FILL = 5.0
LONG = 20.0


def dot(left, right):
    return jnp.dot(left, right, preferred_element_type=F32)


def dot_nt(left, right):
    return lax.dot_general(left, right, (((1,), (1,)), ((), ())), preferred_element_type=F32)


def dot_tn(left, right):
    return lax.dot_general(left, right, (((0,), (0,)), ((), ())), preferred_element_type=F32)


def row_of(vector_ref):
    return vector_ref[...].reshape(1, vector_ref.shape[0])


def inverse_rms(resid):
    return lax.rsqrt(jnp.mean(resid * resid, -1, keepdims=True) + EPSILON)


def norm_back(resid, gain, incoming):
    scale = inverse_rms(resid)
    weighted = incoming * gain
    inner = jnp.mean(weighted * resid, -1, keepdims=True)
    grad = scale * weighted - resid * (scale * scale * scale * inner)
    gain_grad = jnp.sum(incoming * resid * scale, 0, keepdims=True)
    return grad, gain_grad


def groups_of(width):
    return [(start, min(2 * HEAD_DIM, width - start)) for start in range(0, width, 2 * HEAD_DIM)]


def head_mask(count, which, value):
    lane = lax.broadcasted_iota(jnp.int32, (1, count), 1)
    return jnp.where(lane // HEAD_DIM == which, value, 0.0).astype(BF16)


def stacked_heads(rows, value):
    width = rows.shape[1]
    if width == HEAD_DIM:
        return rows * jnp.asarray(value, BF16)
    return jnp.concatenate([rows * head_mask(width, inside, value) for inside in range(width // HEAD_DIM)], 0)


def own_blocks(product, count):
    rows = product.shape[1] // count
    return [
        product[inside * HEAD_DIM : (inside + 1) * HEAD_DIM, inside * rows : (inside + 1) * rows]
        for inside in range(count)
    ]


def heads_forward(queries, keys, values_turned, finish, probs_ref):
    rows = queries.shape[0]
    parts = []
    for start, width in groups_of(queries.shape[1]):
        head, count = start // HEAD_DIM, width // HEAD_DIM
        stacked = stacked_heads(queries[:, start : start + width], SCALE)
        logits = finish(head, count, dot_nt(keys[:, start : start + width], stacked))
        expo = jnp.exp(logits - jnp.max(logits, 0, keepdims=True))
        probs = (expo * (1.0 / jnp.sum(expo, 0, keepdims=True))).astype(BF16)
        probs_ref[:, head * rows : (head + count) * rows] = probs
        parts += own_blocks(dot(values_turned[start : start + width], probs), count)
    return jnp.concatenate(parts, 0).astype(BF16)


def heads_backward(grad_context, keys_turned, values, probs_ref, grad_logits_ref):
    rows = grad_context.shape[0]
    parts = []
    for start, width in groups_of(grad_context.shape[1]):
        head, count = start // HEAD_DIM, width // HEAD_DIM
        place = slice(head * rows, (head + count) * rows)
        stacked = stacked_heads(grad_context[:, start : start + width], 1.0)
        grad_probs = dot_nt(values[:, start : start + width], stacked)
        probs = probs_ref[:, place].astype(F32)
        weighted = jnp.sum(grad_probs * probs, 0, keepdims=True)
        grad_logits = (probs * (grad_probs - weighted)).astype(BF16)
        grad_logits_ref[:, place] = grad_logits
        parts += own_blocks(SCALE * dot(keys_turned[start : start + width], grad_logits), count)
    return jnp.concatenate(parts, 0).astype(BF16)


def heads_spread(matrix_ref, rows, factor):
    length = rows.shape[0]
    parts = []
    for start, width in groups_of(rows.shape[1]):
        head, count = start // HEAD_DIM, width // HEAD_DIM
        stacked = stacked_heads(rows[:, start : start + width], 1.0)
        parts.append(factor * dot(matrix_ref[:, head * length : (head + count) * length], stacked))
    return jnp.concatenate(parts, 1).astype(BF16)


def own_rows(core, half):
    return pl.ds(pl.multiple_of(core * half, half), half)


def bucket_onehot(bucket_ref, buckets):
    wanted = lax.broadcasted_iota(jnp.int32, (buckets, bucket_ref.shape[1]), 0)
    return jnp.where(bucket_ref[...] == wanted, 1.0, 0.0)


def add_kernel(left_ref, right_ref, out_ref):
    out_ref[...] = (left_ref[...].astype(F32) + right_ref[...].astype(F32)).astype(out_ref.dtype)


def first_kernel(out):
    out[...] = jnp.zeros_like(out)


def step_kernel(enc_len, objective, language, info, mask):
    info[...] = jnp.full(info.shape, objective[0] * LANGS + language[0], jnp.int32)
    rows = mask.shape[0] // 4
    row = lax.broadcasted_iota(jnp.int32, mask.shape, 0)
    block = row // rows
    flip = jnp.where(block % 2 == 1, 1, 0) + jnp.where(block >= 2, 2, 0)
    position = (lax.axis_index("tensor") ^ flip) * rows + row % rows
    mask[...] = jnp.where(position < enc_len[0], 0.0, NEGATIVE)


def self_sum_kernel(own, first, second, out):
    rows = first.shape[0]
    out[:rows] = both(own[:rows], first[...]).astype(BF16)
    out[rows : 2 * rows] = both(own[rows:], second[...]).astype(BF16)
    out[2 * rows :] = jnp.zeros((out.shape[0] - 2 * rows, out.shape[1]), BF16)


def self_forward_kernel(
    dec_len, bucket, table, x, gain, w_query, w_key, w_value, w_output,
    keep, send, more, normed_out, query_out, context_out, probs_out, dec_out, whole,
):
    dec_out[...] = jnp.full(dec_out.shape, dec_len[0], jnp.int32)
    length = x.shape[0]
    resid = x[...].astype(F32)
    normed = (resid * inverse_rms(resid) * row_of(gain)).astype(BF16)
    normed_out[...] = normed
    queries = dot_nt(normed, w_query[...]).astype(BF16)
    keys = dot_nt(normed, w_key[...]).astype(BF16)
    values = dot_nt(w_value[...], normed).astype(BF16)
    query_out[...] = queries
    by_distance = lax.dot_general(
        table[...],
        bucket_onehot(bucket, table.shape[1]),
        (((1,), (0,)), ((), ())),
        precision=lax.Precision.HIGHEST,
        preferred_element_type=F32,
    )
    row = lax.broadcasted_iota(jnp.int32, (length, length), 0)
    column = lax.broadcasted_iota(jnp.int32, (length, length), 1)
    allowed = (row <= column) & (row < dec_len[0])

    def finish(head, count, scores):
        parts = []
        for inside in range(count):
            spread = jnp.broadcast_to(by_distance[head + inside : head + inside + 1], (length, length))
            bias = pltpu.roll(spread, 0, 1, stride=1, stride_axis=0)
            part = scores[:, inside * length : (inside + 1) * length]
            parts.append(jnp.where(allowed, part + bias, NEGATIVE))
        return jnp.concatenate(parts, 1) if count > 1 else parts[0]

    context = heads_forward(queries, keys, values, finish, probs_out)
    context_out[...] = context.T
    whole[...] = dot_tn(context, w_output[...]).astype(BF16)
    half = keep.shape[0]
    core = lax.axis_index("tensor") % 2
    keep[...] = whole[own_rows(core, half), :]
    rows = send.shape[0]
    send[...] = whole[own_rows(2 - 2 * core, rows), :]
    more[...] = whole[own_rows(3 - 2 * core, rows), :]


def source_rows(parts, start, wk_own, wv_own, wk_peer, wv_peer, k_own, v_own, k_peer, v_peer):
    rows = parts[0].shape[0]
    for index, part in enumerate(parts):
        place = slice(start + index * rows, start + (index + 1) * rows)
        for weight, out in ((wk_own, k_own), (wk_peer, k_peer)):
            out[place, :] = dot_nt(part[...], weight[...]).astype(BF16)
        for weight, out in ((wv_own, v_own), (wv_peer, v_peer)):
            out[:, place] = dot_nt(weight[...], part[...]).astype(BF16)


def source_first_kernel(first, *refs):
    source_rows([first], 0, *refs)


def source_second_kernel(
    first, second, third, wk_own, wv_own, wk_peer, wv_peer, early_k_own, early_v_own, early_k_peer, early_v_peer,
    k_own, v_own, k_peer, v_peer,
):
    rows = first.shape[0]
    for early, out in ((early_k_own, k_own), (early_k_peer, k_peer)):
        out[:rows] = early[...]
    for early, out in ((early_v_own, v_own), (early_v_peer, v_peer)):
        out[:, :rows] = early[...]
    source_rows([first, second, third], rows, wk_own, wv_own, wk_peer, wv_peer, k_own, v_own, k_peer, v_peer)


def source_back_kernel(
    normed, w_key, w_value, e0, e1, e2, e3, wk_own, wv_own, wk_peer, wv_peer,
    keys_turned, values, k_own, v_own, k_peer, v_peer,
):
    keys_turned[...] = dot_nt(w_key[...], normed[...]).astype(BF16)
    values[...] = dot_nt(normed[...], w_value[...]).astype(BF16)
    rows = e0.shape[0]
    for index, part in enumerate((e0, e2, e1, e3)):
        place = slice(index * rows, (index + 1) * rows)
        for weight, out in ((wk_own, k_own), (wk_peer, k_peer)):
            out[:, place] = dot_nt(weight[...], part[...]).astype(BF16)
        for weight, out in ((wv_own, v_own), (wv_peer, v_peer)):
            out[place, :] = dot_nt(part[...], weight[...]).astype(BF16)


def out_grad_kernel(info, dec_len, token_weights, cotangent, grad_own, branch_own, branch_peer):
    half = grad_own.shape[0]
    length = cotangent.shape[0]
    core = lax.axis_index("tensor") % 2
    row = lax.broadcasted_iota(jnp.int32, token_weights.shape, 0)
    weights = jnp.sum(jnp.where(row == info[:1, :1], token_weights[...], 0.0), 0, keepdims=True)
    position = lax.broadcasted_iota(jnp.int32, (1, length), 1)
    weights = jnp.where(position < dec_len[:1, :1], weights, 0.0)

    def rows_of(side):
        row = lax.broadcasted_iota(jnp.int32, (half, length), 0) + side * half
        column = lax.broadcasted_iota(jnp.int32, (half, length), 1)
        factor = jnp.sum(jnp.where(row == column, weights, 0.0), -1, keepdims=True)
        return cotangent[own_rows(side, half), :].astype(F32) * factor

    own = rows_of(core)
    grad_own[...] = own
    branch_own[...] = own.astype(BF16)
    branch_peer[...] = rows_of(1 - core).astype(BF16)


def act_grad_kernel(branch, down_own, down_peer, own, peer):
    own[...] = dot_nt(branch[...], down_own[...])
    peer[...] = dot_nt(branch[...], down_peer[...])


def cross_forward_kernel(
    mask, chip_own, chip_other, x, gain, wq_own, wq_peer, wo_own, wo_peer, k_own, v_own, k_peer, v_peer,
    partial_out, hidden_out, normed_out, q_own, q_peer, context_own, probs_own, probs_peer, pack,
):
    half, width = hidden_out.shape
    core = lax.axis_index("tensor") % 2
    resid = x[own_rows(core, half), :].astype(F32)
    resid = resid + both(chip_own[:half], chip_other[:half])
    hidden_out[...] = resid
    normed = (resid * inverse_rms(resid) * row_of(gain)).astype(BF16)
    normed_out[...] = normed
    pack[:, :width] = normed

    def finish(head, count, scores):
        return scores + jnp.concatenate([mask[...]] * count, 1)

    queries = dot_nt(normed, wq_own[...]).astype(BF16)
    q_own[...] = queries
    first = heads_forward(queries, k_own[...], v_own[...], finish, probs_own)
    context_own[...] = first.T
    queries = dot_nt(normed, wq_peer[...]).astype(BF16)
    q_peer[...] = queries
    second = heads_forward(queries, k_peer[...], v_peer[...], finish, probs_peer)
    pack[:, width:] = second.T
    partial_out[...] = (dot_tn(first, wo_own[...]) + dot_tn(second, wo_peer[...])).astype(BF16)


def through_units(normed, up, act_grad):
    pre = dot(normed, up[...])
    square = pre * pre
    tanh = jnp.tanh(0.7978845608028654 * (pre + 0.044715 * square * pre))
    half_sum = 0.5 * (1.0 + tanh)
    slope = half_sum + 0.5 * pre * (1.0 - tanh * tanh) * (
        0.7978845608028654 * (1.0 + 3.0 * 0.044715 * square)
    )
    return (pre * half_sum).astype(BF16), (act_grad[...] * slope).astype(BF16)


def ffn_peer_kernel(chip_own, chip_other, hidden, gain, up_peer, act_grad_peer, hidden_out, normed_out, part_out, pack):
    width = hidden.shape[1]
    resid = hidden[...] + both(chip_own[...], chip_other[...])
    hidden_out[...] = resid
    normed = (resid * inverse_rms(resid) * row_of(gain)).astype(BF16)
    normed_out[...] = normed
    pack[:, :width] = normed
    act, grad_pre = through_units(normed, up_peer, act_grad_peer)
    units = act.shape[1]
    pack[:, width : width + units] = act
    pack[:, width + units :] = grad_pre
    part_out[...] = dot_nt(grad_pre, up_peer[...])


def ffn_own_kernel(normed, up_own, act_grad_own, part, partial_out, act_own, grad_pre_own):
    act, grad_pre = through_units(normed[...], up_own, act_grad_own)
    act_own[...] = act
    grad_pre_own[...] = grad_pre
    partial_out[...] = (part[...] + dot_nt(grad_pre, up_own[...])).astype(BF16)


def ffn_out_kernel(act_own, pack, down_own, down_peer, out):
    units = act_own.shape[1]
    width = out.shape[1]
    total = dot(act_own[...], down_own[...]) + dot(pack[:, width : width + units], down_peer[...])
    out[...] = total.astype(BF16)


def write_blocks(whole, columns, first_bit, rest_bits, size, targets):
    index = lax.axis_index("dp")
    count = 1 << len(rest_bits)
    for first, target in enumerate(targets):
        for entry in range(count):
            relative = first << first_bit
            for place, bit in enumerate(rest_bits):
                if entry >> (len(rest_bits) - 1 - place) & 1:
                    relative |= 1 << bit
            block = index ^ relative
            target[entry] = whole[pl.ds(pl.multiple_of(block * size, size), size), columns]


def emit(whole, outs, order, size, columns=slice(None)):
    if order is None:
        outs[0][...] = whole[:, columns]
    else:
        write_blocks(whole, columns, order[0], order[1:], size, outs)


def ffn_weights_kernel(orders, size, normed, pack, act_own, grad_pre_own, branch_own, branch_peer, *refs):
    *outs, whole, left, right = refs
    half, width = normed.shape
    units = act_own.shape[1]
    left[:half] = normed[...]
    left[half:] = pack[:, :width]
    right[:half] = grad_pre_own[...]
    right[half:] = pack[:, width + units :]
    whole[...] = dot_tn(left[...], right[...]).astype(BF16)
    count = 1 if orders[0] is None else 2
    emit(whole, outs[:count], orders[0], size)
    left[:half] = branch_own[...]
    left[half:] = branch_peer[...]
    right[:half] = act_own[...]
    right[half:] = pack[:, width : width + units]
    whole[...] = dot_tn(left[...], right[...]).astype(BF16)
    emit(whole, outs[count:], orders[1], size)


def cross_backward_kernel(
    chip_own, chip_other, hidden, gain, grad_out, wo_own, wo_peer, k_own, v_own, k_peer, v_peer,
    probs_own, probs_peer, wq_own, wq_peer,
    partial_out, grad_hidden, gain_grad, gl_own, gl_peer, gc_own, gc_peer, gq_own, branch, pack,
):
    incoming = chip_own[...].astype(F32) + chip_other[...].astype(F32)
    added, gain_terms = norm_back(hidden[...], row_of(gain), incoming)
    gain_grad[...] = jnp.broadcast_to(gain_terms, gain_grad.shape)
    grad = grad_out[...] + added
    grad_hidden[...] = grad
    rounded = grad.astype(BF16)
    branch[...] = rounded
    width = rounded.shape[1]
    pack[:, :width] = rounded
    context = dot_nt(rounded, wo_own[...]).astype(BF16)
    gc_own[...] = context
    queries = heads_backward(context, k_own[...], v_own[...], probs_own, gl_own)
    gq_own[...] = queries.T
    total = dot_tn(queries, wq_own[...])
    context = dot_nt(rounded, wo_peer[...]).astype(BF16)
    gc_peer[...] = context
    queries = heads_backward(context, k_peer[...], v_peer[...], probs_peer, gl_peer)
    pack[:, width:] = queries.T
    total = total + dot_tn(queries, wq_peer[...])
    partial_out[...] = total.astype(BF16)


def source_grad_kernel(gl_peer, probs_peer, gc_peer, q_peer, out):
    span = out.shape[0] // 2
    rows = span // 4
    for start, grads in (
        (0, heads_spread(gl_peer, q_peer[...], SCALE)),
        (span, heads_spread(probs_peer, gc_peer[...], 1.0)),
    ):
        for block in range(4):
            there = start + (block ^ 1) * rows
            out[there : there + rows] = grads[block * rows : (block + 1) * rows]


def cross_weights_kernel(
    orders, size, gl_own, probs_own, gc_own, q_own, other, e0, e1, e2, e3, normed, pack_forward,
    branch, pack_backward, context_own, gq_own, *refs,
):
    *outs, source, whole, left, right = refs
    count = len(outs) // 2
    span = other.shape[0] // 2
    half, width = normed.shape
    columns = q_own.shape[1]
    source[:, :columns] = low_sum(heads_spread(gl_own, q_own[...], SCALE), other[:span])
    source[:, columns:] = low_sum(heads_spread(probs_own, gc_own[...], 1.0), other[span:])
    for index, part in enumerate((e0, e2, e1, e3)):
        left[index * half : (index + 1) * half] = part[...]
    whole[:, : 2 * columns] = dot_tn(left[...], source[...]).astype(BF16)
    left[:half] = normed[...]
    left[half : 2 * half] = pack_forward[:, :width]
    left[2 * half : 3 * half] = branch[...]
    left[3 * half :] = pack_backward[:, :width]
    right[...] = jnp.zeros_like(right)
    right[:half, :columns] = gq_own[...]
    right[half : 2 * half, :columns] = pack_backward[:, width:]
    right[2 * half : 3 * half, columns:] = context_own[...]
    right[3 * half :, columns:] = pack_forward[:, width:]
    whole[:, 2 * columns :] = dot_tn(left[...], right[...]).astype(BF16)
    wide = outs[0].shape[-1]
    emit(whole, outs[:count], orders[0], size, columns=slice(0, wide))
    emit(whole, outs[count:], orders[1], size, columns=slice(wide, None))


def encoded_kernel(source, wk_own, wv_own, keep, send):
    columns = wk_own.shape[0]
    terms = dot(source[:, :columns], wk_own[...]) + dot(source[:, columns:], wv_own[...])
    terms = terms.astype(BF16)
    rows = keep.shape[0] // 2
    for block in range(4):
        target = send if block % 2 else keep
        target[block // 2 * rows : (block // 2 + 1) * rows] = terms[block * rows : (block + 1) * rows]


def self_norm_kernel(chip_own, chip_other, hidden, gain, grad_hidden, gain_ffn, grad_out, pack):
    half = hidden.shape[0]
    incoming = chip_own[...].astype(F32) + chip_other[...].astype(F32)
    added, gain_terms = norm_back(hidden[...], row_of(gain), incoming)
    grad = grad_hidden[...] + added
    grad_out[...] = grad
    pack[:half] = grad.astype(BF16)
    row = lax.broadcasted_iota(jnp.int32, (EXTRA, hidden.shape[1]), 0)
    extra = jnp.where(row == 0, gain_terms, 0.0) + jnp.where(row == 1, gain_ffn[:1], 0.0)
    pack[half:] = extra.astype(BF16)


def high_low(vector):
    high = vector.astype(BF16).astype(F32)
    row = lax.broadcasted_iota(jnp.int32, (EXTRA, vector.shape[1]), 0)
    return (jnp.where(row == 0, high, 0.0) + jnp.where(row == 1, vector - high, 0.0)).astype(BF16)


def of_high_low(rows):
    rows = rows.astype(F32)
    return rows[:1] + rows[1:2]


def self_backward_kernel(
    pack_own, pack_peer, w_output, w_query, w_key, w_value, queries, keys, values, probs, x,
    keep, send, branch_out, gq_out, gk_out, gv_out, gl_out, whole,
):
    half = keep.shape[0] - EXTRA
    core = lax.axis_index("tensor") % 2
    branch_out[own_rows(core, half), :] = pack_own[:half]
    branch_out[own_rows(1 - core, half), :] = pack_peer[:half]
    context = dot_nt(branch_out[...], w_output[...]).astype(BF16)
    grad_queries = heads_backward(context, keys[...], values[...], probs, gl_out)
    grad_keys = heads_spread(gl_out, queries[...], SCALE)
    grad_values = heads_spread(probs, context, 1.0)
    gq_out[...] = grad_queries.T
    gk_out[...] = grad_keys
    gv_out[...] = grad_values
    total = dot_tn(grad_queries, w_query[...]) + dot(grad_keys, w_key[...]) + dot(grad_values, w_value[...])
    whole[...] = total.astype(BF16)
    keep[:half] = whole[own_rows(core, half), :]
    send[:half] = whole[own_rows(1 - core, half), :]
    resid = x[...].astype(F32)
    gain_terms = high_low(jnp.sum(total * resid * inverse_rms(resid), 0, keepdims=True))
    keep[half:] = gain_terms
    send[half:] = gain_terms


def input_sum_kernel(own, peer, out):
    half = out.shape[0] - EXTRA
    out[:half] = both(own[:half], peer[:half]).astype(BF16)
    out[half:] = high_low(of_high_low(own[half:]) + of_high_low(peer[half:]))


def self_weights_kernel(
    orders, size, buckets, normed, branch, gq, gk, gv, context, gl, bucket, pack_own, pack_peer, *refs
):
    *outs, extra_out, whole, right, left = refs
    count = len(outs) // 2
    length, columns = gq.shape
    half = pack_own.shape[0] - EXTRA
    right[:length, :columns] = gq[...]
    right[:length, columns:] = gk[...]
    whole[:, : 2 * columns] = dot_tn(normed[...], right[:length]).astype(BF16)
    left[:length] = normed[...]
    left[length:] = branch[...]
    right[...] = jnp.zeros_like(right)
    right[:length, :columns] = gv[...]
    right[length:, columns:] = context[...]
    whole[:, 2 * columns :] = dot_tn(left[...], right[...]).astype(BF16)
    wide = outs[0].shape[-1]
    emit(whole, outs[:count], orders[0], size, columns=slice(0, wide))
    onehot = bucket_onehot(bucket, buckets)
    row = lax.broadcasted_iota(jnp.int32, (length, length), 0)
    column = lax.broadcasted_iota(jnp.int32, (length, length), 1)
    turn = jnp.where(row + column == length - 1, 1.0, 0.0).astype(BF16)
    place = lax.broadcasted_iota(jnp.int32, (8, length), 0)
    sums = jnp.zeros((8, length), F32)
    heads = gl.shape[1] // length
    for head in range(heads):
        skewed = pltpu.roll(dot(turn, gl[:, head * length : (head + 1) * length]), 1, 1, stride=1, stride_axis=0)
        sums = sums + jnp.where(place == head, jnp.sum(skewed, 0, keepdims=True), 0.0)
    table = lax.dot_general(
        sums, onehot, (((1,), (1,)), ((), ())), precision=lax.Precision.HIGHEST, preferred_element_type=F32
    )
    gains = both(pack_own[half:], pack_peer[half:])
    narrow = outs[-1].shape[-1]
    first, count_rows = extra_rows(gains.shape[1], narrow, heads)
    extra = vector_rows(gains[:1], narrow, count_rows, 0) + vector_rows(gains[1:2], narrow, count_rows, 1)
    table = jnp.concatenate([table, jnp.zeros((8, narrow - buckets), F32)], 1)
    row = lax.broadcasted_iota(jnp.int32, (count_rows, narrow), 0)
    for head in range(heads):
        extra = extra + jnp.where(row == first + head, table[head : head + 1], 0.0)
    extra_out[...] = extra.astype(BF16)
    emit(whole, outs[count:], orders[1], size, columns=slice(wide, None))


def extra_rows(width, wide, heads):
    first = -(-3 * (width // wide) // 4) * 4
    return first, -(-(first + heads) // 16) * 16


def vector_rows(vector, wide, count, which):
    rows = vector.shape[1] // wide
    row = lax.broadcasted_iota(jnp.int32, (count, wide), 0)
    placed = jnp.zeros((count, wide), F32)
    for index in range(rows):
        piece = vector[:, index * wide : (index + 1) * wide]
        placed = placed + jnp.where(row == which * rows + index, piece, 0.0)
    return placed


def encoded_sum_kernel(own, other, keep, send):
    rows = keep.shape[0]
    keep[...] = low_sum(own[:rows], other[:rows])
    send[...] = low_sum(own[rows:], other[rows:])


def input_grad_kernel(chip_own, chip_other, x, gain, grad_hidden, hidden_two, out_own, out_other, pack):
    half = hidden_two.shape[0]
    resid = x[own_rows(lax.axis_index("tensor") % 2, half), :].astype(F32)
    added, _ = norm_back(resid, row_of(gain), both(chip_own[:half], chip_other[:half]))
    pack[:half] = (grad_hidden[...] + added).astype(BF16)
    pack[half:] = (hidden_two[...] + both(out_own[...], out_other[...])).astype(BF16)


def rows_kernel(own, peer, input_grad, layer_out, token):
    half = own.shape[0] // 2
    core = lax.axis_index("tensor") % 2
    for place, out in ((0, input_grad), (half, layer_out)):
        out[own_rows(core, half), :] = own[place : place + half]
        out[own_rows(1 - core, half), :] = peer[place : place + half]
    token[...] = own[: token.shape[0], : token.shape[1]]


def both(left, right):
    return left.astype(F32) + right.astype(F32)


def low_sum(left, right):
    return both(left, right).astype(BF16)


def ffn_second_kernel(up_keep, up_got, down_keep, down_got, up_send, up_next, down_send, down_next):
    for keep, got, send, new in (
        (up_keep, up_got, up_send, up_next),
        (down_keep, down_got, down_send, down_next),
    ):
        for entry in range(2):
            new[entry] = low_sum(keep[entry], got[entry])
            send[entry] = low_sum(keep[2 + entry], got[2 + entry])


def ffn_third_kernel(up_keep, up_got, down_keep, down_got, send, keep):
    size = up_keep.shape[1]
    for entry, target in enumerate((keep, send)):
        target[:size] = low_sum(up_keep[entry], up_got[entry])
        target[size:] = low_sum(down_keep[entry], down_got[entry])


def round_three_kernel(
    ca_keep, ca_got, cb_keep, cb_got, sa_send, sb_send, extra, x_send, zo_send, ca_next, cb_next
):
    for entry in range(2):
        ca_next[entry] = low_sum(ca_keep[entry], ca_got[entry])
        cb_next[entry] = low_sum(cb_keep[entry], cb_got[entry])
    base = spread_out(x_send, [low_sum(cb_keep[2 + entry], cb_got[2 + entry]) for entry in range(2)])
    spread_out(x_send, [sa_send[entry] for entry in range(4)], base)
    base = spread_out(zo_send, [low_sum(ca_keep[2 + entry], ca_got[2 + entry]) for entry in range(2)])
    base = spread_out(zo_send, [sb_send[entry] for entry in range(4)], base)
    spread_out(zo_send, [extra[...]], base)


def gain_kernel(chip_own, chip_other, out):
    half = chip_own.shape[0] - EXTRA
    gain = of_high_low(chip_own[half:]) + of_high_low(chip_other[half:])
    out[...] = vector_rows(gain, out.shape[1], out.shape[0], 0).astype(BF16)


def spread_out(target, parts, start=0):
    for part in parts:
        rows = part.shape[0]
        for side in range(part.shape[1] // PIECE):
            target[start : start + rows] = part[:, side * PIECE : (side + 1) * PIECE]
            start += rows
    return start


def gathered(source, rows, wide, start):
    pieces = [source[start + side * rows : start + (side + 1) * rows] for side in range(wide // PIECE)]
    return jnp.concatenate(pieces, 1) if len(pieces) > 1 else pieces[0]


def round_four_kernel(
    x_got, zo_got, ca_keep, cb_keep, sa_keep, sb_keep, extra, gains, gains_got,
    cross_send, cross_keep, sa_send, sa_next, sb_send, sb_next,
):
    size, ca_wide = ca_keep.shape[1:]
    cb_wide = cb_keep.shape[2]
    large, small = sa_keep.shape[2], sb_keep.shape[2]
    zo_base = 2 * size * ca_wide // PIECE
    x_base = 2 * size * cb_wide // PIECE
    for entry, target in enumerate((cross_keep, cross_send)):
        part = low_sum(ca_keep[entry], gathered(zo_got, size, ca_wide, entry * (zo_base // 2)))
        base = spread_out(target, [part])
        part = low_sum(cb_keep[entry], gathered(x_got, size, cb_wide, entry * (x_base // 2)))
        spread_out(target, [part], base)
    gain = low_sum(gains[...], gains_got[...])
    step = size * (small // PIECE)
    extra = low_sum(extra[...], gathered(zo_got, extra.shape[0], small, zo_base + 4 * step))
    for first, sa_out, sb_out in ((0, sa_next, sb_next), (2, sa_send, sb_send)):
        for entry in range(2):
            part = slice(entry * size, (entry + 1) * size)
            start = x_base + (first + entry) * size * (large // PIECE)
            part_sum = low_sum(sa_keep[first + entry], gathered(x_got, size, large, start))
            base = spread_out(sa_out, [part_sum], entry * size * (large // PIECE))
            start = zo_base + (first + entry) * step
            sb_out[part] = low_sum(sb_keep[first + entry], gathered(zo_got, size, small, start))
        sa_out[base:] = gain
        sb_out[2 * size :] = extra


def round_five_kernel(size, sa_keep, sa_got, sb_keep, sb_got, send, keep):
    small = sb_keep.shape[1]
    extra_count = sb_keep.shape[0] - 2 * size
    step = (sa_keep.shape[0] - EXTRA) // 2
    large = step // size * PIECE
    gain = both(sa_keep[2 * step :], sa_got[2 * step :])
    gain = jnp.concatenate([gain[index : index + 1] for index in range((large + small) // PIECE)], 1)
    extra = vector_rows(gain, small, extra_count, 2) + both(sb_keep[2 * size :], sb_got[2 * size :])
    extra = extra.astype(BF16)
    for entry, target in enumerate((keep, send)):
        part = slice(entry * size, (entry + 1) * size)
        whole = slice(entry * step, (entry + 1) * step)
        target[:step] = low_sum(sa_keep[whole], sa_got[whole])
        part = jnp.concatenate([low_sum(sb_keep[part], sb_got[part]), extra], 0)
        spread_out(target, [part], step)


def ffn_final_kernel(keep, got, up, down):
    size = up.shape[0]
    up[...] = both(keep[:size], got[:size])
    down[...] = both(keep[size:], got[size:])


def cross_final_kernel(keep, got, key, value, query, output):
    size, count = key.shape
    total = both(gathered(keep, size, 4 * count, 0), gathered(got, size, 4 * count, 0))
    for place, out in enumerate((key, value, query)):
        out[...] = total[:, place * count : (place + 1) * count]
    output[...] = total[:, 3 * count :].T


def self_final_kernel(
    large, keep, got, encoded_own, encoded_other,
    encoded_grad, query, key, value, output, table, gain_two, gain_three, gain_one,
):
    encoded_grad[...] = low_sum(encoded_own[...], encoded_other[...])
    size, count = key.shape
    small = 4 * count - large
    start = size * (large // PIECE)
    first = both(gathered(keep, size, large, 0), gathered(got, size, large, 0))
    table_row, more = extra_rows(4 * count, small, table.shape[0])
    more += size
    second = both(gathered(keep, more, small, start), gathered(got, more, small, start))
    total = jnp.concatenate([first, second[:size]], 1)
    for place, out in enumerate((query, key, value)):
        out[...] = total[:, place * count : (place + 1) * count]
    output[...] = total[:, 3 * count :].T
    extra = second[size:]
    table[...] = extra[table_row : table_row + table.shape[0], : table.shape[1]]
    wide = 4 * count
    back = wide - lax.axis_index("dp") * size
    rows = wide // small
    for which, out in enumerate((gain_two, gain_three, gain_one)):
        pieces = [extra[which * rows + index : which * rows + index + 1] for index in range(rows)]
        whole = jnp.concatenate(pieces, 1)
        out[...] = pltpu.roll(jnp.broadcast_to(whole, (8, wide)), back, 1)[:1, :size]


def run(kernel, name, outs, ins, us=0.0, scratch=(), scalars=0, far=0, sems=0, after=(), limit=VMEM_LIMIT):
    shapes = [jax.ShapeDtypeStruct(shape, dtype) for shape, dtype in outs]
    idle = len(after)
    body = kernel
    if idle:

        def body(*refs):
            kernel(*refs[: len(ins)], *refs[len(ins) + idle :])

    vmem = pl.BlockSpec(memory_space=pltpu.VMEM)
    hbm = pl.BlockSpec(memory_space=pltpu.HBM)
    free = pl.BlockSpec(memory_space=pl.ANY)
    smem = pl.BlockSpec(memory_space=pltpu.SMEM)
    place = [smem] * scalars + [hbm] * far + [vmem] * (len(ins) - scalars - far) + [free] * idle
    ins = [
        pltpu.with_memory_space_constraint(item, pltpu.HBM) if spec is hbm else item for item, spec in zip(ins, place)
    ]
    result = pl.pallas_call(
        body,
        out_shape=shapes,
        in_specs=place,
        out_specs=[vmem] * len(shapes),
        scratch_shapes=[pltpu.VMEM(shape, dtype) for shape, dtype in scratch]
        + ([pltpu.SemaphoreType.DMA((sems,))] if sems else []),
        compiler_params=pltpu.CompilerParams(vmem_limit_bytes=limit),
        cost_estimate=pl.CostEstimate(flops=int(us * 1.15e9), bytes_accessed=0, transcendentals=0),
        name=name,
    )(*ins, *after)
    return result[0] if len(shapes) == 1 else result


def listed(result):
    return list(result) if isinstance(result, (list, tuple)) else [result]


def to_core(value):
    return lax.ppermute(value, "tensor", [(i, i ^ 1) for i in range(lax.axis_size("tensor"))])


def to_chip(value):
    return lax.ppermute(value, "tensor", [(i, i ^ 2) for i in range(lax.axis_size("tensor"))])


def to_peer(value, bit):
    return lax.ppermute(value, "dp", [(i, i ^ (1 << bit)) for i in range(lax.axis_size("dp"))])


def on_device(
    inputs, encoded, dec_len, enc_len, language, objective, distance_bucket, token_weights, cotangent,
    gain_self, self_query, self_key, self_value, self_output, bias_table,
    gain_cross, cross_query, cross_key, cross_value, cross_output, gain_ffn, ffn_up, ffn_down,
):
    seqs, length, width = inputs.shape
    half = length // 2
    columns = self_query.shape[1]
    heads = columns // HEAD_DIM
    units = ffn_up.shape[1]
    span_part = encoded.shape[1]
    span = span_part * lax.axis_size("tensor")
    dp = lax.axis_size("dp")
    size = width // dp
    bits = dp.bit_length() - 1
    halving = bits == 3 and dp == 8 and size % 16 == 0
    along_x, along_z = ((0, 1, 2), (1, 0, 2)) if halving else (None, None)
    latest = []

    def go(kernel, name, outs, ins, last=False, **how):
        after = [item for item in latest if not any(item is one for one in ins)]
        result = run(kernel, name, outs, ins, after=after, **how)
        if not last:
            results = result if isinstance(result, (list, tuple)) else [result]
            latest[:] = [min(results, key=lambda item: item.size * item.dtype.itemsize)]
        return result

    def plus(left, right, name):
        return go(add_kernel, name, [(left.shape, left.dtype)], [left, right])

    def payload(order, wide):
        if order is None:
            return [((width, wide), BF16)]
        return [((dp // 2, size, wide), BF16)] * 2

    x = inputs.reshape(length, width)
    cot = cotangent.reshape(length, width)
    gain_one, gain_two, gain_three = gain_self, gain_cross, gain_ffn
    self_query, self_key, self_value = self_query.T, self_key.T, self_value.T
    cross_query, cross_key, cross_value = cross_query.T, cross_key.T, cross_value.T
    table = bias_table.T
    bucket = distance_bucket.reshape(1, length)
    e0 = encoded.reshape(span_part, width)

    first = go(first_kernel, "first", [((8, 128), F32)], [], us=LONG)
    key_source, value_source, _ = lax.optimization_barrier((cross_key, cross_value, first))
    e1 = to_chip(e0)
    e2 = to_core(e0)
    wk_peer = to_core(key_source)
    wv_peer = to_core(value_source)
    keep, send, more, normed_one, query_one, context_one, probs_one, dec_rows = go(
        self_forward_kernel, "self_forward",
        [((half, width), BF16)] + [((half // 2, width), BF16)] * 2 + [((length, width), BF16)]
        + [((length, columns), BF16)] * 2 + [((length, heads * length), BF16), ((8, 128), jnp.int32)],
        [dec_len, bucket, table, x, gain_one, self_query, self_key, self_value, self_output],
        scratch=[((length, width), BF16)], scalars=1, us=3.5,
    )
    first_half, second_half = to_core(send), to_core(more)
    early = go(
        source_first_kernel, "source_first", [((span_part, columns), BF16), ((columns, span_part), BF16)] * 2,
        [e0, cross_key, cross_value, wk_peer, wv_peer],
    )
    chip_one = go(self_sum_kernel, "self_sum", [((half + EXTRA, width), BF16)], [keep, first_half, second_half])
    other_one = to_chip(chip_one)
    wq_peer = to_core(cross_query)
    wo_peer = to_core(cross_output)
    e3 = to_core(e1)
    late = go(
        source_second_kernel, "source_second", [((span, columns), BF16), ((columns, span), BF16)] * 2,
        [e2, e1, e3, cross_key, cross_value, wk_peer, wv_peer, *early],
    )
    enc_len, objective, language, _ = lax.optimization_barrier((enc_len, objective, language, late[0]))
    info, mask = go(
        step_kernel, "step", [((8, 128), jnp.int32), ((span, half), F32)], [enc_len, objective, language], scalars=3
    )
    up_source, down_source, _ = lax.optimization_barrier((ffn_up, ffn_down, late[0]))
    down_peer = to_core(down_source)
    up_peer = to_core(up_source)

    partial_two, hidden_one, normed_two, q_own, q_peer, context_own, probs_own, probs_peer, pack_forward = go(
        cross_forward_kernel, "cross_forward",
        [((half, width), BF16), ((half, width), F32), ((half, width), BF16)] + [((half, columns), BF16)] * 3
        + [((span, heads * half), BF16)] * 2 + [((half, width + columns), BF16)],
        [mask, chip_one, other_one, x, gain_two, cross_query, wq_peer, cross_output, wo_peer, *late],
    )
    other_two = to_chip(partial_two)
    pack_forward_peer = to_core(pack_forward)
    grad_full, branch_three, branch_three_peer = go(
        out_grad_kernel, "out_grad", [((half, width), F32)] + [((half, width), BF16)] * 2,
        [info, dec_rows, token_weights, cot], us=LONG,
    )
    act_grad, act_grad_peer = go(
        act_grad_kernel, "act_grad", [((half, units), F32)] * 2, [branch_three, ffn_down, down_peer]
    )
    key_one, value_one, k_own, v_own, k_peer, v_peer = go(
        source_back_kernel, "source_back",
        [((columns, length), BF16), ((length, columns), BF16)] + [((columns, span), BF16), ((span, columns), BF16)] * 2,
        [normed_one, self_key, self_value, e0, e1, e2, e3, cross_key, cross_value, wk_peer, wv_peer],
    )

    latest.append(pack_forward_peer)
    hidden_two, normed_three, part_three, pack_ffn = go(
        ffn_peer_kernel, "ffn_peer",
        [((half, width), F32), ((half, width), BF16), ((half, width), F32), ((half, width + 2 * units), BF16)],
        [partial_two, other_two, hidden_one, gain_three, up_peer, act_grad_peer],
    )
    pack_ffn_peer = to_core(pack_ffn)
    partial_three, act_own, grad_pre_own = go(
        ffn_own_kernel, "ffn_own", [((half, width), BF16)] + [((half, units), BF16)] * 2,
        [normed_three, ffn_up, act_grad, part_three],
    )
    other_three = to_chip(partial_three)

    def ffn_weights(*refs):
        ffn_weights_kernel((along_x, along_z), size, *refs)

    ffn_payloads = go(
        ffn_weights, "ffn_weights", payload(along_x, width) + payload(along_z, width),
        [normed_three, pack_ffn_peer, act_own, grad_pre_own, branch_three, branch_three_peer],
        scratch=[((width, units), BF16), ((length, width), BF16), ((length, units), BF16)], us=FILL,
    )

    (partial_four, grad_two, gain_grad_three, gl_own, gl_peer, gc_own, gc_peer, gq_own, branch_two,
     pack_backward) = go(
        cross_backward_kernel, "cross_backward",
        [((half, width), BF16), ((half, width), F32), ((8, width), F32)] + [((span, heads * half), BF16)] * 2
        + [((half, columns), BF16)] * 3 + [((half, width), BF16), ((half, width + columns), BF16)],
        [partial_three, other_three, hidden_two, gain_three, grad_full, cross_output, wo_peer,
         k_own, v_own, k_peer, v_peer, probs_own, probs_peer, cross_query, wq_peer],
    )
    other_four = to_chip(partial_four)
    pack_backward_peer = to_core(pack_backward)
    source_grad = go(
        source_grad_kernel, "source_grad", [((2 * span, columns), BF16)], [gl_peer, probs_peer, gc_peer, q_peer]
    )
    source_grad_peer = to_core(source_grad)
    wide = 2 * columns
    ca_wide, cb_wide = (CROSS_X, 2 * wide - CROSS_X) if halving else (wide, wide)

    def cross_weights(*refs):
        cross_weights_kernel((along_x, along_z), size, *refs)

    *cross_payload, source_total = go(
        cross_weights, "cross_weights",
        payload(along_x, ca_wide) + payload(along_z, cb_wide) + [((span, wide), BF16)],
        [gl_own, probs_own, gc_own, q_own, source_grad_peer, e0, e1, e2, e3, normed_two, pack_forward_peer,
         branch_two, pack_backward_peer, context_own, gq_own],
        scratch=[((width, 2 * wide), BF16), ((span, width), BF16), ((4 * half, wide), BF16)],
    )
    ca_payload, cb_payload = cross_payload[: len(cross_payload) // 2], cross_payload[len(cross_payload) // 2 :]
    branch_out = go(ffn_out_kernel, "ffn_out", [((half, width), BF16)], [act_own, pack_ffn, ffn_down, down_peer])

    grad_one, pack_self = go(
        self_norm_kernel, "self_norm", [((half, width), F32), ((half + EXTRA, width), BF16)],
        [partial_four, other_four, hidden_one, gain_two, grad_two, gain_grad_three],
    )
    pack_self_peer = to_core(pack_self)

    if halving:
        up_keep, up_send, down_keep, down_send = ffn_payloads
        half_sent = ((2, size, width), BF16)
        up_send, up_keep, down_send, down_keep = go(
            ffn_second_kernel, "ffn_second", [half_sent] * 4,
            [up_keep, to_peer(up_send, 0), down_keep, to_peer(down_send, 1)], us=1.0,
        )
        up_got = to_peer(up_send, 1)
        down_got = to_peer(down_send, 0)

    keep, send, branch_one, gq_one, gk_one, gv_one, gl_one = go(
        self_backward_kernel, "self_backward",
        [((half + EXTRA, width), BF16)] * 2 + [((length, width), BF16)] + [((length, columns), BF16)] * 3
        + [((length, heads * length), BF16)],
        [pack_self, pack_self_peer, self_output, self_query, self_key, self_value, query_one, key_one, value_one,
         probs_one, x],
        scratch=[((length, width), BF16)],
    )
    got = to_core(send)
    large, small = (SELF_X, 2 * wide - SELF_X) if halving else (wide, wide)
    table_row, extra_count = extra_rows(width, small, heads)

    def self_weights(*refs):
        self_weights_kernel((along_x, along_z), size, table.shape[1], *refs)

    *self_payload, extra = listed(go(
        self_weights, "self_weights",
        payload(along_x, large) + payload(along_z, small) + [((extra_count, small), BF16)],
        [normed_one, branch_one, gq_one, gk_one, gv_one, context_one, gl_one, bucket, pack_self, pack_self_peer],
        scratch=[((width, 2 * wide), BF16), ((2 * length, wide), BF16), ((2 * length, width), BF16)],
    ))
    sa_payload, sb_payload = self_payload[: len(self_payload) // 2], self_payload[len(self_payload) // 2 :]

    if halving:
        ca_keep, ca_send = ca_payload
        cb_keep, cb_send = cb_payload
        sa_keep, sa_send = sa_payload
        sb_keep, sb_send = sb_payload
        more = size + extra_count
        x_rows = (2 * size * cb_wide + 4 * size * large) // PIECE
        zo_rows = (2 * size * ca_wide + (4 * size + extra_count) * small) // PIECE
        x_send, zo_send, ca_keep, cb_keep = go(
            round_three_kernel, "round_three",
            [((x_rows, PIECE), BF16), ((zo_rows, PIECE), BF16), ((2, size, ca_wide), BF16), ((2, size, cb_wide), BF16)],
            [ca_keep, to_peer(ca_send, 0), cb_keep, to_peer(cb_send, 1), sa_send, sb_send, extra], us=1.6,
        )
        x_got = to_peer(x_send, 0)
        zo_got = to_peer(zo_send, 1)

    chip_five = go(input_sum_kernel, "input_sum", [(keep.shape, BF16)], [keep, got])
    other_five = to_chip(chip_five)

    if halving:
        ffn_send, ffn_keep = go(
            ffn_third_kernel, "ffn_third", [((2 * size, width), BF16)] * 2, [up_keep, up_got, down_keep, down_got]
        )
        ffn_got = to_peer(ffn_send, 2)
        gains = go(gain_kernel, "gain", [((EXTRA, PIECE), BF16)], [chip_five, other_five], us=LONG)
        gains_got = to_peer(gains, 0)
        branch_source, _ = lax.optimization_barrier((branch_out, gains))
    else:
        branch_source = branch_out
    out_other = to_chip(branch_source)

    if halving:
        rows = 2 * size + extra_count
        cross_send, cross_keep, sa_send, sa_keep, sb_send, sb_keep = go(
            round_four_kernel, "round_four",
            [((size * 2 * wide // PIECE, PIECE), BF16)] * 2 + [((2 * size * large // PIECE + EXTRA, PIECE), BF16)] * 2
            + [((rows, small), BF16)] * 2,
            [x_got, zo_got, ca_keep, cb_keep, sa_keep, sb_keep, extra, gains, gains_got],
        )
        sa_got = to_peer(sa_send, 1)
        sb_got = to_peer(sb_send, 0)

    pack_rows = go(
        input_grad_kernel, "input_grad", [((2 * half, width), BF16)],
        [chip_five, other_five, x, gain_one, grad_one, hidden_two, branch_out, out_other],
    )
    pack_rows_peer = to_core(pack_rows)
    if halving:
        cross_send, _ = lax.optimization_barrier((cross_send, pack_rows))
        cross_got = to_peer(cross_send, 2)

    encoded_keep, encoded_send = go(
        encoded_kernel, "encoded", [((span // 2, width), BF16)] * 2, [source_total, cross_key, cross_value]
    )
    encoded_got = to_core(encoded_send)

    if halving:
        up, down = go(ffn_final_kernel, "ffn_final", [((size, width), F32)] * 2, [ffn_keep, ffn_got], us=LONG, last=True)

    encoded_part, encoded_pass = go(
        encoded_sum_kernel, "encoded_sum", [((span_part, width), BF16)] * 2, [encoded_keep, encoded_got]
    )
    encoded_other = to_chip(encoded_pass)

    if halving:
        rows = (size * large + more * small) // PIECE

        def round_five(*refs):
            round_five_kernel(size, *refs)

        self_send, self_keep = go(
            round_five, "round_five", [((rows, PIECE), BF16)] * 2, [sa_keep, sa_got, sb_keep, sb_got]
        )
        self_got = to_peer(self_send, 2)
        square = ((size, columns), F32)
        turned = ((columns, size), F32)
        grad_cross_key, grad_cross_value, grad_cross_query, grad_cross_output = go(
            cross_final_kernel, "cross_final", [square] * 3 + [turned], [cross_keep, cross_got], us=LONG, last=True
        )

    input_grad, layer_out, _ = go(
        rows_kernel, "rows", [((length, width), BF16)] * 2 + [((16, 128), BF16)], [pack_rows, pack_rows_peer]
    )

    if halving:

        def self_final(*refs):
            self_final_kernel(large, *refs)

        (encoded_grad, grad_self_query, grad_self_key, grad_self_value, grad_self_output, grad_table, grad_gain_two,
         grad_gain_three, grad_gain_one) = go(
            self_final, "self_final",
            [((span_part, width), BF16)] + [square] * 3 + [turned, (table.shape, F32)] + [((1, size), F32)] * 3,
            [self_keep, self_got, encoded_part, encoded_other], last=True,
        )
        grad_gain_one, grad_gain_two, grad_gain_three = (
            item.reshape(size) for item in (grad_gain_one, grad_gain_two, grad_gain_three)
        )
    else:
        index = lax.axis_index("dp")

        def gain_part(*rows):
            row = lax.psum(jnp.concatenate(rows, 0).astype(F32), "dp")
            return lax.dynamic_slice(row, (index * size,), (size,))

        def scattered(item):
            return lax.psum_scatter(item.astype(F32), "dp", scatter_dimension=0, tiled=True)

        def pair_of(item):
            item = scattered(item)
            return item[:, :columns], item[:, columns:]

        up, down = (scattered(item) for item in ffn_payloads)
        grad_cross_key, grad_cross_value = pair_of(ca_payload[0])
        grad_cross_query, grad_cross_output = pair_of(cb_payload[0])
        grad_self_query, grad_self_key = pair_of(sa_payload[0])
        grad_self_value, grad_self_output = pair_of(sb_payload[0])
        grad_cross_output, grad_self_output = grad_cross_output.T, grad_self_output.T
        grad_table = lax.psum(extra[table_row : table_row + heads, : table.shape[1]].astype(F32), "dp")
        encoded_grad = plus(encoded_part, encoded_other, "encoded_grad")
        gain_rows = [item[half : half + 2] for item in (chip_five, other_five)]
        grad_gain_one = gain_part(jnp.sum(jnp.concatenate(gain_rows, 0).astype(F32), 0))
        grad_gain_two = gain_part(extra[0], extra[1])
        grad_gain_three = gain_part(extra[2], extra[3])

    return (
        layer_out.reshape(seqs, length, width),
        input_grad.reshape(seqs, length, width),
        encoded_grad.reshape(seqs, span_part, width),
        grad_gain_one,
        grad_self_query,
        grad_self_key,
        grad_self_value,
        grad_self_output,
        grad_table.T,
        grad_gain_two,
        grad_cross_query,
        grad_cross_key,
        grad_cross_value,
        grad_cross_output,
        grad_gain_three,
        up,
        down.T,
    )


def solution(mesh):
    return jax.shard_map(
        on_device,
        mesh=mesh,
        in_specs=(
            P("dp", None, None),
            P("dp", "tensor", None),
            P("dp"),
            P("dp"),
            P("dp"),
            P("dp"),
            P(),
            P(),
            P("dp", None, None),
            P(),
            P(None, "tensor"),
            P(None, "tensor"),
            P(None, "tensor"),
            P("tensor", None),
            P(None, "tensor"),
            P(),
            P(None, "tensor"),
            P(None, "tensor"),
            P(None, "tensor"),
            P("tensor", None),
            P(),
            P(None, "tensor"),
            P("tensor", None),
        ),
        out_specs=(
            P("dp", None, None),
            P("dp", None, None),
            P("dp", "tensor", None),
            P("dp"),
            P("dp", "tensor"),
            P("dp", "tensor"),
            P("dp", "tensor"),
            P("tensor", "dp"),
            P(None, "tensor"),
            P("dp"),
            P("dp", "tensor"),
            P("dp", "tensor"),
            P("dp", "tensor"),
            P("tensor", "dp"),
            P("dp"),
            P("dp", "tensor"),
            P("tensor", "dp"),
        ),
        check_vma=False,
    )
```

```python
import jax
import jax.numpy as jnp
from jax import lax
from jax.experimental import pallas as pl
from jax.experimental.pallas import tpu as pltpu
from jax.sharding import PartitionSpec as P

HEAD_DIM = 64
LANGS = 8
EPSILON = 1e-06
SCALE = 0.125
NEGATIVE = -1e30
F32 = jnp.float32
BF16 = jnp.bfloat16
VMEM_LIMIT = 20 * 1024 * 1024
EXTRA = 16
PIECE = 128
CROSS_X = 384
SELF_X = 512
FILL = 5.0
LONG = 20.0


def dot(left, right):
    return jnp.dot(left, right, preferred_element_type=F32)


def dot_nt(left, right):
    return lax.dot_general(left, right, (((1,), (1,)), ((), ())), preferred_element_type=F32)


def dot_tn(left, right):
    return lax.dot_general(left, right, (((0,), (0,)), ((), ())), preferred_element_type=F32)


def row_of(vector_ref):
    return vector_ref[...].reshape(1, vector_ref.shape[0])


def inverse_rms(resid):
    return lax.rsqrt(jnp.mean(resid * resid, -1, keepdims=True) + EPSILON)


def norm_back(resid, gain, incoming):
    scale = inverse_rms(resid)
    weighted = incoming * gain
    inner = jnp.mean(weighted * resid, -1, keepdims=True)
    grad = scale * weighted - resid * (scale * scale * scale * inner)
    gain_grad = jnp.sum(incoming * resid * scale, 0, keepdims=True)
    return grad, gain_grad


def groups_of(width):
    return [(start, min(2 * HEAD_DIM, width - start)) for start in range(0, width, 2 * HEAD_DIM)]


def head_mask(count, which, value):
    lane = lax.broadcasted_iota(jnp.int32, (1, count), 1)
    return jnp.where(lane // HEAD_DIM == which, value, 0.0).astype(BF16)


def stacked_heads(rows, value):
    width = rows.shape[1]
    if width == HEAD_DIM:
        return rows * jnp.asarray(value, BF16)
    return jnp.concatenate([rows * head_mask(width, inside, value) for inside in range(width // HEAD_DIM)], 0)


def own_blocks(product, count):
    rows = product.shape[1] // count
    return [
        product[inside * HEAD_DIM : (inside + 1) * HEAD_DIM, inside * rows : (inside + 1) * rows]
        for inside in range(count)
    ]


def heads_forward(queries, keys, values_turned, finish, probs_ref):
    rows = queries.shape[0]
    parts = []
    for start, width in groups_of(queries.shape[1]):
        head, count = start // HEAD_DIM, width // HEAD_DIM
        stacked = stacked_heads(queries[:, start : start + width], SCALE)
        logits = finish(head, count, dot_nt(keys[:, start : start + width], stacked))
        expo = jnp.exp(logits - jnp.max(logits, 0, keepdims=True))
        probs = (expo * (1.0 / jnp.sum(expo, 0, keepdims=True))).astype(BF16)
        probs_ref[:, head * rows : (head + count) * rows] = probs
        parts += own_blocks(dot(values_turned[start : start + width], probs), count)
    return jnp.concatenate(parts, 0).astype(BF16)


def heads_backward(grad_context, keys_turned, values, probs_ref, grad_logits_ref):
    rows = grad_context.shape[0]
    parts = []
    for start, width in groups_of(grad_context.shape[1]):
        head, count = start // HEAD_DIM, width // HEAD_DIM
        place = slice(head * rows, (head + count) * rows)
        stacked = stacked_heads(grad_context[:, start : start + width], 1.0)
        grad_probs = dot_nt(values[:, start : start + width], stacked)
        probs = probs_ref[:, place].astype(F32)
        weighted = jnp.sum(grad_probs * probs, 0, keepdims=True)
        grad_logits = (probs * (grad_probs - weighted)).astype(BF16)
        grad_logits_ref[:, place] = grad_logits
        parts += own_blocks(SCALE * dot(keys_turned[start : start + width], grad_logits), count)
    return jnp.concatenate(parts, 0).astype(BF16)


def heads_spread(matrix_ref, rows, factor):
    length = rows.shape[0]
    parts = []
    for start, width in groups_of(rows.shape[1]):
        head, count = start // HEAD_DIM, width // HEAD_DIM
        stacked = stacked_heads(rows[:, start : start + width], 1.0)
        parts.append(factor * dot(matrix_ref[:, head * length : (head + count) * length], stacked))
    return jnp.concatenate(parts, 1).astype(BF16)


def own_rows(core, half):
    return pl.ds(pl.multiple_of(core * half, half), half)


def bucket_onehot(bucket_ref, buckets):
    wanted = lax.broadcasted_iota(jnp.int32, (buckets, bucket_ref.shape[1]), 0)
    return jnp.where(bucket_ref[...] == wanted, 1.0, 0.0)


def add_kernel(left_ref, right_ref, out_ref):
    out_ref[...] = (left_ref[...].astype(F32) + right_ref[...].astype(F32)).astype(out_ref.dtype)


def first_kernel(out):
    out[...] = jnp.zeros_like(out)


def step_kernel(enc_len, objective, language, info, mask):
    info[...] = jnp.full(info.shape, objective[0] * LANGS + language[0], jnp.int32)
    rows = mask.shape[0] // 4
    row = lax.broadcasted_iota(jnp.int32, mask.shape, 0)
    block = row // rows
    flip = jnp.where(block % 2 == 1, 1, 0) + jnp.where(block >= 2, 2, 0)
    position = (lax.axis_index("tensor") ^ flip) * rows + row % rows
    mask[...] = jnp.where(position < enc_len[0], 0.0, NEGATIVE)


def self_sum_kernel(own, first, second, out):
    rows = first.shape[0]
    out[:rows] = both(own[:rows], first[...]).astype(BF16)
    out[rows : 2 * rows] = both(own[rows:], second[...]).astype(BF16)
    out[2 * rows :] = jnp.zeros((out.shape[0] - 2 * rows, out.shape[1]), BF16)


def self_forward_kernel(
    dec_len, bucket, table, x, gain, w_query, w_key, w_value, w_output,
    keep, send, more, normed_out, query_out, context_out, probs_out, dec_out, whole,
):
    dec_out[...] = jnp.full(dec_out.shape, dec_len[0], jnp.int32)
    length = x.shape[0]
    resid = x[...].astype(F32)
    normed = (resid * inverse_rms(resid) * row_of(gain)).astype(BF16)
    normed_out[...] = normed
    queries = dot_nt(normed, w_query[...]).astype(BF16)
    keys = dot_nt(normed, w_key[...]).astype(BF16)
    values = dot_nt(w_value[...], normed).astype(BF16)
    query_out[...] = queries
    by_distance = lax.dot_general(
        table[...],
        bucket_onehot(bucket, table.shape[1]),
        (((1,), (0,)), ((), ())),
        precision=lax.Precision.HIGHEST,
        preferred_element_type=F32,
    )
    row = lax.broadcasted_iota(jnp.int32, (length, length), 0)
    column = lax.broadcasted_iota(jnp.int32, (length, length), 1)
    allowed = (row <= column) & (row < dec_len[0])

    def finish(head, count, scores):
        parts = []
        for inside in range(count):
            spread = jnp.broadcast_to(by_distance[head + inside : head + inside + 1], (length, length))
            bias = pltpu.roll(spread, 0, 1, stride=1, stride_axis=0)
            part = scores[:, inside * length : (inside + 1) * length]
            parts.append(jnp.where(allowed, part + bias, NEGATIVE))
        return jnp.concatenate(parts, 1) if count > 1 else parts[0]

    context = heads_forward(queries, keys, values, finish, probs_out)
    context_out[...] = context.T
    whole[...] = dot_tn(context, w_output[...]).astype(BF16)
    half = keep.shape[0]
    core = lax.axis_index("tensor") % 2
    keep[...] = whole[own_rows(core, half), :]
    rows = send.shape[0]
    send[...] = whole[own_rows(2 - 2 * core, rows), :]
    more[...] = whole[own_rows(3 - 2 * core, rows), :]


def source_rows(parts, start, wk_own, wv_own, wk_peer, wv_peer, k_own, v_own, k_peer, v_peer):
    rows = parts[0].shape[0]
    for index, part in enumerate(parts):
        place = slice(start + index * rows, start + (index + 1) * rows)
        for weight, out in ((wk_own, k_own), (wk_peer, k_peer)):
            out[place, :] = dot_nt(part[...], weight[...]).astype(BF16)
        for weight, out in ((wv_own, v_own), (wv_peer, v_peer)):
            out[:, place] = dot_nt(weight[...], part[...]).astype(BF16)


def source_first_kernel(first, *refs):
    source_rows([first], 0, *refs)


def source_second_kernel(
    first, second, third, wk_own, wv_own, wk_peer, wv_peer, early_k_own, early_v_own, early_k_peer, early_v_peer,
    k_own, v_own, k_peer, v_peer,
):
    rows = first.shape[0]
    for early, out in ((early_k_own, k_own), (early_k_peer, k_peer)):
        out[:rows] = early[...]
    for early, out in ((early_v_own, v_own), (early_v_peer, v_peer)):
        out[:, :rows] = early[...]
    source_rows([first, second, third], rows, wk_own, wv_own, wk_peer, wv_peer, k_own, v_own, k_peer, v_peer)


def source_back_kernel(
    normed, w_key, w_value, e0, e1, e2, e3, wk_own, wv_own, wk_peer, wv_peer,
    keys_turned, values, k_own, v_own, k_peer, v_peer,
):
    keys_turned[...] = dot_nt(w_key[...], normed[...]).astype(BF16)
    values[...] = dot_nt(normed[...], w_value[...]).astype(BF16)
    rows = e0.shape[0]
    for index, part in enumerate((e0, e2, e1, e3)):
        place = slice(index * rows, (index + 1) * rows)
        for weight, out in ((wk_own, k_own), (wk_peer, k_peer)):
            out[:, place] = dot_nt(weight[...], part[...]).astype(BF16)
        for weight, out in ((wv_own, v_own), (wv_peer, v_peer)):
            out[place, :] = dot_nt(part[...], weight[...]).astype(BF16)


def out_grad_kernel(info, dec_len, token_weights, cotangent, grad_own, branch_own, branch_peer):
    half = grad_own.shape[0]
    length = cotangent.shape[0]
    core = lax.axis_index("tensor") % 2
    row = lax.broadcasted_iota(jnp.int32, token_weights.shape, 0)
    weights = jnp.sum(jnp.where(row == info[:1, :1], token_weights[...], 0.0), 0, keepdims=True)
    position = lax.broadcasted_iota(jnp.int32, (1, length), 1)
    weights = jnp.where(position < dec_len[:1, :1], weights, 0.0)

    def rows_of(side):
        row = lax.broadcasted_iota(jnp.int32, (half, length), 0) + side * half
        column = lax.broadcasted_iota(jnp.int32, (half, length), 1)
        factor = jnp.sum(jnp.where(row == column, weights, 0.0), -1, keepdims=True)
        return cotangent[own_rows(side, half), :].astype(F32) * factor

    own = rows_of(core)
    grad_own[...] = own
    branch_own[...] = own.astype(BF16)
    branch_peer[...] = rows_of(1 - core).astype(BF16)


def act_grad_kernel(branch, down_own, down_peer, own, peer):
    own[...] = dot_nt(branch[...], down_own[...])
    peer[...] = dot_nt(branch[...], down_peer[...])


def cross_forward_kernel(
    mask, chip_own, chip_other, x, gain, wq_own, wq_peer, wo_own, wo_peer, k_own, v_own, k_peer, v_peer,
    partial_out, hidden_out, normed_out, q_own, q_peer, context_own, probs_own, probs_peer, pack,
):
    half, width = hidden_out.shape
    core = lax.axis_index("tensor") % 2
    resid = x[own_rows(core, half), :].astype(F32)
    resid = resid + both(chip_own[:half], chip_other[:half])
    hidden_out[...] = resid
    normed = (resid * inverse_rms(resid) * row_of(gain)).astype(BF16)
    normed_out[...] = normed
    pack[:, :width] = normed

    def finish(head, count, scores):
        return scores + jnp.concatenate([mask[...]] * count, 1)

    queries = dot_nt(normed, wq_own[...]).astype(BF16)
    q_own[...] = queries
    first = heads_forward(queries, k_own[...], v_own[...], finish, probs_own)
    context_own[...] = first.T
    queries = dot_nt(normed, wq_peer[...]).astype(BF16)
    q_peer[...] = queries
    second = heads_forward(queries, k_peer[...], v_peer[...], finish, probs_peer)
    pack[:, width:] = second.T
    partial_out[...] = (dot_tn(first, wo_own[...]) + dot_tn(second, wo_peer[...])).astype(BF16)


def through_units(normed, up, act_grad):
    pre = dot(normed, up[...])
    square = pre * pre
    tanh = jnp.tanh(0.7978845608028654 * (pre + 0.044715 * square * pre))
    half_sum = 0.5 * (1.0 + tanh)
    slope = half_sum + 0.5 * pre * (1.0 - tanh * tanh) * (
        0.7978845608028654 * (1.0 + 3.0 * 0.044715 * square)
    )
    return (pre * half_sum).astype(BF16), (act_grad[...] * slope).astype(BF16)


def ffn_peer_kernel(chip_own, chip_other, hidden, gain, up_peer, act_grad_peer, hidden_out, normed_out, part_out, pack):
    width = hidden.shape[1]
    resid = hidden[...] + both(chip_own[...], chip_other[...])
    hidden_out[...] = resid
    normed = (resid * inverse_rms(resid) * row_of(gain)).astype(BF16)
    normed_out[...] = normed
    pack[:, :width] = normed
    act, grad_pre = through_units(normed, up_peer, act_grad_peer)
    units = act.shape[1]
    pack[:, width : width + units] = act
    pack[:, width + units :] = grad_pre
    part_out[...] = dot_nt(grad_pre, up_peer[...])


def ffn_own_kernel(normed, up_own, act_grad_own, part, partial_out, act_own, grad_pre_own):
    act, grad_pre = through_units(normed[...], up_own, act_grad_own)
    act_own[...] = act
    grad_pre_own[...] = grad_pre
    partial_out[...] = (part[...] + dot_nt(grad_pre, up_own[...])).astype(BF16)


def ffn_out_kernel(act_own, pack, down_own, down_peer, out):
    units = act_own.shape[1]
    width = out.shape[1]
    total = dot(act_own[...], down_own[...]) + dot(pack[:, width : width + units], down_peer[...])
    out[...] = total.astype(BF16)


def write_blocks(whole, columns, first_bit, rest_bits, size, targets):
    index = lax.axis_index("dp")
    count = 1 << len(rest_bits)
    for first, target in enumerate(targets):
        for entry in range(count):
            relative = first << first_bit
            for place, bit in enumerate(rest_bits):
                if entry >> (len(rest_bits) - 1 - place) & 1:
                    relative |= 1 << bit
            block = index ^ relative
            target[entry] = whole[pl.ds(pl.multiple_of(block * size, size), size), columns]


def emit(whole, outs, order, size, columns=slice(None)):
    if order is None:
        outs[0][...] = whole[:, columns]
    else:
        write_blocks(whole, columns, order[0], order[1:], size, outs)


def ffn_weights_kernel(orders, size, normed, pack, act_own, grad_pre_own, branch_own, branch_peer, *refs):
    *outs, whole, left, right = refs
    half, width = normed.shape
    units = act_own.shape[1]
    left[:half] = normed[...]
    left[half:] = pack[:, :width]
    right[:half] = grad_pre_own[...]
    right[half:] = pack[:, width + units :]
    whole[...] = dot_tn(left[...], right[...]).astype(BF16)
    count = 1 if orders[0] is None else 2
    emit(whole, outs[:count], orders[0], size)
    left[:half] = branch_own[...]
    left[half:] = branch_peer[...]
    right[:half] = act_own[...]
    right[half:] = pack[:, width : width + units]
    whole[...] = dot_tn(left[...], right[...]).astype(BF16)
    emit(whole, outs[count:], orders[1], size)


def cross_backward_kernel(
    chip_own, chip_other, hidden, gain, grad_out, wo_own, wo_peer, k_own, v_own, k_peer, v_peer,
    probs_own, probs_peer, wq_own, wq_peer,
    partial_out, grad_hidden, gain_grad, gl_own, gl_peer, gc_own, gc_peer, gq_own, branch, pack,
):
    incoming = chip_own[...].astype(F32) + chip_other[...].astype(F32)
    added, gain_terms = norm_back(hidden[...], row_of(gain), incoming)
    gain_grad[...] = jnp.broadcast_to(gain_terms, gain_grad.shape)
    grad = grad_out[...] + added
    grad_hidden[...] = grad
    rounded = grad.astype(BF16)
    branch[...] = rounded
    width = rounded.shape[1]
    pack[:, :width] = rounded
    context = dot_nt(rounded, wo_own[...]).astype(BF16)
    gc_own[...] = context
    queries = heads_backward(context, k_own[...], v_own[...], probs_own, gl_own)
    gq_own[...] = queries.T
    total = dot_tn(queries, wq_own[...])
    context = dot_nt(rounded, wo_peer[...]).astype(BF16)
    gc_peer[...] = context
    queries = heads_backward(context, k_peer[...], v_peer[...], probs_peer, gl_peer)
    pack[:, width:] = queries.T
    total = total + dot_tn(queries, wq_peer[...])
    partial_out[...] = total.astype(BF16)


def source_grad_kernel(gl_peer, probs_peer, gc_peer, q_peer, out):
    span = out.shape[0] // 2
    rows = span // 4
    for start, grads in (
        (0, heads_spread(gl_peer, q_peer[...], SCALE)),
        (span, heads_spread(probs_peer, gc_peer[...], 1.0)),
    ):
        for block in range(4):
            there = start + (block ^ 1) * rows
            out[there : there + rows] = grads[block * rows : (block + 1) * rows]


def cross_weights_kernel(
    orders, size, gl_own, probs_own, gc_own, q_own, other, e0, e1, e2, e3, normed, pack_forward,
    branch, pack_backward, context_own, gq_own, *refs,
):
    *outs, source, whole, left, right = refs
    count = len(outs) // 2
    span = other.shape[0] // 2
    half, width = normed.shape
    columns = q_own.shape[1]
    source[:, :columns] = low_sum(heads_spread(gl_own, q_own[...], SCALE), other[:span])
    source[:, columns:] = low_sum(heads_spread(probs_own, gc_own[...], 1.0), other[span:])
    for index, part in enumerate((e0, e2, e1, e3)):
        left[index * half : (index + 1) * half] = part[...]
    whole[:, : 2 * columns] = dot_tn(left[...], source[...]).astype(BF16)
    left[:half] = normed[...]
    left[half : 2 * half] = pack_forward[:, :width]
    left[2 * half : 3 * half] = branch[...]
    left[3 * half :] = pack_backward[:, :width]
    right[...] = jnp.zeros_like(right)
    right[:half, :columns] = gq_own[...]
    right[half : 2 * half, :columns] = pack_backward[:, width:]
    right[2 * half : 3 * half, columns:] = context_own[...]
    right[3 * half :, columns:] = pack_forward[:, width:]
    whole[:, 2 * columns :] = dot_tn(left[...], right[...]).astype(BF16)
    wide = outs[0].shape[-1]
    emit(whole, outs[:count], orders[0], size, columns=slice(0, wide))
    emit(whole, outs[count:], orders[1], size, columns=slice(wide, None))


def encoded_kernel(source, wk_own, wv_own, keep, send):
    columns = wk_own.shape[0]
    terms = dot(source[:, :columns], wk_own[...]) + dot(source[:, columns:], wv_own[...])
    terms = terms.astype(BF16)
    rows = keep.shape[0] // 2
    for block in range(4):
        target = send if block % 2 else keep
        target[block // 2 * rows : (block // 2 + 1) * rows] = terms[block * rows : (block + 1) * rows]


def self_norm_kernel(chip_own, chip_other, hidden, gain, grad_hidden, gain_ffn, grad_out, pack):
    half = hidden.shape[0]
    incoming = chip_own[...].astype(F32) + chip_other[...].astype(F32)
    added, gain_terms = norm_back(hidden[...], row_of(gain), incoming)
    grad = grad_hidden[...] + added
    grad_out[...] = grad
    pack[:half] = grad.astype(BF16)
    row = lax.broadcasted_iota(jnp.int32, (EXTRA, hidden.shape[1]), 0)
    extra = jnp.where(row == 0, gain_terms, 0.0) + jnp.where(row == 1, gain_ffn[:1], 0.0)
    pack[half:] = extra.astype(BF16)


def high_low(vector):
    high = vector.astype(BF16).astype(F32)
    row = lax.broadcasted_iota(jnp.int32, (EXTRA, vector.shape[1]), 0)
    return (jnp.where(row == 0, high, 0.0) + jnp.where(row == 1, vector - high, 0.0)).astype(BF16)


def of_high_low(rows):
    rows = rows.astype(F32)
    return rows[:1] + rows[1:2]


def self_backward_kernel(
    pack_own, pack_peer, w_output, w_query, w_key, w_value, queries, keys, values, probs, x,
    keep, send, branch_out, gq_out, gk_out, gv_out, gl_out, whole,
):
    half = keep.shape[0] - EXTRA
    core = lax.axis_index("tensor") % 2
    branch_out[own_rows(core, half), :] = pack_own[:half]
    branch_out[own_rows(1 - core, half), :] = pack_peer[:half]
    context = dot_nt(branch_out[...], w_output[...]).astype(BF16)
    grad_queries = heads_backward(context, keys[...], values[...], probs, gl_out)
    grad_keys = heads_spread(gl_out, queries[...], SCALE)
    grad_values = heads_spread(probs, context, 1.0)
    gq_out[...] = grad_queries.T
    gk_out[...] = grad_keys
    gv_out[...] = grad_values
    total = dot_tn(grad_queries, w_query[...]) + dot(grad_keys, w_key[...]) + dot(grad_values, w_value[...])
    whole[...] = total.astype(BF16)
    keep[:half] = whole[own_rows(core, half), :]
    send[:half] = whole[own_rows(1 - core, half), :]
    resid = x[...].astype(F32)
    gain_terms = high_low(jnp.sum(total * resid * inverse_rms(resid), 0, keepdims=True))
    keep[half:] = gain_terms
    send[half:] = gain_terms


def input_sum_kernel(own, peer, out):
    half = out.shape[0] - EXTRA
    out[:half] = both(own[:half], peer[:half]).astype(BF16)
    out[half:] = high_low(of_high_low(own[half:]) + of_high_low(peer[half:]))


def self_weights_kernel(
    orders, size, buckets, normed, branch, gq, gk, gv, context, gl, bucket, pack_own, pack_peer, *refs
):
    *outs, extra_out, whole, right, left = refs
    count = len(outs) // 2
    length, columns = gq.shape
    half = pack_own.shape[0] - EXTRA
    right[:length, :columns] = gq[...]
    right[:length, columns:] = gk[...]
    whole[:, : 2 * columns] = dot_tn(normed[...], right[:length]).astype(BF16)
    left[:length] = normed[...]
    left[length:] = branch[...]
    right[...] = jnp.zeros_like(right)
    right[:length, :columns] = gv[...]
    right[length:, columns:] = context[...]
    whole[:, 2 * columns :] = dot_tn(left[...], right[...]).astype(BF16)
    wide = outs[0].shape[-1]
    emit(whole, outs[:count], orders[0], size, columns=slice(0, wide))
    onehot = bucket_onehot(bucket, buckets)
    row = lax.broadcasted_iota(jnp.int32, (length, length), 0)
    column = lax.broadcasted_iota(jnp.int32, (length, length), 1)
    turn = jnp.where(row + column == length - 1, 1.0, 0.0).astype(BF16)
    place = lax.broadcasted_iota(jnp.int32, (8, length), 0)
    sums = jnp.zeros((8, length), F32)
    heads = gl.shape[1] // length
    for head in range(heads):
        skewed = pltpu.roll(dot(turn, gl[:, head * length : (head + 1) * length]), 1, 1, stride=1, stride_axis=0)
        sums = sums + jnp.where(place == head, jnp.sum(skewed, 0, keepdims=True), 0.0)
    table = lax.dot_general(
        sums, onehot, (((1,), (1,)), ((), ())), precision=lax.Precision.HIGHEST, preferred_element_type=F32
    )
    gains = both(pack_own[half:], pack_peer[half:])
    narrow = outs[-1].shape[-1]
    first, count_rows = extra_rows(gains.shape[1], narrow, heads)
    extra = vector_rows(gains[:1], narrow, count_rows, 0) + vector_rows(gains[1:2], narrow, count_rows, 1)
    table = jnp.concatenate([table, jnp.zeros((8, narrow - buckets), F32)], 1)
    row = lax.broadcasted_iota(jnp.int32, (count_rows, narrow), 0)
    for head in range(heads):
        extra = extra + jnp.where(row == first + head, table[head : head + 1], 0.0)
    extra_out[...] = extra.astype(BF16)
    emit(whole, outs[count:], orders[1], size, columns=slice(wide, None))


def extra_rows(width, wide, heads):
    first = -(-3 * (width // wide) // 4) * 4
    return first, -(-(first + heads) // 16) * 16


def vector_rows(vector, wide, count, which):
    rows = vector.shape[1] // wide
    row = lax.broadcasted_iota(jnp.int32, (count, wide), 0)
    placed = jnp.zeros((count, wide), F32)
    for index in range(rows):
        piece = vector[:, index * wide : (index + 1) * wide]
        placed = placed + jnp.where(row == which * rows + index, piece, 0.0)
    return placed


def encoded_sum_kernel(own, other, keep, send):
    rows = keep.shape[0]
    keep[...] = low_sum(own[:rows], other[:rows])
    send[...] = low_sum(own[rows:], other[rows:])


def input_grad_kernel(chip_own, chip_other, x, gain, grad_hidden, hidden_two, out_own, out_other, pack):
    half = hidden_two.shape[0]
    resid = x[own_rows(lax.axis_index("tensor") % 2, half), :].astype(F32)
    added, _ = norm_back(resid, row_of(gain), both(chip_own[:half], chip_other[:half]))
    pack[:half] = (grad_hidden[...] + added).astype(BF16)
    pack[half:] = (hidden_two[...] + both(out_own[...], out_other[...])).astype(BF16)


def rows_kernel(own, peer, input_grad, layer_out, token):
    half = own.shape[0] // 2
    core = lax.axis_index("tensor") % 2
    for place, out in ((0, input_grad), (half, layer_out)):
        out[own_rows(core, half), :] = own[place : place + half]
        out[own_rows(1 - core, half), :] = peer[place : place + half]
    token[...] = own[: token.shape[0], : token.shape[1]]


def both(left, right):
    return left.astype(F32) + right.astype(F32)


def low_sum(left, right):
    return both(left, right).astype(BF16)


def ffn_second_kernel(up_keep, up_got, down_keep, down_got, up_send, up_next, down_send, down_next):
    for keep, got, send, new in (
        (up_keep, up_got, up_send, up_next),
        (down_keep, down_got, down_send, down_next),
    ):
        for entry in range(2):
            new[entry] = low_sum(keep[entry], got[entry])
            send[entry] = low_sum(keep[2 + entry], got[2 + entry])


def ffn_third_kernel(up_keep, up_got, down_keep, down_got, send, keep):
    size = up_keep.shape[1]
    for entry, target in enumerate((keep, send)):
        target[:size] = low_sum(up_keep[entry], up_got[entry])
        target[size:] = low_sum(down_keep[entry], down_got[entry])


def round_three_kernel(
    ca_keep, ca_got, cb_keep, cb_got, sa_send, sb_send, extra, x_send, zo_send, ca_next, cb_next
):
    for entry in range(2):
        ca_next[entry] = low_sum(ca_keep[entry], ca_got[entry])
        cb_next[entry] = low_sum(cb_keep[entry], cb_got[entry])
    base = spread_out(x_send, [low_sum(cb_keep[2 + entry], cb_got[2 + entry]) for entry in range(2)])
    spread_out(x_send, [sa_send[entry] for entry in range(4)], base)
    base = spread_out(zo_send, [low_sum(ca_keep[2 + entry], ca_got[2 + entry]) for entry in range(2)])
    base = spread_out(zo_send, [sb_send[entry] for entry in range(4)], base)
    spread_out(zo_send, [extra[...]], base)


def gain_kernel(chip_own, chip_other, out):
    half = chip_own.shape[0] - EXTRA
    gain = of_high_low(chip_own[half:]) + of_high_low(chip_other[half:])
    out[...] = vector_rows(gain, out.shape[1], out.shape[0], 0).astype(BF16)


def spread_out(target, parts, start=0):
    for part in parts:
        rows = part.shape[0]
        for side in range(part.shape[1] // PIECE):
            target[start : start + rows] = part[:, side * PIECE : (side + 1) * PIECE]
            start += rows
    return start


def gathered(source, rows, wide, start):
    pieces = [source[start + side * rows : start + (side + 1) * rows] for side in range(wide // PIECE)]
    return jnp.concatenate(pieces, 1) if len(pieces) > 1 else pieces[0]


def round_four_kernel(
    x_got, zo_got, ca_keep, cb_keep, sa_keep, sb_keep, extra, gains, gains_got,
    cross_send, cross_keep, sa_send, sa_next, sb_send, sb_next,
):
    size, ca_wide = ca_keep.shape[1:]
    cb_wide = cb_keep.shape[2]
    large, small = sa_keep.shape[2], sb_keep.shape[2]
    zo_base = 2 * size * ca_wide // PIECE
    x_base = 2 * size * cb_wide // PIECE
    for entry, target in enumerate((cross_keep, cross_send)):
        part = low_sum(ca_keep[entry], gathered(zo_got, size, ca_wide, entry * (zo_base // 2)))
        base = spread_out(target, [part])
        part = low_sum(cb_keep[entry], gathered(x_got, size, cb_wide, entry * (x_base // 2)))
        spread_out(target, [part], base)
    gain = low_sum(gains[...], gains_got[...])
    step = size * (small // PIECE)
    extra = low_sum(extra[...], gathered(zo_got, extra.shape[0], small, zo_base + 4 * step))
    for first, sa_out, sb_out in ((0, sa_next, sb_next), (2, sa_send, sb_send)):
        for entry in range(2):
            part = slice(entry * size, (entry + 1) * size)
            start = x_base + (first + entry) * size * (large // PIECE)
            part_sum = low_sum(sa_keep[first + entry], gathered(x_got, size, large, start))
            base = spread_out(sa_out, [part_sum], entry * size * (large // PIECE))
            start = zo_base + (first + entry) * step
            sb_out[part] = low_sum(sb_keep[first + entry], gathered(zo_got, size, small, start))
        sa_out[base:] = gain
        sb_out[2 * size :] = extra


def round_five_kernel(size, sa_keep, sa_got, sb_keep, sb_got, send, keep):
    small = sb_keep.shape[1]
    extra_count = sb_keep.shape[0] - 2 * size
    step = (sa_keep.shape[0] - EXTRA) // 2
    large = step // size * PIECE
    gain = both(sa_keep[2 * step :], sa_got[2 * step :])
    gain = jnp.concatenate([gain[index : index + 1] for index in range((large + small) // PIECE)], 1)
    extra = vector_rows(gain, small, extra_count, 2) + both(sb_keep[2 * size :], sb_got[2 * size :])
    extra = extra.astype(BF16)
    for entry, target in enumerate((keep, send)):
        part = slice(entry * size, (entry + 1) * size)
        whole = slice(entry * step, (entry + 1) * step)
        target[:step] = low_sum(sa_keep[whole], sa_got[whole])
        part = jnp.concatenate([low_sum(sb_keep[part], sb_got[part]), extra], 0)
        spread_out(target, [part], step)


def ffn_final_kernel(keep, got, up, down):
    size = up.shape[0]
    up[...] = both(keep[:size], got[:size])
    down[...] = both(keep[size:], got[size:])


def cross_final_kernel(keep, got, key, value, query, output):
    size, count = key.shape
    total = both(gathered(keep, size, 4 * count, 0), gathered(got, size, 4 * count, 0))
    for place, out in enumerate((key, value, query)):
        out[...] = total[:, place * count : (place + 1) * count]
    output[...] = total[:, 3 * count :].T


def encoded_out_kernel(own, other, out, token):
    out[...] = low_sum(own[...], other[...])
    token[...] = own[: token.shape[0], : token.shape[1]]


def self_final_kernel(
    large, keep, got, query, key, value, output, table, gain_two, gain_three, gain_one
):
    size, count = key.shape
    small = 4 * count - large
    start = size * (large // PIECE)
    first = both(gathered(keep, size, large, 0), gathered(got, size, large, 0))
    table_row, more = extra_rows(4 * count, small, table.shape[0])
    more += size
    second = both(gathered(keep, more, small, start), gathered(got, more, small, start))
    total = jnp.concatenate([first, second[:size]], 1)
    for place, out in enumerate((query, key, value)):
        out[...] = total[:, place * count : (place + 1) * count]
    output[...] = total[:, 3 * count :].T
    extra = second[size:]
    table[...] = extra[table_row : table_row + table.shape[0], : table.shape[1]]
    wide = 4 * count
    back = wide - lax.axis_index("dp") * size
    rows = wide // small
    for which, out in enumerate((gain_two, gain_three, gain_one)):
        pieces = [extra[which * rows + index : which * rows + index + 1] for index in range(rows)]
        whole = jnp.concatenate(pieces, 1)
        out[...] = pltpu.roll(jnp.broadcast_to(whole, (8, wide)), back, 1)[:1, :size]


def run(kernel, name, outs, ins, us=0.0, scratch=(), scalars=0, far=0, sems=0, after=(), limit=VMEM_LIMIT):
    shapes = [jax.ShapeDtypeStruct(shape, dtype) for shape, dtype in outs]
    idle = len(after)
    body = kernel
    if idle:

        def body(*refs):
            kernel(*refs[: len(ins)], *refs[len(ins) + idle :])

    vmem = pl.BlockSpec(memory_space=pltpu.VMEM)
    hbm = pl.BlockSpec(memory_space=pltpu.HBM)
    free = pl.BlockSpec(memory_space=pl.ANY)
    smem = pl.BlockSpec(memory_space=pltpu.SMEM)
    place = [smem] * scalars + [hbm] * far + [vmem] * (len(ins) - scalars - far) + [free] * idle
    ins = [
        pltpu.with_memory_space_constraint(item, pltpu.HBM) if spec is hbm else item for item, spec in zip(ins, place)
    ]
    result = pl.pallas_call(
        body,
        out_shape=shapes,
        in_specs=place,
        out_specs=[vmem] * len(shapes),
        scratch_shapes=[pltpu.VMEM(shape, dtype) for shape, dtype in scratch]
        + ([pltpu.SemaphoreType.DMA((sems,))] if sems else []),
        compiler_params=pltpu.CompilerParams(vmem_limit_bytes=limit),
        cost_estimate=pl.CostEstimate(flops=int(us * 1.15e9), bytes_accessed=0, transcendentals=0),
        name=name,
    )(*ins, *after)
    return result[0] if len(shapes) == 1 else result


def listed(result):
    return list(result) if isinstance(result, (list, tuple)) else [result]


def to_core(value):
    return lax.ppermute(value, "tensor", [(i, i ^ 1) for i in range(lax.axis_size("tensor"))])


def to_chip(value):
    return lax.ppermute(value, "tensor", [(i, i ^ 2) for i in range(lax.axis_size("tensor"))])


def to_peer(value, bit):
    return lax.ppermute(value, "dp", [(i, i ^ (1 << bit)) for i in range(lax.axis_size("dp"))])


def on_device(
    inputs, encoded, dec_len, enc_len, language, objective, distance_bucket, token_weights, cotangent,
    gain_self, self_query, self_key, self_value, self_output, bias_table,
    gain_cross, cross_query, cross_key, cross_value, cross_output, gain_ffn, ffn_up, ffn_down,
):
    seqs, length, width = inputs.shape
    half = length // 2
    columns = self_query.shape[1]
    heads = columns // HEAD_DIM
    units = ffn_up.shape[1]
    span_part = encoded.shape[1]
    span = span_part * lax.axis_size("tensor")
    dp = lax.axis_size("dp")
    size = width // dp
    bits = dp.bit_length() - 1
    halving = bits == 3 and dp == 8 and size % 16 == 0
    along_x, along_z = ((0, 1, 2), (1, 0, 2)) if halving else (None, None)
    latest = []

    def go(kernel, name, outs, ins, last=False, **how):
        after = [item for item in latest if not any(item is one for one in ins)]
        result = run(kernel, name, outs, ins, after=after, **how)
        if not last:
            results = result if isinstance(result, (list, tuple)) else [result]
            latest[:] = [min(results, key=lambda item: item.size * item.dtype.itemsize)]
        return result

    def plus(left, right, name):
        return go(add_kernel, name, [(left.shape, left.dtype)], [left, right])

    def payload(order, wide):
        if order is None:
            return [((width, wide), BF16)]
        return [((dp // 2, size, wide), BF16)] * 2

    x = inputs.reshape(length, width)
    cot = cotangent.reshape(length, width)
    gain_one, gain_two, gain_three = gain_self, gain_cross, gain_ffn
    self_query, self_key, self_value = self_query.T, self_key.T, self_value.T
    cross_query, cross_key, cross_value = cross_query.T, cross_key.T, cross_value.T
    table = bias_table.T
    bucket = distance_bucket.reshape(1, length)
    e0 = encoded.reshape(span_part, width)

    first = go(first_kernel, "first", [((8, 128), F32)], [], us=LONG)
    key_source, value_source, _ = lax.optimization_barrier((cross_key, cross_value, first))
    e1 = to_chip(e0)
    e2 = to_core(e0)
    wk_peer = to_core(key_source)
    wv_peer = to_core(value_source)
    keep, send, more, normed_one, query_one, context_one, probs_one, dec_rows = go(
        self_forward_kernel, "self_forward",
        [((half, width), BF16)] + [((half // 2, width), BF16)] * 2 + [((length, width), BF16)]
        + [((length, columns), BF16)] * 2 + [((length, heads * length), BF16), ((8, 128), jnp.int32)],
        [dec_len, bucket, table, x, gain_one, self_query, self_key, self_value, self_output],
        scratch=[((length, width), BF16)], scalars=1, us=3.5,
    )
    first_half, second_half = to_core(send), to_core(more)
    early = go(
        source_first_kernel, "source_first", [((span_part, columns), BF16), ((columns, span_part), BF16)] * 2,
        [e0, cross_key, cross_value, wk_peer, wv_peer],
    )
    chip_one = go(self_sum_kernel, "self_sum", [((half + EXTRA, width), BF16)], [keep, first_half, second_half])
    other_one = to_chip(chip_one)
    wq_peer = to_core(cross_query)
    wo_peer = to_core(cross_output)
    e3 = to_core(e1)
    late = go(
        source_second_kernel, "source_second", [((span, columns), BF16), ((columns, span), BF16)] * 2,
        [e2, e1, e3, cross_key, cross_value, wk_peer, wv_peer, *early],
    )
    enc_len, objective, language, _ = lax.optimization_barrier((enc_len, objective, language, late[0]))
    info, mask = go(
        step_kernel, "step", [((8, 128), jnp.int32), ((span, half), F32)], [enc_len, objective, language], scalars=3
    )
    up_source, down_source, _ = lax.optimization_barrier((ffn_up, ffn_down, late[0]))
    down_peer = to_core(down_source)
    up_peer = to_core(up_source)

    partial_two, hidden_one, normed_two, q_own, q_peer, context_own, probs_own, probs_peer, pack_forward = go(
        cross_forward_kernel, "cross_forward",
        [((half, width), BF16), ((half, width), F32), ((half, width), BF16)] + [((half, columns), BF16)] * 3
        + [((span, heads * half), BF16)] * 2 + [((half, width + columns), BF16)],
        [mask, chip_one, other_one, x, gain_two, cross_query, wq_peer, cross_output, wo_peer, *late],
    )
    other_two = to_chip(partial_two)
    pack_forward_peer = to_core(pack_forward)
    grad_full, branch_three, branch_three_peer = go(
        out_grad_kernel, "out_grad", [((half, width), F32)] + [((half, width), BF16)] * 2,
        [info, dec_rows, token_weights, cot], us=LONG,
    )
    act_grad, act_grad_peer = go(
        act_grad_kernel, "act_grad", [((half, units), F32)] * 2, [branch_three, ffn_down, down_peer]
    )
    key_one, value_one, k_own, v_own, k_peer, v_peer = go(
        source_back_kernel, "source_back",
        [((columns, length), BF16), ((length, columns), BF16)] + [((columns, span), BF16), ((span, columns), BF16)] * 2,
        [normed_one, self_key, self_value, e0, e1, e2, e3, cross_key, cross_value, wk_peer, wv_peer],
    )

    latest.append(pack_forward_peer)
    hidden_two, normed_three, part_three, pack_ffn = go(
        ffn_peer_kernel, "ffn_peer",
        [((half, width), F32), ((half, width), BF16), ((half, width), F32), ((half, width + 2 * units), BF16)],
        [partial_two, other_two, hidden_one, gain_three, up_peer, act_grad_peer],
    )
    pack_ffn_peer = to_core(pack_ffn)
    partial_three, act_own, grad_pre_own = go(
        ffn_own_kernel, "ffn_own", [((half, width), BF16)] + [((half, units), BF16)] * 2,
        [normed_three, ffn_up, act_grad, part_three],
    )
    other_three = to_chip(partial_three)

    def ffn_weights(*refs):
        ffn_weights_kernel((along_x, along_z), size, *refs)

    ffn_payloads = go(
        ffn_weights, "ffn_weights", payload(along_x, width) + payload(along_z, width),
        [normed_three, pack_ffn_peer, act_own, grad_pre_own, branch_three, branch_three_peer],
        scratch=[((width, units), BF16), ((length, width), BF16), ((length, units), BF16)], us=FILL,
    )

    (partial_four, grad_two, gain_grad_three, gl_own, gl_peer, gc_own, gc_peer, gq_own, branch_two,
     pack_backward) = go(
        cross_backward_kernel, "cross_backward",
        [((half, width), BF16), ((half, width), F32), ((8, width), F32)] + [((span, heads * half), BF16)] * 2
        + [((half, columns), BF16)] * 3 + [((half, width), BF16), ((half, width + columns), BF16)],
        [partial_three, other_three, hidden_two, gain_three, grad_full, cross_output, wo_peer,
         k_own, v_own, k_peer, v_peer, probs_own, probs_peer, cross_query, wq_peer],
    )
    other_four = to_chip(partial_four)
    pack_backward_peer = to_core(pack_backward)
    source_grad = go(
        source_grad_kernel, "source_grad", [((2 * span, columns), BF16)], [gl_peer, probs_peer, gc_peer, q_peer]
    )
    source_grad_peer = to_core(source_grad)
    wide = 2 * columns
    ca_wide, cb_wide = (CROSS_X, 2 * wide - CROSS_X) if halving else (wide, wide)

    def cross_weights(*refs):
        cross_weights_kernel((along_x, along_z), size, *refs)

    *cross_payload, source_total = go(
        cross_weights, "cross_weights",
        payload(along_x, ca_wide) + payload(along_z, cb_wide) + [((span, wide), BF16)],
        [gl_own, probs_own, gc_own, q_own, source_grad_peer, e0, e1, e2, e3, normed_two, pack_forward_peer,
         branch_two, pack_backward_peer, context_own, gq_own],
        scratch=[((width, 2 * wide), BF16), ((span, width), BF16), ((4 * half, wide), BF16)],
    )
    ca_payload, cb_payload = cross_payload[: len(cross_payload) // 2], cross_payload[len(cross_payload) // 2 :]
    branch_out = go(ffn_out_kernel, "ffn_out", [((half, width), BF16)], [act_own, pack_ffn, ffn_down, down_peer])

    grad_one, pack_self = go(
        self_norm_kernel, "self_norm", [((half, width), F32), ((half + EXTRA, width), BF16)],
        [partial_four, other_four, hidden_one, gain_two, grad_two, gain_grad_three],
    )
    pack_self_peer = to_core(pack_self)

    if halving:
        up_keep, up_send, down_keep, down_send = ffn_payloads
        half_sent = ((2, size, width), BF16)
        up_send, up_keep, down_send, down_keep = go(
            ffn_second_kernel, "ffn_second", [half_sent] * 4,
            [up_keep, to_peer(up_send, 0), down_keep, to_peer(down_send, 1)], us=1.0,
        )
        up_got = to_peer(up_send, 1)
        down_got = to_peer(down_send, 0)

    keep, send, branch_one, gq_one, gk_one, gv_one, gl_one = go(
        self_backward_kernel, "self_backward",
        [((half + EXTRA, width), BF16)] * 2 + [((length, width), BF16)] + [((length, columns), BF16)] * 3
        + [((length, heads * length), BF16)],
        [pack_self, pack_self_peer, self_output, self_query, self_key, self_value, query_one, key_one, value_one,
         probs_one, x],
        scratch=[((length, width), BF16)],
    )
    got = to_core(send)
    large, small = (SELF_X, 2 * wide - SELF_X) if halving else (wide, wide)
    table_row, extra_count = extra_rows(width, small, heads)

    def self_weights(*refs):
        self_weights_kernel((along_x, along_z), size, table.shape[1], *refs)

    *self_payload, extra = listed(go(
        self_weights, "self_weights",
        payload(along_x, large) + payload(along_z, small) + [((extra_count, small), BF16)],
        [normed_one, branch_one, gq_one, gk_one, gv_one, context_one, gl_one, bucket, pack_self, pack_self_peer],
        scratch=[((width, 2 * wide), BF16), ((2 * length, wide), BF16), ((2 * length, width), BF16)],
    ))
    sa_payload, sb_payload = self_payload[: len(self_payload) // 2], self_payload[len(self_payload) // 2 :]

    if halving:
        ca_keep, ca_send = ca_payload
        cb_keep, cb_send = cb_payload
        sa_keep, sa_send = sa_payload
        sb_keep, sb_send = sb_payload
        more = size + extra_count
        x_rows = (2 * size * cb_wide + 4 * size * large) // PIECE
        zo_rows = (2 * size * ca_wide + (4 * size + extra_count) * small) // PIECE
        x_send, zo_send, ca_keep, cb_keep = go(
            round_three_kernel, "round_three",
            [((x_rows, PIECE), BF16), ((zo_rows, PIECE), BF16), ((2, size, ca_wide), BF16), ((2, size, cb_wide), BF16)],
            [ca_keep, to_peer(ca_send, 0), cb_keep, to_peer(cb_send, 1), sa_send, sb_send, extra], us=1.6,
        )
        x_got = to_peer(x_send, 0)
        zo_got = to_peer(zo_send, 1)

    chip_five = go(input_sum_kernel, "input_sum", [(keep.shape, BF16)], [keep, got])
    other_five = to_chip(chip_five)

    if halving:
        ffn_send, ffn_keep = go(
            ffn_third_kernel, "ffn_third", [((2 * size, width), BF16)] * 2, [up_keep, up_got, down_keep, down_got]
        )
        ffn_got = to_peer(ffn_send, 2)
        gains = go(gain_kernel, "gain", [((EXTRA, PIECE), BF16)], [chip_five, other_five], us=LONG)
        gains_got = to_peer(gains, 0)
        branch_source, _ = lax.optimization_barrier((branch_out, gains))
    else:
        branch_source = branch_out
    out_other = to_chip(branch_source)

    if halving:
        rows = 2 * size + extra_count
        cross_send, cross_keep, sa_send, sa_keep, sb_send, sb_keep = go(
            round_four_kernel, "round_four",
            [((size * 2 * wide // PIECE, PIECE), BF16)] * 2 + [((2 * size * large // PIECE + EXTRA, PIECE), BF16)] * 2
            + [((rows, small), BF16)] * 2,
            [x_got, zo_got, ca_keep, cb_keep, sa_keep, sb_keep, extra, gains, gains_got],
        )
        sa_got = to_peer(sa_send, 1)
        sb_got = to_peer(sb_send, 0)

    pack_rows = go(
        input_grad_kernel, "input_grad", [((2 * half, width), BF16)],
        [chip_five, other_five, x, gain_one, grad_one, hidden_two, branch_out, out_other],
    )
    pack_rows_peer = to_core(pack_rows)
    if halving:
        cross_send, _ = lax.optimization_barrier((cross_send, pack_rows))
        cross_got = to_peer(cross_send, 2)

    encoded_keep, encoded_send = go(
        encoded_kernel, "encoded", [((span // 2, width), BF16)] * 2, [source_total, cross_key, cross_value]
    )
    encoded_got = to_core(encoded_send)

    if halving:
        up, down = go(ffn_final_kernel, "ffn_final", [((size, width), F32)] * 2, [ffn_keep, ffn_got], us=LONG, last=True)

    encoded_part, encoded_pass = go(
        encoded_sum_kernel, "encoded_sum", [((span_part, width), BF16)] * 2, [encoded_keep, encoded_got]
    )
    encoded_other = to_chip(encoded_pass)

    if halving:
        rows = (size * large + more * small) // PIECE

        def round_five(*refs):
            round_five_kernel(size, *refs)

        self_send, self_keep = go(
            round_five, "round_five", [((rows, PIECE), BF16)] * 2, [sa_keep, sa_got, sb_keep, sb_got]
        )
        self_got = to_peer(self_send, 2)
        square = ((size, columns), F32)
        turned = ((columns, size), F32)
        grad_cross_key, grad_cross_value, grad_cross_query, grad_cross_output = go(
            cross_final_kernel, "cross_final", [square] * 3 + [turned], [cross_keep, cross_got], us=LONG, last=True
        )

    input_grad, layer_out, _ = go(
        rows_kernel, "rows", [((length, width), BF16)] * 2 + [((16, 128), BF16)], [pack_rows, pack_rows_peer]
    )

    if halving:

        def self_final(*refs):
            self_final_kernel(large, *refs)

        encoded_grad, _ = go(
            encoded_out_kernel, "encoded_out", [((span_part, width), BF16), ((16, 128), BF16)],
            [encoded_part, encoded_other],
        )
        (grad_self_query, grad_self_key, grad_self_value, grad_self_output, grad_table, grad_gain_two,
         grad_gain_three, grad_gain_one) = go(
            self_final, "self_final",
            [square] * 3 + [turned, (table.shape, F32)] + [((1, size), F32)] * 3, [self_keep, self_got], last=True,
        )
        grad_gain_one, grad_gain_two, grad_gain_three = (
            item.reshape(size) for item in (grad_gain_one, grad_gain_two, grad_gain_three)
        )
    else:
        index = lax.axis_index("dp")

        def gain_part(*rows):
            row = lax.psum(jnp.concatenate(rows, 0).astype(F32), "dp")
            return lax.dynamic_slice(row, (index * size,), (size,))

        def scattered(item):
            return lax.psum_scatter(item.astype(F32), "dp", scatter_dimension=0, tiled=True)

        def pair_of(item):
            item = scattered(item)
            return item[:, :columns], item[:, columns:]

        up, down = (scattered(item) for item in ffn_payloads)
        grad_cross_key, grad_cross_value = pair_of(ca_payload[0])
        grad_cross_query, grad_cross_output = pair_of(cb_payload[0])
        grad_self_query, grad_self_key = pair_of(sa_payload[0])
        grad_self_value, grad_self_output = pair_of(sb_payload[0])
        grad_cross_output, grad_self_output = grad_cross_output.T, grad_self_output.T
        grad_table = lax.psum(extra[table_row : table_row + heads, : table.shape[1]].astype(F32), "dp")
        encoded_grad = plus(encoded_part, encoded_other, "encoded_grad")
        gain_rows = [item[half : half + 2] for item in (chip_five, other_five)]
        grad_gain_one = gain_part(jnp.sum(jnp.concatenate(gain_rows, 0).astype(F32), 0))
        grad_gain_two = gain_part(extra[0], extra[1])
        grad_gain_three = gain_part(extra[2], extra[3])

    return (
        layer_out.reshape(seqs, length, width),
        input_grad.reshape(seqs, length, width),
        encoded_grad.reshape(seqs, span_part, width),
        grad_gain_one,
        grad_self_query,
        grad_self_key,
        grad_self_value,
        grad_self_output,
        grad_table.T,
        grad_gain_two,
        grad_cross_query,
        grad_cross_key,
        grad_cross_value,
        grad_cross_output,
        grad_gain_three,
        up,
        down.T,
    )


def solution(mesh):
    return jax.shard_map(
        on_device,
        mesh=mesh,
        in_specs=(
            P("dp", None, None),
            P("dp", "tensor", None),
            P("dp"),
            P("dp"),
            P("dp"),
            P("dp"),
            P(),
            P(),
            P("dp", None, None),
            P(),
            P(None, "tensor"),
            P(None, "tensor"),
            P(None, "tensor"),
            P("tensor", None),
            P(None, "tensor"),
            P(),
            P(None, "tensor"),
            P(None, "tensor"),
            P(None, "tensor"),
            P("tensor", None),
            P(),
            P(None, "tensor"),
            P("tensor", None),
        ),
        out_specs=(
            P("dp", None, None),
            P("dp", None, None),
            P("dp", "tensor", None),
            P("dp"),
            P("dp", "tensor"),
            P("dp", "tensor"),
            P("dp", "tensor"),
            P("tensor", "dp"),
            P(None, "tensor"),
            P("dp"),
            P("dp", "tensor"),
            P("dp", "tensor"),
            P("dp", "tensor"),
            P("tensor", "dp"),
            P("dp"),
            P("dp", "tensor"),
            P("tensor", "dp"),
        ),
        check_vma=False,
    )
```
